32 devices in a mesh: seq: 8 (over z, y), head: 4 (over x, core).
Axes of the slice: x: 2, y: 2, z: 4, core: 2. Of those that a mesh axis runs over, the one named last changes fastest.
Arguments:
- acts: bfloat16 [8192, 1024], P('seq', 'head'), may hold values from -6 to 6
- cotangent: bfloat16 [8192, 1024], P('seq', 'head'), may hold values from -6 to 6
- lengths: int32 [8], replicated, may hold values from 1 to 2048, 8192 in all
- keep_mask: int32 [8192], P('seq'), may hold values 0 or 1
- ln_gain: float32 [2, 2, 1024], replicated, may hold values from 0.25 to 1.75
- ln_bias: float32 [2, 2, 1024], replicated, may hold values from -4 to 4
- qkv_w: bfloat16 [2, 1024, 3072], P(None, None, 'head'), may hold values from -0.1875 to 0.1875
- qkv_b: float32 [2, 3072], P(None, 'head'), may hold values from -4 to 4
- feat_w: float32 [2, 16, 64], P(None, 'head'), may hold values from 0.25 to 4
- out_w: bfloat16 [2, 1024, 1024], P(None, None, 'head'), may hold values from -1 to 1
- up_w: bfloat16 [2, 1024, 4096], P(None, None, 'head'), may hold values from -0.1875 to 0.1875
- up_b: float32 [2, 4096], P(None, 'head'), may hold values from -4 to 4
- down_w: bfloat16 [2, 1024, 4096], P(None, None, 'head'), may hold values from -0.09375 to 0.09375
- res_b: float32 [2, 1024], replicated, may hold values from -6 to 6
Outputs:
- out_acts: float32 [8192, 1024], P('seq', 'head')
- d_acts: float32 [8192, 1024], P('seq', 'head')
- d_qkv_w: float32 [2, 1024, 3072], P(None, 'seq', 'head')
- d_out_w: float32 [2, 1024, 1024], P(None, 'seq', 'head')
- d_up_w: float32 [2, 1024, 4096], P(None, 'seq', 'head')
- d_down_w: float32 [2, 1024, 4096], P(None, 'seq', 'head')
- d_qkv_b: float32 [2, 3072], P(None, 'head')
- d_up_b: float32 [2, 4096], P(None, 'head')
- d_feat: float32 [2, 16, 64], P(None, 'head')
- d_ln_gain: float32 [2, 2, 1024], P(None, None, 'head')
- d_ln_bias: float32 [2, 2, 1024], P(None, None, 'head')
- d_res_b: float32 [2, 1024], P(None, 'head')
The draws below stay inside these ranges and needn't reach their ends.
Inputs may be any that keep to these rules, and one draw needn't show every extreme that they name: The lengths sum to 8192; one of them is exactly 2048.
All inputs are finite; a program needn't handle non-finite values. No bound on the sum of `keep_mask` on one device may be relied on, other than what follows from the above.
Results may differ from the reference program's by a relative error of at most 0.03.
Values may be sent and summed in bfloat16 or wider, within the bound.
A program may use at most 192 MiB of HBM per device.

```python
import math
import jax
import jax.numpy as jnp
import numpy as np
from jax import lax

D = 1024
HEADS = 16
HEAD_DIM = 64
ROT = 16
FF = 4096
FEATURES = 64
BLOCK = 64
LAYERS = 2
TOKENS = 8192
SEQS = 8
LONGEST = 2048


def touch_ends(values, own_key, smallest, top_value):
    spot = [jax.random.randint(jax.random.fold_in(own_key, axis), (), 0, length) for axis, length in enumerate(values.shape)]
    longest = values.shape.index(max(values.shape))
    neighbour = spot[:longest] + [(spot[longest] + 1) % values.shape[longest]] + spot[longest + 1:]
    return values.at[tuple(spot)].set(smallest).at[tuple(neighbour)].set(top_value)


def spiked(entries, key, source, target, shards_of, factor):
    owner, partner = [(jnp.arange(entries.shape[position]) // (entries.shape[position] // shards_of)).reshape([-1 if axis == position else 1 for axis in range(entries.ndim)]) for position in (source, target)]
    chosen = jax.random.permutation(key, shards_of)[partner]
    strong = (owner == chosen) | (owner == (partner + shards_of // 2) % shards_of)
    return jnp.where(strong, factor * entries, entries)


def shard_levels(own_key, dims, split, low, largest):
    def one(axis_at, shards_of):
        heights = jax.random.uniform(jax.random.fold_in(jax.random.fold_in(own_key, 6), axis_at), (shards_of,), jnp.float32, low / len(split), largest / len(split))
        return jnp.repeat(jnp.exp(heights), dims[axis_at] // shards_of).reshape((-1,) + (1,) * (len(dims) - axis_at - 1))

    factor_of = one(*split[0])
    for cut in split[1:]:
        factor_of = factor_of * one(*cut)
    return factor_of


def length_profile(count, total, most, skew):
    loads = [(1 << 20) // math.isqrt(standing ** skew) + 1 for standing in range(2, count + 1)]
    spare, holding = total - most - (count - 1), [1] * (count - 1)
    while spare > 0:
        movable = [i for i in range(count - 1) if holding[i] < most]
        mass, left = sum([loads[i] for i in movable]), spare
        for i in movable:
            more = min(most - holding[i], max(1, left * loads[i] // mass), spare)
            holding[i] = holding[i] + more
            spare = spare - more
    return np.array([most] + holding)


def ragged(own_key, number_of, total, bound, slope):
    if number_of == 2:
        one = jax.random.randint(own_key, (), max(1, total - bound), min(bound, total - 1) + 1)
        return jnp.stack([one, total - one])
    sizes = jnp.asarray(length_profile(number_of, total, bound, slope), jnp.int32)
    couples = (number_of - 1) // 2
    giver, sink = sizes[1:1 + 2 * couples:2], sizes[2:2 + 2 * couples:2]
    slack = jnp.minimum(giver - 1, bound - sink)
    shifted = jax.random.randint(jax.random.fold_in(own_key, 1), (couples,), 0, 1 << 20) % (slack + 1)
    sizes = sizes.at[1:1 + 2 * couples:2].set(giver - shifted).at[2:2 + 2 * couples:2].set(sink + shifted)
    return sizes[jax.random.permutation(jax.random.fold_in(own_key, 2), number_of)]


def noise(stream_key, extent, deviation, most, split=(), kind=jnp.bfloat16):
    values = deviation * jax.random.normal(stream_key, extent, jnp.float32)
    if split:
        values = values * shard_levels(stream_key, extent, split, -0.22, 0.18)
    return jnp.clip(values, -most, most).astype(kind)


def gaussian_with(own_key, shape, scale, bound, pieces, heavy, kind=jnp.bfloat16):
    drawn = scale * jax.random.normal(own_key, shape, jnp.float32)
    if pieces:
        drawn = drawn * shard_levels(own_key, shape, pieces, -0.22, 0.18)
    return jnp.clip(spiked(drawn, jax.random.fold_in(own_key, 3), *heavy), -bound, bound).astype(kind)


def setup_inputs(seed: int = 0) -> dict:
    key_of = jax.random.split(jax.random.key(seed), 15)
    acts = noise(key_of[0], (TOKENS, D), 1.0, 6.0, ((0, 8), (1, 4)))
    cotangent = gaussian_with(key_of[1], (TOKENS, D), 1.0, 6.0, ((0, 8), (1, 4)), (0, 1, 8, 2.0))
    lengths = ragged(key_of[2], SEQS, TOKENS, LONGEST, 1).astype(jnp.int32)
    keep_mask = touch_ends((jax.random.randint(key_of[3], (TOKENS,), 0, 8) < 7).astype(jnp.int32), jax.random.fold_in(key_of[3], 1), 0, 1)
    ln_gain = jnp.clip(1.0 + 0.15 * jax.random.normal(key_of[4], (LAYERS, 2, D), jnp.float32), 0.25, 1.75)
    ln_bias = noise(key_of[5], (LAYERS, 2, D), 0.3, 4.0, (), jnp.float32)
    qkv_w = noise(key_of[6], (LAYERS, D, 3 * D), D ** -0.5, 0.1875, ((2, 4),))
    qkv_b = noise(key_of[7], (LAYERS, 3 * D), 0.3, 4.0, ((1, 4),), jnp.float32)
    feat_w = jnp.clip(jnp.exp(math.log(4.0) - 2.7725887 * jax.random.uniform(key_of[8], (LAYERS, HEADS, FEATURES), jnp.float32) ** shard_levels(key_of[8], (LAYERS, HEADS, FEATURES), ((1, 4),), -0.2, 0.2)), 0.25, 4.0)
    out_w = noise(key_of[9], (LAYERS, D, D), (D // 32) ** -0.5, 1.0, ((2, 4),))
    up_w = noise(key_of[10], (LAYERS, D, FF), D ** -0.5, 0.1875, ((2, 4),))
    up_b = noise(key_of[11], (LAYERS, FF), 0.3, 4.0, ((1, 4),), jnp.float32)
    down_w = noise(key_of[12], (LAYERS, D, FF), FF ** -0.5, 0.09375, ((2, 4),))
    res_b = noise(key_of[13], (LAYERS, D), 0.5, 6.0, (), jnp.float32)
    return {"acts": acts, "cotangent": cotangent, "lengths": lengths, "keep_mask": keep_mask, "ln_gain": ln_gain, "ln_bias": ln_bias, "qkv_w": qkv_w, "qkv_b": qkv_b, "feat_w": feat_w, "out_w": out_w, "up_w": up_w, "up_b": up_b, "down_w": down_w, "res_b": res_b}


EPSILON = 1e-05
ROTARY_BASE = 10000.0
HIGHEST = lax.Precision.HIGHEST

@jax.custom_vjp
def low(v):
    return lax.optimization_barrier(v.astype(jnp.bfloat16)).astype(jnp.float32)

@jax.custom_vjp
def low_back(v):
    return v

def low_keep(v):
    return (low(v), None)

def low_pass(kept, grad):
    return (grad,)

def back_keep(v):
    return (v, None)

def back_low(kept, grad):
    return (low(grad),)
low.defvjp(low_keep, low_pass)
low_back.defvjp(back_keep, back_low)

def prime_numbers(count):
    found = []
    candidate = 2
    while len(found) < count:
        if all((candidate % prime != 0 for prime in found)):
            found.append(candidate)
        candidate = candidate + 1
    return found

def sample_points(rows, columns):
    roots = np.sqrt(np.array(prime_numbers(2 * columns)) * 1.0)
    fractions = roots - np.floor(roots)
    grid = np.outer(np.arange(1, rows + 1) * 1.0, fractions) % 1.0
    radius = np.sqrt(-2.0 * np.log(1.0 - grid[:, :columns]))
    return jnp.asarray(radius * np.cos(2.0 * math.pi * grid[:, columns:]), dtype=jnp.float32)

def cosine_table(size):
    wave = np.arange(size)[:, None] * 1.0
    place = np.arange(size)[None, :] * 1.0
    table = np.cos(math.pi * (place + 0.5) * wave / size) * math.sqrt(2.0 / size)
    table = table * np.where(wave == 0, math.sqrt(0.5), 1.0)
    return jnp.asarray(table, dtype=jnp.float32)

def rotate_pairs(vectors, positions):
    half = ROT // 2
    rates = ROTARY_BASE ** (-2.0 * jnp.arange(half, dtype=jnp.float32) / ROT)
    phase = positions[:, None] * rates[None, :]
    cosine = jnp.cos(phase)[:, None, :]
    sine = jnp.sin(phase)[:, None, :]
    first = vectors[..., :half]
    second = vectors[..., half:ROT]
    return jnp.concatenate([first * cosine - second * sine, second * cosine + first * sine, vectors[..., ROT:]], axis=-1)

def feature_maps(projected, positions, keep, weights, cosine, points):
    count = projected.shape[0]
    heads = projected.shape[1] // (3 * HEAD_DIM)
    parts = projected.reshape(count, heads, 3, HEAD_DIM)
    queries = rotate_pairs(parts[:, :, 0], positions)
    keys = rotate_pairs(parts[:, :, 1], positions)
    scale = HEAD_DIM ** (-0.5)
    query_turn = jnp.einsum('thd,ed->the', queries, cosine, precision=HIGHEST) * scale
    key_turn = jnp.einsum('thd,ed->the', keys, cosine, precision=HIGHEST) * scale
    query_feat = jnp.exp(jnp.einsum('the,fe->thf', query_turn, points, precision=HIGHEST))
    key_norm = 0.5 * lax.optimization_barrier(jnp.sum(key_turn * key_turn, axis=-1, keepdims=True))
    key_feat = keep[:, None, None] * weights[None] * jnp.exp(jnp.einsum('the,fe->thf', key_turn, points, precision=HIGHEST) - key_norm)
    return (query_feat, key_feat, parts[:, :, 2])

def segment_of(index, starts):
    return lax.optimization_barrier(jnp.sum((starts[None, 1:] <= index[:, None]).astype(jnp.int32), axis=1))

def attend_all(query_feat, key_feat, values, segment, before, after):
    blocks = TOKENS // BLOCK
    heads = query_feat.shape[1]
    order = jnp.arange(BLOCK)
    lower = order[:, None] >= order[None, :]

    def advance(carry, inputs):
        state, total = carry
        query_block, key_block, value_block, seg_block, label_before, label_after = inputs
        pairs = ((seg_block[:, None] == seg_block[None, :]) & lower).astype(jnp.float32)
        scores = low_back(jnp.einsum('thf,shf->hts', query_block, key_block, precision=HIGHEST) * pairs[None])
        inner_den = lax.optimization_barrier(jnp.sum(scores, axis=-1))
        inner_num = low_back(jnp.einsum('hts,shd->thd', low(scores), value_block, precision=HIGHEST))
        use_state = (seg_block == label_before).astype(jnp.float32)
        outer_num = use_state[:, None, None] * jnp.einsum('thf,hfd->thd', query_block, state, precision=HIGHEST)
        outer_den = use_state[:, None] * jnp.einsum('thf,hf->th', query_block, total, precision=HIGHEST)
        in_state = (seg_block == label_after).astype(jnp.float32)[:, None, None]
        masked_keys = key_block * in_state
        passing = (label_after == label_before).astype(jnp.float32)
        state = passing * state + jnp.einsum('thf,thd->hfd', masked_keys, value_block, precision=HIGHEST)
        total = passing * total + lax.optimization_barrier(jnp.sum(masked_keys, axis=0))
        return ((state, total), (inner_num + outer_num, inner_den.T + outer_den))
    inputs = (query_feat.reshape(blocks, BLOCK, heads, FEATURES), key_feat.reshape(blocks, BLOCK, heads, FEATURES), values.reshape(blocks, BLOCK, heads, HEAD_DIM), segment.reshape(blocks, BLOCK), before, after)
    start = (jnp.zeros((heads, FEATURES, HEAD_DIM), jnp.float32), jnp.zeros((heads, FEATURES), jnp.float32))
    unused, (numer, denom) = lax.scan(jax.checkpoint(advance), start, inputs)
    return (numer.reshape(TOKENS, heads, HEAD_DIM), denom.reshape(TOKENS, heads))

def reference(acts, cotangent, lengths, keep_mask, ln_gain, ln_bias, qkv_w, qkv_b, feat_w, out_w, up_w, up_b, down_w, res_b):
    starts = (jnp.cumsum(lengths) - lengths).astype(jnp.int32)
    slots = jnp.arange(TOKENS, dtype=jnp.int32)
    segment = segment_of(slots, starts)
    begins = lax.optimization_barrier(jnp.max(jnp.where(starts[None, :] <= slots[:, None], starts[None, :], 0), axis=1))
    positions = (slots - begins).astype(jnp.float32)
    block_first = BLOCK * jnp.arange(TOKENS // BLOCK, dtype=jnp.int32)
    before = segment_of(block_first - 1, starts)
    after = segment_of(block_first + BLOCK - 1, starts)
    keep = keep_mask.astype(jnp.float32)
    cosine = cosine_table(HEAD_DIM)
    points = sample_points(FEATURES, HEAD_DIM)

    def forward(residual, gains, biases, w_qkv, b_qkv, w_feat, w_out, w_up, b_up, w_down, b_res):
        for layer in range(LAYERS):
            center = residual - lax.optimization_barrier(jnp.mean(residual, axis=-1, keepdims=True))
            normed = center * lax.rsqrt(lax.optimization_barrier(jnp.mean(center * center, axis=-1, keepdims=True)) + EPSILON)
            attention_input = low(normed * gains[layer, 0] + biases[layer, 0])
            feed_input = low(normed * gains[layer, 1] + biases[layer, 1])
            projected = low_back(jnp.dot(attention_input, w_qkv[layer], precision=HIGHEST) + b_qkv[layer])
            query_feat, key_feat, values = feature_maps(projected, positions, keep, w_feat[layer], cosine, points)
            numer, denom = attend_all(low(query_feat), low(key_feat), low(values), segment, before, after)
            attended = keep[:, None, None] * numer / (denom + 1.0 - keep[:, None])[:, :, None]
            attended = low(attended.reshape(TOKENS, D))
            raised = low_back(jnp.dot(feed_input, w_up[layer], precision=HIGHEST) + b_up[layer])
            activated = low(jax.nn.gelu(raised, approximate=False))
            branch = low_back(jnp.dot(attended, w_out[layer].T, precision=HIGHEST) + jnp.dot(activated, w_down[layer].T, precision=HIGHEST))
            residual = residual + branch + b_res[layer]
        return residual
    result, pullback = jax.vjp(forward, acts.astype(jnp.float32), ln_gain.astype(jnp.float32), ln_bias.astype(jnp.float32), qkv_w.astype(jnp.float32), qkv_b.astype(jnp.float32), feat_w.astype(jnp.float32), out_w.astype(jnp.float32), up_w.astype(jnp.float32), up_b.astype(jnp.float32), down_w.astype(jnp.float32), res_b.astype(jnp.float32))
    grads = pullback(cotangent.astype(jnp.float32))
    return (result, grads[0], grads[3], grads[6], grads[7], grads[9], grads[4], grads[8], grads[5], grads[1], grads[2], grads[10])
```

```python
import functools
import math

import jax
import jax.numpy as jnp
import numpy as np
from jax import lax
from jax.experimental import pallas as pl
from jax.experimental.pallas import tpu as pltpu
from jax.sharding import PartitionSpec as P

D = 1024
HEAD_DIM = 64
ROT = 16
FEATURES = 64
LAYERS = 2
CHUNK = 256

EPSILON = 1e-05
ROTARY_BASE = 10000.0
HIGHEST = lax.Precision.HIGHEST
BF = jnp.bfloat16
F32 = jnp.float32
STATE_ROWS = 72
VMEM_BYTES = 56 * 1024 * 1024


def prime_numbers(count):
    found = []
    candidate = 2
    while len(found) < count:
        if all((candidate % prime != 0 for prime in found)):
            found.append(candidate)
        candidate = candidate + 1
    return found


def sample_points(rows, columns):
    roots = np.sqrt(np.array(prime_numbers(2 * columns)) * 1.0)
    fractions = roots - np.floor(roots)
    grid = np.outer(np.arange(1, rows + 1) * 1.0, fractions) % 1.0
    radius = np.sqrt(-2.0 * np.log(1.0 - grid[:, :columns]))
    return radius * np.cos(2.0 * math.pi * grid[:, columns:])


def cosine_table(size):
    wave = np.arange(size)[:, None] * 1.0
    place = np.arange(size)[None, :] * 1.0
    table = np.cos(math.pi * (place + 0.5) * wave / size) * math.sqrt(2.0 / size)
    return table * np.where(wave == 0, math.sqrt(0.5), 1.0)


def dot_nn(a, b, precision=None):
    return lax.dot_general(
        a, b, (((1,), (0,)), ((), ())), precision=precision, preferred_element_type=F32
    )


def dot_nt(a, b, precision=None):
    return lax.dot_general(
        a, b, (((1,), (1,)), ((), ())), precision=precision, preferred_element_type=F32
    )


def dot_tn(a, b, precision=None):
    return lax.dot_general(
        a, b, (((0,), (0,)), ((), ())), precision=precision, preferred_element_type=F32
    )


def halves(wide):
    high = wide.astype(BF)
    return high, (wide - high.astype(F32)).astype(BF)


def lane_of(shape):
    return lax.broadcasted_iota(jnp.int32, shape, 1)


def row_of(shape):
    return lax.broadcasted_iota(jnp.int32, shape, 0)


def swap_pairs(x):
    width = x.shape[1]
    later = pltpu.roll(x, width - ROT // 2, 1)
    earlier = pltpu.roll(x, ROT // 2, 1)
    return jnp.where(lane_of(x.shape) % ROT < ROT // 2, later, earlier)


def twice(table):
    return jnp.concatenate([table, table], axis=1)


def block_diagonal(width):
    shape = (width, width)
    return (row_of(shape) // HEAD_DIM) == (lane_of(shape) // HEAD_DIM)


def pack_state(full):
    width = full.shape[0]
    kept = jnp.where(block_diagonal(width), full, 0.0)
    packed = kept[0:FEATURES]
    for head in range(1, width // FEATURES):
        packed = packed + kept[head * FEATURES : (head + 1) * FEATURES]
    return packed


def unpack_state(packed):
    width = packed.shape[1]
    tall = jnp.concatenate([packed] * (width // FEATURES), axis=0)
    return jnp.where(block_diagonal(width), tall, 0.0)


def head_sum(values, ones):
    high, low = halves(values)
    return dot_nn(high, ones) + dot_nn(low, ones)


def call(kernel, name, grid, in_specs, out_specs, out_shape, scratch, flops, args, prefetch=0):
    moved = sum(int(np.prod(a.shape)) * a.dtype.itemsize for a in list(args) + list(out_shape))
    return pl.pallas_call(
        kernel,
        name=name,
        grid_spec=pltpu.PrefetchScalarGridSpec(
            num_scalar_prefetch=prefetch,
            grid=grid,
            in_specs=in_specs,
            out_specs=out_specs,
            scratch_shapes=scratch,
        ),
        out_shape=out_shape,
        compiler_params=pltpu.CompilerParams(vmem_limit_bytes=VMEM_BYTES),
        cost_estimate=pl.CostEstimate(flops=int(flops), bytes_accessed=moved, transcendentals=0),
    )(*args)


def full(shape):
    return pl.BlockSpec(shape, lambda *i: (0,) * len(shape))


def rowed(width):
    return pl.BlockSpec((CHUNK, width), lambda i: (i, 0))


def rowed_back(width, count):
    return pl.BlockSpec((CHUNK, width), lambda i: (count - 1 - i, 0))


def project_kernel(pieces, *refs):
    inputs = refs[:pieces]
    (
        res_b,
        scale,
        w_ref,
        b_ref,
        cos_ref,
        sin_ref,
        begin_ref,
        keep_ref,
        last_ref,
        feat_ref,
        map_ref,
        ones_ref,
        ai_ref,
        fi_ref,
        normed_ref,
        unit_ref,
        inv_ref,
        qf_ref,
        kf_ref,
        v_ref,
        k_ref,
        state_ref,
        sum_ref,
    ) = refs[pieces:]
    step = pl.program_id(0)
    width = inputs[0].shape[1]
    group = 4
    parts = []
    for r in range(group):
        part = inputs[r][...].astype(F32)
        if pieces > group:
            part = part + inputs[group + r][...].astype(F32) + res_b[:, r * width : (r + 1) * width]
        parts.append(part)
    x = jnp.concatenate(parts, axis=1)
    mean = jnp.sum(x, axis=1, keepdims=True) * (1.0 / D)
    center = x - mean
    inverse = lax.rsqrt(jnp.sum(center * center, axis=1, keepdims=True) * (1.0 / D) + EPSILON)
    normed = center * inverse
    inv_ref[...] = inverse
    normed_ref[...] = normed.astype(BF)
    unit_ref[...] = normed[:, :width]
    attention_input = (normed * scale[0:1] + scale[1:2]).astype(BF)
    ai_ref[...] = attention_input
    fi_ref[...] = (normed * scale[2:3] + scale[3:4]).astype(BF)
    projected = dot_nn(attention_input, w_ref[...]) + b_ref[...]
    a = map_ref.shape[0]
    q = projected[:, :a]
    k = projected[:, a : 2 * a]
    v = projected[:, 2 * a :].astype(BF)
    cos = twice(cos_ref[...])
    sin = twice(sin_ref[...])
    q_turn = q * cos + swap_pairs(q) * sin
    k_turn = k * cos + swap_pairs(k) * sin
    query_feat = jnp.exp(dot_nn(q_turn, map_ref[...], HIGHEST))
    key_norm = head_sum(k * k, ones_ref[...]) * (0.5 / HEAD_DIM)
    key_feat = (
        keep_ref[...] * feat_ref[...] * jnp.exp(dot_nn(k_turn, map_ref[...], HIGHEST) - key_norm)
    ).astype(BF)
    qf_ref[...] = query_feat.astype(BF)
    kf_ref[...] = key_feat
    v_ref[...] = v
    k_ref[...] = k.astype(BF)
    place = (row_of((CHUNK, 1)) + step * CHUNK).astype(F32)
    masked = jnp.where(place >= last_ref[...], key_feat.astype(F32), 0.0)

    @pl.when(step == 0)
    def _():
        sum_ref[...] = jnp.zeros_like(sum_ref)
        state_ref[...] = jnp.zeros_like(state_ref)

    sum_ref[...] += dot_tn(masked.astype(BF), v)
    state_ref[FEATURES : FEATURES + 1, :] += jnp.sum(masked, axis=0, keepdims=True)

    @pl.when(step == pl.num_programs(0) - 1)
    def _():
        state_ref[0:FEATURES, :] = pack_state(sum_ref[...])


def project(inputs, res_b, scale, w, b, tables, feat, consts):
    rows, width = inputs[0].shape
    a = feat.shape[1]
    steps = rows // CHUNK
    cos, sin, begin, keep, last = tables
    args = list(inputs) + [
        res_b,
        scale,
        w,
        b,
        cos,
        sin,
        begin,
        keep,
        last,
        feat,
        consts["map_t"],
        consts["ones"],
    ]
    in_specs = [rowed(width)] * len(inputs) + [
        full(res_b.shape),
        full(scale.shape),
        full(w.shape),
        full(b.shape),
        rowed(cos.shape[1]),
        rowed(sin.shape[1]),
        rowed(1),
        rowed(1),
        full((1, 1)),
        full(feat.shape),
        full((a, a)),
        full((a, a)),
    ]
    out = [
        ((rows, D), BF),
        ((rows, D), BF),
        ((rows, D), BF),
        ((rows, width), F32),
        ((rows, 1), F32),
        ((rows, a), BF),
        ((rows, a), BF),
        ((rows, a), BF),
        ((rows, a), BF),
    ]
    out_specs = [rowed(shape[1]) for shape, kind in out] + [full((STATE_ROWS, a))]
    out_shape = [jax.ShapeDtypeStruct(*o) for o in out] + [
        jax.ShapeDtypeStruct((STATE_ROWS, a), F32)
    ]
    return call(
        functools.partial(project_kernel, len(inputs)),
        "project",
        (steps,),
        in_specs,
        out_specs,
        out_shape,
        [pltpu.VMEM((a, a), F32)],
        2 * rows * D * 3 * a * 2,
        args,
    )


def raise_kernel(fi_ref, w_ref, b_ref, act_ref, slope_ref):
    raised = dot_nn(fi_ref[...], w_ref[...]) + b_ref[...]
    cumulative = 0.5 + 0.5 * lax.erf(raised * math.sqrt(0.5))
    density = jnp.exp(raised * raised * -0.5) * (1.0 / math.sqrt(2.0 * math.pi))
    act_ref[...] = (raised * cumulative).astype(BF)
    slope_ref[...] = (cumulative + raised * density).astype(BF)


def raise_up(fi, w, b):
    rows = fi.shape[0]
    hidden = w.shape[1]
    return call(
        raise_kernel,
        "raise_up",
        (rows // CHUNK,),
        [rowed(D), full(w.shape), full(b.shape)],
        [rowed(hidden)] * 2,
        [jax.ShapeDtypeStruct((rows, hidden), BF)] * 2,
        [],
        2 * rows * D * hidden * 3,
        [fi, w, b],
    )


def pair_mask(begin, step):
    shape = (CHUNK, CHUNK)
    t = row_of(shape)
    s = lane_of(shape)
    return (s <= t) & ((s + step * CHUNK).astype(F32) >= begin)


def attend_kernel(
    qf_ref,
    kf_ref,
    v_ref,
    begin_ref,
    keep_ref,
    in_ref,
    act_ref,
    ow_ref,
    dw_ref,
    ones_ref,
    near_ref,
    far_ref,
    att_ref,
    low_ref,
    ratio_ref,
    states_ref,
    totals_ref,
    state,
    total,
):
    step = pl.program_id(0)

    @pl.when(step == 0)
    def _():
        state[...] = unpack_state(in_ref[0:FEATURES, :])
        total[...] = jnp.broadcast_to(in_ref[FEATURES : FEATURES + 1, :], total.shape)

    q = qf_ref[...]
    k = kf_ref[...]
    v = v_ref[...]
    begin = begin_ref[...]
    keep = keep_ref[...]
    ones = ones_ref[...]
    a = q.shape[1]
    mask = pair_mask(begin, step)
    head_of = lane_of((1, a)) // HEAD_DIM
    held = state[...]
    held_total = total[0:1, :]
    states_ref[0] = held
    totals_ref[0] = total[...]
    base = (step * CHUNK).astype(F32)
    use = jnp.where(begin < base, 1.0, 0.0)
    high, low = halves(held)
    num = use * (dot_nn(q, high) + dot_nn(q, low))
    den = use * head_sum(q.astype(F32) * held_total, ones)
    for head in range(a // HEAD_DIM):
        own = (head_of == head).astype(BF)
        scores = dot_nt(q * own, k)
        scores_low = jnp.where(mask, scores, 0.0).astype(BF)
        num = num + dot_nn(scores_low, v * own)
        den = den + dot_nn(scores_low, jnp.broadcast_to(own, (CHUNK, a)))
    ratio = keep / (den + 1.0 - keep)
    att = num * ratio
    att_low = att.astype(BF)
    ratio_ref[...] = ratio
    att_ref[...] = att
    low_ref[...] = att_low
    end = begin[CHUNK - 1 : CHUNK, :]
    place = (row_of((CHUNK, 1)) + step * CHUNK).astype(F32)
    masked = jnp.where(place >= end, k.astype(F32), 0.0)
    passing = jnp.where(end < base, 1.0, 0.0)
    state[...] = passing * held + jnp.where(
        block_diagonal(a), dot_tn(masked.astype(BF), v), 0.0
    )
    total[...] = jnp.broadcast_to(
        passing * held_total + jnp.sum(masked, axis=0, keepdims=True), total.shape
    )
    branch = (dot_nt(att_low, ow_ref[...]) + dot_nt(act_ref[...], dw_ref[...])).astype(BF)
    w = D // 4
    near_ref[0] = branch[:, 0:w]
    near_ref[1] = branch[:, 2 * w : 3 * w]
    far_ref[0] = branch[:, w : 2 * w]
    far_ref[1] = branch[:, 3 * w :]


def attend(qf, kf, v, begin, keep, state_in, act, out_w, down_w, consts):
    rows, a = qf.shape
    steps = rows // CHUNK
    hidden = act.shape[1]
    quarter = pl.BlockSpec((2, CHUNK, D // 4), lambda i: (0, i, 0))
    return call(
        attend_kernel,
        "attend",
        (steps,),
        [
            rowed(a),
            rowed(a),
            rowed(a),
            rowed(1),
            rowed(1),
            full((STATE_ROWS, a)),
            rowed(hidden),
            full(out_w.shape),
            full(down_w.shape),
            full((a, a)),
        ],
        [
            quarter,
            quarter,
            rowed(a),
            rowed(a),
            rowed(a),
            pl.BlockSpec((1, a, a), lambda i: (i, 0, 0)),
            pl.BlockSpec((1, 8, a), lambda i: (i, 0, 0)),
        ],
        [
            jax.ShapeDtypeStruct((2, rows, D // 4), BF),
            jax.ShapeDtypeStruct((2, rows, D // 4), BF),
            jax.ShapeDtypeStruct((rows, a), F32),
            jax.ShapeDtypeStruct((rows, a), BF),
            jax.ShapeDtypeStruct((rows, a), F32),
            jax.ShapeDtypeStruct((steps, a, a), F32),
            jax.ShapeDtypeStruct((steps, 8, a), F32),
        ],
        [pltpu.VMEM((a, a), F32), pltpu.VMEM((8, a), F32)],
        2 * rows * D * (hidden + a) * 2,
        [qf, kf, v, begin, keep, state_in, act, out_w, down_w, consts["ones"]],
    )


def lower_kernel(
    g0,
    g1,
    g2,
    g3,
    dw_ref,
    ow_ref,
    slope_ref,
    ratio_ref,
    att_ref,
    qf_ref,
    begin_ref,
    ones_ref,
    grad_ref,
    raised_ref,
    num_ref,
    den_ref,
    bias_ref,
    entry_ref,
    sum_ref,
):
    step = pl.program_id(0)

    @pl.when(step == 0)
    def _():
        sum_ref[...] = jnp.zeros_like(sum_ref)
        entry_ref[...] = jnp.zeros_like(entry_ref)
        bias_ref[...] = jnp.zeros_like(bias_ref)

    grad = jnp.concatenate([g0[...], g1[...], g2[...], g3[...]], axis=1)
    grad_ref[...] = grad
    d_att = dot_nn(grad, ow_ref[...])
    d_num = (d_att * ratio_ref[...]).astype(BF)
    d_den = -head_sum(d_num.astype(F32) * att_ref[...], ones_ref[...])
    num_ref[...] = d_num
    den_ref[...] = d_den
    entering = jnp.where(begin_ref[...] < 0.0, qf_ref[...].astype(F32), 0.0)
    sum_ref[...] += dot_tn(entering.astype(BF), d_num)
    entry_ref[FEATURES : FEATURES + 1, :] += jnp.sum(entering * d_den, axis=0, keepdims=True)
    d_raised = (dot_nn(grad, dw_ref[...]) * slope_ref[...].astype(F32)).astype(BF)
    raised_ref[...] = d_raised
    bias_ref[...] += jnp.sum(d_raised.astype(F32), axis=0, keepdims=True)

    @pl.when(step == pl.num_programs(0) - 1)
    def _():
        entry_ref[0:FEATURES, :] = pack_state(sum_ref[...])


def lower(grads, down_w, out_w, slope, ratio, att, qf, begin, consts):
    rows, width = grads[0].shape
    hidden = slope.shape[1]
    a = att.shape[1]
    return call(
        lower_kernel,
        "lower",
        (rows // CHUNK,),
        [rowed(width)] * 4
        + [
            full(down_w.shape),
            full(out_w.shape),
            rowed(hidden),
            rowed(a),
            rowed(a),
            rowed(a),
            rowed(1),
            full((a, a)),
        ],
        [
            rowed(D),
            rowed(hidden),
            rowed(a),
            rowed(a),
            full((1, hidden)),
            full((STATE_ROWS, a)),
        ],
        [
            jax.ShapeDtypeStruct((rows, D), BF),
            jax.ShapeDtypeStruct((rows, hidden), BF),
            jax.ShapeDtypeStruct((rows, a), BF),
            jax.ShapeDtypeStruct((rows, a), F32),
            jax.ShapeDtypeStruct((1, hidden), F32),
            jax.ShapeDtypeStruct((STATE_ROWS, a), F32),
        ],
        [pltpu.VMEM((a, a), F32)],
        2 * rows * D * (hidden + a) * 2,
        list(grads) + [down_w, out_w, slope, ratio, att, qf, begin, consts["ones"]],
    )


def back_kernel(
    qf_ref,
    kf_ref,
    v_ref,
    k_ref,
    num_ref,
    den_ref,
    begin_ref,
    cos_ref,
    sin_ref,
    states_ref,
    totals_ref,
    exit_ref,
    map_ref,
    ones_ref,
    w_ref,
    up_ref,
    raised_ref,
    normed_ref,
    scale_ref,
    proj_ref,
    near_ref,
    far_ref,
    rows_ref,
    bias_ref,
    feat_ref,
    sums_ref,
    state,
    total,
):
    turn = pl.program_id(0)
    step = pl.num_programs(0) - 1 - turn

    @pl.when(turn == 0)
    def _():
        state[...] = unpack_state(exit_ref[0:FEATURES, :])
        total[...] = jnp.broadcast_to(exit_ref[FEATURES : FEATURES + 1, :], total.shape)
        bias_ref[...] = jnp.zeros_like(bias_ref)
        feat_ref[...] = jnp.zeros_like(feat_ref)
        sums_ref[...] = jnp.zeros_like(sums_ref)

    q = qf_ref[...]
    k = kf_ref[...]
    v = v_ref[...]
    d_num = num_ref[...]
    d_den = den_ref[...]
    begin = begin_ref[...]
    ones = ones_ref[...]
    a = q.shape[1]
    mask = pair_mask(begin, step)
    head_of = lane_of((1, a)) // HEAD_DIM
    base = (step * CHUNK).astype(F32)
    use = jnp.where(begin < base, 1.0, 0.0)
    end = begin[CHUNK - 1 : CHUNK, :]
    place = (row_of((CHUNK, 1)) + step * CHUNK).astype(F32)
    inside = jnp.where(place >= end, 1.0, 0.0)
    passing = jnp.where(end < base, 1.0, 0.0)
    held_high, held_low = halves(states_ref[0])
    held_total = totals_ref[0][0:1, :]
    after = state[...]
    after_total = total[0:1, :]
    after_high, after_low = halves(after)
    q_wide = q.astype(F32)
    k_wide = k.astype(F32)
    masked = (k_wide * inside).astype(BF)
    d_q = use * (dot_nt(d_num, held_high) + dot_nt(d_num, held_low) + d_den * held_total)
    d_k = inside * (dot_nt(v, after_high) + dot_nt(v, after_low) + after_total)
    d_v = dot_nn(masked, after_high) + dot_nn(masked, after_low)
    for head in range(a // HEAD_DIM):
        own = (head_of == head).astype(BF)
        q_own = q * own
        num_own = d_num * own
        scores_low = jnp.where(mask, dot_nt(q_own, k), 0.0).astype(BF)
        column = d_den[:, head * HEAD_DIM : head * HEAD_DIM + 1]
        d_scores = jnp.where(mask, dot_nt(num_own, v) + column, 0.0).astype(BF)
        d_q = d_q + dot_nn(d_scores, k * own)
        d_k = d_k + dot_tn(d_scores, q_own)
        d_v = d_v + dot_tn(scores_low, num_own)
    q_used = q_wide * use
    state[...] = passing * after + jnp.where(
        block_diagonal(a), dot_tn(q_used.astype(BF), d_num), 0.0
    )
    total[...] = jnp.broadcast_to(
        passing * after_total + jnp.sum(q_used * d_den, axis=0, keepdims=True), total.shape
    )
    cos = twice(cos_ref[...])
    sin = twice(sin_ref[...])
    d_query = dot_nn(d_q * q_wide, map_ref[...], HIGHEST)
    d_query = d_query * cos - swap_pairs(d_query) * sin
    d_key_log = d_k * k_wide
    feat_ref[...] += jnp.sum(d_key_log, axis=0, keepdims=True)
    d_key = dot_nn(d_key_log, map_ref[...], HIGHEST)
    d_key = d_key * cos - swap_pairs(d_key) * sin
    d_key = d_key - head_sum(d_key_log, ones) * k_ref[...].astype(F32) * (1.0 / HEAD_DIM)
    d_proj = jnp.concatenate([d_query, d_key, d_v], axis=1).astype(BF)
    proj_ref[...] = d_proj
    bias_ref[...] += jnp.sum(d_proj.astype(F32), axis=0, keepdims=True)
    normed = normed_ref[...].astype(F32)
    scale = scale_ref[...]
    d_attention = dot_nt(d_proj, w_ref[...])
    d_feed = dot_nt(raised_ref[...], up_ref[...])
    sums_ref[0:1, :] += jnp.sum(d_attention * normed, axis=0, keepdims=True)
    sums_ref[1:2, :] += jnp.sum(d_feed * normed, axis=0, keepdims=True)
    sums_ref[2:3, :] += jnp.sum(d_attention, axis=0, keepdims=True)
    sums_ref[3:4, :] += jnp.sum(d_feed, axis=0, keepdims=True)
    d_normed = (d_attention * scale[0:1] + d_feed * scale[2:3]).astype(BF)
    w = D // 4
    near_ref[0] = d_normed[:, 0:w]
    near_ref[1] = d_normed[:, 2 * w : 3 * w]
    far_ref[0] = d_normed[:, w : 2 * w]
    far_ref[1] = d_normed[:, 3 * w :]
    high, low = halves(d_normed.astype(F32) * normed)
    row = jnp.ones((8, D), BF)
    first = dot_nt(row, d_normed)
    second = dot_nt(row, high) + dot_nt(row, low)
    rows_ref[...] = jnp.where(row_of(first.shape) == 0, first, second)


def back(kept, d_num, d_den, d_raised, exit_state, tables, w_qkv, up_w, scale, consts):
    qf, kf, v, k, normed, states, totals = kept
    cos, sin, begin, keep, last = tables
    rows, a = qf.shape
    n = rows // CHUNK
    hidden = d_raised.shape[1]
    args = [
        qf,
        kf,
        v,
        k,
        d_num,
        d_den,
        begin,
        cos,
        sin,
        states,
        totals,
        exit_state,
        consts["map"],
        consts["ones"],
        w_qkv,
        up_w,
        d_raised,
        normed,
        scale,
    ]
    quarter = pl.BlockSpec((2, CHUNK, D // 4), lambda i: (0, n - 1 - i, 0))
    in_specs = (
        [rowed_back(a, n)] * 6
        + [rowed_back(1, n), rowed_back(cos.shape[1], n), rowed_back(sin.shape[1], n)]
        + [
            pl.BlockSpec((1, a, a), lambda i: (n - 1 - i, 0, 0)),
            pl.BlockSpec((1, 8, a), lambda i: (n - 1 - i, 0, 0)),
            full((STATE_ROWS, a)),
            full((a, a)),
            full((a, a)),
            full(w_qkv.shape),
            full(up_w.shape),
            rowed_back(hidden, n),
            rowed_back(D, n),
            full(scale.shape),
        ]
    )
    out_specs = [
        rowed_back(3 * a, n),
        quarter,
        quarter,
        pl.BlockSpec((8, CHUNK), lambda i: (0, n - 1 - i)),
        full((1, 3 * a)),
        full((1, a)),
        full((8, D)),
    ]
    out_shape = [
        jax.ShapeDtypeStruct((rows, 3 * a), BF),
        jax.ShapeDtypeStruct((2, rows, D // 4), BF),
        jax.ShapeDtypeStruct((2, rows, D // 4), BF),
        jax.ShapeDtypeStruct((8, rows), F32),
        jax.ShapeDtypeStruct((1, 3 * a), F32),
        jax.ShapeDtypeStruct((1, a), F32),
        jax.ShapeDtypeStruct((8, D), F32),
    ]
    return call(
        back_kernel,
        "attend_back",
        (n,),
        in_specs,
        out_specs,
        out_shape,
        [pltpu.VMEM((a, a), F32), pltpu.VMEM((8, a), F32)],
        2 * rows * D * (hidden + 3 * a) * 3,
        args,
    )


def weight_kernel(count, h_ref, x_ref, *refs):
    del h_ref
    x = x_ref[...]
    out = refs[count]
    at = 0
    for y in refs[:count]:
        width = y.shape[1]
        out[:, at : at + width] = dot_tn(x, y[...]).astype(BF)
        at += width


def weight_grad(h, x, ys):
    rows = x.shape[0]
    columns = sum(y.shape[1] for y in ys)
    tile = D // 4
    return call(
        functools.partial(weight_kernel, len(ys)),
        "weight_grad",
        (4,),
        [pl.BlockSpec((rows, tile), lambda i, h: (0, lax.bitwise_xor(i, h[0])))]
        + [full(y.shape) for y in ys],
        [pl.BlockSpec((tile, columns), lambda i, h: (i, 0))],
        [jax.ShapeDtypeStruct((D, columns), BF)],
        [],
        2 * rows * D * columns,
        [h, x] + list(ys),
        prefetch=1,
    )[0]


def exchange(value, axis, step):
    count = lax.axis_size(axis)
    return lax.ppermute(value, axis, [(i, i ^ step) for i in range(count)])


def shifted(value, axis, step):
    count = lax.axis_size(axis)
    return lax.ppermute(
        value, axis, [(i, i + step) for i in range(count) if 0 <= i + step < count]
    )


def gather_heads(own):
    across = exchange(own, "head", 2)
    beside = exchange(own, "head", 1)
    return [own, beside, across, exchange(across, "head", 1)]


def scatter_heads(near, far):
    got = exchange(far, "head", 1)
    across = exchange(near[1] + got[1], "head", 2)
    return near[0].astype(F32) + got[0].astype(F32) + across.astype(F32)


def on_device(
    acts,
    cotangent,
    lengths,
    keep_mask,
    ln_gain,
    ln_bias,
    qkv_w,
    qkv_b,
    feat_w,
    out_w,
    up_w,
    up_b,
    down_w,
    res_b,
):
    rows, width = acts.shape
    heads = feat_w.shape[1]
    a = heads * HEAD_DIM
    n = lax.axis_size("seq")
    tokens = rows * n
    longest = 2048 if tokens <= 8192 else 4096
    hops = -(-longest // rows)
    h = lax.axis_index("head").astype(jnp.int32)
    first = lax.axis_index("seq") * rows

    def relative(array, axis):
        return jnp.concatenate(
            [
                lax.dynamic_slice_in_dim(array, lax.bitwise_xor(h, r) * width, width, axis)
                for r in range(4)
            ],
            axis,
        )

    pieces = gather_heads(acts)
    gains = relative(ln_gain, 2)
    biases = relative(ln_bias, 2)
    res = relative(res_b, 1)
    by_kind = qkv_w.reshape(LAYERS, D, heads, 3, HEAD_DIM)
    by_kind = jnp.transpose(by_kind, (0, 1, 3, 2, 4)).reshape(LAYERS, D, 3 * a)
    w_qkv = relative(by_kind, 1)
    w_up = relative(up_w, 1)
    w_out = relative(out_w, 1)
    w_down = relative(down_w, 1)
    b_qkv = jnp.transpose(qkv_b.reshape(LAYERS, heads, 3, HEAD_DIM), (0, 2, 1, 3))
    b_qkv = b_qkv.reshape(LAYERS, 1, 3 * a)
    scales = [
        jnp.concatenate(
            [
                jnp.stack([gains[l, 0], biases[l, 0], gains[l, 1], biases[l, 1]]),
                jnp.zeros((4, D), F32),
            ]
        )
        for l in range(LAYERS)
    ]
    feats = feat_w.reshape(LAYERS, 1, a)

    starts = (jnp.cumsum(lengths) - lengths).astype(jnp.int32)

    def begin_of(slots):
        return jnp.max(jnp.where(starts[None, :] <= slots[:, None], starts[None, :], 0), axis=1)

    slots = first + jnp.arange(rows, dtype=jnp.int32)
    begins = begin_of(slots)
    positions = (slots - begins).astype(F32)
    begin = (begins - first).astype(F32)[:, None]
    keep = keep_mask.astype(F32)[:, None]
    last = begin[rows - 1 :, :]
    half = ROT // 2
    rates = np.zeros(HEAD_DIM)
    rates[:half] = ROTARY_BASE ** (-2.0 * np.arange(half) / ROT)
    rates[half:ROT] = rates[:half]
    sign = np.zeros(HEAD_DIM)
    sign[:half] = -1.0
    sign[half:ROT] = 1.0
    phase = positions[:, None] * jnp.asarray(np.tile(rates, 2), F32)[None, :]
    cos = jnp.cos(phase)
    sin = jnp.sin(phase) * jnp.asarray(np.tile(sign, 2), F32)[None, :]
    tables = (cos, sin, begin, keep, last)
    fold = sample_points(FEATURES, HEAD_DIM) @ cosine_table(HEAD_DIM) / math.sqrt(HEAD_DIM)
    eye = np.eye(heads)
    consts = {
        "map": jnp.asarray(np.kron(eye, fold), F32),
        "map_t": jnp.asarray(np.kron(eye, fold.T), F32),
        "ones": jnp.asarray(np.kron(eye, np.ones((HEAD_DIM, HEAD_DIM))), BF),
    }

    def linked(step):
        edge = first - 1 if step > 0 else first + rows * -step - 1
        held = first + rows - 1 if step < 0 else first - 1 - (step - 1) * rows
        return (begin_of(jnp.reshape(edge, (1,)))[0] <= held).astype(F32)

    def entering(state, sign):
        total = shifted(state, "seq", sign)
        for step in range(2, hops + 1):
            total = total + shifted(state, "seq", sign * step) * linked(sign * step)
        return total

    own = acts.astype(F32)
    inputs = pieces
    kept = []
    for l in range(LAYERS):
        ai, fi, normed, unit, inverse, qf, kf, v, k, state = project(
            inputs, res[0:1], scales[l], w_qkv[l], b_qkv[l], tables, feats[l], consts
        )
        state_in = entering(state, 1)
        act, slope = raise_up(fi, w_up[l], up_b[l][None, :])
        near, far, att, att_low, ratio, states, totals = attend(
            qf, kf, v, begin, keep, state_in, act, w_out[l], w_down[l], consts
        )
        branch = scatter_heads(near, far)
        if l + 1 < LAYERS:
            branch = branch.astype(BF)
            inputs = pieces + gather_heads(branch)
        own = own + branch.astype(F32) + res[l, :width]
        kept.append(
            (
                (qf, kf, v, k, normed, states, totals),
                ai,
                fi,
                unit,
                inverse,
                act,
                slope,
                att,
                att_low,
                ratio,
            )
        )
    out_acts = own

    upstream = cotangent.astype(F32)
    h_vec = h.reshape(1)
    matrices = [None] * LAYERS
    smalls = [None] * LAYERS
    sums = [None] * LAYERS
    for l in reversed(range(LAYERS)):
        local, ai, fi, unit, inverse, act, slope, att, att_low, ratio = kept[l]
        d_res = jnp.sum(upstream, axis=0)
        grads = gather_heads(upstream.astype(BF))
        grad, d_raised, d_num, d_den, d_up_b, entry = lower(
            grads, w_down[l], w_out[l], slope, ratio, att, local[0], begin, consts
        )
        exit_state = entering(entry, -1)
        d_down_out = weight_grad(h_vec, grad, [act, att_low])
        d_up = weight_grad(h_vec, fi, [d_raised])
        d_proj, near, far, row_sums, d_qkv_b, d_feat, column_sums = back(
            local, d_num, d_den, d_raised, exit_state, tables, w_qkv[l], w_up[l], scales[l], consts
        )
        d_qkv = weight_grad(h_vec, ai, [d_proj])
        row_sums = row_sums + exchange(row_sums, "head", 1)
        row_sums = row_sums + exchange(row_sums, "head", 2)
        d_normed = scatter_heads(near, far)
        upstream = upstream + inverse * (
            d_normed - row_sums[0][:, None] / D - unit * row_sums[1][:, None] / D
        )
        matrices[l] = lax.psum_scatter(
            jnp.concatenate([d_qkv, d_down_out, d_up], axis=1),
            "seq",
            scatter_dimension=0,
            tiled=True,
        ).astype(F32)
        sums[l] = column_sums[:4]
        smalls[l] = jnp.concatenate([d_qkv_b[0], d_up_b[0], d_feat[0], d_res])

    column_sums = jnp.stack(sums).reshape(LAYERS, 4, 4, width)
    near = jnp.stack([column_sums[:, :, 0], column_sums[:, :, 2]])
    far = jnp.stack([column_sums[:, :, 1], column_sums[:, :, 3]])
    norm_sums = scatter_heads(near, far)
    bundle = jnp.concatenate([norm_sums.reshape(LAYERS, 4 * width), jnp.stack(smalls)], axis=1)
    step = 1
    while step < n:
        bundle = bundle + exchange(bundle, "seq", step)
        step *= 2
    at = 0
    taken = []
    for size in (2 * width, 2 * width, 3 * a, d_up_b.shape[1], a, width):
        taken.append(bundle[:, at : at + size])
        at += size
    d_gain, d_bias, d_qkv_b, d_up_b, d_feat, d_res = taken

    hidden = up_w.shape[2]
    both = jnp.stack(matrices)
    share = both.shape[1]
    d_qkv = both[:, :, : 3 * a].reshape(LAYERS, share, 3, heads, HEAD_DIM)
    d_qkv = jnp.transpose(d_qkv, (0, 1, 3, 2, 4)).reshape(LAYERS, share, 3 * a)
    d_down = both[:, :, 3 * a : 3 * a + hidden]
    d_out = both[:, :, 3 * a + hidden : 4 * a + hidden]
    d_up = both[:, :, 4 * a + hidden :]
    d_qkv_b = d_qkv_b.reshape(LAYERS, 3, heads, HEAD_DIM)
    d_qkv_b = jnp.transpose(d_qkv_b, (0, 2, 1, 3)).reshape(LAYERS, 3 * a)
    return (
        out_acts,
        upstream,
        d_qkv,
        d_out,
        d_up,
        d_down,
        d_qkv_b,
        d_up_b,
        (d_feat / feats[:, 0]).reshape(LAYERS, heads, FEATURES),
        d_gain.reshape(LAYERS, 2, width),
        d_bias.reshape(LAYERS, 2, width),
        d_res,
    )


def solution(mesh):
    return jax.shard_map(
        on_device,
        mesh=mesh,
        in_specs=(
            P("seq", "head"),
            P("seq", "head"),
            P(),
            P("seq"),
            P(),
            P(),
            P(None, None, "head"),
            P(None, "head"),
            P(None, "head", None),
            P(None, None, "head"),
            P(None, None, "head"),
            P(None, "head"),
            P(None, None, "head"),
            P(),
        ),
        out_specs=(
            P("seq", "head"),
            P("seq", "head"),
            P(None, "seq", "head"),
            P(None, "seq", "head"),
            P(None, "seq", "head"),
            P(None, "seq", "head"),
            P(None, "head"),
            P(None, "head"),
            P(None, "head", None),
            P(None, None, "head"),
            P(None, None, "head"),
            P(None, "head"),
        ),
        check_vma=False,
    )
```

```python
import functools
import math

import jax
import jax.numpy as jnp
import numpy as np
from jax import lax
from jax.experimental import pallas as pl
from jax.experimental.pallas import tpu as pltpu
from jax.sharding import PartitionSpec as P

D = 1024
HEAD_DIM = 64
ROT = 16
FEATURES = 64
LAYERS = 2
CHUNK = 256

EPSILON = 1e-05
ROTARY_BASE = 10000.0
HIGHEST = lax.Precision.HIGHEST
BF = jnp.bfloat16
F32 = jnp.float32
STATE_ROWS = 72
VMEM_BYTES = 56 * 1024 * 1024


def prime_numbers(count):
    found = []
    candidate = 2
    while len(found) < count:
        if all((candidate % prime != 0 for prime in found)):
            found.append(candidate)
        candidate = candidate + 1
    return found


def sample_points(rows, columns):
    roots = np.sqrt(np.array(prime_numbers(2 * columns)) * 1.0)
    fractions = roots - np.floor(roots)
    grid = np.outer(np.arange(1, rows + 1) * 1.0, fractions) % 1.0
    radius = np.sqrt(-2.0 * np.log(1.0 - grid[:, :columns]))
    return radius * np.cos(2.0 * math.pi * grid[:, columns:])


def cosine_table(size):
    wave = np.arange(size)[:, None] * 1.0
    place = np.arange(size)[None, :] * 1.0
    table = np.cos(math.pi * (place + 0.5) * wave / size) * math.sqrt(2.0 / size)
    return table * np.where(wave == 0, math.sqrt(0.5), 1.0)


def dot_nn(a, b, precision=None):
    return lax.dot_general(
        a, b, (((1,), (0,)), ((), ())), precision=precision, preferred_element_type=F32
    )


def dot_nt(a, b, precision=None):
    return lax.dot_general(
        a, b, (((1,), (1,)), ((), ())), precision=precision, preferred_element_type=F32
    )


def dot_tn(a, b, precision=None):
    return lax.dot_general(
        a, b, (((0,), (0,)), ((), ())), precision=precision, preferred_element_type=F32
    )


def halves(wide):
    high = wide.astype(BF)
    return high, (wide - high.astype(F32)).astype(BF)


def lane_of(shape):
    return lax.broadcasted_iota(jnp.int32, shape, 1)


def row_of(shape):
    return lax.broadcasted_iota(jnp.int32, shape, 0)


def swap_pairs(x):
    width = x.shape[1]
    later = pltpu.roll(x, width - ROT // 2, 1)
    earlier = pltpu.roll(x, ROT // 2, 1)
    return jnp.where(lane_of(x.shape) % ROT < ROT // 2, later, earlier)


def twice(table):
    return jnp.concatenate([table, table], axis=1)


def block_columns(h, r, width):
    return pl.ds(pl.multiple_of(lax.bitwise_xor(h, r) * width, width), width)


def split_heads(projected):
    heads = projected.shape[1] // (3 * HEAD_DIM)
    return [
        jnp.concatenate(
            [
                projected[:, (3 * j + kind) * HEAD_DIM : (3 * j + kind + 1) * HEAD_DIM]
                for j in range(heads)
            ],
            axis=1,
        )
        for kind in range(3)
    ]


def join_heads(q, k, v):
    heads = q.shape[1] // HEAD_DIM
    return jnp.concatenate(
        [
            part[:, j * HEAD_DIM : (j + 1) * HEAD_DIM]
            for j in range(heads)
            for part in (q, k, v)
        ],
        axis=1,
    )


def block_diagonal(width):
    shape = (width, width)
    return (row_of(shape) // HEAD_DIM) == (lane_of(shape) // HEAD_DIM)


def pack_state(full):
    width = full.shape[0]
    kept = jnp.where(block_diagonal(width), full, 0.0)
    packed = kept[0:FEATURES]
    for head in range(1, width // FEATURES):
        packed = packed + kept[head * FEATURES : (head + 1) * FEATURES]
    return packed


def unpack_state(packed):
    width = packed.shape[1]
    tall = jnp.concatenate([packed] * (width // FEATURES), axis=0)
    return jnp.where(block_diagonal(width), tall, 0.0)


def head_sum(values, ones):
    high, low = halves(values)
    return dot_nn(high, ones) + dot_nn(low, ones)


def call(kernel, name, grid, in_specs, out_specs, out_shape, scratch, flops, args, prefetch=0):
    moved = sum(int(np.prod(a.shape)) * a.dtype.itemsize for a in list(args) + list(out_shape))
    return pl.pallas_call(
        kernel,
        name=name,
        grid_spec=pltpu.PrefetchScalarGridSpec(
            num_scalar_prefetch=prefetch,
            grid=grid,
            in_specs=in_specs,
            out_specs=out_specs,
            scratch_shapes=scratch,
        ),
        out_shape=out_shape,
        compiler_params=pltpu.CompilerParams(vmem_limit_bytes=VMEM_BYTES),
        cost_estimate=pl.CostEstimate(flops=int(flops), bytes_accessed=moved, transcendentals=0),
    )(*args)


def full(shape):
    return pl.BlockSpec(shape, lambda *i: (0,) * len(shape))


def rowed(width):
    return pl.BlockSpec((CHUNK, width), lambda i: (i, 0))


def rowed_back(width, count):
    return pl.BlockSpec((CHUNK, width), lambda i: (count - 1 - i, 0))


def project_kernel(pieces, *refs):
    inputs = refs[:pieces]
    (
        res_b,
        scale,
        w_ref,
        b_ref,
        cos_ref,
        sin_ref,
        begin_ref,
        keep_ref,
        last_ref,
        feat_ref,
        map_ref,
        ones_ref,
        ai_ref,
        fi_ref,
        normed_ref,
        unit_ref,
        inv_ref,
        qf_ref,
        kf_ref,
        v_ref,
        k_ref,
        state_ref,
        sum_ref,
        whole,
    ) = refs[pieces:]
    step = pl.program_id(0)
    h = lax.axis_index("head")
    width = inputs[0].shape[1]
    group = 4
    for r in range(group):
        part = inputs[r][...].astype(F32)
        if pieces > group:
            part = part + inputs[group + r][...].astype(F32) + res_b[:, block_columns(h, r, width)]
        whole[:, block_columns(h, r, width)] = part
    x = whole[...]
    mean = jnp.sum(x, axis=1, keepdims=True) * (1.0 / D)
    center = x - mean
    inverse = lax.rsqrt(jnp.sum(center * center, axis=1, keepdims=True) * (1.0 / D) + EPSILON)
    normed = center * inverse
    inv_ref[...] = inverse
    normed_ref[...] = normed.astype(BF)
    whole[...] = normed
    unit_ref[...] = whole[:, block_columns(h, 0, width)]
    attention_input = (normed * scale[0:1] + scale[1:2]).astype(BF)
    ai_ref[...] = attention_input
    fi_ref[...] = (normed * scale[2:3] + scale[3:4]).astype(BF)
    projected = dot_nn(attention_input, w_ref[...]) + b_ref[...]
    q, k, v = split_heads(projected)
    v = v.astype(BF)
    cos = twice(cos_ref[...])
    sin = twice(sin_ref[...])
    q_turn = q * cos + swap_pairs(q) * sin
    k_turn = k * cos + swap_pairs(k) * sin
    query_feat = jnp.exp(dot_nn(q_turn, map_ref[...], HIGHEST))
    key_norm = head_sum(k * k, ones_ref[...]) * (0.5 / HEAD_DIM)
    key_feat = (
        keep_ref[...] * feat_ref[...] * jnp.exp(dot_nn(k_turn, map_ref[...], HIGHEST) - key_norm)
    ).astype(BF)
    qf_ref[...] = query_feat.astype(BF)
    kf_ref[...] = key_feat
    v_ref[...] = v
    k_ref[...] = k.astype(BF)
    place = (row_of((CHUNK, 1)) + step * CHUNK).astype(F32)
    masked = jnp.where(place >= last_ref[...], key_feat.astype(F32), 0.0)

    @pl.when(step == 0)
    def _():
        sum_ref[...] = jnp.zeros_like(sum_ref)
        state_ref[...] = jnp.zeros_like(state_ref)

    sum_ref[...] += dot_tn(masked.astype(BF), v)
    state_ref[FEATURES : FEATURES + 1, :] += jnp.sum(masked, axis=0, keepdims=True)

    @pl.when(step == pl.num_programs(0) - 1)
    def _():
        state_ref[0:FEATURES, :] = pack_state(sum_ref[...])


def project(inputs, res_b, scale, w, b, tables, feat, consts):
    rows, width = inputs[0].shape
    a = feat.shape[1]
    steps = rows // CHUNK
    cos, sin, begin, keep, last = tables
    args = list(inputs) + [
        res_b,
        scale,
        w,
        b,
        cos,
        sin,
        begin,
        keep,
        last,
        feat,
        consts["map_t"],
        consts["ones"],
    ]
    in_specs = [rowed(width)] * len(inputs) + [
        full(res_b.shape),
        full(scale.shape),
        full(w.shape),
        full(b.shape),
        rowed(cos.shape[1]),
        rowed(sin.shape[1]),
        rowed(1),
        rowed(1),
        full((1, 1)),
        full(feat.shape),
        full((a, a)),
        full((a, a)),
    ]
    out = [
        ((rows, D), BF),
        ((rows, D), BF),
        ((rows, D), BF),
        ((rows, width), F32),
        ((rows, 1), F32),
        ((rows, a), BF),
        ((rows, a), BF),
        ((rows, a), BF),
        ((rows, a), BF),
    ]
    out_specs = [rowed(shape[1]) for shape, kind in out] + [full((STATE_ROWS, a))]
    out_shape = [jax.ShapeDtypeStruct(*o) for o in out] + [
        jax.ShapeDtypeStruct((STATE_ROWS, a), F32)
    ]
    return call(
        functools.partial(project_kernel, len(inputs)),
        "project",
        (steps,),
        in_specs,
        out_specs,
        out_shape,
        [pltpu.VMEM((a, a), F32), pltpu.VMEM((CHUNK, D), F32)],
        2 * rows * D * 3 * a * 2,
        args,
    )


def raise_kernel(fi_ref, w_ref, b_ref, act_ref, slope_ref):
    raised = dot_nn(fi_ref[...], w_ref[...]) + b_ref[...]
    cumulative = 0.5 + 0.5 * lax.erf(raised * math.sqrt(0.5))
    density = jnp.exp(raised * raised * -0.5) * (1.0 / math.sqrt(2.0 * math.pi))
    act_ref[...] = (raised * cumulative).astype(BF)
    slope_ref[...] = (cumulative + raised * density).astype(BF)


def raise_up(fi, w, b):
    rows = fi.shape[0]
    hidden = w.shape[1]
    return call(
        raise_kernel,
        "raise_up",
        (rows // CHUNK,),
        [rowed(D), full(w.shape), full(b.shape)],
        [rowed(hidden)] * 2,
        [jax.ShapeDtypeStruct((rows, hidden), BF)] * 2,
        [],
        2 * rows * D * hidden * 3,
        [fi, w, b],
    )


def pair_mask(begin, step):
    shape = (CHUNK, CHUNK)
    t = row_of(shape)
    s = lane_of(shape)
    return (s <= t) & ((s + step * CHUNK).astype(F32) >= begin)


def spread(h, whole, near_ref, far_ref):
    w = D // 4
    near_ref[0] = whole[:, block_columns(h, 0, w)]
    near_ref[1] = whole[:, block_columns(h, 2, w)]
    far_ref[0] = whole[:, block_columns(h, 1, w)]
    far_ref[1] = whole[:, block_columns(h, 3, w)]


def attend_kernel(
    qf_ref,
    kf_ref,
    v_ref,
    begin_ref,
    keep_ref,
    in_ref,
    act_ref,
    ow_ref,
    dw_ref,
    ones_ref,
    near_ref,
    far_ref,
    att_ref,
    low_ref,
    ratio_ref,
    states_ref,
    totals_ref,
    state,
    total,
    whole,
):
    step = pl.program_id(0)
    h = lax.axis_index("head")

    @pl.when(step == 0)
    def _():
        state[...] = unpack_state(in_ref[0:FEATURES, :])
        total[...] = jnp.broadcast_to(in_ref[FEATURES : FEATURES + 1, :], total.shape)

    q = qf_ref[...]
    k = kf_ref[...]
    v = v_ref[...]
    begin = begin_ref[...]
    keep = keep_ref[...]
    ones = ones_ref[...]
    a = q.shape[1]
    mask = pair_mask(begin, step)
    head_of = lane_of((1, a)) // HEAD_DIM
    held = state[...]
    held_total = total[0:1, :]
    states_ref[0] = held
    totals_ref[0] = total[...]
    base = (step * CHUNK).astype(F32)
    use = jnp.where(begin < base, 1.0, 0.0)
    high, low = halves(held)
    num = use * (dot_nn(q, high) + dot_nn(q, low))
    den = use * head_sum(q.astype(F32) * held_total, ones)
    for head in range(a // HEAD_DIM):
        own = (head_of == head).astype(BF)
        scores = dot_nt(q * own, k)
        scores_low = jnp.where(mask, scores, 0.0).astype(BF)
        num = num + dot_nn(scores_low, v * own)
        den = den + dot_nn(scores_low, jnp.broadcast_to(own, (CHUNK, a)))
    ratio = keep / (den + 1.0 - keep)
    att = num * ratio
    att_low = att.astype(BF)
    ratio_ref[...] = ratio
    att_ref[...] = att
    low_ref[...] = att_low
    end = begin[CHUNK - 1 : CHUNK, :]
    place = (row_of((CHUNK, 1)) + step * CHUNK).astype(F32)
    masked = jnp.where(place >= end, k.astype(F32), 0.0)
    passing = jnp.where(end < base, 1.0, 0.0)
    state[...] = passing * held + jnp.where(
        block_diagonal(a), dot_tn(masked.astype(BF), v), 0.0
    )
    total[...] = jnp.broadcast_to(
        passing * held_total + jnp.sum(masked, axis=0, keepdims=True), total.shape
    )
    whole[...] = (dot_nt(att_low, ow_ref[...]) + dot_nt(act_ref[...], dw_ref[...])).astype(BF)
    spread(h, whole, near_ref, far_ref)


def attend(qf, kf, v, begin, keep, state_in, act, out_w, down_w, consts):
    rows, a = qf.shape
    steps = rows // CHUNK
    hidden = act.shape[1]
    quarter = pl.BlockSpec((2, CHUNK, D // 4), lambda i: (0, i, 0))
    return call(
        attend_kernel,
        "attend",
        (steps,),
        [
            rowed(a),
            rowed(a),
            rowed(a),
            rowed(1),
            rowed(1),
            full((STATE_ROWS, a)),
            rowed(hidden),
            full(out_w.shape),
            full(down_w.shape),
            full((a, a)),
        ],
        [
            quarter,
            quarter,
            rowed(a),
            rowed(a),
            rowed(a),
            pl.BlockSpec((1, a, a), lambda i: (i, 0, 0)),
            pl.BlockSpec((1, 8, a), lambda i: (i, 0, 0)),
        ],
        [
            jax.ShapeDtypeStruct((2, rows, D // 4), BF),
            jax.ShapeDtypeStruct((2, rows, D // 4), BF),
            jax.ShapeDtypeStruct((rows, a), F32),
            jax.ShapeDtypeStruct((rows, a), BF),
            jax.ShapeDtypeStruct((rows, a), F32),
            jax.ShapeDtypeStruct((steps, a, a), F32),
            jax.ShapeDtypeStruct((steps, 8, a), F32),
        ],
        [pltpu.VMEM((a, a), F32), pltpu.VMEM((8, a), F32), pltpu.VMEM((CHUNK, D), BF)],
        2 * rows * D * (hidden + a) * 2,
        [qf, kf, v, begin, keep, state_in, act, out_w, down_w, consts["ones"]],
    )


def lower_kernel(
    g0,
    g1,
    g2,
    g3,
    dw_ref,
    ow_ref,
    slope_ref,
    ratio_ref,
    att_ref,
    qf_ref,
    begin_ref,
    ones_ref,
    grad_ref,
    raised_ref,
    num_ref,
    den_ref,
    bias_ref,
    entry_ref,
    sum_ref,
):
    step = pl.program_id(0)

    @pl.when(step == 0)
    def _():
        sum_ref[...] = jnp.zeros_like(sum_ref)
        entry_ref[...] = jnp.zeros_like(entry_ref)
        bias_ref[...] = jnp.zeros_like(bias_ref)

    h = lax.axis_index("head")
    for r, part in enumerate((g0, g1, g2, g3)):
        grad_ref[:, block_columns(h, r, part.shape[1])] = part[...]
    grad = grad_ref[...]
    d_att = dot_nn(grad, ow_ref[...])
    d_num = (d_att * ratio_ref[...]).astype(BF)
    d_den = -head_sum(d_num.astype(F32) * att_ref[...], ones_ref[...])
    num_ref[...] = d_num
    den_ref[...] = d_den
    entering = jnp.where(begin_ref[...] < 0.0, qf_ref[...].astype(F32), 0.0)
    sum_ref[...] += dot_tn(entering.astype(BF), d_num)
    entry_ref[FEATURES : FEATURES + 1, :] += jnp.sum(entering * d_den, axis=0, keepdims=True)
    d_raised = (dot_nn(grad, dw_ref[...]) * slope_ref[...].astype(F32)).astype(BF)
    raised_ref[...] = d_raised
    bias_ref[...] += jnp.sum(d_raised.astype(F32), axis=0, keepdims=True)

    @pl.when(step == pl.num_programs(0) - 1)
    def _():
        entry_ref[0:FEATURES, :] = pack_state(sum_ref[...])


def lower(grads, down_w, out_w, slope, ratio, att, qf, begin, consts):
    rows, width = grads[0].shape
    hidden = slope.shape[1]
    a = att.shape[1]
    return call(
        lower_kernel,
        "lower",
        (rows // CHUNK,),
        [rowed(width)] * 4
        + [
            full(down_w.shape),
            full(out_w.shape),
            rowed(hidden),
            rowed(a),
            rowed(a),
            rowed(a),
            rowed(1),
            full((a, a)),
        ],
        [
            rowed(D),
            rowed(hidden),
            rowed(a),
            rowed(a),
            full((1, hidden)),
            full((STATE_ROWS, a)),
        ],
        [
            jax.ShapeDtypeStruct((rows, D), BF),
            jax.ShapeDtypeStruct((rows, hidden), BF),
            jax.ShapeDtypeStruct((rows, a), BF),
            jax.ShapeDtypeStruct((rows, a), F32),
            jax.ShapeDtypeStruct((1, hidden), F32),
            jax.ShapeDtypeStruct((STATE_ROWS, a), F32),
        ],
        [pltpu.VMEM((a, a), F32)],
        2 * rows * D * (hidden + a) * 2,
        list(grads) + [down_w, out_w, slope, ratio, att, qf, begin, consts["ones"]],
    )


def back_kernel(
    qf_ref,
    kf_ref,
    v_ref,
    k_ref,
    num_ref,
    den_ref,
    begin_ref,
    cos_ref,
    sin_ref,
    states_ref,
    totals_ref,
    exit_ref,
    map_ref,
    ones_ref,
    w_ref,
    up_ref,
    raised_ref,
    normed_ref,
    scale_ref,
    proj_ref,
    near_ref,
    far_ref,
    rows_ref,
    bias_ref,
    feat_ref,
    sums_ref,
    state,
    total,
    whole,
):
    h = lax.axis_index("head")
    turn = pl.program_id(0)
    step = pl.num_programs(0) - 1 - turn

    @pl.when(turn == 0)
    def _():
        state[...] = unpack_state(exit_ref[0:FEATURES, :])
        total[...] = jnp.broadcast_to(exit_ref[FEATURES : FEATURES + 1, :], total.shape)
        bias_ref[...] = jnp.zeros_like(bias_ref)
        feat_ref[...] = jnp.zeros_like(feat_ref)
        sums_ref[...] = jnp.zeros_like(sums_ref)

    q = qf_ref[...]
    k = kf_ref[...]
    v = v_ref[...]
    d_num = num_ref[...]
    d_den = den_ref[...]
    begin = begin_ref[...]
    ones = ones_ref[...]
    a = q.shape[1]
    mask = pair_mask(begin, step)
    head_of = lane_of((1, a)) // HEAD_DIM
    base = (step * CHUNK).astype(F32)
    use = jnp.where(begin < base, 1.0, 0.0)
    end = begin[CHUNK - 1 : CHUNK, :]
    place = (row_of((CHUNK, 1)) + step * CHUNK).astype(F32)
    inside = jnp.where(place >= end, 1.0, 0.0)
    passing = jnp.where(end < base, 1.0, 0.0)
    held_high, held_low = halves(states_ref[0])
    held_total = totals_ref[0][0:1, :]
    after = state[...]
    after_total = total[0:1, :]
    after_high, after_low = halves(after)
    q_wide = q.astype(F32)
    k_wide = k.astype(F32)
    masked = (k_wide * inside).astype(BF)
    d_q = use * (dot_nt(d_num, held_high) + dot_nt(d_num, held_low) + d_den * held_total)
    d_k = inside * (dot_nt(v, after_high) + dot_nt(v, after_low) + after_total)
    d_v = dot_nn(masked, after_high) + dot_nn(masked, after_low)
    for head in range(a // HEAD_DIM):
        own = (head_of == head).astype(BF)
        q_own = q * own
        num_own = d_num * own
        scores_low = jnp.where(mask, dot_nt(q_own, k), 0.0).astype(BF)
        column = d_den[:, head * HEAD_DIM : head * HEAD_DIM + 1]
        d_scores = jnp.where(mask, dot_nt(num_own, v) + column, 0.0).astype(BF)
        d_q = d_q + dot_nn(d_scores, k * own)
        d_k = d_k + dot_tn(d_scores, q_own)
        d_v = d_v + dot_tn(scores_low, num_own)
    q_used = q_wide * use
    state[...] = passing * after + jnp.where(
        block_diagonal(a), dot_tn(q_used.astype(BF), d_num), 0.0
    )
    total[...] = jnp.broadcast_to(
        passing * after_total + jnp.sum(q_used * d_den, axis=0, keepdims=True), total.shape
    )
    cos = twice(cos_ref[...])
    sin = twice(sin_ref[...])
    d_query = dot_nn(d_q * q_wide, map_ref[...], HIGHEST)
    d_query = d_query * cos - swap_pairs(d_query) * sin
    d_key_log = d_k * k_wide
    feat_ref[...] += jnp.sum(d_key_log, axis=0, keepdims=True)
    d_key = dot_nn(d_key_log, map_ref[...], HIGHEST)
    d_key = d_key * cos - swap_pairs(d_key) * sin
    d_key = d_key - head_sum(d_key_log, ones) * k_ref[...].astype(F32) * (1.0 / HEAD_DIM)
    d_proj = join_heads(d_query, d_key, d_v).astype(BF)
    proj_ref[...] = d_proj
    bias_ref[...] += jnp.sum(d_proj.astype(F32), axis=0, keepdims=True)
    normed = normed_ref[...].astype(F32)
    scale = scale_ref[...]
    d_attention = dot_nt(d_proj, w_ref[...])
    d_feed = dot_nt(raised_ref[...], up_ref[...])
    sums_ref[0:1, :] += jnp.sum(d_attention * normed, axis=0, keepdims=True)
    sums_ref[1:2, :] += jnp.sum(d_feed * normed, axis=0, keepdims=True)
    sums_ref[2:3, :] += jnp.sum(d_attention, axis=0, keepdims=True)
    sums_ref[3:4, :] += jnp.sum(d_feed, axis=0, keepdims=True)
    d_normed = (d_attention * scale[0:1] + d_feed * scale[2:3]).astype(BF)
    whole[...] = d_normed
    spread(h, whole, near_ref, far_ref)
    high, low = halves(d_normed.astype(F32) * normed)
    row = jnp.ones((8, D), BF)
    first = dot_nt(row, d_normed)
    second = dot_nt(row, high) + dot_nt(row, low)
    rows_ref[...] = jnp.where(row_of(first.shape) == 0, first, second)


def back(kept, d_num, d_den, d_raised, exit_state, tables, w_qkv, up_w, scale, consts):
    qf, kf, v, k, normed, states, totals = kept
    cos, sin, begin, keep, last = tables
    rows, a = qf.shape
    n = rows // CHUNK
    hidden = d_raised.shape[1]
    args = [
        qf,
        kf,
        v,
        k,
        d_num,
        d_den,
        begin,
        cos,
        sin,
        states,
        totals,
        exit_state,
        consts["map"],
        consts["ones"],
        w_qkv,
        up_w,
        d_raised,
        normed,
        scale,
    ]
    quarter = pl.BlockSpec((2, CHUNK, D // 4), lambda i: (0, n - 1 - i, 0))
    in_specs = (
        [rowed_back(a, n)] * 6
        + [rowed_back(1, n), rowed_back(cos.shape[1], n), rowed_back(sin.shape[1], n)]
        + [
            pl.BlockSpec((1, a, a), lambda i: (n - 1 - i, 0, 0)),
            pl.BlockSpec((1, 8, a), lambda i: (n - 1 - i, 0, 0)),
            full((STATE_ROWS, a)),
            full((a, a)),
            full((a, a)),
            full(w_qkv.shape),
            full(up_w.shape),
            rowed_back(hidden, n),
            rowed_back(D, n),
            full(scale.shape),
        ]
    )
    out_specs = [
        rowed_back(3 * a, n),
        quarter,
        quarter,
        pl.BlockSpec((8, CHUNK), lambda i: (0, n - 1 - i)),
        full((1, 3 * a)),
        full((1, a)),
        full((8, D)),
    ]
    out_shape = [
        jax.ShapeDtypeStruct((rows, 3 * a), BF),
        jax.ShapeDtypeStruct((2, rows, D // 4), BF),
        jax.ShapeDtypeStruct((2, rows, D // 4), BF),
        jax.ShapeDtypeStruct((8, rows), F32),
        jax.ShapeDtypeStruct((1, 3 * a), F32),
        jax.ShapeDtypeStruct((1, a), F32),
        jax.ShapeDtypeStruct((8, D), F32),
    ]
    return call(
        back_kernel,
        "attend_back",
        (n,),
        in_specs,
        out_specs,
        out_shape,
        [pltpu.VMEM((a, a), F32), pltpu.VMEM((8, a), F32), pltpu.VMEM((CHUNK, D), BF)],
        2 * rows * D * (hidden + 3 * a) * 3,
        args,
    )


def weight_kernel(count, x_ref, *refs):
    x = x_ref[...]
    out = refs[count]
    at = 0
    for y in refs[:count]:
        width = y.shape[1]
        out[:, at : at + width] = dot_tn(x, y[...]).astype(BF)
        at += width


def weight_grad(x, ys):
    rows = x.shape[0]
    columns = sum(y.shape[1] for y in ys)
    tile = D // 4
    return call(
        functools.partial(weight_kernel, len(ys)),
        "weight_grad",
        (D // tile,),
        [pl.BlockSpec((rows, tile), lambda i: (0, i))] + [full(y.shape) for y in ys],
        [pl.BlockSpec((tile, columns), lambda i: (i, 0))],
        [jax.ShapeDtypeStruct((D, columns), BF)],
        [],
        2 * rows * D * columns,
        [x] + list(ys),
    )[0]


def ring_place(index, n):
    return jnp.where(index % 2 == 0, index // 2, n - 1 - index // 2)


def ring_index(place, n):
    return jnp.where(place < n // 2, 2 * place, 2 * (n - 1 - place) + 1)


def ring_kernel(n, parts, sources, *refs):
    count = len(parts)
    source = refs[:sources]
    out = refs[sources : 2 * sources]
    held = refs[2 * sources : 2 * sources + count]
    send_sem, recv_sem = refs[2 * sources + count :]
    share = D // n
    place = ring_place(lax.axis_index("seq"), n)
    right = ring_index(lax.rem(place + 1, n), n)
    left = ring_index(lax.rem(place + n - 1, n), n)
    barrier = pltpu.get_barrier_semaphore()
    for neighbour in (left, right):
        pl.semaphore_signal(
            barrier,
            inc=1,
            device_id={"seq": neighbour},
            device_id_type=pl.DeviceIdType.MESH,
        )
    pl.semaphore_wait(barrier, 2)

    def own(part, step):
        array, start, width, way = part
        ahead = lax.rem(place - way * (1 + step) + 2 * n, n)
        rows = pl.ds(pl.multiple_of(ring_index(ahead, n) * share, share), share)
        return source[array].at[rows, pl.ds(start, width)]

    def send(r, step, block):
        return pltpu.make_async_remote_copy(
            src_ref=block,
            dst_ref=held[r].at[step],
            send_sem=send_sem.at[r, step],
            recv_sem=recv_sem.at[r, step],
            device_id={"seq": right if parts[r][3] > 0 else left},
            device_id_type=pl.DeviceIdType.MESH,
        )

    for r in range(count):
        send(r, 0, own(parts[r], 0)).start()

    def turn(step, carry):
        for r in range(count):
            block = held[r].at[step - 1]
            send(r, step - 1, block).wait_recv()
            block[...] = (block[...].astype(F32) + own(parts[r], step)[...].astype(F32)).astype(BF)
            send(r, step, block).start()
        return carry

    lax.fori_loop(1, n - 1, turn, 0)
    for r in range(count):
        block = held[r].at[n - 2]
        send(r, n - 2, block).wait_recv()
        array, start, width, way = parts[r]
        out[array][:, pl.ds(start, width)] = block[...].astype(F32) + own(parts[r], n - 1)[
            ...
        ].astype(F32)

    def finish(step, carry):
        for r in range(count):
            send(r, step, held[r].at[step]).wait_send()
        return carry

    lax.fori_loop(0, n - 1, finish, 0)


def ring_sum(arrays, parts, ident):
    n = lax.axis_size("seq")
    share = D // n
    space = pl.BlockSpec(memory_space=pltpu.VMEM)
    return pl.pallas_call(
        functools.partial(ring_kernel, n, parts, len(arrays)),
        name="ring_sum",
        in_specs=[space] * len(arrays),
        out_specs=[space] * len(arrays),
        out_shape=[jax.ShapeDtypeStruct((share, x.shape[1]), F32) for x in arrays],
        scratch_shapes=[pltpu.VMEM((n - 1, share, part[2]), BF) for part in parts]
        + [
            pltpu.SemaphoreType.DMA((len(parts), n - 1)),
            pltpu.SemaphoreType.DMA((len(parts), n - 1)),
        ],
        compiler_params=pltpu.CompilerParams(
            collective_id=ident, has_side_effects=True, vmem_limit_bytes=VMEM_BYTES
        ),
        cost_estimate=pl.CostEstimate(flops=10**8, bytes_accessed=10**8, transcendentals=0),
    )(*arrays)


def exchange(value, axis, step):
    count = lax.axis_size(axis)
    return lax.ppermute(value, axis, [(i, i ^ step) for i in range(count)])


def shifted(value, axis, step):
    count = lax.axis_size(axis)
    return lax.ppermute(
        value, axis, [(i, i + step) for i in range(count) if 0 <= i + step < count]
    )


def gather_heads(own):
    across = exchange(own, "head", 2)
    beside = exchange(own, "head", 1)
    return [own, beside, across, exchange(across, "head", 1)]


def scatter_heads(near, far):
    got = exchange(far, "head", 1)
    across = exchange(near[1] + got[1], "head", 2)
    return near[0].astype(F32) + got[0].astype(F32) + across.astype(F32)


def on_device(
    acts,
    cotangent,
    lengths,
    keep_mask,
    ln_gain,
    ln_bias,
    qkv_w,
    qkv_b,
    feat_w,
    out_w,
    up_w,
    up_b,
    down_w,
    res_b,
):
    rows, width = acts.shape
    heads = feat_w.shape[1]
    a = heads * HEAD_DIM
    n = lax.axis_size("seq")
    tokens = rows * n
    longest = 2048 if tokens <= 8192 else 4096
    hops = -(-longest // rows)
    h = lax.axis_index("head").astype(jnp.int32)
    first = lax.axis_index("seq") * rows

    def relative(array, axis):
        return jnp.concatenate(
            [
                lax.dynamic_slice_in_dim(array, lax.bitwise_xor(h, r) * width, width, axis)
                for r in range(4)
            ],
            axis,
        )

    pieces = gather_heads(acts)
    res = lax.dynamic_slice_in_dim(res_b, h * width, width, 1)
    scales = jnp.stack([ln_gain, ln_bias], axis=2).reshape(LAYERS, 4, D)
    feats = feat_w.reshape(LAYERS, 1, a)

    starts = (jnp.cumsum(lengths) - lengths).astype(jnp.int32)

    def begin_of(slots):
        return jnp.max(jnp.where(starts[None, :] <= slots[:, None], starts[None, :], 0), axis=1)

    slots = first + jnp.arange(rows, dtype=jnp.int32)
    begins = begin_of(slots)
    positions = (slots - begins).astype(F32)
    begin = (begins - first).astype(F32)[:, None]
    keep = keep_mask.astype(F32)[:, None]
    last = begin[rows - 1 :, :]
    half = ROT // 2
    rates = np.zeros(HEAD_DIM)
    rates[:half] = ROTARY_BASE ** (-2.0 * np.arange(half) / ROT)
    rates[half:ROT] = rates[:half]
    sign = np.zeros(HEAD_DIM)
    sign[:half] = -1.0
    sign[half:ROT] = 1.0
    phase = positions[:, None] * jnp.asarray(np.tile(rates, 2), F32)[None, :]
    cos = jnp.cos(phase)
    sin = jnp.sin(phase) * jnp.asarray(np.tile(sign, 2), F32)[None, :]
    tables = (cos, sin, begin, keep, last)
    fold = sample_points(FEATURES, HEAD_DIM) @ cosine_table(HEAD_DIM) / math.sqrt(HEAD_DIM)
    eye = np.eye(heads)
    consts = {
        "map": jnp.asarray(np.kron(eye, fold), F32),
        "map_t": jnp.asarray(np.kron(eye, fold.T), F32),
        "ones": jnp.asarray(np.kron(eye, np.ones((HEAD_DIM, HEAD_DIM))), BF),
    }

    def linked(step):
        edge = first - 1 if step > 0 else first + rows * -step - 1
        held = first + rows - 1 if step < 0 else first - 1 - (step - 1) * rows
        return (begin_of(jnp.reshape(edge, (1,)))[0] <= held).astype(F32)

    def entering(state, sign):
        total = shifted(state, "seq", sign)
        for step in range(2, hops + 1):
            total = total + shifted(state, "seq", sign * step) * linked(sign * step)
        return total

    own = acts.astype(F32)
    inputs = pieces
    kept = []
    for l in range(LAYERS):
        ai, fi, normed, unit, inverse, qf, kf, v, k, state = project(
            inputs, res_b[0:1], scales[l], qkv_w[l], qkv_b[l][None, :], tables, feats[l], consts
        )
        state_in = entering(state, 1)
        act, slope = raise_up(fi, up_w[l], up_b[l][None, :])
        near, far, att, att_low, ratio, states, totals = attend(
            qf, kf, v, begin, keep, state_in, act, out_w[l], down_w[l], consts
        )
        branch = scatter_heads(near, far)
        if l + 1 < LAYERS:
            branch = branch.astype(BF)
            inputs = pieces + gather_heads(branch)
        own = own + branch.astype(F32) + res[l]
        kept.append(
            (
                (qf, kf, v, k, normed, states, totals),
                ai,
                fi,
                unit,
                inverse,
                act,
                slope,
                att,
                att_low,
                ratio,
            )
        )
    out_acts = own

    upstream = cotangent.astype(F32)
    matrices = [None] * LAYERS
    smalls = [None] * LAYERS
    sums = [None] * LAYERS
    for l in reversed(range(LAYERS)):
        local, ai, fi, unit, inverse, act, slope, att, att_low, ratio = kept[l]
        d_res = jnp.sum(upstream, axis=0)
        grads = gather_heads(upstream.astype(BF))
        grad, d_raised, d_num, d_den, d_up_b, entry = lower(
            grads, down_w[l], out_w[l], slope, ratio, att, local[0], begin, consts
        )
        exit_state = entering(entry, -1)
        d_down_out = weight_grad(grad, [act, att_low])
        d_up = weight_grad(fi, [d_raised])
        d_proj, near, far, row_sums, d_qkv_b, d_feat, column_sums = back(
            local, d_num, d_den, d_raised, exit_state, tables, qkv_w[l], up_w[l], scales[l], consts
        )
        d_qkv = weight_grad(ai, [d_proj])
        row_sums = row_sums + exchange(row_sums, "head", 1)
        row_sums = row_sums + exchange(row_sums, "head", 2)
        d_normed = scatter_heads(near, far)
        upstream = upstream + inverse * (
            d_normed - row_sums[0][:, None] / D - unit * row_sums[1][:, None] / D
        )
        if l == 0 and n == 8:
            parts = (
                (0, 0, 640, 1),
                (0, 640, 640, 1),
                (1, 0, 256, 1),
                (1, 256, 768, -1),
                (2, 0, 768, -1),
            )
            matrices[l] = ring_sum([d_down_out, d_up, d_qkv], parts, 1)
        else:
            summed = lax.psum_scatter(
                jnp.concatenate([d_down_out, d_up, d_qkv], axis=1),
                "seq",
                scatter_dimension=0,
                tiled=True,
            ).astype(F32)
            at = d_down_out.shape[1]
            matrices[l] = (
                summed[:, :at],
                summed[:, at : at + d_up.shape[1]],
                summed[:, at + d_up.shape[1] :],
            )
        sums[l] = column_sums[:4]
        smalls[l] = jnp.concatenate([d_qkv_b[0], d_up_b[0], d_feat[0], d_res])

    column_sums = relative(jnp.stack(sums), 2).reshape(LAYERS, 4, 4, width)
    near = jnp.stack([column_sums[:, :, 0], column_sums[:, :, 2]])
    far = jnp.stack([column_sums[:, :, 1], column_sums[:, :, 3]])
    norm_sums = scatter_heads(near, far)
    bundle = jnp.concatenate([norm_sums.reshape(LAYERS, 4 * width), jnp.stack(smalls)], axis=1)
    step = 1
    while step < n:
        bundle = bundle + exchange(bundle, "seq", step)
        step *= 2
    at = 0
    taken = []
    for size in (2 * width, 2 * width, 3 * a, d_up_b.shape[1], a, width):
        taken.append(bundle[:, at : at + size])
        at += size
    d_gain, d_bias, d_qkv_b, d_up_b, d_feat, d_res = taken

    hidden = up_w.shape[2]
    d_down = jnp.stack([m[0][:, :hidden] for m in matrices])
    d_out = jnp.stack([m[0][:, hidden:] for m in matrices])
    d_up = jnp.stack([m[1] for m in matrices])
    d_qkv = jnp.stack([m[2] for m in matrices])
    return (
        out_acts,
        upstream,
        d_qkv,
        d_out,
        d_up,
        d_down,
        d_qkv_b,
        d_up_b,
        (d_feat / feats[:, 0]).reshape(LAYERS, heads, FEATURES),
        d_gain.reshape(LAYERS, 2, width),
        d_bias.reshape(LAYERS, 2, width),
        d_res,
    )


def solution(mesh):
    return jax.shard_map(
        on_device,
        mesh=mesh,
        in_specs=(
            P("seq", "head"),
            P("seq", "head"),
            P(),
            P("seq"),
            P(),
            P(),
            P(None, None, "head"),
            P(None, "head"),
            P(None, "head", None),
            P(None, None, "head"),
            P(None, None, "head"),
            P(None, "head"),
            P(None, None, "head"),
            P(),
        ),
        out_specs=(
            P("seq", "head"),
            P("seq", "head"),
            P(None, "seq", "head"),
            P(None, "seq", "head"),
            P(None, "seq", "head"),
            P(None, "seq", "head"),
            P(None, "head"),
            P(None, "head"),
            P(None, "head", None),
            P(None, None, "head"),
            P(None, None, "head"),
            P(None, "head"),
        ),
        check_vma=False,
    )
```

```python
import functools
import math

import jax
import jax.numpy as jnp
import numpy as np
from jax import lax
from jax.experimental import pallas as pl
from jax.experimental.pallas import tpu as pltpu
from jax.sharding import PartitionSpec as P

D = 1024
HEAD_DIM = 64
ROT = 16
FEATURES = 64
LAYERS = 2
CHUNK = 256

EPSILON = 1e-05
ROTARY_BASE = 10000.0
HIGHEST = lax.Precision.HIGHEST
BF = jnp.bfloat16
F32 = jnp.float32
STATE_ROWS = 72
VMEM_BYTES = 56 * 1024 * 1024


def prime_numbers(count):
    found = []
    candidate = 2
    while len(found) < count:
        if all((candidate % prime != 0 for prime in found)):
            found.append(candidate)
        candidate = candidate + 1
    return found


def sample_points(rows, columns):
    roots = np.sqrt(np.array(prime_numbers(2 * columns)) * 1.0)
    fractions = roots - np.floor(roots)
    grid = np.outer(np.arange(1, rows + 1) * 1.0, fractions) % 1.0
    radius = np.sqrt(-2.0 * np.log(1.0 - grid[:, :columns]))
    return radius * np.cos(2.0 * math.pi * grid[:, columns:])


def cosine_table(size):
    wave = np.arange(size)[:, None] * 1.0
    place = np.arange(size)[None, :] * 1.0
    table = np.cos(math.pi * (place + 0.5) * wave / size) * math.sqrt(2.0 / size)
    return table * np.where(wave == 0, math.sqrt(0.5), 1.0)


def dot_nn(a, b, precision=None):
    return lax.dot_general(
        a, b, (((1,), (0,)), ((), ())), precision=precision, preferred_element_type=F32
    )


def dot_nt(a, b, precision=None):
    return lax.dot_general(
        a, b, (((1,), (1,)), ((), ())), precision=precision, preferred_element_type=F32
    )


def dot_tn(a, b, precision=None):
    return lax.dot_general(
        a, b, (((0,), (0,)), ((), ())), precision=precision, preferred_element_type=F32
    )


def halves(wide):
    high = wide.astype(BF)
    return high, (wide - high.astype(F32)).astype(BF)


def lane_of(shape):
    return lax.broadcasted_iota(jnp.int32, shape, 1)


def row_of(shape):
    return lax.broadcasted_iota(jnp.int32, shape, 0)


def swap_pairs(x):
    width = x.shape[1]
    later = pltpu.roll(x, width - ROT // 2, 1)
    earlier = pltpu.roll(x, ROT // 2, 1)
    return jnp.where(lane_of(x.shape) % ROT < ROT // 2, later, earlier)


def twice(table):
    return jnp.concatenate([table, table], axis=1)


def block_columns(h, r, width):
    return pl.ds(pl.multiple_of(lax.bitwise_xor(h, r) * width, width), width)


def split_heads(projected):
    heads = projected.shape[1] // (3 * HEAD_DIM)
    return [
        jnp.concatenate(
            [
                projected[:, (3 * j + kind) * HEAD_DIM : (3 * j + kind + 1) * HEAD_DIM]
                for j in range(heads)
            ],
            axis=1,
        )
        for kind in range(3)
    ]


def join_heads(q, k, v):
    heads = q.shape[1] // HEAD_DIM
    return jnp.concatenate(
        [
            part[:, j * HEAD_DIM : (j + 1) * HEAD_DIM]
            for j in range(heads)
            for part in (q, k, v)
        ],
        axis=1,
    )


def block_diagonal(width):
    shape = (width, width)
    return (row_of(shape) // HEAD_DIM) == (lane_of(shape) // HEAD_DIM)


def pack_state(full):
    width = full.shape[0]
    kept = jnp.where(block_diagonal(width), full, 0.0)
    packed = kept[0:FEATURES]
    for head in range(1, width // FEATURES):
        packed = packed + kept[head * FEATURES : (head + 1) * FEATURES]
    return packed


def unpack_state(packed):
    width = packed.shape[1]
    tall = jnp.concatenate([packed] * (width // FEATURES), axis=0)
    return jnp.where(block_diagonal(width), tall, 0.0)


def head_sum(values, ones):
    high, low = halves(values)
    return dot_nn(high, ones) + dot_nn(low, ones)


def call(kernel, name, grid, in_specs, out_specs, out_shape, scratch, flops, args, prefetch=0):
    moved = sum(int(np.prod(a.shape)) * a.dtype.itemsize for a in list(args) + list(out_shape))
    return pl.pallas_call(
        kernel,
        name=name,
        grid_spec=pltpu.PrefetchScalarGridSpec(
            num_scalar_prefetch=prefetch,
            grid=grid,
            in_specs=in_specs,
            out_specs=out_specs,
            scratch_shapes=scratch,
        ),
        out_shape=out_shape,
        compiler_params=pltpu.CompilerParams(vmem_limit_bytes=VMEM_BYTES),
        cost_estimate=pl.CostEstimate(flops=int(flops), bytes_accessed=moved, transcendentals=0),
    )(*args)


def full(shape):
    return pl.BlockSpec(shape, lambda *i: (0,) * len(shape))


def rowed(width):
    return pl.BlockSpec((CHUNK, width), lambda i: (i, 0))


def rowed_back(width, count):
    return pl.BlockSpec((CHUNK, width), lambda i: (count - 1 - i, 0))


def layered(array, l):
    return pl.BlockSpec((None,) + array.shape[1:], lambda *i: (l, 0, 0))


def rows_at(c):
    return pl.ds(pl.multiple_of(c * CHUNK, CHUNK), CHUNK)


def push(source, target, send, recv, where):
    return pltpu.make_async_remote_copy(
        src_ref=source,
        dst_ref=target,
        send_sem=send,
        recv_sem=recv,
        device_id=where,
        device_id_type=pl.DeviceIdType.MESH,
    )


class Gather:
    def __init__(self, h, own, buffers, sems):
        self.own = own
        self.beside, self.across, self.corner = buffers
        self.send, self.recv = sems
        self.near = {"head": lax.bitwise_xor(h, 1)}
        self.far = {"head": lax.bitwise_xor(h, 2)}

    @staticmethod
    def scratch(rows, width):
        count = rows // CHUNK
        return [pltpu.VMEM((rows, width), BF)] * 3 + [pltpu.SemaphoreType.DMA((3, count))] * 2

    def copy(self, kind, c):
        source, target, where = (
            (self.own, self.across, self.far),
            (self.own, self.beside, self.near),
            (self.across, self.corner, self.near),
        )[kind]
        rows = rows_at(c)
        return push(
            source.at[rows, :],
            target.at[rows, :],
            self.send.at[kind, c],
            self.recv.at[kind, c],
            where,
        )

    def start(self, c):
        self.copy(0, c).start()
        self.copy(1, c).start()

    def relay(self, c):
        self.copy(0, c).wait_recv()
        self.copy(2, c).start()

    def ready(self, c):
        self.copy(1, c).wait_recv()
        self.copy(2, c).wait_recv()

    def pieces(self, c):
        rows = rows_at(c)
        return [ref[rows, :] for ref in (self.own, self.beside, self.across, self.corner)]

    def finish(self, c):
        for kind in range(3):
            self.copy(kind, c).wait_send()


class Scatter:
    def __init__(self, h, buffers, sems):
        self.near, self.far, self.got, self.middle, self.across = buffers
        self.send, self.recv = sems
        self.beside = {"head": lax.bitwise_xor(h, 1)}
        self.beyond = {"head": lax.bitwise_xor(h, 2)}

    @staticmethod
    def scratch(rows, width):
        count = rows // CHUNK
        return (
            [pltpu.VMEM((2, rows, width), BF)] * 3
            + [pltpu.VMEM((rows, width), BF)] * 2
            + [pltpu.SemaphoreType.DMA((2, count))] * 2
        )

    def copy(self, kind, c):
        rows = rows_at(c)
        if kind == 0:
            source, target, where = (
                self.far.at[:, rows, :],
                self.got.at[:, rows, :],
                self.beside,
            )
        else:
            source, target, where = self.middle.at[rows, :], self.across.at[rows, :], self.beyond
        return push(source, target, self.send.at[kind, c], self.recv.at[kind, c], where)

    def put(self, h, c, whole):
        rows = rows_at(c)
        w = self.near.shape[2]
        self.near[0, rows, :] = whole[:, block_columns(h, 0, w)]
        self.near[1, rows, :] = whole[:, block_columns(h, 2, w)]
        self.far[0, rows, :] = whole[:, block_columns(h, 1, w)]
        self.far[1, rows, :] = whole[:, block_columns(h, 3, w)]
        self.copy(0, c).start()

    def relay(self, c):
        self.copy(0, c).wait_recv()
        rows = rows_at(c)
        self.middle[rows, :] = (
            self.near[1, rows, :].astype(F32) + self.got[1, rows, :].astype(F32)
        ).astype(BF)
        self.copy(1, c).start()

    def total(self, c):
        self.copy(1, c).wait_recv()
        rows = rows_at(c)
        return (
            self.near[0, rows, :].astype(F32)
            + self.got[0, rows, :].astype(F32)
            + self.across[rows, :].astype(F32)
        )

    def finish(self, c):
        self.copy(0, c).wait_send()
        self.copy(1, c).wait_send()


def begin_scalar(lengths, slot):
    def one(j, carry):
        at, best = carry
        at = at + lengths[j - 1]
        return at, jnp.where(at <= slot, at, best)

    return lax.fori_loop(1, lengths.shape[0], one, (jnp.int32(0), jnp.int32(0)))[1]


def begin_column(lengths, slots):
    def one(j, carry):
        at, best = carry
        at = at + lengths[j - 1]
        return at, jnp.where(slots >= at, at, best)

    return lax.fori_loop(1, lengths.shape[0], one, (jnp.int32(0), jnp.zeros_like(slots)))[1]


class HandOver:
    def __init__(self, n, hops, rows, sign, packed, buffer, sems):
        self.n, self.hops, self.rows, self.sign = n, hops, rows, sign
        self.packed, self.buffer = packed, buffer
        self.send, self.recv = sems
        self.here = lax.axis_index("seq")

    @staticmethod
    def scratch(hops, width):
        return [pltpu.VMEM((hops, STATE_ROWS, width), F32)] + [
            pltpu.SemaphoreType.DMA((hops,))
        ] * 2

    def inside(self, index):
        return (index >= 0) & (index < self.n)

    def copy(self, j):
        return push(
            self.packed,
            self.buffer.at[j - 1],
            self.send.at[j - 1],
            self.recv.at[j - 1],
            {"seq": lax.rem(self.here + self.sign * j + self.n, self.n)},
        )

    def clear(self):
        self.buffer[...] = jnp.zeros_like(self.buffer)

    def start(self):
        for j in range(1, self.hops + 1):

            @pl.when(self.inside(self.here + self.sign * j))
            def _(j=j):
                self.copy(j).start()

    def total(self, lengths):
        first = self.here * self.rows
        result = None
        for j in range(1, self.hops + 1):

            @pl.when(self.inside(self.here - self.sign * j))
            def _(j=j):
                self.copy(j).wait_recv()

            @pl.when(self.inside(self.here + self.sign * j))
            def _(j=j):
                self.copy(j).wait_send()

            if self.sign > 0:
                edge, held = first - 1, first - 1 - (j - 1) * self.rows
            else:
                edge, held = first + j * self.rows - 1, first + self.rows - 1
            linked = (begin_scalar(lengths, edge) <= held).astype(F32)
            part = self.buffer[j - 1] * linked
            result = part if result is None else result + part
        return result


def greet(h, n, hops):
    barrier = pltpu.get_barrier_semaphore()

    def signal(where):
        pl.semaphore_signal(barrier, inc=1, device_id=where, device_id_type=pl.DeviceIdType.MESH)

    signal({"head": lax.bitwise_xor(h, 1)})
    signal({"head": lax.bitwise_xor(h, 2)})
    here = lax.axis_index("seq")
    expected = jnp.int32(2)
    for j in range(1, hops + 1):
        for sign in (1, -1):
            there = here + sign * j
            inside = (there >= 0) & (there < n)

            @pl.when(inside)
            def _(there=there):
                signal({"seq": lax.rem(there + n, n)})

            expected = expected + inside.astype(jnp.int32)
    pl.semaphore_wait(barrier, expected)


PROJECT_KINDS = (
    ("ai", D, BF),
    ("fi", D, BF),
    ("normed", D, BF),
    ("unit", D // 4, F32),
    ("inverse", 1, F32),
    ("qf", None, BF),
    ("kf", None, BF),
    ("v", None, BF),
    ("k", None, BF),
)


def project_outputs(rows, a):
    return [jax.ShapeDtypeStruct((rows, width or a), kind) for name, width, kind in PROJECT_KINDS]


def project_chunk(l, h, c, last, x, params, tables, whole, out, packed, summed):
    gain, bias, w_ref, b_ref, feat_ref, map_ref, ones_ref = params
    cos, sin, keep = tables
    ai_ref, fi_ref, normed_ref, unit_ref, inv_ref, qf_ref, kf_ref, v_ref, k_ref = out
    mean = jnp.sum(x, axis=1, keepdims=True) * (1.0 / D)
    center = x - mean
    inverse = lax.rsqrt(jnp.sum(center * center, axis=1, keepdims=True) * (1.0 / D) + EPSILON)
    normed = center * inverse
    inv_ref[...] = inverse
    normed_ref[...] = normed.astype(BF)
    whole[...] = normed
    unit_ref[...] = whole[:, block_columns(h, 0, unit_ref.shape[1])]
    attention_input = (normed * gain[l, 0:1] + bias[l, 0:1]).astype(BF)
    ai_ref[...] = attention_input
    fi_ref[...] = (normed * gain[l, 1:2] + bias[l, 1:2]).astype(BF)
    projected = dot_nn(attention_input, w_ref[...]) + b_ref[l : l + 1, :]
    q, k, v = split_heads(projected)
    v = v.astype(BF)
    q_turn = q * cos + swap_pairs(q) * sin
    k_turn = k * cos + swap_pairs(k) * sin
    query_feat = jnp.exp(dot_nn(q_turn, map_ref[...], HIGHEST))
    key_norm = head_sum(k * k, ones_ref[...]) * (0.5 / HEAD_DIM)
    key_feat = (
        keep
        * feat_ref[l : l + 1, :]
        * jnp.exp(dot_nn(k_turn, map_ref[...], HIGHEST) - key_norm)
    ).astype(BF)
    qf_ref[...] = query_feat.astype(BF)
    kf_ref[...] = key_feat
    v_ref[...] = v
    k_ref[...] = k.astype(BF)
    place = (row_of((CHUNK, 1)) + c * CHUNK).astype(F32)
    masked = jnp.where(place >= last, key_feat.astype(F32), 0.0)

    @pl.when(c == 0)
    def _():
        summed[...] = jnp.zeros_like(summed)
        packed[...] = jnp.zeros_like(packed)

    summed[...] += dot_tn(masked.astype(BF), v)
    packed[FEATURES : FEATURES + 1, :] += jnp.sum(masked, axis=0, keepdims=True)


def raise_chunk(l, fi, w_ref, b_ref, act_ref, slope_ref):
    raised = dot_nn(fi, w_ref[...]) + b_ref[l : l + 1, :]
    cumulative = 0.5 + 0.5 * lax.erf(raised * math.sqrt(0.5))
    density = jnp.exp(raised * raised * -0.5) * (1.0 / math.sqrt(2.0 * math.pi))
    act_ref[...] = (raised * cumulative).astype(BF)
    slope_ref[...] = (cumulative + raised * density).astype(BF)


def remote_call(kernel, name, ident, grid, in_specs, out_specs, out_shape, scratch, flops, args):
    moved = sum(int(np.prod(a.shape)) * a.dtype.itemsize for a in list(args) + list(out_shape))
    return pl.pallas_call(
        kernel,
        name=name,
        grid=grid,
        in_specs=in_specs,
        out_specs=out_specs,
        scratch_shapes=scratch,
        out_shape=out_shape,
        compiler_params=pltpu.CompilerParams(
            collective_id=ident, has_side_effects=True, vmem_limit_bytes=VMEM_BYTES
        ),
        cost_estimate=pl.CostEstimate(flops=int(flops), bytes_accessed=moved, transcendentals=0),
    )(*args)


def enter_kernel(n, hops, *refs):
    (
        lengths,
        acts,
        keep,
        gain,
        bias,
        w_ref,
        b_ref,
        feat_ref,
        map_ref,
        ones_ref,
        rate_ref,
        full_ref,
        cos_ref,
        sin_ref,
        begin_ref,
    ) = refs[:15]
    out = refs[15:24]
    state_ref = refs[24]
    gather_refs = refs[25:30]
    hand_refs = refs[30:33]
    packed, summed, whole = refs[33:]
    c = pl.program_id(0)
    count = pl.num_programs(0)
    h = lax.axis_index("head")
    rows, width = acts.shape
    first = lax.axis_index("seq") * rows
    gather = Gather(h, acts, gather_refs[:3], gather_refs[3:])
    hand = HandOver(n, hops, rows, 1, packed, hand_refs[0], hand_refs[1:])

    @pl.when(c == 0)
    def _():
        hand.clear()
        greet(h, n, hops)
        for i in range(rows // CHUNK):
            gather.start(i)

    slots = row_of((CHUNK, 1)) + c * CHUNK + first
    begins = begin_column(lengths, slots)
    begin_ref[...] = (begins - first).astype(F32)
    phase = (slots - begins).astype(F32) * rate_ref[0:1, :]
    cos_ref[...] = jnp.cos(phase)
    sin_ref[...] = jnp.sin(phase) * rate_ref[1:2, :]

    @pl.when(c == 0)
    def _():
        gather.relay(0)

    gather.ready(c)
    for r, part in enumerate(gather.pieces(c)):
        full_ref[:, block_columns(h, r, width)] = part
    last = (begin_scalar(lengths, first + rows - 1) - first).astype(F32)
    params = (gain, bias, w_ref, b_ref, feat_ref, map_ref, ones_ref)
    tables = (twice(cos_ref[...]), twice(sin_ref[...]), keep[...])
    project_chunk(
        0, h, c, last, full_ref[...].astype(F32), params, tables, whole, out, packed, summed
    )

    @pl.when(c + 1 < count)
    def _():
        gather.relay(c + 1)

    @pl.when(c + 1 == count)
    def _():
        packed[0:FEATURES, :] = pack_state(summed[...])
        hand.start()
        for i in range(rows // CHUNK):
            gather.finish(i)
        state_ref[...] = hand.total(lengths)


def enter(n, hops, lengths, acts, keep, gain, bias, qkv_w, qkv_b, feats, rates, consts):
    rows, width = acts.shape
    a = feats.shape[1]
    args = [lengths, acts, keep, gain, bias, qkv_w, qkv_b, feats, consts["map_t"], consts["ones"], rates]
    in_specs = [
        pl.BlockSpec(memory_space=pltpu.SMEM),
        full(acts.shape),
        rowed(1),
        full(gain.shape),
        full(bias.shape),
        layered(qkv_w, 0),
        full(qkv_b.shape),
        full(feats.shape),
        full((a, a)),
        full((a, a)),
        full(rates.shape),
    ]
    table = rates.shape[1]
    out_shape = [
        jax.ShapeDtypeStruct((rows, D), BF),
        jax.ShapeDtypeStruct((rows, table), F32),
        jax.ShapeDtypeStruct((rows, table), F32),
        jax.ShapeDtypeStruct((rows, 1), F32),
    ] + project_outputs(rows, a)
    out_specs = [rowed(o.shape[1]) for o in out_shape] + [full((STATE_ROWS, a))]
    out_shape = out_shape + [jax.ShapeDtypeStruct((STATE_ROWS, a), F32)]
    scratch = (
        Gather.scratch(rows, width)
        + HandOver.scratch(hops, a)
        + [pltpu.VMEM((STATE_ROWS, a), F32), pltpu.VMEM((a, a), F32), pltpu.VMEM((CHUNK, D), F32)]
    )
    return remote_call(
        functools.partial(enter_kernel, n, hops),
        "enter",
        2,
        (rows // CHUNK,),
        in_specs,
        out_specs,
        out_shape,
        scratch,
        2 * rows * D * 3 * a * 2,
        args,
    )


def between_kernel(n, hops, l, *refs):
    (
        lengths,
        qf_ref,
        kf_ref,
        v_ref,
        begin_ref,
        keep_ref,
        in_ref,
        fi_in,
        up_ref,
        up_b,
        ow_ref,
        dw_ref,
        ones_ref,
        full_ref,
        res_b,
        gain,
        bias,
        w_ref,
        b_ref,
        feat_ref,
        map_ref,
        cos_ref,
        sin_ref,
        keep_next,
        up_next,
    ) = refs[:25]
    (att_ref, low_ref, ratio_ref, states_ref, totals_ref, act_ref, slope_ref) = refs[25:32]
    own_ref = refs[32]
    out = refs[33:42]
    act_next, slope_next, state_ref = refs[42:45]
    gather_refs = refs[45:50]
    scatter_refs = refs[50:57]
    hand_refs = refs[57:60]
    mine, packed, summed, whole, whole_low, state, total = refs[60:]
    step = pl.program_id(0)
    count = pl.num_programs(0) // 2
    h = lax.axis_index("head")
    rows, width = mine.shape
    first = lax.axis_index("seq") * rows
    chunks = rows // CHUNK
    gather = Gather(h, mine, gather_refs[:3], gather_refs[3:])
    scatter = Scatter(h, scatter_refs[:5], scatter_refs[5:])
    hand = HandOver(n, hops, rows, 1, packed, hand_refs[0], hand_refs[1:])

    def send_sum(c):
        mine[rows_at(c), :] = scatter.total(c).astype(BF)
        gather.start(c)

    @pl.when(step == 0)
    def _():
        hand.clear()
        greet(h, n, hops)

    @pl.when(step < count)
    def _():
        raise_chunk(l, fi_in[...], up_ref, up_b, act_ref, slope_ref)

        @pl.when(step >= 1)
        def _():
            scatter.relay(step - 1)

        @pl.when(step >= 2)
        def _():
            send_sum(step - 2)

        attention_chunk(
            step,
            (qf_ref, kf_ref, v_ref, begin_ref, keep_ref, in_ref, ones_ref),
            (att_ref, low_ref, ratio_ref, states_ref, totals_ref),
            state,
            total,
        )
        whole_low[...] = (
            dot_nt(low_ref[...], ow_ref[...]) + dot_nt(act_ref[...], dw_ref[...])
        ).astype(BF)
        scatter.put(h, step, whole_low)

        @pl.when(step >= 3)
        def _():
            gather.relay(step - 3)

    @pl.when(step >= count)
    def _():
        c = step - count

        @pl.when(step == count)
        def _():
            scatter.relay(chunks - 1)
            send_sum(chunks - 2)

        gather.ready(c)
        for r, part in enumerate(gather.pieces(c)):
            whole[:, block_columns(h, r, width)] = part.astype(F32)
        x = full_ref[...].astype(F32) + whole[...] + res_b[l : l + 1, :]
        whole[...] = x
        own_ref[...] = whole[:, block_columns(h, 0, width)]
        last = (begin_scalar(lengths, first + rows - 1) - first).astype(F32)
        params = (gain, bias, w_ref, b_ref, feat_ref, map_ref, ones_ref)
        tables = (twice(cos_ref[...]), twice(sin_ref[...]), keep_next[...])
        project_chunk(l + 1, h, c, last, x, params, tables, whole, out, packed, summed)

        @pl.when(c == 0)
        def _():
            send_sum(chunks - 1)

        @pl.when(c + 1 < chunks)
        def _():
            gather.relay(c + 1)

        @pl.when(c + 1 == chunks)
        def _():
            packed[0:FEATURES, :] = pack_state(summed[...])
            hand.start()

        raise_chunk(l + 1, out[1][...], up_next, up_b, act_next, slope_next)

        @pl.when(c + 1 == chunks)
        def _():
            for i in range(chunks):
                gather.finish(i)
                scatter.finish(i)
            state_ref[...] = hand.total(lengths)


def between(
    n, hops, l, lengths, made, tables, state_in, full_acts, params, consts
):
    gain, bias, qkv_w, qkv_b, feats, up_w, up_b, out_w, down_w, res_b = params
    cos, sin, begin, keep = tables
    ai, fi, normed, unit, inverse, qf, kf, v, k = made
    rows, a = qf.shape
    hidden = up_w.shape[2]
    chunks = rows // CHUNK
    width = D // 4

    def early(w):
        return pl.BlockSpec((CHUNK, w), lambda i: (jnp.minimum(i, chunks - 1), 0))

    def late(w):
        return pl.BlockSpec((CHUNK, w), lambda i: (jnp.maximum(i - chunks, 0), 0))

    args = [
        lengths, qf, kf, v, begin, keep, state_in, fi, up_w, up_b, out_w, down_w, consts["ones"],
        full_acts, res_b, gain, bias, qkv_w, qkv_b, feats, consts["map_t"], cos, sin, keep, up_w,
    ]
    in_specs = [
        pl.BlockSpec(memory_space=pltpu.SMEM),
        early(a),
        early(a),
        early(a),
        early(1),
        early(1),
        full((STATE_ROWS, a)),
        early(D),
        layered(up_w, l),
        full(up_b.shape),
        layered(out_w, l),
        layered(down_w, l),
        full((a, a)),
        late(D),
        full(res_b.shape),
        full(gain.shape),
        full(bias.shape),
        layered(qkv_w, l + 1),
        full(qkv_b.shape),
        full(feats.shape),
        full((a, a)),
        late(cos.shape[1]),
        late(sin.shape[1]),
        late(1),
        layered(up_w, l + 1),
    ]

    def shaped(w, kind):
        return jax.ShapeDtypeStruct((rows, w), kind)

    first = [
        (early(a), shaped(a, F32)),
        (early(a), shaped(a, BF)),
        (early(a), shaped(a, F32)),
        (
            pl.BlockSpec((1, a, a), lambda i: (jnp.minimum(i, chunks - 1), 0, 0)),
            jax.ShapeDtypeStruct((chunks, a, a), F32),
        ),
        (
            pl.BlockSpec((1, 8, a), lambda i: (jnp.minimum(i, chunks - 1), 0, 0)),
            jax.ShapeDtypeStruct((chunks, 8, a), F32),
        ),
        (early(hidden), shaped(hidden, BF)),
        (early(hidden), shaped(hidden, BF)),
    ]
    second = [(late(width), shaped(width, F32))]
    second += [(late(o.shape[1]), o) for o in project_outputs(rows, a)]
    second += [(late(hidden), shaped(hidden, BF))] * 2
    second += [(full((STATE_ROWS, a)), jax.ShapeDtypeStruct((STATE_ROWS, a), F32))]
    both = first + second
    scratch = (
        Gather.scratch(rows, width)
        + Scatter.scratch(rows, width)
        + HandOver.scratch(hops, a)
        + [
            pltpu.VMEM((rows, width), BF),
            pltpu.VMEM((STATE_ROWS, a), F32),
            pltpu.VMEM((a, a), F32),
            pltpu.VMEM((CHUNK, D), F32),
            pltpu.VMEM((CHUNK, D), BF),
            pltpu.VMEM((a, a), F32),
            pltpu.VMEM((8, a), F32),
        ]
    )
    return remote_call(
        functools.partial(between_kernel, n, hops, l),
        "between",
        3,
        (2 * chunks,),
        in_specs,
        [spec for spec, shape in both],
        [shape for spec, shape in both],
        scratch,
        2 * rows * D * (hidden * 3 + 4 * a) * 2,
        args,
    )


def pair_mask(begin, step):
    shape = (CHUNK, CHUNK)
    t = row_of(shape)
    s = lane_of(shape)
    return (s <= t) & ((s + step * CHUNK).astype(F32) >= begin)


def spread(h, whole, near_ref, far_ref):
    w = D // 4
    near_ref[0] = whole[:, block_columns(h, 0, w)]
    near_ref[1] = whole[:, block_columns(h, 2, w)]
    far_ref[0] = whole[:, block_columns(h, 1, w)]
    far_ref[1] = whole[:, block_columns(h, 3, w)]


def attention_chunk(step, refs, out, state, total):
    qf_ref, kf_ref, v_ref, begin_ref, keep_ref, in_ref, ones_ref = refs
    att_ref, low_ref, ratio_ref, states_ref, totals_ref = out

    @pl.when(step == 0)
    def _():
        state[...] = unpack_state(in_ref[0:FEATURES, :])
        total[...] = jnp.broadcast_to(in_ref[FEATURES : FEATURES + 1, :], total.shape)

    q = qf_ref[...]
    k = kf_ref[...]
    v = v_ref[...]
    begin = begin_ref[...]
    keep = keep_ref[...]
    ones = ones_ref[...]
    a = q.shape[1]
    mask = pair_mask(begin, step)
    head_of = lane_of((1, a)) // HEAD_DIM
    held = state[...]
    held_total = total[0:1, :]
    states_ref[0] = held
    totals_ref[0] = total[...]
    base = (step * CHUNK).astype(F32)
    use = jnp.where(begin < base, 1.0, 0.0)
    high, low = halves(held)
    num = use * (dot_nn(q, high) + dot_nn(q, low))
    den = use * head_sum(q.astype(F32) * held_total, ones)
    for head in range(a // HEAD_DIM):
        own = (head_of == head).astype(BF)
        scores = dot_nt(q * own, k)
        scores_low = jnp.where(mask, scores, 0.0).astype(BF)
        num = num + dot_nn(scores_low, v * own)
        den = den + dot_nn(scores_low, jnp.broadcast_to(own, (CHUNK, a)))
    ratio = keep / (den + 1.0 - keep)
    att = num * ratio
    ratio_ref[...] = ratio
    att_ref[...] = att
    low_ref[...] = att.astype(BF)
    end = begin[CHUNK - 1 : CHUNK, :]
    place = (row_of((CHUNK, 1)) + step * CHUNK).astype(F32)
    masked = jnp.where(place >= end, k.astype(F32), 0.0)
    passing = jnp.where(end < base, 1.0, 0.0)
    state[...] = passing * held + jnp.where(
        block_diagonal(a), dot_tn(masked.astype(BF), v), 0.0
    )
    total[...] = jnp.broadcast_to(
        passing * held_total + jnp.sum(masked, axis=0, keepdims=True), total.shape
    )


def attend_kernel(
    qf_ref,
    kf_ref,
    v_ref,
    begin_ref,
    keep_ref,
    in_ref,
    act_ref,
    ow_ref,
    dw_ref,
    ones_ref,
    near_ref,
    far_ref,
    att_ref,
    low_ref,
    ratio_ref,
    states_ref,
    totals_ref,
    state,
    total,
    whole,
):
    step = pl.program_id(0)
    h = lax.axis_index("head")
    attention_chunk(
        step,
        (qf_ref, kf_ref, v_ref, begin_ref, keep_ref, in_ref, ones_ref),
        (att_ref, low_ref, ratio_ref, states_ref, totals_ref),
        state,
        total,
    )
    whole[...] = (dot_nt(low_ref[...], ow_ref[...]) + dot_nt(act_ref[...], dw_ref[...])).astype(BF)
    spread(h, whole, near_ref, far_ref)


def attend(l, qf, kf, v, begin, keep, state_in, act, out_w, down_w, consts):
    rows, a = qf.shape
    steps = rows // CHUNK
    hidden = act.shape[1]
    quarter = pl.BlockSpec((2, CHUNK, D // 4), lambda i: (0, i, 0))
    return call(
        attend_kernel,
        "attend",
        (steps,),
        [
            rowed(a),
            rowed(a),
            rowed(a),
            rowed(1),
            rowed(1),
            full((STATE_ROWS, a)),
            rowed(hidden),
            layered(out_w, l),
            layered(down_w, l),
            full((a, a)),
        ],
        [
            quarter,
            quarter,
            rowed(a),
            rowed(a),
            rowed(a),
            pl.BlockSpec((1, a, a), lambda i: (i, 0, 0)),
            pl.BlockSpec((1, 8, a), lambda i: (i, 0, 0)),
        ],
        [
            jax.ShapeDtypeStruct((2, rows, D // 4), BF),
            jax.ShapeDtypeStruct((2, rows, D // 4), BF),
            jax.ShapeDtypeStruct((rows, a), F32),
            jax.ShapeDtypeStruct((rows, a), BF),
            jax.ShapeDtypeStruct((rows, a), F32),
            jax.ShapeDtypeStruct((steps, a, a), F32),
            jax.ShapeDtypeStruct((steps, 8, a), F32),
        ],
        [pltpu.VMEM((a, a), F32), pltpu.VMEM((8, a), F32), pltpu.VMEM((CHUNK, D), BF)],
        2 * rows * D * (hidden + a) * 2,
        [qf, kf, v, begin, keep, state_in, act, out_w, down_w, consts["ones"]],
    )


def lower_kernel(
    g0,
    g1,
    g2,
    g3,
    dw_ref,
    ow_ref,
    slope_ref,
    ratio_ref,
    att_ref,
    qf_ref,
    begin_ref,
    ones_ref,
    grad_ref,
    raised_ref,
    num_ref,
    den_ref,
    bias_ref,
    entry_ref,
    sum_ref,
):
    step = pl.program_id(0)

    @pl.when(step == 0)
    def _():
        sum_ref[...] = jnp.zeros_like(sum_ref)
        entry_ref[...] = jnp.zeros_like(entry_ref)
        bias_ref[...] = jnp.zeros_like(bias_ref)

    h = lax.axis_index("head")
    for r, part in enumerate((g0, g1, g2, g3)):
        grad_ref[:, block_columns(h, r, part.shape[1])] = part[...]
    grad = grad_ref[...]
    d_att = dot_nn(grad, ow_ref[...])
    d_num = (d_att * ratio_ref[...]).astype(BF)
    d_den = -head_sum(d_num.astype(F32) * att_ref[...], ones_ref[...])
    num_ref[...] = d_num
    den_ref[...] = d_den
    entering = jnp.where(begin_ref[...] < 0.0, qf_ref[...].astype(F32), 0.0)
    sum_ref[...] += dot_tn(entering.astype(BF), d_num)
    entry_ref[FEATURES : FEATURES + 1, :] += jnp.sum(entering * d_den, axis=0, keepdims=True)
    d_raised = (dot_nn(grad, dw_ref[...]) * slope_ref[...].astype(F32)).astype(BF)
    raised_ref[...] = d_raised
    bias_ref[...] += jnp.sum(d_raised.astype(F32), axis=0, keepdims=True)

    @pl.when(step == pl.num_programs(0) - 1)
    def _():
        entry_ref[0:FEATURES, :] = pack_state(sum_ref[...])


def lower(l, grads, down_w, out_w, slope, ratio, att, qf, begin, consts):
    rows, width = grads[0].shape
    hidden = slope.shape[1]
    a = att.shape[1]
    return call(
        lower_kernel,
        "lower",
        (rows // CHUNK,),
        [rowed(width)] * 4
        + [
            layered(down_w, l),
            layered(out_w, l),
            rowed(hidden),
            rowed(a),
            rowed(a),
            rowed(a),
            rowed(1),
            full((a, a)),
        ],
        [
            rowed(D),
            rowed(hidden),
            rowed(a),
            rowed(a),
            full((1, hidden)),
            full((STATE_ROWS, a)),
        ],
        [
            jax.ShapeDtypeStruct((rows, D), BF),
            jax.ShapeDtypeStruct((rows, hidden), BF),
            jax.ShapeDtypeStruct((rows, a), BF),
            jax.ShapeDtypeStruct((rows, a), F32),
            jax.ShapeDtypeStruct((1, hidden), F32),
            jax.ShapeDtypeStruct((STATE_ROWS, a), F32),
        ],
        [pltpu.VMEM((a, a), F32)],
        2 * rows * D * (hidden + a) * 2,
        list(grads) + [down_w, out_w, slope, ratio, att, qf, begin, consts["ones"]],
    )


def back_kernel(
    l,
    qf_ref,
    kf_ref,
    v_ref,
    k_ref,
    num_ref,
    den_ref,
    begin_ref,
    cos_ref,
    sin_ref,
    states_ref,
    totals_ref,
    exit_ref,
    map_ref,
    ones_ref,
    w_ref,
    up_ref,
    raised_ref,
    normed_ref,
    scale_ref,
    proj_ref,
    near_ref,
    far_ref,
    rows_ref,
    bias_ref,
    feat_ref,
    sums_ref,
    state,
    total,
    whole,
):
    h = lax.axis_index("head")
    turn = pl.program_id(0)
    step = pl.num_programs(0) - 1 - turn

    @pl.when(turn == 0)
    def _():
        state[...] = unpack_state(exit_ref[0:FEATURES, :])
        total[...] = jnp.broadcast_to(exit_ref[FEATURES : FEATURES + 1, :], total.shape)
        bias_ref[...] = jnp.zeros_like(bias_ref)
        feat_ref[...] = jnp.zeros_like(feat_ref)
        sums_ref[...] = jnp.zeros_like(sums_ref)

    q = qf_ref[...]
    k = kf_ref[...]
    v = v_ref[...]
    d_num = num_ref[...]
    d_den = den_ref[...]
    begin = begin_ref[...]
    ones = ones_ref[...]
    a = q.shape[1]
    mask = pair_mask(begin, step)
    head_of = lane_of((1, a)) // HEAD_DIM
    base = (step * CHUNK).astype(F32)
    use = jnp.where(begin < base, 1.0, 0.0)
    end = begin[CHUNK - 1 : CHUNK, :]
    place = (row_of((CHUNK, 1)) + step * CHUNK).astype(F32)
    inside = jnp.where(place >= end, 1.0, 0.0)
    passing = jnp.where(end < base, 1.0, 0.0)
    held_high, held_low = halves(states_ref[0])
    held_total = totals_ref[0][0:1, :]
    after = state[...]
    after_total = total[0:1, :]
    after_high, after_low = halves(after)
    q_wide = q.astype(F32)
    k_wide = k.astype(F32)
    masked = (k_wide * inside).astype(BF)
    d_q = use * (dot_nt(d_num, held_high) + dot_nt(d_num, held_low) + d_den * held_total)
    d_k = inside * (dot_nt(v, after_high) + dot_nt(v, after_low) + after_total)
    d_v = dot_nn(masked, after_high) + dot_nn(masked, after_low)
    for head in range(a // HEAD_DIM):
        own = (head_of == head).astype(BF)
        q_own = q * own
        num_own = d_num * own
        scores_low = jnp.where(mask, dot_nt(q_own, k), 0.0).astype(BF)
        column = d_den[:, head * HEAD_DIM : head * HEAD_DIM + 1]
        d_scores = jnp.where(mask, dot_nt(num_own, v) + column, 0.0).astype(BF)
        d_q = d_q + dot_nn(d_scores, k * own)
        d_k = d_k + dot_tn(d_scores, q_own)
        d_v = d_v + dot_tn(scores_low, num_own)
    q_used = q_wide * use
    state[...] = passing * after + jnp.where(
        block_diagonal(a), dot_tn(q_used.astype(BF), d_num), 0.0
    )
    total[...] = jnp.broadcast_to(
        passing * after_total + jnp.sum(q_used * d_den, axis=0, keepdims=True), total.shape
    )
    cos = twice(cos_ref[...])
    sin = twice(sin_ref[...])
    d_query = dot_nn(d_q * q_wide, map_ref[...], HIGHEST)
    d_query = d_query * cos - swap_pairs(d_query) * sin
    d_key_log = d_k * k_wide
    feat_ref[...] += jnp.sum(d_key_log, axis=0, keepdims=True)
    d_key = dot_nn(d_key_log, map_ref[...], HIGHEST)
    d_key = d_key * cos - swap_pairs(d_key) * sin
    d_key = d_key - head_sum(d_key_log, ones) * k_ref[...].astype(F32) * (1.0 / HEAD_DIM)
    d_proj = join_heads(d_query, d_key, d_v).astype(BF)
    proj_ref[...] = d_proj
    bias_ref[...] += jnp.sum(d_proj.astype(F32), axis=0, keepdims=True)
    normed = normed_ref[...].astype(F32)
    d_attention = dot_nt(d_proj, w_ref[...])
    d_feed = dot_nt(raised_ref[...], up_ref[...])
    sums_ref[0:1, :] += jnp.sum(d_attention * normed, axis=0, keepdims=True)
    sums_ref[1:2, :] += jnp.sum(d_feed * normed, axis=0, keepdims=True)
    sums_ref[2:3, :] += jnp.sum(d_attention, axis=0, keepdims=True)
    sums_ref[3:4, :] += jnp.sum(d_feed, axis=0, keepdims=True)
    d_normed = (d_attention * scale_ref[l, 0:1] + d_feed * scale_ref[l, 1:2]).astype(BF)
    whole[...] = d_normed
    spread(h, whole, near_ref, far_ref)
    high, low = halves(d_normed.astype(F32) * normed)
    row = jnp.ones((8, D), BF)
    first = dot_nt(row, d_normed)
    second = dot_nt(row, high) + dot_nt(row, low)
    rows_ref[...] = jnp.where(row_of(first.shape) == 0, first, second)


def back(l, kept, d_num, d_den, d_raised, exit_state, tables, w_qkv, up_w, gain, consts):
    qf, kf, v, k, normed, states, totals = kept
    cos, sin, begin, keep = tables
    rows, a = qf.shape
    n = rows // CHUNK
    hidden = d_raised.shape[1]
    args = [
        qf,
        kf,
        v,
        k,
        d_num,
        d_den,
        begin,
        cos,
        sin,
        states,
        totals,
        exit_state,
        consts["map"],
        consts["ones"],
        w_qkv,
        up_w,
        d_raised,
        normed,
        gain,
    ]
    quarter = pl.BlockSpec((2, CHUNK, D // 4), lambda i: (0, n - 1 - i, 0))
    in_specs = (
        [rowed_back(a, n)] * 6
        + [rowed_back(1, n), rowed_back(cos.shape[1], n), rowed_back(sin.shape[1], n)]
        + [
            pl.BlockSpec((1, a, a), lambda i: (n - 1 - i, 0, 0)),
            pl.BlockSpec((1, 8, a), lambda i: (n - 1 - i, 0, 0)),
            full((STATE_ROWS, a)),
            full((a, a)),
            full((a, a)),
            layered(w_qkv, l),
            layered(up_w, l),
            rowed_back(hidden, n),
            rowed_back(D, n),
            full(gain.shape),
        ]
    )
    out_specs = [
        rowed_back(3 * a, n),
        quarter,
        quarter,
        pl.BlockSpec((8, CHUNK), lambda i: (0, n - 1 - i)),
        full((1, 3 * a)),
        full((1, a)),
        full((8, D)),
    ]
    out_shape = [
        jax.ShapeDtypeStruct((rows, 3 * a), BF),
        jax.ShapeDtypeStruct((2, rows, D // 4), BF),
        jax.ShapeDtypeStruct((2, rows, D // 4), BF),
        jax.ShapeDtypeStruct((8, rows), F32),
        jax.ShapeDtypeStruct((1, 3 * a), F32),
        jax.ShapeDtypeStruct((1, a), F32),
        jax.ShapeDtypeStruct((8, D), F32),
    ]
    return call(
        functools.partial(back_kernel, l),
        "attend_back",
        (n,),
        in_specs,
        out_specs,
        out_shape,
        [pltpu.VMEM((a, a), F32), pltpu.VMEM((8, a), F32), pltpu.VMEM((CHUNK, D), BF)],
        2 * rows * D * (hidden + 3 * a) * 3,
        args,
    )


def weight_kernel(count, x_ref, *refs):
    x = x_ref[...]
    out = refs[count]
    at = 0
    for y in refs[:count]:
        width = y.shape[1]
        out[:, at : at + width] = dot_tn(x, y[...]).astype(BF)
        at += width


def weight_grad(x, ys):
    rows = x.shape[0]
    columns = sum(y.shape[1] for y in ys)
    tile = D // 4
    return call(
        functools.partial(weight_kernel, len(ys)),
        "weight_grad",
        (D // tile,),
        [pl.BlockSpec((rows, tile), lambda i: (0, i))] + [full(y.shape) for y in ys],
        [pl.BlockSpec((tile, columns), lambda i: (i, 0))],
        [jax.ShapeDtypeStruct((D, columns), BF)],
        [],
        2 * rows * D * columns,
        [x] + list(ys),
    )[0]


def ring_place(index, n):
    return jnp.where(index % 2 == 0, index // 2, n - 1 - index // 2)


def ring_index(place, n):
    return jnp.where(place < n // 2, 2 * place, 2 * (n - 1 - place) + 1)


def ring_kernel(n, parts, sources, *refs):
    count = len(parts)
    source = refs[:sources]
    out = refs[sources : 2 * sources]
    held = refs[2 * sources : 2 * sources + count]
    send_sem, recv_sem = refs[2 * sources + count :]
    share = D // n
    place = ring_place(lax.axis_index("seq"), n)
    right = ring_index(lax.rem(place + 1, n), n)
    left = ring_index(lax.rem(place + n - 1, n), n)
    barrier = pltpu.get_barrier_semaphore()
    for neighbour in (left, right):
        pl.semaphore_signal(
            barrier,
            inc=1,
            device_id={"seq": neighbour},
            device_id_type=pl.DeviceIdType.MESH,
        )
    pl.semaphore_wait(barrier, 2)

    def own(part, step):
        array, start, width, way = part
        ahead = lax.rem(place - way * (1 + step) + 2 * n, n)
        rows = pl.ds(pl.multiple_of(ring_index(ahead, n) * share, share), share)
        return source[array].at[rows, pl.ds(start, width)]

    def send(r, step, block):
        return pltpu.make_async_remote_copy(
            src_ref=block,
            dst_ref=held[r].at[step],
            send_sem=send_sem.at[r, step],
            recv_sem=recv_sem.at[r, step],
            device_id={"seq": right if parts[r][3] > 0 else left},
            device_id_type=pl.DeviceIdType.MESH,
        )

    for r in range(count):
        send(r, 0, own(parts[r], 0)).start()

    def turn(step, carry):
        for r in range(count):
            block = held[r].at[step - 1]
            send(r, step - 1, block).wait_recv()
            block[...] = (block[...].astype(F32) + own(parts[r], step)[...].astype(F32)).astype(BF)
            send(r, step, block).start()
        return carry

    lax.fori_loop(1, n - 1, turn, 0)
    for r in range(count):
        block = held[r].at[n - 2]
        send(r, n - 2, block).wait_recv()
        array, start, width, way = parts[r]
        out[array][:, pl.ds(start, width)] = block[...].astype(F32) + own(parts[r], n - 1)[
            ...
        ].astype(F32)

    def finish(step, carry):
        for r in range(count):
            send(r, step, held[r].at[step]).wait_send()
        return carry

    lax.fori_loop(0, n - 1, finish, 0)


def ring_sum(arrays, parts, ident):
    n = lax.axis_size("seq")
    share = D // n
    space = pl.BlockSpec(memory_space=pltpu.VMEM)
    return pl.pallas_call(
        functools.partial(ring_kernel, n, parts, len(arrays)),
        name="ring_sum",
        in_specs=[space] * len(arrays),
        out_specs=[space] * len(arrays),
        out_shape=[jax.ShapeDtypeStruct((share, x.shape[1]), F32) for x in arrays],
        scratch_shapes=[pltpu.VMEM((n - 1, share, part[2]), BF) for part in parts]
        + [
            pltpu.SemaphoreType.DMA((len(parts), n - 1)),
            pltpu.SemaphoreType.DMA((len(parts), n - 1)),
        ],
        compiler_params=pltpu.CompilerParams(
            collective_id=ident, has_side_effects=True, vmem_limit_bytes=VMEM_BYTES
        ),
        cost_estimate=pl.CostEstimate(flops=10**8, bytes_accessed=10**8, transcendentals=0),
    )(*arrays)


def exchange(value, axis, step):
    count = lax.axis_size(axis)
    return lax.ppermute(value, axis, [(i, i ^ step) for i in range(count)])


def shifted(value, axis, step):
    count = lax.axis_size(axis)
    return lax.ppermute(
        value, axis, [(i, i + step) for i in range(count) if 0 <= i + step < count]
    )


def gather_heads(own):
    across = exchange(own, "head", 2)
    beside = exchange(own, "head", 1)
    return [own, beside, across, exchange(across, "head", 1)]


def scatter_heads(near, far):
    got = exchange(far, "head", 1)
    across = exchange(near[1] + got[1], "head", 2)
    return near[0].astype(F32) + got[0].astype(F32) + across.astype(F32)


def on_device(
    acts,
    cotangent,
    lengths,
    keep_mask,
    ln_gain,
    ln_bias,
    qkv_w,
    qkv_b,
    feat_w,
    out_w,
    up_w,
    up_b,
    down_w,
    res_b,
):
    rows, width = acts.shape
    heads = feat_w.shape[1]
    a = heads * HEAD_DIM
    n = lax.axis_size("seq")
    tokens = rows * n
    longest = 2048 if tokens <= 8192 else 4096
    hops = -(-longest // rows)
    h = lax.axis_index("head").astype(jnp.int32)
    first = lax.axis_index("seq") * rows

    def relative(array, axis):
        return jnp.concatenate(
            [
                lax.dynamic_slice_in_dim(array, lax.bitwise_xor(h, r) * width, width, axis)
                for r in range(4)
            ],
            axis,
        )

    res = lax.dynamic_slice_in_dim(res_b, h * width, width, 1)
    feats = feat_w.reshape(LAYERS, a)
    keep = keep_mask.astype(F32)[:, None]
    half = ROT // 2
    rates = np.zeros((2, HEAD_DIM))
    rates[0, :half] = ROTARY_BASE ** (-2.0 * np.arange(half) / ROT)
    rates[0, half:ROT] = rates[0, :half]
    rates[1, :half] = -1.0
    rates[1, half:ROT] = 1.0
    rates = jnp.asarray(np.tile(rates, (1, 2)), F32)

    starts = (jnp.cumsum(lengths) - lengths).astype(jnp.int32)

    def begin_of(slots):
        return jnp.max(jnp.where(starts[None, :] <= slots[:, None], starts[None, :], 0), axis=1)

    fold = sample_points(FEATURES, HEAD_DIM) @ cosine_table(HEAD_DIM) / math.sqrt(HEAD_DIM)
    eye = np.eye(heads)
    consts = {
        "map": jnp.asarray(np.kron(eye, fold), F32),
        "map_t": jnp.asarray(np.kron(eye, fold.T), F32),
        "ones": jnp.asarray(np.kron(eye, np.ones((HEAD_DIM, HEAD_DIM))), BF),
    }

    def linked(step):
        edge = first - 1 if step > 0 else first + rows * -step - 1
        held = first + rows - 1 if step < 0 else first - 1 - (step - 1) * rows
        return (begin_of(jnp.reshape(edge, (1,)))[0] <= held).astype(F32)

    def entering(state, sign):
        total = shifted(state, "seq", sign)
        for step in range(2, hops + 1):
            total = total + shifted(state, "seq", sign * step) * linked(sign * step)
        return total

    full_acts, cos, sin, begin, *made = enter(
        n, hops, lengths, acts, keep, ln_gain, ln_bias, qkv_w, qkv_b, feats, rates, consts
    )
    tables = (cos, sin, begin, keep)
    params = (ln_gain, ln_bias, qkv_w, qkv_b, feats, up_w, up_b, out_w, down_w, res_b)
    first_made, state_in = made[:9], made[9]
    att, att_low, ratio, states, totals, act, slope, own, *made = between(
        n, hops, 0, lengths, first_made, tables, state_in, full_acts, params, consts
    )

    def keep_layer(made, states, totals, act, slope, att, att_low, ratio):
        ai, fi, normed, unit, inverse, qf, kf, v, k = made
        local = (qf, kf, v, k, normed, states, totals)
        return (local, ai, fi, unit, inverse, act, slope, att, att_low, ratio)

    kept = [keep_layer(first_made, states, totals, act, slope, att, att_low, ratio)]
    made, act, slope, state_in = made[:9], made[9], made[10], made[11]
    qf, kf, v = made[5:8]
    near, far, att, att_low, ratio, states, totals = attend(
        1, qf, kf, v, begin, keep, state_in, act, out_w, down_w, consts
    )
    kept.append(keep_layer(made, states, totals, act, slope, att, att_low, ratio))
    out_acts = own + scatter_heads(near, far) + res[1]

    upstream = cotangent.astype(F32)
    matrices = [None] * LAYERS
    smalls = [None] * LAYERS
    sums = [None] * LAYERS
    for l in reversed(range(LAYERS)):
        local, ai, fi, unit, inverse, act, slope, att, att_low, ratio = kept[l]
        d_res = jnp.sum(upstream, axis=0)
        grads = gather_heads(upstream.astype(BF))
        grad, d_raised, d_num, d_den, d_up_b, entry = lower(
            l, grads, down_w, out_w, slope, ratio, att, local[0], begin, consts
        )
        exit_state = entering(entry, -1)
        d_down_out = weight_grad(grad, [act, att_low])
        d_up = weight_grad(fi, [d_raised])
        d_proj, near, far, row_sums, d_qkv_b, d_feat, column_sums = back(
            l, local, d_num, d_den, d_raised, exit_state, tables, qkv_w, up_w, ln_gain, consts
        )
        d_qkv = weight_grad(ai, [d_proj])
        row_sums = row_sums + exchange(row_sums, "head", 1)
        row_sums = row_sums + exchange(row_sums, "head", 2)
        d_normed = scatter_heads(near, far)
        upstream = upstream + inverse * (
            d_normed - row_sums[0][:, None] / D - unit * row_sums[1][:, None] / D
        )
        if l == 0 and n == 8:
            parts = (
                (0, 0, 640, 1),
                (0, 640, 640, 1),
                (1, 0, 256, 1),
                (1, 256, 768, -1),
                (2, 0, 768, -1),
            )
            matrices[l] = ring_sum([d_down_out, d_up, d_qkv], parts, 1)
        else:
            summed = lax.psum_scatter(
                jnp.concatenate([d_down_out, d_up, d_qkv], axis=1),
                "seq",
                scatter_dimension=0,
                tiled=True,
            ).astype(F32)
            at = d_down_out.shape[1]
            matrices[l] = (
                summed[:, :at],
                summed[:, at : at + d_up.shape[1]],
                summed[:, at + d_up.shape[1] :],
            )
        sums[l] = column_sums[:4]
        smalls[l] = jnp.concatenate([d_qkv_b[0], d_up_b[0], d_feat[0], d_res])

    column_sums = relative(jnp.stack(sums), 2).reshape(LAYERS, 4, 4, width)
    near = jnp.stack([column_sums[:, :, 0], column_sums[:, :, 2]])
    far = jnp.stack([column_sums[:, :, 1], column_sums[:, :, 3]])
    norm_sums = scatter_heads(near, far)
    bundle = jnp.concatenate([norm_sums.reshape(LAYERS, 4 * width), jnp.stack(smalls)], axis=1)
    step = 1
    while step < n:
        bundle = bundle + exchange(bundle, "seq", step)
        step *= 2
    at = 0
    taken = []
    for size in (2 * width, 2 * width, 3 * a, d_up_b.shape[1], a, width):
        taken.append(bundle[:, at : at + size])
        at += size
    d_gain, d_bias, d_qkv_b, d_up_b, d_feat, d_res = taken

    hidden = up_w.shape[2]
    d_down = jnp.stack([m[0][:, :hidden] for m in matrices])
    d_out = jnp.stack([m[0][:, hidden:] for m in matrices])
    d_up = jnp.stack([m[1] for m in matrices])
    d_qkv = jnp.stack([m[2] for m in matrices])
    return (
        out_acts,
        upstream,
        d_qkv,
        d_out,
        d_up,
        d_down,
        d_qkv_b,
        d_up_b,
        (d_feat / feats).reshape(LAYERS, heads, FEATURES),
        d_gain.reshape(LAYERS, 2, width),
        d_bias.reshape(LAYERS, 2, width),
        d_res,
    )


def solution(mesh):
    return jax.shard_map(
        on_device,
        mesh=mesh,
        in_specs=(
            P("seq", "head"),
            P("seq", "head"),
            P(),
            P("seq"),
            P(),
            P(),
            P(None, None, "head"),
            P(None, "head"),
            P(None, "head", None),
            P(None, None, "head"),
            P(None, None, "head"),
            P(None, "head"),
            P(None, None, "head"),
            P(),
        ),
        out_specs=(
            P("seq", "head"),
            P("seq", "head"),
            P(None, "seq", "head"),
            P(None, "seq", "head"),
            P(None, "seq", "head"),
            P(None, "seq", "head"),
            P(None, "head"),
            P(None, "head"),
            P(None, "head", None),
            P(None, None, "head"),
            P(None, None, "head"),
            P(None, "head"),
        ),
        check_vma=False,
    )
```

```python
import functools
import math

import jax
import jax.numpy as jnp
import numpy as np
from jax import lax
from jax.experimental import pallas as pl
from jax.experimental.pallas import tpu as pltpu
from jax.sharding import PartitionSpec as P

D = 1024
HEAD_DIM = 64
ROT = 16
FEATURES = 64
LAYERS = 2
CHUNK = 256

EPSILON = 1e-05
ROTARY_BASE = 10000.0
HIGHEST = lax.Precision.HIGHEST
BF = jnp.bfloat16
F32 = jnp.float32
STATE_ROWS = 72
VMEM_BYTES = 56 * 1024 * 1024


def prime_numbers(count):
    found = []
    candidate = 2
    while len(found) < count:
        if all((candidate % prime != 0 for prime in found)):
            found.append(candidate)
        candidate = candidate + 1
    return found


def sample_points(rows, columns):
    roots = np.sqrt(np.array(prime_numbers(2 * columns)) * 1.0)
    fractions = roots - np.floor(roots)
    grid = np.outer(np.arange(1, rows + 1) * 1.0, fractions) % 1.0
    radius = np.sqrt(-2.0 * np.log(1.0 - grid[:, :columns]))
    return radius * np.cos(2.0 * math.pi * grid[:, columns:])


def cosine_table(size):
    wave = np.arange(size)[:, None] * 1.0
    place = np.arange(size)[None, :] * 1.0
    table = np.cos(math.pi * (place + 0.5) * wave / size) * math.sqrt(2.0 / size)
    return table * np.where(wave == 0, math.sqrt(0.5), 1.0)


def dot_nn(a, b, precision=None):
    return lax.dot_general(
        a, b, (((1,), (0,)), ((), ())), precision=precision, preferred_element_type=F32
    )


def dot_nt(a, b, precision=None):
    return lax.dot_general(
        a, b, (((1,), (1,)), ((), ())), precision=precision, preferred_element_type=F32
    )


def dot_tn(a, b, precision=None):
    return lax.dot_general(
        a, b, (((0,), (0,)), ((), ())), precision=precision, preferred_element_type=F32
    )


def halves(wide):
    high = wide.astype(BF)
    return high, (wide - high.astype(F32)).astype(BF)


def lane_of(shape):
    return lax.broadcasted_iota(jnp.int32, shape, 1)


def row_of(shape):
    return lax.broadcasted_iota(jnp.int32, shape, 0)


def swap_pairs(x):
    width = x.shape[1]
    later = pltpu.roll(x, width - ROT // 2, 1)
    earlier = pltpu.roll(x, ROT // 2, 1)
    return jnp.where(lane_of(x.shape) % ROT < ROT // 2, later, earlier)


def twice(table):
    return jnp.concatenate([table, table], axis=1)


def block_columns(h, r, width):
    return pl.ds(pl.multiple_of(lax.bitwise_xor(h, r) * width, width), width)


def split_heads(projected):
    heads = projected.shape[1] // (3 * HEAD_DIM)
    return [
        jnp.concatenate(
            [
                projected[:, (3 * j + kind) * HEAD_DIM : (3 * j + kind + 1) * HEAD_DIM]
                for j in range(heads)
            ],
            axis=1,
        )
        for kind in range(3)
    ]


def join_heads(q, k, v):
    heads = q.shape[1] // HEAD_DIM
    return jnp.concatenate(
        [
            part[:, j * HEAD_DIM : (j + 1) * HEAD_DIM]
            for j in range(heads)
            for part in (q, k, v)
        ],
        axis=1,
    )


def block_diagonal(width):
    shape = (width, width)
    return (row_of(shape) // HEAD_DIM) == (lane_of(shape) // HEAD_DIM)


def pack_state(full):
    width = full.shape[0]
    kept = jnp.where(block_diagonal(width), full, 0.0)
    packed = kept[0:FEATURES]
    for head in range(1, width // FEATURES):
        packed = packed + kept[head * FEATURES : (head + 1) * FEATURES]
    return packed


def unpack_state(packed):
    width = packed.shape[1]
    tall = jnp.concatenate([packed] * (width // FEATURES), axis=0)
    return jnp.where(block_diagonal(width), tall, 0.0)


def head_sum(values, ones):
    high, low = halves(values)
    return dot_nn(high, ones) + dot_nn(low, ones)


def full(shape):
    return pl.BlockSpec(shape, lambda *i: (0,) * len(shape))


def rowed(width):
    return pl.BlockSpec((CHUNK, width), lambda i: (i, 0))


def layered(array, l):
    return pl.BlockSpec((None,) + array.shape[1:], lambda *i: (l, 0, 0))


def rows_at(c):
    return pl.ds(pl.multiple_of(c * CHUNK, CHUNK), CHUNK)


def push(source, target, send, recv, where):
    return pltpu.make_async_remote_copy(
        src_ref=source,
        dst_ref=target,
        send_sem=send,
        recv_sem=recv,
        device_id=where,
        device_id_type=pl.DeviceIdType.MESH,
    )


class Gather:
    def __init__(self, h, own, buffers, sems):
        self.own = own
        self.beside, self.across, self.corner = buffers
        self.send, self.recv = sems
        self.near = {"head": lax.bitwise_xor(h, 1)}
        self.far = {"head": lax.bitwise_xor(h, 2)}

    @staticmethod
    def scratch(rows, width):
        count = rows // CHUNK
        return [pltpu.VMEM((rows, width), BF)] * 3 + [pltpu.SemaphoreType.DMA((3, count))] * 2

    def copy(self, kind, c):
        source, target, where = (
            (self.own, self.across, self.far),
            (self.own, self.beside, self.near),
            (self.across, self.corner, self.near),
        )[kind]
        rows = rows_at(c)
        return push(
            source.at[rows, :],
            target.at[rows, :],
            self.send.at[kind, c],
            self.recv.at[kind, c],
            where,
        )

    def start(self, c):
        self.copy(0, c).start()
        self.copy(1, c).start()

    def relay(self, c):
        self.copy(0, c).wait_recv()
        self.copy(2, c).start()

    def ready(self, c):
        self.copy(1, c).wait_recv()
        self.copy(2, c).wait_recv()

    def pieces(self, c):
        rows = rows_at(c)
        return [ref[rows, :] for ref in (self.own, self.beside, self.across, self.corner)]

    def finish(self, c):
        for kind in range(3):
            self.copy(kind, c).wait_send()


class Scatter:
    def __init__(self, h, buffers, sems):
        self.near, self.far, self.got, self.middle, self.across = buffers
        self.send, self.recv = sems
        self.beside = {"head": lax.bitwise_xor(h, 1)}
        self.beyond = {"head": lax.bitwise_xor(h, 2)}

    @staticmethod
    def scratch(rows, width):
        count = rows // CHUNK
        return (
            [pltpu.VMEM((2, rows, width), BF)] * 3
            + [pltpu.VMEM((rows, width), BF)] * 2
            + [pltpu.SemaphoreType.DMA((2, count))] * 2
        )

    def copy(self, kind, c):
        rows = rows_at(c)
        if kind == 0:
            source, target, where = (
                self.far.at[:, rows, :],
                self.got.at[:, rows, :],
                self.beside,
            )
        else:
            source, target, where = self.middle.at[rows, :], self.across.at[rows, :], self.beyond
        return push(source, target, self.send.at[kind, c], self.recv.at[kind, c], where)

    def put(self, h, c, whole):
        rows = rows_at(c)
        w = self.near.shape[2]
        self.near[0, rows, :] = whole[:, block_columns(h, 0, w)]
        self.near[1, rows, :] = whole[:, block_columns(h, 2, w)]
        self.far[0, rows, :] = whole[:, block_columns(h, 1, w)]
        self.far[1, rows, :] = whole[:, block_columns(h, 3, w)]
        self.copy(0, c).start()

    def relay(self, c):
        self.copy(0, c).wait_recv()
        rows = rows_at(c)
        self.middle[rows, :] = (
            self.near[1, rows, :].astype(F32) + self.got[1, rows, :].astype(F32)
        ).astype(BF)
        self.copy(1, c).start()

    def total(self, c):
        self.copy(1, c).wait_recv()
        rows = rows_at(c)
        return (
            self.near[0, rows, :].astype(F32)
            + self.got[0, rows, :].astype(F32)
            + self.across[rows, :].astype(F32)
        )

    def finish(self, c):
        self.copy(0, c).wait_send()
        self.copy(1, c).wait_send()


def begin_scalar(lengths, slot):
    def one(j, carry):
        at, best = carry
        at = at + lengths[j - 1]
        return at, jnp.where(at <= slot, at, best)

    return lax.fori_loop(1, lengths.shape[0], one, (jnp.int32(0), jnp.int32(0)))[1]


def begin_column(lengths, slots):
    def one(j, carry):
        at, best = carry
        at = at + lengths[j - 1]
        return at, jnp.where(slots >= at, at, best)

    return lax.fori_loop(1, lengths.shape[0], one, (jnp.int32(0), jnp.zeros_like(slots)))[1]


class HandOver:
    def __init__(self, n, hops, rows, sign, packed, buffer, sems):
        self.n, self.hops, self.rows, self.sign = n, hops, rows, sign
        self.packed, self.buffer = packed, buffer
        self.send, self.recv = sems
        self.here = lax.axis_index("seq")

    @staticmethod
    def scratch(hops, width):
        return [pltpu.VMEM((hops, STATE_ROWS, width), F32)] + [
            pltpu.SemaphoreType.DMA((hops,))
        ] * 2

    def inside(self, index):
        return (index >= 0) & (index < self.n)

    def copy(self, j):
        return push(
            self.packed,
            self.buffer.at[j - 1],
            self.send.at[j - 1],
            self.recv.at[j - 1],
            {"seq": lax.rem(self.here + self.sign * j + self.n, self.n)},
        )

    def clear(self):
        self.buffer[...] = jnp.zeros_like(self.buffer)

    def start(self):
        for j in range(1, self.hops + 1):

            @pl.when(self.inside(self.here + self.sign * j))
            def _(j=j):
                self.copy(j).start()

    def total(self, lengths):
        first = self.here * self.rows
        result = None
        for j in range(1, self.hops + 1):

            @pl.when(self.inside(self.here - self.sign * j))
            def _(j=j):
                self.copy(j).wait_recv()

            @pl.when(self.inside(self.here + self.sign * j))
            def _(j=j):
                self.copy(j).wait_send()

            if self.sign > 0:
                edge, held = first - 1, first - 1 - (j - 1) * self.rows
            else:
                edge, held = first + j * self.rows - 1, first + self.rows - 1
            linked = (begin_scalar(lengths, edge) <= held).astype(F32)
            part = self.buffer[j - 1] * linked
            result = part if result is None else result + part
        return result


def greet(h, n, hops):
    barrier = pltpu.get_barrier_semaphore()

    def signal(where):
        pl.semaphore_signal(barrier, inc=1, device_id=where, device_id_type=pl.DeviceIdType.MESH)

    signal({"head": lax.bitwise_xor(h, 1)})
    signal({"head": lax.bitwise_xor(h, 2)})
    here = lax.axis_index("seq")
    expected = jnp.int32(2)
    for j in range(1, hops + 1):
        for sign in (1, -1):
            there = here + sign * j
            inside = (there >= 0) & (there < n)

            @pl.when(inside)
            def _(there=there):
                signal({"seq": lax.rem(there + n, n)})

            expected = expected + inside.astype(jnp.int32)
    pl.semaphore_wait(barrier, expected)


PROJECT_KINDS = (
    ("ai", D, BF),
    ("fi", D, BF),
    ("normed", D, BF),
    ("unit", D // 4, F32),
    ("inverse", 1, F32),
    ("qf", None, BF),
    ("kf", None, BF),
    ("v", None, BF),
    ("k", None, BF),
)


def project_outputs(rows, a):
    return [jax.ShapeDtypeStruct((rows, width or a), kind) for name, width, kind in PROJECT_KINDS]


def project_chunk(l, h, c, last, x, params, tables, whole, out, packed, summed):
    gain, bias, w_ref, b_ref, feat_ref, map_ref, ones_ref = params
    cos, sin, keep = tables
    ai_ref, fi_ref, normed_ref, unit_ref, inv_ref, qf_ref, kf_ref, v_ref, k_ref = out
    mean = jnp.sum(x, axis=1, keepdims=True) * (1.0 / D)
    center = x - mean
    inverse = lax.rsqrt(jnp.sum(center * center, axis=1, keepdims=True) * (1.0 / D) + EPSILON)
    normed = center * inverse
    inv_ref[...] = inverse
    normed_ref[...] = normed.astype(BF)
    whole[...] = normed
    unit_ref[...] = whole[:, block_columns(h, 0, unit_ref.shape[1])]
    attention_input = (normed * gain[l, 0:1] + bias[l, 0:1]).astype(BF)
    ai_ref[...] = attention_input
    fi_ref[...] = (normed * gain[l, 1:2] + bias[l, 1:2]).astype(BF)
    projected = dot_nn(attention_input, w_ref[...]) + b_ref[l : l + 1, :]
    q, k, v = split_heads(projected)
    v = v.astype(BF)
    q_turn = q * cos + swap_pairs(q) * sin
    k_turn = k * cos + swap_pairs(k) * sin
    query_feat = jnp.exp(dot_nn(q_turn, map_ref[...], HIGHEST))
    key_norm = head_sum(k * k, ones_ref[...]) * (0.5 / HEAD_DIM)
    key_feat = (
        keep
        * feat_ref[l : l + 1, :]
        * jnp.exp(dot_nn(k_turn, map_ref[...], HIGHEST) - key_norm)
    ).astype(BF)
    qf_ref[...] = query_feat.astype(BF)
    kf_ref[...] = key_feat
    v_ref[...] = v
    k_ref[...] = k.astype(BF)
    place = (row_of((CHUNK, 1)) + c * CHUNK).astype(F32)
    masked = jnp.where(place >= last, key_feat.astype(F32), 0.0)

    @pl.when(c == 0)
    def _():
        summed[...] = jnp.zeros_like(summed)
        packed[...] = jnp.zeros_like(packed)

    summed[...] += dot_tn(masked.astype(BF), v)
    packed[FEATURES : FEATURES + 1, :] += jnp.sum(masked, axis=0, keepdims=True)


def raise_chunk(l, fi, w_ref, b_ref, act_ref, slope_ref):
    raised = dot_nn(fi, w_ref[...]) + b_ref[l : l + 1, :]
    cumulative = 0.5 + 0.5 * lax.erf(raised * math.sqrt(0.5))
    density = jnp.exp(raised * raised * -0.5) * (1.0 / math.sqrt(2.0 * math.pi))
    act_ref[...] = (raised * cumulative).astype(BF)
    slope_ref[...] = (cumulative + raised * density).astype(BF)


def remote_call(kernel, name, ident, grid, in_specs, out_specs, out_shape, scratch, flops, args):
    moved = sum(int(np.prod(a.shape)) * a.dtype.itemsize for a in list(args) + list(out_shape))
    return pl.pallas_call(
        kernel,
        name=name,
        grid=grid,
        in_specs=in_specs,
        out_specs=out_specs,
        scratch_shapes=scratch,
        out_shape=out_shape,
        compiler_params=pltpu.CompilerParams(
            collective_id=ident, has_side_effects=True, vmem_limit_bytes=VMEM_BYTES
        ),
        cost_estimate=pl.CostEstimate(flops=int(flops), bytes_accessed=moved, transcendentals=0),
    )(*args)


def enter_kernel(n, hops, *refs):
    (
        lengths,
        acts,
        keep,
        gain,
        bias,
        w_ref,
        b_ref,
        feat_ref,
        map_ref,
        ones_ref,
        rate_ref,
        full_ref,
        cos_ref,
        sin_ref,
        begin_ref,
    ) = refs[:15]
    out = refs[15:24]
    state_ref = refs[24]
    gather_refs = refs[25:30]
    hand_refs = refs[30:33]
    packed, summed, whole = refs[33:]
    c = pl.program_id(0)
    count = pl.num_programs(0)
    h = lax.axis_index("head")
    rows, width = acts.shape
    first = lax.axis_index("seq") * rows
    gather = Gather(h, acts, gather_refs[:3], gather_refs[3:])
    hand = HandOver(n, hops, rows, 1, packed, hand_refs[0], hand_refs[1:])

    @pl.when(c == 0)
    def _():
        hand.clear()
        greet(h, n, hops)
        for i in range(rows // CHUNK):
            gather.start(i)

    slots = row_of((CHUNK, 1)) + c * CHUNK + first
    begins = begin_column(lengths, slots)
    begin_ref[...] = (begins - first).astype(F32)
    phase = (slots - begins).astype(F32) * rate_ref[0:1, :]
    cos_ref[...] = jnp.cos(phase)
    sin_ref[...] = jnp.sin(phase) * rate_ref[1:2, :]

    @pl.when(c == 0)
    def _():
        gather.relay(0)

    gather.ready(c)
    for r, part in enumerate(gather.pieces(c)):
        full_ref[:, block_columns(h, r, width)] = part
    last = (begin_scalar(lengths, first + rows - 1) - first).astype(F32)
    params = (gain, bias, w_ref, b_ref, feat_ref, map_ref, ones_ref)
    tables = (twice(cos_ref[...]), twice(sin_ref[...]), keep[...])
    project_chunk(
        0, h, c, last, full_ref[...].astype(F32), params, tables, whole, out, packed, summed
    )

    @pl.when(c + 1 < count)
    def _():
        gather.relay(c + 1)

    @pl.when(c + 1 == count)
    def _():
        packed[0:FEATURES, :] = pack_state(summed[...])
        hand.start()
        for i in range(rows // CHUNK):
            gather.finish(i)
        state_ref[...] = hand.total(lengths)


def enter(n, hops, lengths, acts, keep, gain, bias, qkv_w, qkv_b, feats, rates, consts):
    rows, width = acts.shape
    a = feats.shape[1]
    args = [lengths, acts, keep, gain, bias, qkv_w, qkv_b, feats, consts["map_t"], consts["ones"], rates]
    in_specs = [
        pl.BlockSpec(memory_space=pltpu.SMEM),
        full(acts.shape),
        rowed(1),
        full(gain.shape),
        full(bias.shape),
        layered(qkv_w, 0),
        full(qkv_b.shape),
        full(feats.shape),
        full((a, a)),
        full((a, a)),
        full(rates.shape),
    ]
    table = rates.shape[1]
    out_shape = [
        jax.ShapeDtypeStruct((rows, D), BF),
        jax.ShapeDtypeStruct((rows, table), F32),
        jax.ShapeDtypeStruct((rows, table), F32),
        jax.ShapeDtypeStruct((rows, 1), F32),
    ] + project_outputs(rows, a)
    out_specs = [rowed(o.shape[1]) for o in out_shape] + [full((STATE_ROWS, a))]
    out_shape = out_shape + [jax.ShapeDtypeStruct((STATE_ROWS, a), F32)]
    scratch = (
        Gather.scratch(rows, width)
        + HandOver.scratch(hops, a)
        + [pltpu.VMEM((STATE_ROWS, a), F32), pltpu.VMEM((a, a), F32), pltpu.VMEM((CHUNK, D), F32)]
    )
    return remote_call(
        functools.partial(enter_kernel, n, hops),
        "enter",
        2,
        (rows // CHUNK,),
        in_specs,
        out_specs,
        out_shape,
        scratch,
        2 * rows * D * 3 * a * 2,
        args,
    )


def between_kernel(n, hops, l, *refs):
    (
        lengths,
        qf_ref,
        kf_ref,
        v_ref,
        begin_ref,
        keep_ref,
        in_ref,
        fi_in,
        up_ref,
        up_b,
        ow_ref,
        dw_ref,
        ones_ref,
        full_ref,
        res_b,
        gain,
        bias,
        w_ref,
        b_ref,
        feat_ref,
        map_ref,
        cos_ref,
        sin_ref,
        keep_next,
        up_next,
    ) = refs[:25]
    (att_ref, low_ref, ratio_ref, states_ref, totals_ref, act_ref, slope_ref) = refs[25:32]
    own_ref = refs[32]
    out = refs[33:42]
    act_next, slope_next, state_ref = refs[42:45]
    gather_refs = refs[45:50]
    scatter_refs = refs[50:57]
    hand_refs = refs[57:60]
    mine, packed, summed, whole, whole_low, state, total = refs[60:]
    step = pl.program_id(0)
    count = pl.num_programs(0) // 2
    h = lax.axis_index("head")
    rows, width = mine.shape
    first = lax.axis_index("seq") * rows
    chunks = rows // CHUNK
    gather = Gather(h, mine, gather_refs[:3], gather_refs[3:])
    scatter = Scatter(h, scatter_refs[:5], scatter_refs[5:])
    hand = HandOver(n, hops, rows, 1, packed, hand_refs[0], hand_refs[1:])

    def send_sum(c):
        mine[rows_at(c), :] = scatter.total(c).astype(BF)
        gather.start(c)

    @pl.when(step == 0)
    def _():
        hand.clear()
        greet(h, n, hops)

    @pl.when(step < count)
    def _():
        raise_chunk(l, fi_in[...], up_ref, up_b, act_ref, slope_ref)

        @pl.when(step >= 1)
        def _():
            scatter.relay(step - 1)

        @pl.when(step >= 2)
        def _():
            send_sum(step - 2)

        attention_chunk(
            step,
            (qf_ref, kf_ref, v_ref, begin_ref, keep_ref, in_ref, ones_ref),
            (att_ref, low_ref, ratio_ref, states_ref, totals_ref),
            state,
            total,
        )
        whole_low[...] = (
            dot_nt(low_ref[...], ow_ref[...]) + dot_nt(act_ref[...], dw_ref[...])
        ).astype(BF)
        scatter.put(h, step, whole_low)

        @pl.when(step >= 3)
        def _():
            gather.relay(step - 3)

    @pl.when(step >= count)
    def _():
        c = step - count

        @pl.when(step == count)
        def _():
            scatter.relay(chunks - 1)
            send_sum(chunks - 2)

        gather.ready(c)
        for r, part in enumerate(gather.pieces(c)):
            whole[:, block_columns(h, r, width)] = part.astype(F32)
        x = full_ref[...].astype(F32) + whole[...] + res_b[l : l + 1, :]
        whole[...] = x
        own_ref[...] = whole[:, block_columns(h, 0, width)]
        last = (begin_scalar(lengths, first + rows - 1) - first).astype(F32)
        params = (gain, bias, w_ref, b_ref, feat_ref, map_ref, ones_ref)
        tables = (twice(cos_ref[...]), twice(sin_ref[...]), keep_next[...])
        project_chunk(l + 1, h, c, last, x, params, tables, whole, out, packed, summed)

        @pl.when(c == 0)
        def _():
            send_sum(chunks - 1)

        @pl.when(c + 1 < chunks)
        def _():
            gather.relay(c + 1)

        @pl.when(c + 1 == chunks)
        def _():
            packed[0:FEATURES, :] = pack_state(summed[...])
            hand.start()

        raise_chunk(l + 1, out[1][...], up_next, up_b, act_next, slope_next)

        @pl.when(c + 1 == chunks)
        def _():
            for i in range(chunks):
                gather.finish(i)
                scatter.finish(i)
            state_ref[...] = hand.total(lengths)


def between(
    n, hops, l, lengths, made, tables, state_in, full_acts, params, consts
):
    gain, bias, qkv_w, qkv_b, feats, up_w, up_b, out_w, down_w, res_b = params
    cos, sin, begin, keep = tables
    ai, fi, normed, unit, inverse, qf, kf, v, k = made
    rows, a = qf.shape
    hidden = up_w.shape[2]
    chunks = rows // CHUNK
    width = D // 4

    def early(w):
        return pl.BlockSpec((CHUNK, w), lambda i: (jnp.minimum(i, chunks - 1), 0))

    def late(w):
        return pl.BlockSpec((CHUNK, w), lambda i: (jnp.maximum(i - chunks, 0), 0))

    args = [
        lengths, qf, kf, v, begin, keep, state_in, fi, up_w, up_b, out_w, down_w, consts["ones"],
        full_acts, res_b, gain, bias, qkv_w, qkv_b, feats, consts["map_t"], cos, sin, keep, up_w,
    ]
    in_specs = [
        pl.BlockSpec(memory_space=pltpu.SMEM),
        early(a),
        early(a),
        early(a),
        early(1),
        early(1),
        full((STATE_ROWS, a)),
        early(D),
        layered(up_w, l),
        full(up_b.shape),
        layered(out_w, l),
        layered(down_w, l),
        full((a, a)),
        late(D),
        full(res_b.shape),
        full(gain.shape),
        full(bias.shape),
        layered(qkv_w, l + 1),
        full(qkv_b.shape),
        full(feats.shape),
        full((a, a)),
        late(cos.shape[1]),
        late(sin.shape[1]),
        late(1),
        layered(up_w, l + 1),
    ]

    def shaped(w, kind):
        return jax.ShapeDtypeStruct((rows, w), kind)

    first = [
        (early(a), shaped(a, F32)),
        (early(a), shaped(a, BF)),
        (early(a), shaped(a, F32)),
        (
            pl.BlockSpec((1, a, a), lambda i: (jnp.minimum(i, chunks - 1), 0, 0)),
            jax.ShapeDtypeStruct((chunks, a, a), F32),
        ),
        (
            pl.BlockSpec((1, 8, a), lambda i: (jnp.minimum(i, chunks - 1), 0, 0)),
            jax.ShapeDtypeStruct((chunks, 8, a), F32),
        ),
        (early(hidden), shaped(hidden, BF)),
        (early(hidden), shaped(hidden, BF)),
    ]
    second = [(late(width), shaped(width, F32))]
    second += [(late(o.shape[1]), o) for o in project_outputs(rows, a)]
    second += [(late(hidden), shaped(hidden, BF))] * 2
    second += [(full((STATE_ROWS, a)), jax.ShapeDtypeStruct((STATE_ROWS, a), F32))]
    both = first + second
    scratch = (
        Gather.scratch(rows, width)
        + Scatter.scratch(rows, width)
        + HandOver.scratch(hops, a)
        + [
            pltpu.VMEM((rows, width), BF),
            pltpu.VMEM((STATE_ROWS, a), F32),
            pltpu.VMEM((a, a), F32),
            pltpu.VMEM((CHUNK, D), F32),
            pltpu.VMEM((CHUNK, D), BF),
            pltpu.VMEM((a, a), F32),
            pltpu.VMEM((8, a), F32),
        ]
    )
    return remote_call(
        functools.partial(between_kernel, n, hops, l),
        "between",
        3,
        (2 * chunks,),
        in_specs,
        [spec for spec, shape in both],
        [shape for spec, shape in both],
        scratch,
        2 * rows * D * (hidden * 3 + 4 * a) * 2,
        args,
    )


def pair_mask(begin, step):
    shape = (CHUNK, CHUNK)
    t = row_of(shape)
    s = lane_of(shape)
    return (s <= t) & ((s + step * CHUNK).astype(F32) >= begin)


def attention_chunk(step, refs, out, state, total):
    qf_ref, kf_ref, v_ref, begin_ref, keep_ref, in_ref, ones_ref = refs
    att_ref, low_ref, ratio_ref, states_ref, totals_ref = out

    @pl.when(step == 0)
    def _():
        state[...] = unpack_state(in_ref[0:FEATURES, :])
        total[...] = jnp.broadcast_to(in_ref[FEATURES : FEATURES + 1, :], total.shape)

    q = qf_ref[...]
    k = kf_ref[...]
    v = v_ref[...]
    begin = begin_ref[...]
    keep = keep_ref[...]
    ones = ones_ref[...]
    a = q.shape[1]
    mask = pair_mask(begin, step)
    head_of = lane_of((1, a)) // HEAD_DIM
    held = state[...]
    held_total = total[0:1, :]
    states_ref[0] = held
    totals_ref[0] = total[...]
    base = (step * CHUNK).astype(F32)
    use = jnp.where(begin < base, 1.0, 0.0)
    high, low = halves(held)
    num = use * (dot_nn(q, high) + dot_nn(q, low))
    den = use * head_sum(q.astype(F32) * held_total, ones)
    for head in range(a // HEAD_DIM):
        own = (head_of == head).astype(BF)
        scores = dot_nt(q * own, k)
        scores_low = jnp.where(mask, scores, 0.0).astype(BF)
        num = num + dot_nn(scores_low, v * own)
        den = den + dot_nn(scores_low, jnp.broadcast_to(own, (CHUNK, a)))
    ratio = keep / (den + 1.0 - keep)
    att = num * ratio
    ratio_ref[...] = ratio
    att_ref[...] = att
    low_ref[...] = att.astype(BF)
    end = begin[CHUNK - 1 : CHUNK, :]
    place = (row_of((CHUNK, 1)) + step * CHUNK).astype(F32)
    masked = jnp.where(place >= end, k.astype(F32), 0.0)
    passing = jnp.where(end < base, 1.0, 0.0)
    state[...] = passing * held + jnp.where(
        block_diagonal(a), dot_tn(masked.astype(BF), v), 0.0
    )
    total[...] = jnp.broadcast_to(
        passing * held_total + jnp.sum(masked, axis=0, keepdims=True), total.shape
    )


class Names:
    pass


def named_call(kernel, name, ident, grid, ins, outs, scratch, flops):
    labels, groups = list(ins) + list(outs), list(scratch)

    def body(*refs):
        names = Names()
        for label, ref in zip(labels, refs):
            setattr(names, label, ref)
        at = len(labels)
        for label in groups:
            size = len(scratch[label])
            held = refs[at : at + size]
            setattr(names, label, held if size > 1 else held[0])
            at += size
        kernel(names)

    result = remote_call(
        body,
        name,
        ident,
        grid,
        [spec for array, spec in ins.values()],
        [spec for shape, spec in outs.values()],
        [shape for shape, spec in outs.values()],
        [item for label in groups for item in scratch[label]],
        flops,
        [array for array, spec in ins.values()],
    )
    return dict(zip(outs, result))


def fixed(shape):
    return pl.BlockSpec(shape, lambda *i: (0,) * len(shape), pipeline_mode=pl.Buffered(1))


def layer_of(array, l):
    return pl.BlockSpec(
        (None,) + array.shape[1:], lambda *i: (l, 0, 0), pipeline_mode=pl.Buffered(1)
    )


def clipped(step, low, count):
    return jnp.minimum(jnp.maximum(step - low, 0), count - 1)


def up_rows(width, low, count):
    return pl.BlockSpec((CHUNK, width), lambda i: (clipped(i, low, count), 0))


def down_rows(width, low, count):
    return pl.BlockSpec((CHUNK, width), lambda i: (count - 1 - clipped(i, low, count), 0))


def down_cube(shape, low, count):
    return pl.BlockSpec(
        (1,) + shape, lambda i: (count - 1 - clipped(i, low, count),) + (0,) * len(shape)
    )


def struct(shape, kind):
    return jax.ShapeDtypeStruct(shape, kind)


def lower_chunk(grad, refs, out, summed, packed, start):
    dw_ref, ow_ref, slope_ref, ratio_ref, att_ref, qf_ref, begin_ref, ones_ref = refs
    num_ref, den_ref, bias_ref = out

    @pl.when(start)
    def _():
        summed[...] = jnp.zeros_like(summed)
        packed[...] = jnp.zeros_like(packed)
        bias_ref[...] = jnp.zeros_like(bias_ref)

    d_att = dot_nn(grad, ow_ref[...])
    d_num = (d_att * ratio_ref[...]).astype(BF)
    d_den = -head_sum(d_num.astype(F32) * att_ref[...], ones_ref[...])
    num_ref[...] = d_num
    den_ref[...] = d_den
    entering = jnp.where(begin_ref[...] < 0.0, qf_ref[...].astype(F32), 0.0)
    summed[...] += dot_tn(entering.astype(BF), d_num)
    packed[FEATURES : FEATURES + 1, :] += jnp.sum(entering * d_den, axis=0, keepdims=True)
    d_raised = (dot_nn(grad, dw_ref[...]) * slope_ref[...].astype(F32)).astype(BF)
    bias_ref[...] += jnp.sum(d_raised.astype(F32), axis=0, keepdims=True)
    return d_raised


def tile_at(i):
    return pl.ds(pl.multiple_of(i * CHUNK, CHUNK), CHUNK)


def weight_tile(i, x_ref, ys, out_ref):
    x = x_ref[:, tile_at(i)]
    at = 0
    for y in ys:
        width = y.shape[1]
        out_ref[:, at : at + width] = dot_tn(x, y[...]).astype(BF)
        at += width


def attention_back(turn, step, refs, state, total):
    (
        qf_ref,
        kf_ref,
        v_ref,
        num_ref,
        den_ref,
        begin_ref,
        states_ref,
        totals_ref,
        exit_ref,
    ) = refs

    @pl.when(turn == 0)
    def _():
        state[...] = unpack_state(exit_ref[0:FEATURES, :])
        total[...] = jnp.broadcast_to(exit_ref[FEATURES : FEATURES + 1, :], total.shape)

    q = qf_ref[...]
    k = kf_ref[...]
    v = v_ref[...]
    d_num = num_ref[...]
    d_den = den_ref[...]
    begin = begin_ref[...]
    a = q.shape[1]
    mask = pair_mask(begin, step)
    head_of = lane_of((1, a)) // HEAD_DIM
    base = (step * CHUNK).astype(F32)
    use = jnp.where(begin < base, 1.0, 0.0)
    end = begin[CHUNK - 1 : CHUNK, :]
    place = (row_of((CHUNK, 1)) + step * CHUNK).astype(F32)
    inside = jnp.where(place >= end, 1.0, 0.0)
    passing = jnp.where(end < base, 1.0, 0.0)
    held_high, held_low = halves(states_ref[0])
    held_total = totals_ref[0][0:1, :]
    after = state[...]
    after_total = total[0:1, :]
    after_high, after_low = halves(after)
    masked = (k.astype(F32) * inside).astype(BF)
    d_q = use * (dot_nt(d_num, held_high) + dot_nt(d_num, held_low) + d_den * held_total)
    d_k = inside * (dot_nt(v, after_high) + dot_nt(v, after_low) + after_total)
    d_v = dot_nn(masked, after_high) + dot_nn(masked, after_low)
    for head in range(a // HEAD_DIM):
        own = (head_of == head).astype(BF)
        q_own = q * own
        num_own = d_num * own
        scores_low = jnp.where(mask, dot_nt(q_own, k), 0.0).astype(BF)
        column = d_den[:, head * HEAD_DIM : head * HEAD_DIM + 1]
        d_scores = jnp.where(mask, dot_nt(num_own, v) + column, 0.0).astype(BF)
        d_q = d_q + dot_nn(d_scores, k * own)
        d_k = d_k + dot_tn(d_scores, q_own)
        d_v = d_v + dot_tn(scores_low, num_own)
    q_used = q.astype(F32) * use
    state[...] = passing * after + jnp.where(
        block_diagonal(a), dot_tn(q_used.astype(BF), d_num), 0.0
    )
    total[...] = jnp.broadcast_to(
        passing * after_total + jnp.sum(q_used * d_den, axis=0, keepdims=True), total.shape
    )
    return d_q, d_k, d_v


def features_back(grads, refs, feat_ref, bias_ref, start):
    d_q, d_k, d_v = grads
    qf_ref, kf_ref, k_ref, cos_ref, sin_ref, map_ref, ones_ref = refs

    @pl.when(start)
    def _():
        feat_ref[...] = jnp.zeros_like(feat_ref)
        bias_ref[...] = jnp.zeros_like(bias_ref)

    cos = twice(cos_ref[...])
    sin = twice(sin_ref[...])
    d_query = dot_nn(d_q * qf_ref[...].astype(F32), map_ref[...], HIGHEST)
    d_query = d_query * cos - swap_pairs(d_query) * sin
    d_key_log = d_k * kf_ref[...].astype(F32)
    feat_ref[...] += jnp.sum(d_key_log, axis=0, keepdims=True)
    d_key = dot_nn(d_key_log, map_ref[...], HIGHEST)
    d_key = d_key * cos - swap_pairs(d_key) * sin
    d_key = d_key - head_sum(d_key_log, ones_ref[...]) * k_ref[...].astype(F32) * (1.0 / HEAD_DIM)
    d_proj = join_heads(d_query, d_key, d_v).astype(BF)
    bias_ref[...] += jnp.sum(d_proj.astype(F32), axis=0, keepdims=True)
    return d_proj


def inputs_back(l, d_proj, raised_ref, w_ref, up_ref, normed_ref, gain, sums_ref, start):
    @pl.when(start)
    def _():
        sums_ref[...] = jnp.zeros_like(sums_ref)

    normed = normed_ref[...].astype(F32)
    d_attention = dot_nt(d_proj, w_ref[...])
    d_feed = dot_nt(raised_ref[...], up_ref[...])
    sums_ref[0:1, :] += jnp.sum(d_attention * normed, axis=0, keepdims=True)
    sums_ref[1:2, :] += jnp.sum(d_feed * normed, axis=0, keepdims=True)
    sums_ref[2:3, :] += jnp.sum(d_attention, axis=0, keepdims=True)
    sums_ref[3:4, :] += jnp.sum(d_feed, axis=0, keepdims=True)
    d_normed = (d_attention * gain[l, 0:1] + d_feed * gain[l, 1:2]).astype(BF)
    high, low = halves(d_normed.astype(F32) * normed)
    row = jnp.ones((8, D), BF)
    first = dot_nt(row, d_normed)
    second = dot_nt(row, high) + dot_nt(row, low)
    return d_normed, jnp.where(row_of(first.shape) == 0, first, second)


class RowSum:
    def __init__(self, h, buffers, sems):
        self.own, self.got, self.middle, self.across = buffers
        self.send, self.recv = sems
        self.beside = {"head": lax.bitwise_xor(h, 1)}
        self.beyond = {"head": lax.bitwise_xor(h, 2)}

    @staticmethod
    def scratch(rows):
        count = rows // CHUNK
        return [pltpu.VMEM((count, 8, CHUNK), F32)] * 4 + [pltpu.SemaphoreType.DMA((2, count))] * 2

    def copy(self, kind, c):
        source, target, where = (
            (self.own, self.got, self.beside),
            (self.middle, self.across, self.beyond),
        )[kind]
        return push(
            source.at[c], target.at[c], self.send.at[kind, c], self.recv.at[kind, c], where
        )

    def put(self, c, value):
        self.own[c] = value
        self.copy(0, c).start()

    def relay(self, c):
        self.copy(0, c).wait_recv()
        self.middle[c] = self.own[c] + self.got[c]
        self.copy(1, c).start()

    def total(self, c):
        self.copy(1, c).wait_recv()
        value = self.middle[c] + self.across[c]
        shape = (8, 128)
        eye = (row_of(shape) == lane_of(shape)).astype(F32)
        columns = dot_tn(value, eye, HIGHEST)
        return columns[:, 0:1], columns[:, 1:2]

    def finish(self, c):
        self.copy(0, c).wait_send()
        self.copy(1, c).wait_send()


def norm_back(before, inverse, unit, d_normed, sums):
    first, second = sums
    return before + inverse * (d_normed - first * (1.0 / D) - unit * (second * (1.0 / D)))


def ring_place(index, n):
    return jnp.where(index % 2 == 0, index // 2, n - 1 - index // 2)


def ring_index(place, n):
    return jnp.where(place < n // 2, 2 * place, 2 * (n - 1 - place) + 1)


class Ring:
    def __init__(self, n, parts, source, held, sems):
        self.n, self.parts, self.source, self.held = n, parts, source, held
        self.send_sem, self.recv_sem = sems
        self.share = D // n
        self.place = ring_place(lax.axis_index("seq"), n)
        self.right = ring_index(lax.rem(self.place + 1, n), n)
        self.left = ring_index(lax.rem(self.place + n - 1, n), n)

    @staticmethod
    def buffers(n, parts):
        return [pltpu.VMEM((n - 1, D // n, part[2]), BF) for part in parts]

    @staticmethod
    def sems(n, parts):
        return [pltpu.SemaphoreType.DMA((len(parts), n - 1))] * 2

    def own(self, part, step):
        array, start, width, way = part
        n = self.n
        ahead = lax.rem(self.place - way * (1 + step) + 2 * n, n)
        rows = pl.ds(pl.multiple_of(ring_index(ahead, n) * self.share, self.share), self.share)
        return self.source[array].at[rows, pl.ds(start, width)]

    def copy(self, r, step, block):
        return push(
            block,
            self.held[r].at[step],
            self.send_sem.at[r, step],
            self.recv_sem.at[r, step],
            {"seq": self.right if self.parts[r][3] > 0 else self.left},
        )

    def start(self):
        for r, part in enumerate(self.parts):
            self.copy(r, 0, self.own(part, 0)).start()

    def tick(self, step):
        for r, part in enumerate(self.parts):
            block = self.held[r].at[step - 1]
            self.copy(r, step - 1, block).wait_recv()
            block[...] = (block[...].astype(F32) + self.own(part, step)[...].astype(F32)).astype(BF)
            self.copy(r, step, block).start()

    def ticks(self, low, high):
        def one(step, carry):
            self.tick(step)
            return carry

        lax.fori_loop(low, high, one, 0)

    def finish(self, out):
        n = self.n
        for r, part in enumerate(self.parts):
            block = self.held[r].at[n - 2]
            self.copy(r, n - 2, block).wait_recv()
            array, start, width, way = part
            out[array][:, pl.ds(start, width)] = block[...].astype(F32) + self.own(part, n - 1)[
                ...
            ].astype(F32)

        def one(step, carry):
            for r in range(len(self.parts)):
                self.copy(r, step, self.held[r].at[step]).wait_send()
            return carry

        lax.fori_loop(0, n - 1, one, 0)


def crest_kernel(n, hops, l, z):
    step = pl.program_id(0)
    h = lax.axis_index("head")
    rows, width = z.cotangent.shape
    count = rows // CHUNK
    gather = Gather(h, z.cotangent, z.gather[:3], z.gather[3:])
    scatter = Scatter(h, z.scatter[:5], z.scatter[5:])
    hand = HandOver(n, hops, rows, -1, z.packed, z.hand[0], z.hand[1:])

    @pl.when(step == 0)
    def _():
        hand.clear()
        greet(h, n, hops)
        for c in range(count):
            gather.start(c)

    @pl.when(step < count)
    def _():
        attention_chunk(
            step,
            (z.qf, z.kf, z.v, z.begin, z.keep, z.state_in, z.ones),
            (z.att, z.low_now, z.ratio, z.states, z.totals),
            z.state,
            z.total,
        )

        @pl.when(step >= 1)
        def _():
            scatter.relay(step - 1)

        here = rows_at(step)
        low = z.low_now[...]
        z.low[here, :] = low
        z.att_all[here, :] = z.att[...]
        z.ratio_all[here, :] = z.ratio[...]
        z.whole[...] = (dot_nt(low, z.out_w[...]) + dot_nt(z.act[here, :], z.down_w[...])).astype(
            BF
        )
        scatter.put(h, step, z.whole)
        gather.relay(step)

    @pl.when((step >= count) & (step < 2 * count))
    def _():
        c = step - count

        @pl.when(c == 0)
        def _():
            scatter.relay(count - 1)

        gather.ready(c)
        here = rows_at(c)
        for r, part in enumerate(gather.pieces(c)):
            z.grad[here, block_columns(h, r, width)] = part
        d_raised = lower_chunk(
            z.grad[here, :],
            (
                z.down_w,
                z.out_w,
                z.slope,
                z.ratio_all.at[here, :],
                z.att_all.at[here, :],
                z.qf_late,
                z.begin_late,
                z.ones,
            ),
            (z.d_num, z.d_den, z.d_up_b),
            z.summed,
            z.packed,
            c == 0,
        )
        z.d_raised[...] = d_raised
        z.raised_all[here, :] = d_raised

        @pl.when(c == 0)
        def _():
            z.d_res[...] = jnp.zeros_like(z.d_res)

        z.d_res[...] += jnp.sum(z.cotangent[here, :].astype(F32), axis=0, keepdims=True)

        @pl.when(c + 1 == count)
        def _():
            z.packed[0:FEATURES, :] = pack_state(z.summed[...])
            hand.start()

    @pl.when(step >= 2 * count)
    def _():
        c = step - 2 * count
        weight_tile(c, z.grad, (z.act, z.low), z.d_down_out)
        weight_tile(c, z.fi, (z.raised_all,), z.d_up)
        columns = pl.ds(pl.multiple_of(h * width, width), width)
        z.out[...] = z.own[...] + scatter.total(c) + z.res_b[l : l + 1, columns]

        @pl.when(c + 1 == count)
        def _():
            for i in range(count):
                gather.finish(i)
                scatter.finish(i)
            z.exit_state[...] = hand.total(z.lengths)


def crest(n, hops, l, lengths, made, tables, state_in, act, slope, own, cotangent, params, consts):
    gain, bias, qkv_w, qkv_b, feats, up_w, up_b, out_w, down_w, res_b = params
    cos, sin, begin, keep = tables
    ai, fi, normed, unit, inverse, qf, kf, v, k = made
    rows, a = qf.shape
    hidden = up_w.shape[2]
    count = rows // CHUNK
    width = D // 4

    def early(w):
        return up_rows(w, 0, count)

    def middle(w):
        return up_rows(w, count, count)

    def late(w):
        return up_rows(w, 2 * count, count)

    def cube(shape):
        return pl.BlockSpec(
            (1,) + shape, lambda i: (clipped(i, 0, count),) + (0,) * len(shape)
        )

    ins = {
        "lengths": (lengths, pl.BlockSpec(memory_space=pltpu.SMEM)),
        "cotangent": (cotangent, fixed(cotangent.shape)),
        "qf": (qf, early(a)),
        "kf": (kf, early(a)),
        "v": (v, early(a)),
        "begin": (begin, early(1)),
        "keep": (keep, early(1)),
        "state_in": (state_in, fixed(state_in.shape)),
        "ones": (consts["ones"], fixed((a, a))),
        "act": (act, fixed(act.shape)),
        "fi": (fi, fixed(fi.shape)),
        "out_w": (out_w, layer_of(out_w, l)),
        "down_w": (down_w, layer_of(down_w, l)),
        "slope": (slope, middle(hidden)),
        "qf_late": (qf, middle(a)),
        "begin_late": (begin, middle(1)),
        "own": (own, late(width)),
        "res_b": (res_b, fixed(res_b.shape)),
    }
    outs = {
        "ratio": (struct((rows, a), F32), early(a)),
        "att": (struct((rows, a), F32), early(a)),
        "states": (struct((count, a, a), F32), cube((a, a))),
        "totals": (struct((count, 8, a), F32), cube((8, a))),
        "d_raised": (struct((rows, hidden), BF), middle(hidden)),
        "d_num": (struct((rows, a), BF), middle(a)),
        "d_den": (struct((rows, a), F32), middle(a)),
        "d_up_b": (struct((1, hidden), F32), full((1, hidden))),
        "d_res": (struct((1, width), F32), full((1, width))),
        "d_down_out": (struct((D, hidden + a), BF), late(hidden + a)),
        "d_up": (struct((D, hidden), BF), late(hidden)),
        "out": (struct((rows, width), F32), late(width)),
        "exit_state": (struct((STATE_ROWS, a), F32), full((STATE_ROWS, a))),
    }
    scratch = {
        "gather": Gather.scratch(rows, width),
        "scatter": Scatter.scratch(rows, width),
        "hand": HandOver.scratch(hops, a),
        "packed": [pltpu.VMEM((STATE_ROWS, a), F32)],
        "summed": [pltpu.VMEM((a, a), F32)],
        "state": [pltpu.VMEM((a, a), F32)],
        "total": [pltpu.VMEM((8, a), F32)],
        "whole": [pltpu.VMEM((CHUNK, D), BF)],
        "grad": [pltpu.VMEM((rows, D), BF)],
        "low_now": [pltpu.VMEM((CHUNK, a), BF)],
        "low": [pltpu.VMEM((rows, a), BF)],
        "att_all": [pltpu.VMEM((rows, a), F32)],
        "ratio_all": [pltpu.VMEM((rows, a), F32)],
        "raised_all": [pltpu.VMEM((rows, hidden), BF)],
    }
    return named_call(
        functools.partial(crest_kernel, n, hops, l),
        "crest",
        4,
        (3 * count,),
        ins,
        outs,
        scratch,
        2 * rows * D * (hidden * 4 + 4 * a) * 2,
    )


def back_step(z, l, h, step, count, scatter, row_sum, middle_work):
    c = count - 1 - step
    grads = attention_back(
        step,
        c,
        (z.qf, z.kf, z.v, z.d_num, z.d_den, z.begin, z.states, z.totals, z.exit_state),
        z.state,
        z.total,
    )

    @pl.when(step >= 1)
    def _():
        scatter.relay(c + 1)
        row_sum.relay(c + 1)

    middle_work()
    start = step == 0
    d_proj = features_back(
        grads,
        (z.qf, z.kf, z.k, z.cos, z.sin, z.map, z.ones),
        z.d_feat,
        z.d_qkv_b,
        start,
    )
    z.proj_all[rows_at(c), :] = d_proj
    d_normed, sums = inputs_back(
        l, d_proj, z.d_raised_in, z.qkv_w, z.up_w, z.normed, z.gain, z.sums, start
    )
    z.whole[...] = d_normed
    scatter.put(h, c, z.whole)
    row_sum.put(c, sums)


def back_arrays(l, local, lowered, tables, params, consts, exit_state, count):
    gain, bias, qkv_w, qkv_b, feats, up_w, up_b, out_w, down_w, res_b = params
    cos, sin, begin, keep = tables
    qf, kf, v, k, normed, unit, inverse, states, totals = local
    d_raised, d_num, d_den = lowered
    a = qf.shape[1]

    def early(w):
        return down_rows(w, 0, count)

    return {
        "qf": (qf, early(a)),
        "kf": (kf, early(a)),
        "v": (v, early(a)),
        "k": (k, early(a)),
        "d_num": (d_num, early(a)),
        "d_den": (d_den, early(a)),
        "begin": (begin, early(1)),
        "cos": (cos, early(cos.shape[1])),
        "sin": (sin, early(sin.shape[1])),
        "states": (states, down_cube((a, a), 0, count)),
        "totals": (totals, down_cube((8, a), 0, count)),
        "exit_state": (exit_state, fixed(exit_state.shape)),
        "map": (consts["map"], fixed((a, a))),
        "ones": (consts["ones"], fixed((a, a))),
        "qkv_w": (qkv_w, layer_of(qkv_w, l)),
        "up_w": (up_w, layer_of(up_w, l)),
        "d_raised_in": (d_raised, early(d_raised.shape[1])),
        "normed": (normed, early(D)),
        "gain": (gain, fixed(gain.shape)),
        "unit": (unit, down_rows(unit.shape[1], 2, count)),
        "inverse": (inverse, down_rows(1, 2, count)),
    }


def back_scratch(rows, a, width):
    return {
        "scatter": Scatter.scratch(rows, width),
        "row_sum": RowSum.scratch(rows),
        "state": [pltpu.VMEM((a, a), F32)],
        "total": [pltpu.VMEM((8, a), F32)],
        "whole": [pltpu.VMEM((CHUNK, D), BF)],
        "proj_all": [pltpu.VMEM((rows, 3 * a), BF)],
    }


def turn_kernel(n, hops, l, parts, z):
    step = pl.program_id(0)
    h = lax.axis_index("head")
    rows, width = z.mine.shape
    count = rows // CHUNK
    scatter = Scatter(h, z.scatter[:5], z.scatter[5:])
    row_sum = RowSum(h, z.row_sum[:4], z.row_sum[4:])
    gather = Gather(h, z.mine, z.gather[:3], z.gather[3:])
    hand = HandOver(n, hops, rows, -1, z.packed, z.hand[0], z.hand[1:])
    ring = Ring(n, parts, (z.ring_a, z.ring_b), z.ring_held, z.ring_sems)

    def taken(at):
        sixths = jnp.where(at <= 3, at, jnp.minimum(6, 3 + (at - 3) // 2))
        return 1 + sixths * (n - 2) // 6

    def ring_work():
        ring.ticks(taken(jnp.maximum(step - 1, 0)), taken(step))

    def sum_up(o):
        c = count - 1 - o
        new = norm_back(
            z.before[...].astype(F32), z.inverse[...], z.unit[...], scatter.total(c), row_sum.total(c)
        )
        z.after[...] = new
        z.mine[rows_at(c), :] = new.astype(BF)

        @pl.when(o == 0)
        def _():
            z.d_res[...] = jnp.zeros_like(z.d_res)

        z.d_res[...] += jnp.sum(new, axis=0, keepdims=True)
        gather.start(c)

    @pl.when(step == 0)
    def _():
        hand.clear()
        greet(h, n, hops)
        ring.start()

    @pl.when(step < count)
    def _():
        def middle_work():
            @pl.when(step >= 1)
            def _():
                ring_work()

            @pl.when(step >= 2)
            def _():
                sum_up(step - 2)

        back_step(z, l + 1, h, step, count, scatter, row_sum, middle_work)

        @pl.when(step >= 3)
        def _():
            gather.relay(count - 1 - (step - 3))

    @pl.when((step >= count) & (step < 2 * count))
    def _():
        o = step - count
        c = count - 1 - o

        @pl.when(o == 0)
        def _():
            scatter.relay(0)
            row_sum.relay(0)

        @pl.when(o <= 1)
        def _():
            sum_up(step - 2)

        @pl.when(o == count - 1)
        def _():
            gather.relay(0)

        weight_tile(o, z.ai, (z.proj_all,), z.d_qkv)
        ring_work()
        gather.ready(c)
        here = rows_at(c)
        for r, part in enumerate(gather.pieces(c)):
            z.grad[here, block_columns(h, r, width)] = part
        d_raised = lower_chunk(
            z.grad[here, :],
            (z.down_w, z.out_w, z.slope, z.ratio, z.att, z.qf_late, z.begin_late, z.ones),
            (z.d_num_out, z.d_den_out, z.d_up_b),
            z.summed,
            z.packed,
            o == 0,
        )
        z.d_raised_out[...] = d_raised
        z.raised_all[here, :] = d_raised

        @pl.when(o <= count - 3)
        def _():
            gather.relay(c - 1)

        @pl.when(o + 1 == count)
        def _():
            z.packed[0:FEATURES, :] = pack_state(z.summed[...])
            hand.start()

    @pl.when(step >= 2 * count)
    def _():
        c = step - 2 * count
        weight_tile(c, z.grad, (z.act, z.att_low), z.d_down_out)
        ring_work()
        weight_tile(c, z.fi, (z.raised_all,), z.d_up)

        @pl.when(c + 1 == count)
        def _():
            for i in range(count):
                gather.finish(i)
                scatter.finish(i)
                row_sum.finish(i)
            z.exit_out[...] = hand.total(z.lengths)
            ring.finish((z.sum_a, z.sum_b))


def turn(
    n, hops, l, lengths, local, lowered, exit_state, before, ai, rings, lower_in, tables, params, consts
):
    gain, bias, qkv_w, qkv_b, feats, up_w, up_b, out_w, down_w, res_b = params
    cos, sin, begin, keep = tables
    act, slope, ratio, att, att_low, fi, qf = lower_in
    rows, a = qf.shape
    hidden = up_w.shape[2]
    count = rows // CHUNK
    width = D // 4
    share = D // n
    middle = functools.partial(down_rows, low=count, count=count)

    def late(w):
        return up_rows(w, 2 * count, count)

    parts = (
        (0, 0, 640, 1),
        (0, 640, 512, 1),
        (0, 1152, hidden + a - 1152, -1),
        (1, 0, hidden // 2, -1),
        (1, hidden // 2, hidden // 2, -1),
    )
    ins = {
        "lengths": (lengths, pl.BlockSpec(memory_space=pltpu.SMEM)),
        **back_arrays(l + 1, local, lowered, tables, params, consts, exit_state, count),
        "before": (before, down_rows(width, 2, count)),
        "ai": (ai, fixed(ai.shape)),
        "ring_a": (rings[0], fixed(rings[0].shape)),
        "ring_b": (rings[1], fixed(rings[1].shape)),
        "down_w": (down_w, layer_of(down_w, l)),
        "out_w": (out_w, layer_of(out_w, l)),
        "slope": (slope, middle(hidden)),
        "ratio": (ratio, middle(a)),
        "att": (att, middle(a)),
        "qf_late": (qf, middle(a)),
        "begin_late": (begin, middle(1)),
        "act": (act, fixed(act.shape)),
        "att_low": (att_low, fixed(att_low.shape)),
        "fi": (fi, fixed(fi.shape)),
    }
    outs = {
        "d_feat": (struct((1, a), F32), full((1, a))),
        "d_qkv_b": (struct((1, 3 * a), F32), full((1, 3 * a))),
        "sums": (struct((8, D), F32), full((8, D))),
        "after": (struct((rows, width), F32), down_rows(width, 2, count)),
        "d_res": (struct((1, width), F32), full((1, width))),
        "d_qkv": (struct((D, 3 * a), BF), up_rows(3 * a, count, count)),
        "d_num_out": (struct((rows, a), BF), middle(a)),
        "d_den_out": (struct((rows, a), F32), middle(a)),
        "d_raised_out": (struct((rows, hidden), BF), middle(hidden)),
        "d_up_b": (struct((1, hidden), F32), full((1, hidden))),
        "d_down_out": (struct((D, hidden + a), BF), late(hidden + a)),
        "d_up": (struct((D, hidden), BF), late(hidden)),
        "exit_out": (struct((STATE_ROWS, a), F32), full((STATE_ROWS, a))),
        "sum_a": (struct((share, hidden + a), F32), full((share, hidden + a))),
        "sum_b": (struct((share, hidden), F32), full((share, hidden))),
    }
    scratch = {
        **back_scratch(rows, a, width),
        "gather": Gather.scratch(rows, width),
        "hand": HandOver.scratch(hops, a),
        "ring_held": Ring.buffers(n, parts),
        "ring_sems": Ring.sems(n, parts),
        "mine": [pltpu.VMEM((rows, width), BF)],
        "packed": [pltpu.VMEM((STATE_ROWS, a), F32)],
        "summed": [pltpu.VMEM((a, a), F32)],
        "grad": [pltpu.VMEM((rows, D), BF)],
        "raised_all": [pltpu.VMEM((rows, hidden), BF)],
    }
    return named_call(
        functools.partial(turn_kernel, n, hops, l, parts),
        "turn",
        5,
        (3 * count,),
        ins,
        outs,
        scratch,
        2 * rows * D * (hidden * 4 + 8 * a) * 2,
    )


class Small:
    def __init__(self, h, n, refs, sems):
        self.near, self.far, self.got, self.middle, self.across, self.bundle, self.other = refs
        self.head_send, self.head_recv, self.seq_send, self.seq_recv = sems
        self.h, self.n = h, n
        self.here = lax.axis_index("seq")

    @staticmethod
    def rounds(n):
        return max(1, (n - 1).bit_length())

    @staticmethod
    def scratch(n, width):
        r = Small.rounds(n)
        dma = pltpu.SemaphoreType.DMA
        return (
            [pltpu.VMEM((2, 16, width), F32)] * 3
            + [pltpu.VMEM((16, width), F32)] * 2
            + [pltpu.VMEM((r + 1, 32, width), F32), pltpu.VMEM((r, 32, width), F32)]
            + [dma((2,)), dma((2,)), dma((r,)), dma((r,))]
        )

    def head_copy(self, kind):
        source, target, mask = (
            (self.far, self.got, 1),
            (self.middle, self.across, 2),
        )[kind]
        return push(
            source,
            target,
            self.head_send.at[kind],
            self.head_recv.at[kind],
            {"head": lax.bitwise_xor(self.h, mask)},
        )

    def seq_copy(self, k):
        return push(
            self.bundle.at[k],
            self.other.at[k],
            self.seq_send.at[k],
            self.seq_recv.at[k],
            {"seq": lax.bitwise_xor(self.here, 1 << k)},
        )

    def put(self, sums):
        width = self.near.shape[2]
        for l, ref in enumerate(sums):
            at = slice(8 * l, 8 * l + 8)
            self.near[0, at, :] = ref[:, block_columns(self.h, 0, width)]
            self.near[1, at, :] = ref[:, block_columns(self.h, 2, width)]
            self.far[0, at, :] = ref[:, block_columns(self.h, 1, width)]
            self.far[1, at, :] = ref[:, block_columns(self.h, 3, width)]
        self.head_copy(0).start()

    def relay(self):
        self.head_copy(0).wait_recv()
        self.middle[...] = self.near[1] + self.got[1]
        self.head_copy(1).start()

    def pack(self, rows):
        self.head_copy(1).wait_recv()
        norms = self.near[0] + self.got[0] + self.across[...]
        width = self.near.shape[2]
        self.bundle[0] = jnp.zeros_like(self.bundle[0])
        for l, refs in enumerate(rows):
            self.bundle[0, 16 * l : 16 * l + 4, :] = norms[8 * l : 8 * l + 4]
            at = 16 * l + 4
            for ref in refs:
                for i in range(ref.shape[1] // width):
                    self.bundle[0, at : at + 1, :] = ref[:, i * width : (i + 1) * width]
                    at += 1
        self.seq_copy(0).start()

    def round(self, k):
        self.seq_copy(k).wait_recv()
        self.bundle[k + 1] = self.bundle[k] + self.other[k]
        if k + 1 < self.rounds(self.n):
            self.seq_copy(k + 1).start()

    def finish(self):
        for kind in range(2):
            self.head_copy(kind).wait_send()
        for k in range(self.rounds(self.n)):
            self.seq_copy(k).wait_send()


def greet_all(h, n):
    barrier = pltpu.get_barrier_semaphore()

    def signal(where):
        pl.semaphore_signal(barrier, inc=1, device_id=where, device_id_type=pl.DeviceIdType.MESH)

    signal({"head": lax.bitwise_xor(h, 1)})
    signal({"head": lax.bitwise_xor(h, 2)})
    here = lax.axis_index("seq")
    place = ring_place(here, n)
    signal({"seq": ring_index(lax.rem(place + 1, n), n)})
    signal({"seq": ring_index(lax.rem(place + n - 1, n), n)})
    rounds = Small.rounds(n)
    for k in range(rounds):
        signal({"seq": lax.bitwise_xor(here, 1 << k)})
    pl.semaphore_wait(barrier, 4 + rounds)


def leave_kernel(n, early_parts, late_parts, z):
    step = pl.program_id(0)
    h = lax.axis_index("head")
    rows = z.proj_all.shape[0]
    count = rows // CHUNK
    scatter = Scatter(h, z.scatter[:5], z.scatter[5:])
    row_sum = RowSum(h, z.row_sum[:4], z.row_sum[4:])
    small = Small(h, n, z.small[:7], z.small[7:])
    ring = Ring(n, early_parts, (z.ring_a, z.ring_b, z.ring_c), z.ring_held, z.ring_sems)
    tail = Ring(n, late_parts, (z.d_qkv,), z.tail_held, z.tail_sems)

    def taken(at):
        sixths = jnp.minimum(3, (at + 1) // 2)
        return 1 + sixths * (n - 2) // 6

    def ring_work():
        ring.ticks(taken(jnp.maximum(step - 1, 0)), taken(step))

    def sum_up(o):
        c = count - 1 - o
        z.after[...] = norm_back(
            z.before[...].astype(F32), z.inverse[...], z.unit[...], scatter.total(c), row_sum.total(c)
        )

    @pl.when(step == 0)
    def _():
        greet_all(h, n)
        ring.start()

    @pl.when(step < count)
    def _():
        def middle_work():
            @pl.when(step >= 1)
            def _():
                ring_work()

            @pl.when(step >= 2)
            def _():
                sum_up(step - 2)

        back_step(z, 0, h, step, count, scatter, row_sum, middle_work)

    @pl.when((step >= count) & (step < 2 * count))
    def _():
        o = step - count

        @pl.when(o == 0)
        def _():
            scatter.relay(0)
            row_sum.relay(0)
            small.put((z.sums, z.sums_next))

        z.d_qkv[tile_at(o), :] = dot_tn(z.ai[:, tile_at(o)], z.proj_all[...]).astype(BF)
        ring_work()

        @pl.when(o == 1)
        def _():
            small.relay()

        @pl.when(o == 2)
        def _():
            sum_up(2)
            small.pack(
                (
                    (z.d_qkv_b, z.d_up_b, z.d_feat, z.d_res),
                    (z.d_qkv_b_next, z.d_up_b_next, z.d_feat_next, z.d_res_next),
                )
            )

        @pl.when(o == 3)
        def _():
            sum_up(3)

    @pl.when(step == 2 * count)
    def _():
        tail.start()
        small.round(0)
        low = 1 + 3 * (n - 2) // 6

        def one(k, carry):
            ring.tick(k)
            tail.tick(k - low + 1)
            return carry

        lax.fori_loop(low, n - 1, one, 0)
        for k in range(1, Small.rounds(n)):
            small.round(k)
        z.bundle[...] = small.bundle[Small.rounds(n)]
        ring.finish((z.sum_a, z.sum_b, z.sum_c))
        tail.ticks(n - low, n - 1)
        tail.finish((z.sum_d,))
        small.finish()
        for i in range(count):
            scatter.finish(i)
            row_sum.finish(i)


def leave(n, local, lowered, exit_state, before, ai, rings, small, tables, params, consts):
    qf = local[0]
    rows, a = qf.shape
    hidden = lowered[0].shape[1]
    count = rows // CHUNK
    width = D // 4
    share = D // n
    early_parts = (
        (0, 0, 640, 1),
        (0, 640, 640, 1),
        (2, 0, 256, 1),
        (2, 256, 512, -1),
        (1, 0, 512, -1),
        (1, 512, 512, -1),
    )
    late_parts = ((0, 0, 384, 1), (0, 384, 384, -1))
    own_small, next_small = small

    def after_rows(w):
        return pl.BlockSpec(
            (CHUNK, w),
            lambda i: (
                count - 1 - jnp.where(i < count, clipped(i, 2, 2), 2 + clipped(i, count + 2, 2)),
                0,
            ),
        )

    back_in = back_arrays(0, local, lowered, tables, params, consts, exit_state, count)
    back_in["unit"] = (back_in["unit"][0], after_rows(width))
    back_in["inverse"] = (back_in["inverse"][0], after_rows(1))
    ins = {
        **back_in,
        "before": (before, after_rows(width)),
        "ai": (ai, fixed(ai.shape)),
        "ring_a": (rings[0], fixed(rings[0].shape)),
        "ring_b": (rings[1], fixed(rings[1].shape)),
        "ring_c": (rings[2], fixed(rings[2].shape)),
        "d_up_b": (own_small[0], fixed(own_small[0].shape)),
        "d_res": (own_small[1], fixed(own_small[1].shape)),
        "sums_next": (next_small[0], fixed(next_small[0].shape)),
        "d_qkv_b_next": (next_small[1], fixed(next_small[1].shape)),
        "d_up_b_next": (next_small[2], fixed(next_small[2].shape)),
        "d_feat_next": (next_small[3], fixed(next_small[3].shape)),
        "d_res_next": (next_small[4], fixed(next_small[4].shape)),
    }
    outs = {
        "after": (struct((rows, width), F32), after_rows(width)),
        "bundle": (struct((32, width), F32), full((32, width))),
        "sum_a": (struct((share, hidden + a), F32), full((share, hidden + a))),
        "sum_b": (struct((share, hidden), F32), full((share, hidden))),
        "sum_c": (struct((share, 3 * a), F32), full((share, 3 * a))),
        "sum_d": (struct((share, 3 * a), F32), full((share, 3 * a))),
    }
    scratch = {
        **back_scratch(rows, a, width),
        "small": Small.scratch(n, width),
        "ring_held": Ring.buffers(n, early_parts),
        "ring_sems": Ring.sems(n, early_parts),
        "tail_held": Ring.buffers(n, late_parts),
        "tail_sems": Ring.sems(n, late_parts),
        "d_qkv": [pltpu.VMEM((D, 3 * a), BF)],
        "d_feat": [pltpu.VMEM((1, a), F32)],
        "d_qkv_b": [pltpu.VMEM((1, 3 * a), F32)],
        "sums": [pltpu.VMEM((8, D), F32)],
    }
    return named_call(
        functools.partial(leave_kernel, n, early_parts, late_parts),
        "leave",
        6,
        (2 * count + 1,),
        ins,
        outs,
        scratch,
        2 * rows * D * (hidden + 8 * a) * 3,
    )


def on_device(
    acts,
    cotangent,
    lengths,
    keep_mask,
    ln_gain,
    ln_bias,
    qkv_w,
    qkv_b,
    feat_w,
    out_w,
    up_w,
    up_b,
    down_w,
    res_b,
):
    rows, width = acts.shape
    heads = feat_w.shape[1]
    a = heads * HEAD_DIM
    n = lax.axis_size("seq")
    tokens = rows * n
    longest = 2048 if tokens <= 8192 else 4096
    hops = -(-longest // rows)
    h = lax.axis_index("head").astype(jnp.int32)
    first = lax.axis_index("seq") * rows

    feats = feat_w.reshape(LAYERS, a)
    keep = keep_mask.astype(F32)[:, None]
    half = ROT // 2
    rates = np.zeros((2, HEAD_DIM))
    rates[0, :half] = ROTARY_BASE ** (-2.0 * np.arange(half) / ROT)
    rates[0, half:ROT] = rates[0, :half]
    rates[1, :half] = -1.0
    rates[1, half:ROT] = 1.0
    rates = jnp.asarray(np.tile(rates, (1, 2)), F32)

    fold = sample_points(FEATURES, HEAD_DIM) @ cosine_table(HEAD_DIM) / math.sqrt(HEAD_DIM)
    eye = np.eye(heads)
    consts = {
        "map": jnp.asarray(np.kron(eye, fold), F32),
        "map_t": jnp.asarray(np.kron(eye, fold.T), F32),
        "ones": jnp.asarray(np.kron(eye, np.ones((HEAD_DIM, HEAD_DIM))), BF),
    }

    full_acts, cos, sin, begin, *made = enter(
        n, hops, lengths, acts, keep, ln_gain, ln_bias, qkv_w, qkv_b, feats, rates, consts
    )
    tables = (cos, sin, begin, keep)
    params = (ln_gain, ln_bias, qkv_w, qkv_b, feats, up_w, up_b, out_w, down_w, res_b)
    first_made, state_in = made[:9], made[9]
    att, att_low, ratio, states, totals, act, slope, own, *made = between(
        n, hops, 0, lengths, first_made, tables, state_in, full_acts, params, consts
    )

    def back_local(made, states, totals):
        ai, fi, normed, unit, inverse, qf, kf, v, k = made
        return (qf, kf, v, k, normed, unit, inverse, states, totals)

    local = back_local(first_made, states, totals)
    lower_in = (act, slope, ratio, att, att_low, first_made[1], first_made[5])
    made, act, slope, state_in = made[:9], made[9], made[10], made[11]
    top = crest(
        n, hops, 1, lengths, made, tables, state_in, act, slope, own, cotangent, params, consts
    )
    turned = turn(
        n,
        hops,
        0,
        lengths,
        back_local(made, top["states"], top["totals"]),
        (top["d_raised"], top["d_num"], top["d_den"]),
        top["exit_state"],
        cotangent,
        made[0],
        (top["d_down_out"], top["d_up"]),
        lower_in,
        tables,
        params,
        consts,
    )
    left = leave(
        n,
        local,
        (turned["d_raised_out"], turned["d_num_out"], turned["d_den_out"]),
        turned["exit_out"],
        turned["after"],
        first_made[0],
        (turned["d_down_out"], turned["d_up"], turned["d_qkv"]),
        (
            (turned["d_up_b"], turned["d_res"]),
            (turned["sums"], turned["d_qkv_b"], top["d_up_b"], turned["d_feat"], top["d_res"]),
        ),
        tables,
        params,
        consts,
    )
    hidden = up_w.shape[2]
    down_out = (left["sum_a"], turned["sum_a"])
    bundle = left["bundle"].reshape(LAYERS, 16, width)
    kinds = 3 * a // width
    ups = hidden // width
    at = 4 + kinds + ups
    d_feat = bundle[:, at] / feats
    return (
        top["out"],
        left["after"],
        jnp.stack([left["sum_d"], left["sum_c"]]),
        jnp.stack([m[:, hidden:] for m in down_out]),
        jnp.stack([left["sum_b"], turned["sum_b"]]),
        jnp.stack([m[:, :hidden] for m in down_out]),
        bundle[:, 4 : 4 + kinds].reshape(LAYERS, 3 * a),
        bundle[:, 4 + kinds : at].reshape(LAYERS, hidden),
        d_feat.reshape(LAYERS, heads, FEATURES),
        bundle[:, 0:2],
        bundle[:, 2:4],
        bundle[:, at + 1],
    )


def solution(mesh):
    return jax.shard_map(
        on_device,
        mesh=mesh,
        in_specs=(
            P("seq", "head"),
            P("seq", "head"),
            P(),
            P("seq"),
            P(),
            P(),
            P(None, None, "head"),
            P(None, "head"),
            P(None, "head", None),
            P(None, None, "head"),
            P(None, None, "head"),
            P(None, "head"),
            P(None, None, "head"),
            P(),
        ),
        out_specs=(
            P("seq", "head"),
            P("seq", "head"),
            P(None, "seq", "head"),
            P(None, "seq", "head"),
            P(None, "seq", "head"),
            P(None, "seq", "head"),
            P(None, "head"),
            P(None, "head"),
            P(None, "head", None),
            P(None, None, "head"),
            P(None, None, "head"),
            P(None, "head"),
        ),
        check_vma=False,
    )
```

```python
import functools
import math

import jax
import jax.numpy as jnp
import numpy as np
from jax import lax
from jax.experimental import pallas as pl
from jax.experimental.pallas import tpu as pltpu
from jax.sharding import PartitionSpec as P

D = 1024
HEAD_DIM = 64
ROT = 16
FEATURES = 64
LAYERS = 2
CHUNK = 256

EPSILON = 1e-05
ROTARY_BASE = 10000.0
HIGHEST = lax.Precision.HIGHEST
BF = jnp.bfloat16
F32 = jnp.float32
STATE_ROWS = 72
VMEM_BYTES = 60 * 1024 * 1024


def prime_numbers(count):
    found = []
    candidate = 2
    while len(found) < count:
        if all((candidate % prime != 0 for prime in found)):
            found.append(candidate)
        candidate = candidate + 1
    return found


def sample_points(rows, columns):
    roots = np.sqrt(np.array(prime_numbers(2 * columns)) * 1.0)
    fractions = roots - np.floor(roots)
    grid = np.outer(np.arange(1, rows + 1) * 1.0, fractions) % 1.0
    radius = np.sqrt(-2.0 * np.log(1.0 - grid[:, :columns]))
    return radius * np.cos(2.0 * math.pi * grid[:, columns:])


def cosine_table(size):
    wave = np.arange(size)[:, None] * 1.0
    place = np.arange(size)[None, :] * 1.0
    table = np.cos(math.pi * (place + 0.5) * wave / size) * math.sqrt(2.0 / size)
    return table * np.where(wave == 0, math.sqrt(0.5), 1.0)


def dot_nn(a, b, precision=None):
    return lax.dot_general(
        a, b, (((1,), (0,)), ((), ())), precision=precision, preferred_element_type=F32
    )


def dot_nt(a, b, precision=None):
    return lax.dot_general(
        a, b, (((1,), (1,)), ((), ())), precision=precision, preferred_element_type=F32
    )


def dot_tn(a, b, precision=None):
    return lax.dot_general(
        a, b, (((0,), (0,)), ((), ())), precision=precision, preferred_element_type=F32
    )


def halves(wide):
    high = wide.astype(BF)
    return high, (wide - high.astype(F32)).astype(BF)


def lane_of(shape):
    return lax.broadcasted_iota(jnp.int32, shape, 1)


def row_of(shape):
    return lax.broadcasted_iota(jnp.int32, shape, 0)


def swap_pairs(x):
    width = x.shape[1]
    later = pltpu.roll(x, width - ROT // 2, 1)
    earlier = pltpu.roll(x, ROT // 2, 1)
    return jnp.where(lane_of(x.shape) % ROT < ROT // 2, later, earlier)


def twice(table):
    return jnp.concatenate([table, table], axis=1)


def block_columns(h, r, width):
    return pl.ds(pl.multiple_of(lax.bitwise_xor(h, r) * width, width), width)


def split_heads(projected):
    heads = projected.shape[1] // (3 * HEAD_DIM)
    return [
        jnp.concatenate(
            [
                projected[:, (3 * j + kind) * HEAD_DIM : (3 * j + kind + 1) * HEAD_DIM]
                for j in range(heads)
            ],
            axis=1,
        )
        for kind in range(3)
    ]


def join_heads(q, k, v):
    heads = q.shape[1] // HEAD_DIM
    return jnp.concatenate(
        [
            part[:, j * HEAD_DIM : (j + 1) * HEAD_DIM]
            for j in range(heads)
            for part in (q, k, v)
        ],
        axis=1,
    )


def block_diagonal(width):
    shape = (width, width)
    return (row_of(shape) // HEAD_DIM) == (lane_of(shape) // HEAD_DIM)


def pack_state(full):
    width = full.shape[0]
    kept = jnp.where(block_diagonal(width), full, 0.0)
    packed = kept[0:FEATURES]
    for head in range(1, width // FEATURES):
        packed = packed + kept[head * FEATURES : (head + 1) * FEATURES]
    return packed


def unpack_state(packed):
    width = packed.shape[1]
    tall = jnp.concatenate([packed] * (width // FEATURES), axis=0)
    return jnp.where(block_diagonal(width), tall, 0.0)


def head_sum(values, ones):
    high, low = halves(values)
    return dot_nn(high, ones) + dot_nn(low, ones)


def full(shape):
    return pl.BlockSpec(shape, lambda *i: (0,) * len(shape))


def rowed(width):
    return pl.BlockSpec((CHUNK, width), lambda i: (i, 0))


def layered(array, l):
    return pl.BlockSpec((None,) + array.shape[1:], lambda *i: (l, 0, 0))


def rows_at(c):
    return pl.ds(pl.multiple_of(c * CHUNK, CHUNK), CHUNK)


def push(source, target, send, recv, where):
    return pltpu.make_async_remote_copy(
        src_ref=source,
        dst_ref=target,
        send_sem=send,
        recv_sem=recv,
        device_id=where,
        device_id_type=pl.DeviceIdType.MESH,
    )


class Gather:
    def __init__(self, h, own, buffers, sems):
        self.own = own
        self.beside, self.across, self.corner = buffers
        self.send, self.recv = sems
        self.near = {"head": lax.bitwise_xor(h, 1)}
        self.far = {"head": lax.bitwise_xor(h, 2)}

    @staticmethod
    def scratch(rows, width):
        count = rows // CHUNK
        return [pltpu.VMEM((rows, width), BF)] * 3 + [pltpu.SemaphoreType.DMA((3, count))] * 2

    def copy(self, kind, c):
        source, target, where = (
            (self.own, self.across, self.far),
            (self.own, self.beside, self.near),
            (self.across, self.corner, self.near),
        )[kind]
        rows = rows_at(c)
        return push(
            source.at[rows, :],
            target.at[rows, :],
            self.send.at[kind, c],
            self.recv.at[kind, c],
            where,
        )

    def start(self, c):
        self.copy(0, c).start()
        self.copy(1, c).start()

    def relay(self, c):
        self.copy(0, c).wait_recv()
        self.copy(2, c).start()

    def ready(self, c):
        self.copy(1, c).wait_recv()
        self.copy(2, c).wait_recv()

    def pieces(self, c):
        rows = rows_at(c)
        return [ref[rows, :] for ref in (self.own, self.beside, self.across, self.corner)]

    def finish(self, c):
        for kind in range(3):
            self.copy(kind, c).wait_send()


class Scatter:
    def __init__(self, h, buffers, sems):
        self.near, self.far, self.got, self.middle, self.across = buffers
        self.send, self.recv = sems
        self.beside = {"head": lax.bitwise_xor(h, 1)}
        self.beyond = {"head": lax.bitwise_xor(h, 2)}

    @staticmethod
    def scratch(rows, width):
        count = rows // CHUNK
        return (
            [pltpu.VMEM((2, rows, width), BF)] * 3
            + [pltpu.VMEM((rows, width), BF)] * 2
            + [pltpu.SemaphoreType.DMA((2, count))] * 2
        )

    def copy(self, kind, c):
        rows = rows_at(c)
        if kind == 0:
            source, target, where = (
                self.far.at[:, rows, :],
                self.got.at[:, rows, :],
                self.beside,
            )
        else:
            source, target, where = self.middle.at[rows, :], self.across.at[rows, :], self.beyond
        return push(source, target, self.send.at[kind, c], self.recv.at[kind, c], where)

    def put(self, h, c, whole):
        rows = rows_at(c)
        w = self.near.shape[2]
        self.near[0, rows, :] = whole[:, block_columns(h, 0, w)]
        self.near[1, rows, :] = whole[:, block_columns(h, 2, w)]
        self.far[0, rows, :] = whole[:, block_columns(h, 1, w)]
        self.far[1, rows, :] = whole[:, block_columns(h, 3, w)]
        self.copy(0, c).start()

    def relay(self, c):
        self.copy(0, c).wait_recv()
        rows = rows_at(c)
        self.middle[rows, :] = (
            self.near[1, rows, :].astype(F32) + self.got[1, rows, :].astype(F32)
        ).astype(BF)
        self.copy(1, c).start()

    def total(self, c):
        self.copy(1, c).wait_recv()
        rows = rows_at(c)
        return (
            self.near[0, rows, :].astype(F32)
            + self.got[0, rows, :].astype(F32)
            + self.across[rows, :].astype(F32)
        )

    def finish(self, c):
        self.copy(0, c).wait_send()
        self.copy(1, c).wait_send()


def begin_scalar(lengths, slot):
    def one(j, carry):
        at, best = carry
        at = at + lengths[j - 1]
        return at, jnp.where(at <= slot, at, best)

    return lax.fori_loop(1, lengths.shape[0], one, (jnp.int32(0), jnp.int32(0)))[1]


def begin_column(lengths, slots):
    def one(j, carry):
        at, best = carry
        at = at + lengths[j - 1]
        return at, jnp.where(slots >= at, at, best)

    return lax.fori_loop(1, lengths.shape[0], one, (jnp.int32(0), jnp.zeros_like(slots)))[1]


class HandOver:
    def __init__(self, n, hops, rows, sign, packed, buffer, sems):
        self.n, self.hops, self.rows, self.sign = n, hops, rows, sign
        self.packed, self.buffer = packed, buffer
        self.send, self.recv = sems
        self.here = lax.axis_index("seq")

    @staticmethod
    def scratch(hops, width):
        return [pltpu.VMEM((hops, STATE_ROWS, width), F32)] + [
            pltpu.SemaphoreType.DMA((hops,))
        ] * 2

    def inside(self, index):
        return (index >= 0) & (index < self.n)

    def copy(self, j):
        return push(
            self.packed,
            self.buffer.at[j - 1],
            self.send.at[j - 1],
            self.recv.at[j - 1],
            {"seq": lax.rem(self.here + self.sign * j + self.n, self.n)},
        )

    def clear(self):
        self.buffer[...] = jnp.zeros_like(self.buffer)

    def start(self):
        for j in range(1, self.hops + 1):

            @pl.when(self.inside(self.here + self.sign * j))
            def _(j=j):
                self.copy(j).start()

    def total(self, lengths):
        first = self.here * self.rows
        result = None
        for j in range(1, self.hops + 1):

            @pl.when(self.inside(self.here - self.sign * j))
            def _(j=j):
                self.copy(j).wait_recv()

            @pl.when(self.inside(self.here + self.sign * j))
            def _(j=j):
                self.copy(j).wait_send()

            if self.sign > 0:
                edge, held = first - 1, first - 1 - (j - 1) * self.rows
            else:
                edge, held = first + j * self.rows - 1, first + self.rows - 1
            linked = (begin_scalar(lengths, edge) <= held).astype(F32)
            part = self.buffer[j - 1] * linked
            result = part if result is None else result + part
        return result


def greet(h, n, hops):
    barrier = pltpu.get_barrier_semaphore()

    def signal(where):
        pl.semaphore_signal(barrier, inc=1, device_id=where, device_id_type=pl.DeviceIdType.MESH)

    signal({"head": lax.bitwise_xor(h, 1)})
    signal({"head": lax.bitwise_xor(h, 2)})
    here = lax.axis_index("seq")
    expected = jnp.int32(2)
    for j in range(1, hops + 1):
        for sign in (1, -1):
            there = here + sign * j
            inside = (there >= 0) & (there < n)

            @pl.when(inside)
            def _(there=there):
                signal({"seq": lax.rem(there + n, n)})

            expected = expected + inside.astype(jnp.int32)
    pl.semaphore_wait(barrier, expected)


PROJECT_KINDS = (
    ("ai", D, BF),
    ("fi", D, BF),
    ("normed", D, BF),
    ("unit", D // 4, F32),
    ("inverse", 128, F32),
    ("qf", None, BF),
    ("kf", None, BF),
    ("v", None, BF),
    ("k", None, BF),
)


def feature_row(feat_ref, l):
    return jnp.concatenate([feat_ref[l, j : j + 1, :] for j in range(feat_ref.shape[1])], axis=1)


def project_chunk(l, h, c, last, x, params, tables, whole, out, packed, summed):
    gain, bias, w_ref, b_ref, feat_ref, map_ref, ones_ref = params
    cos, sin, keep = tables
    ai_ref, fi_ref, normed_ref, unit_ref, inv_ref, qf_ref, kf_ref, v_ref, k_ref = out
    mean = jnp.sum(x, axis=1, keepdims=True) * (1.0 / D)
    center = x - mean
    inverse = lax.rsqrt(jnp.sum(center * center, axis=1, keepdims=True) * (1.0 / D) + EPSILON)
    normed = center * inverse
    inv_ref[...] = jnp.broadcast_to(inverse, inv_ref.shape)
    normed_ref[...] = normed.astype(BF)
    whole[...] = normed
    unit_ref[...] = whole[:, block_columns(h, 0, unit_ref.shape[1])]
    attention_input = (normed * gain[l, 0:1] + bias[l, 0:1]).astype(BF)
    ai_ref[...] = attention_input
    fi_ref[...] = (normed * gain[l, 1:2] + bias[l, 1:2]).astype(BF)
    projected = dot_nn(attention_input, w_ref[...]) + b_ref[l : l + 1, :]
    q, k, v = split_heads(projected)
    v = v.astype(BF)
    q_turn = q * cos + swap_pairs(q) * sin
    k_turn = k * cos + swap_pairs(k) * sin
    query_feat = jnp.exp(dot_nn(q_turn, map_ref[...], HIGHEST))
    key_norm = head_sum(k * k, ones_ref[...]) * (0.5 / HEAD_DIM)
    key_feat = (
        keep
        * feature_row(feat_ref, l)
        * jnp.exp(dot_nn(k_turn, map_ref[...], HIGHEST) - key_norm)
    ).astype(BF)
    qf_ref[...] = query_feat.astype(BF)
    kf_ref[...] = key_feat
    v_ref[...] = v
    k_ref[...] = k.astype(BF)
    place = (row_of((CHUNK, 1)) + c * CHUNK).astype(F32)
    masked = jnp.where(place >= last, key_feat.astype(F32), 0.0)

    @pl.when(c == 0)
    def _():
        summed[...] = jnp.zeros_like(summed)
        packed[...] = jnp.zeros_like(packed)

    summed[...] += dot_tn(masked.astype(BF), v)
    packed[FEATURES : FEATURES + 1, :] += jnp.sum(masked, axis=0, keepdims=True)


def raise_chunk(l, fi, w_ref, b_ref, act_ref, slope_ref):
    raised = dot_nn(fi, w_ref[...]) + b_ref[l : l + 1, :]
    cumulative = 0.5 + 0.5 * lax.erf(raised * math.sqrt(0.5))
    density = jnp.exp(raised * raised * -0.5) * (1.0 / math.sqrt(2.0 * math.pi))
    act_ref[...] = (raised * cumulative).astype(BF)
    slope_ref[...] = (cumulative + raised * density).astype(BF)


def remote_call(kernel, name, ident, grid, in_specs, out_specs, out_shape, scratch, flops, args):
    moved = sum(int(np.prod(a.shape)) * a.dtype.itemsize for a in list(args) + list(out_shape))
    return pl.pallas_call(
        kernel,
        name=name,
        grid=grid,
        in_specs=in_specs,
        out_specs=out_specs,
        scratch_shapes=scratch,
        out_shape=out_shape,
        compiler_params=pltpu.CompilerParams(
            collective_id=ident, has_side_effects=True, vmem_limit_bytes=VMEM_BYTES
        ),
        cost_estimate=pl.CostEstimate(flops=int(flops), bytes_accessed=moved, transcendentals=0),
    )(*args)


class Names:
    pass


def named_call(kernel, name, ident, grid, ins, outs, scratch, flops, late=None, sent=None):
    late, sent = late or {}, sent or {}
    shared = {k: v[1] for k, v in sent.items() if isinstance(v, tuple)}
    sent = {k: v[0] if isinstance(v, tuple) else v for k, v in sent.items()}
    labels, groups = list(ins) + list(late) + list(outs) + list(sent), list(scratch)
    layers = {k: v if isinstance(v, tuple) else (v, None) for k, v in late.items()}
    anywhere = pl.BlockSpec(memory_space=pl.ANY)

    def body(*refs):
        names = Names()
        names.late, names.sent = Names(), Names()
        far = {}
        for label, ref in zip(labels, refs):
            if label in late or label in sent:
                far[label] = ref
            else:
                setattr(names, label, ref)
        at = len(labels)
        for label in list(late) + list(sent):
            if label in shared:
                held, sem = getattr(names, shared[label]), refs[at]
                at -= 1
            else:
                held, sem = refs[at], refs[at + 1]
            setattr(names, label, held)
            if label in late:
                layer = layers[label][1]
                source = far[label] if layer is None else far[label].at[layer]
                setattr(names.late, label, pltpu.make_async_copy(source, held, sem))
            else:
                setattr(names.sent, label, pltpu.make_async_copy(held, far[label], sem))
            at += 2
        for label in groups:
            size = len(scratch[label])
            held = refs[at : at + size]
            setattr(names, label, held if size > 1 else held[0])
            at += size
        kernel(names)

    moved = []
    for array, layer in layers.values():
        shape = array.shape if layer is None else array.shape[1:]
        moved += [pltpu.VMEM(shape, array.dtype), pltpu.SemaphoreType.DMA]
    for label, shape in sent.items():
        if label not in shared:
            moved.append(pltpu.VMEM(shape.shape, shape.dtype))
        moved.append(pltpu.SemaphoreType.DMA)
    result = remote_call(
        body,
        name,
        ident,
        grid,
        [spec for array, spec in ins.values()] + [anywhere] * len(late),
        [spec for shape, spec in outs.values()] + [anywhere] * len(sent),
        [shape for shape, spec in outs.values()] + list(sent.values()),
        moved + [item for label in groups for item in scratch[label]],
        flops,
        [array for array, spec in ins.values()] + [array for array, layer in layers.values()],
    )
    return dict(zip(list(outs) + list(sent), result))


def every(names):
    return [getattr(names, label) for label in vars(names)]


def fixed(shape):
    return pl.BlockSpec(shape, lambda *i: (0,) * len(shape), pipeline_mode=pl.Buffered(1))


def layer_of(array, l):
    return pl.BlockSpec(
        (None,) + array.shape[1:], lambda *i: (l, 0, 0), pipeline_mode=pl.Buffered(1)
    )


def clipped(step, low, count):
    return jnp.minimum(jnp.maximum(step - low, 0), count - 1)


def up_rows(width, low, count):
    return pl.BlockSpec((CHUNK, width), lambda i: (clipped(i, low, count), 0))


def down_rows(width, low, count):
    return pl.BlockSpec((CHUNK, width), lambda i: (count - 1 - clipped(i, low, count), 0))


def down_cube(shape, low, count):
    return pl.BlockSpec(
        (1,) + shape, lambda i: (count - 1 - clipped(i, low, count),) + (0,) * len(shape)
    )


def struct(shape, kind):
    return jax.ShapeDtypeStruct(shape, kind)


def project_params(z):
    return (z.gain, z.bias, z.qkv_w, z.qkv_b, z.feats, z.map_t, z.ones)


def project_refs(z):
    return (z.ai, z.fi, z.normed, z.unit, z.inverse, z.qf, z.kf, z.v, z.k)


def project_made(rows, a, spec):
    return dict(
        (name, (struct((rows, width or a), kind), spec(width or a)))
        for name, width, kind in PROJECT_KINDS
    )


class Column:
    def __init__(self, ref, lane):
        self.ref, self.lane = ref, lane

    def __getitem__(self, key):
        rows = slice(None) if key is Ellipsis else key[0]
        return self.ref[rows, self.lane : self.lane + 1]


def begin_keep(ref):
    return Column(ref, 0), Column(ref, 64)


def lanes_to_column(row):
    shape = (row.shape[1], row.shape[1])
    eye = row_of(shape) == lane_of(shape)
    return jnp.sum(jnp.where(eye, row, 0.0), axis=1, keepdims=True)


def enter_kernel(n, z):
    c = pl.program_id(0)
    count = pl.num_programs(0)
    h = lax.axis_index("head")
    rows, width = z.acts.shape
    first = lax.axis_index("seq") * rows
    gather = Gather(h, z.acts, z.gather[:3], z.gather[3:])

    @pl.when(c == 0)
    def _():
        for copy in every(z.late):
            copy.start()
        greet(h, n, 0)
        for i in range(rows // CHUNK):
            gather.start(i)
        for i in range(rows // CHUNK):
            part = slice(i * CHUNK, (i + 1) * CHUNK)
            slots = row_of((CHUNK, 1)) + i * CHUNK + first
            begins = begin_column(z.lengths, slots)
            starts = (begins - first).astype(F32)
            keep = jnp.concatenate(
                [
                    lanes_to_column(z.keep_mask[j : j + 1, :].astype(F32))
                    for j in range(i * CHUNK // 128, (i + 1) * CHUNK // 128)
                ],
                axis=0,
            )
            z.columns[part, :] = jnp.where(lane_of((CHUNK, 128)) < 64, starts, keep)
            phase = (slots - begins).astype(F32) * z.rates[0:1, :]
            z.cos[part, :] = jnp.cos(phase)
            z.sin[part, :] = jnp.sin(phase) * z.rates[1:2, :]
        gather.relay(0)
        for copy in every(z.late):
            copy.wait()

    gather.ready(c)
    for r, part in enumerate(gather.pieces(c)):
        z.full[:, block_columns(h, r, width)] = part
    last = (begin_scalar(z.lengths, first + rows - 1) - first).astype(F32)
    here = rows_at(c)
    keep = begin_keep(z.columns)[1]
    tables = (twice(z.cos[here, :]), twice(z.sin[here, :]), keep[here, :])
    project_chunk(
        0,
        h,
        c,
        last,
        z.full[...].astype(F32),
        project_params(z),
        tables,
        z.whole,
        project_refs(z),
        z.packed,
        z.summed,
    )

    @pl.when(c + 1 < count)
    def _():
        gather.relay(c + 1)

    @pl.when(c + 1 == count)
    def _():
        z.packed[0:FEATURES, :] = pack_state(z.summed[...])
        for i in range(rows // CHUNK):
            gather.finish(i)


def enter(n, lengths, acts, keep_mask, gain, bias, qkv_w, qkv_b, feats, rates, consts):
    rows, width = acts.shape
    a = consts["ones"].shape[0]
    table = rates.shape[1]
    ins = dict(
        lengths=(lengths, pl.BlockSpec(memory_space=pltpu.SMEM)),
        acts=(acts, fixed(acts.shape)),
        keep_mask=(keep_mask, fixed(keep_mask.shape)),
        gain=(gain, fixed(gain.shape)),
        bias=(bias, fixed(bias.shape)),
        qkv_b=(qkv_b, fixed(qkv_b.shape)),
        feats=(feats, fixed(feats.shape)),
        rates=(rates, fixed(rates.shape)),
    )
    late = dict(qkv_w=(qkv_w, 0), map_t=consts["map_t"], ones=consts["ones"])
    outs = dict(
        full=(struct((rows, D), BF), rowed(D)),
        cos=(struct((rows, table), F32), full((rows, table))),
        sin=(struct((rows, table), F32), full((rows, table))),
        columns=(struct((rows, 128), F32), full((rows, 128))),
        **project_made(rows, a, rowed),
        packed=(struct((STATE_ROWS, a), F32), full((STATE_ROWS, a))),
    )
    scratch = dict(
        gather=Gather.scratch(rows, width),
        summed=[pltpu.VMEM((a, a), F32)],
        whole=[pltpu.VMEM((CHUNK, D), F32)],
    )
    return named_call(
        functools.partial(enter_kernel, n),
        "enter",
        2,
        (rows // CHUNK,),
        ins,
        outs,
        scratch,
        2 * rows * D * 3 * a * 2,
        late,
    )


def between_kernel(n, hops, l, z):
    step = pl.program_id(0)
    count = pl.num_programs(0) // 2
    h = lax.axis_index("head")
    rows, width = z.mine.shape
    first = lax.axis_index("seq") * rows
    chunks = rows // CHUNK
    gather = Gather(h, z.mine, z.gather[:3], z.gather[3:])
    begin, keep = begin_keep(z.columns)
    scatter = Scatter(h, z.scatter[:5], z.scatter[5:])
    hand = HandOver(n, hops, rows, 1, z.state_own, z.hand[0], z.hand[1:])

    def send_sum(c):
        z.mine[rows_at(c), :] = scatter.total(c).astype(BF)
        gather.start(c)

    @pl.when(step == 0)
    def _():
        for copy in every(z.late):
            copy.start()
        hand.clear()
        greet(h, n, hops)
        hand.start()
        z.late.up_w.wait()

    @pl.when(step < count)
    def _():
        raise_chunk(l, z.fi_in[...], z.up_w, z.up_b, z.act, z.slope)

        @pl.when(step == 0)
        def _():
            z.state_in[...] = hand.total(z.lengths)

        @pl.when(step >= 3)
        def _():
            gather.relay(step - 3)

        attention_chunk(
            step,
            (z.qf_in, z.kf_in, z.v_in, begin, keep, z.state_in, z.ones),
            (z.att, z.att_low, z.ratio, z.states, z.totals),
            z.state,
            z.total,
        )

        @pl.when(step == 0)
        def _():
            z.late.out_w.wait()
            z.late.down_w.wait()

        @pl.when(step >= 1)
        def _():
            scatter.relay(step - 1)

        z.whole_low[...] = (
            dot_nt(z.att_low[...], z.out_w[...]) + dot_nt(z.act[...], z.down_w[...])
        ).astype(BF)
        scatter.put(h, step, z.whole_low)

        @pl.when(step >= 2)
        def _():
            send_sum(step - 2)

    @pl.when(step >= count)
    def _():
        c = step - count

        @pl.when(c == 0)
        def _():
            scatter.relay(chunks - 1)
            z.late.qkv_w.wait()
            z.late.up_w_next.wait()
            gather.relay(1)

        gather.ready(c)
        for r, part in enumerate(gather.pieces(c)):
            z.whole[:, block_columns(h, r, width)] = part.astype(F32)
        x = z.full[...].astype(F32) + z.whole[...] + z.res_b[l : l + 1, :]
        z.whole[...] = x
        z.own[...] = z.whole[:, block_columns(h, 0, width)]
        last = (begin_scalar(z.lengths, first + rows - 1) - first).astype(F32)
        tables = (twice(z.cos[...]), twice(z.sin[...]), begin_keep(z.columns_next)[1][...])
        project_chunk(
            l + 1,
            h,
            c,
            last,
            x,
            project_params(z),
            tables,
            z.whole,
            project_refs(z),
            z.packed,
            z.summed,
        )

        @pl.when(c == 0)
        def _():
            send_sum(chunks - 2)

        @pl.when(c + 1 == chunks)
        def _():
            z.packed[0:FEATURES, :] = pack_state(z.summed[...])

        raise_chunk(l + 1, z.fi[...], z.up_w_next, z.up_b, z.act_next, z.slope_next)

        @pl.when(c == 0)
        def _():
            send_sum(chunks - 1)

        @pl.when((c >= 1) & (c + 1 < chunks))
        def _():
            gather.relay(c + 1)

        @pl.when(c + 1 == chunks)
        def _():
            for i in range(chunks):
                gather.finish(i)
                scatter.finish(i)


def between(n, hops, l, lengths, entered, params, consts):
    gain, bias, qkv_w, qkv_b, feats, up_w, up_b, out_w, down_w, res_b = params
    rows, a = entered["qf"].shape
    hidden = up_w.shape[2]
    chunks = rows // CHUNK
    width = D // 4

    def early(w):
        return up_rows(w, 0, chunks)

    def after(w):
        return up_rows(w, chunks, chunks)

    def cube(shape):
        return pl.BlockSpec((1,) + shape, lambda i: (clipped(i, 0, chunks),) + (0,) * len(shape))

    table = entered["cos"].shape[1]
    ins = dict(
        lengths=(lengths, pl.BlockSpec(memory_space=pltpu.SMEM)),
        qf_in=(entered["qf"], early(a)),
        kf_in=(entered["kf"], early(a)),
        v_in=(entered["v"], early(a)),
        fi_in=(entered["fi"], early(D)),
        columns=(entered["columns"], early(128)),
        state_own=(entered["packed"], fixed((STATE_ROWS, a))),
        up_b=(up_b, fixed(up_b.shape)),
        ones=(consts["ones"], fixed((a, a))),
        full=(entered["full"], after(D)),
        res_b=(res_b, fixed(res_b.shape)),
        gain=(gain, fixed(gain.shape)),
        bias=(bias, fixed(bias.shape)),
        qkv_b=(qkv_b, fixed(qkv_b.shape)),
        feats=(feats, fixed(feats.shape)),
        map_t=(consts["map_t"], fixed((a, a))),
        cos=(entered["cos"], after(table)),
        sin=(entered["sin"], after(table)),
        columns_next=(entered["columns"], after(128)),
    )
    late = dict(
        up_w=(up_w, l),
        out_w=(out_w, l),
        down_w=(down_w, l),
        qkv_w=(qkv_w, l + 1),
        up_w_next=(up_w, l + 1),
    )
    outs = dict(
        att=(struct((rows, a), F32), early(a)),
        att_low=(struct((rows, a), BF), early(a)),
        ratio=(struct((rows, a), F32), early(a)),
        states=(struct((chunks, a, a), F32), cube((a, a))),
        totals=(struct((chunks, 8, a), F32), cube((8, a))),
        act=(struct((rows, hidden), BF), early(hidden)),
        slope=(struct((rows, hidden), BF), early(hidden)),
        own=(struct((rows, width), F32), after(width)),
        **project_made(rows, a, after),
        act_next=(struct((rows, hidden), BF), after(hidden)),
        slope_next=(struct((rows, hidden), BF), after(hidden)),
        packed=(struct((STATE_ROWS, a), F32), full((STATE_ROWS, a))),
    )
    scratch = dict(
        gather=Gather.scratch(rows, width),
        scatter=Scatter.scratch(rows, width),
        hand=HandOver.scratch(hops, a),
        mine=[pltpu.VMEM((rows, width), BF)],
        state_in=[pltpu.VMEM((STATE_ROWS, a), F32)],
        summed=[pltpu.VMEM((a, a), F32)],
        whole=[pltpu.VMEM((CHUNK, D), F32)],
        whole_low=[pltpu.VMEM((CHUNK, D), BF)],
        state=[pltpu.VMEM((a, a), F32)],
        total=[pltpu.VMEM((8, a), F32)],
    )
    return named_call(
        functools.partial(between_kernel, n, hops, l),
        "between",
        3,
        (2 * chunks,),
        ins,
        outs,
        scratch,
        2 * rows * D * (hidden * 3 + 4 * a) * 2,
        late,
    )


def pair_mask(begin, step):
    shape = (CHUNK, CHUNK)
    t = row_of(shape)
    s = lane_of(shape)
    return (s <= t) & ((s + step * CHUNK).astype(F32) >= begin)


def attention_chunk(step, refs, out, state, total):
    qf_ref, kf_ref, v_ref, begin_ref, keep_ref, in_ref, ones_ref = refs
    att_ref, low_ref, ratio_ref, states_ref, totals_ref = out

    @pl.when(step == 0)
    def _():
        state[...] = unpack_state(in_ref[0:FEATURES, :])
        total[...] = jnp.broadcast_to(in_ref[FEATURES : FEATURES + 1, :], total.shape)

    q = qf_ref[...]
    k = kf_ref[...]
    v = v_ref[...]
    begin = begin_ref[...]
    keep = keep_ref[...]
    ones = ones_ref[...]
    a = q.shape[1]
    mask = pair_mask(begin, step)
    head_of = lane_of((1, a)) // HEAD_DIM
    held = state[...]
    held_total = total[0:1, :]
    states_ref[0] = held
    totals_ref[0] = total[...]
    base = (step * CHUNK).astype(F32)
    use = jnp.where(begin < base, 1.0, 0.0)
    high, low = halves(held)
    num = use * (dot_nn(q, high) + dot_nn(q, low))
    den = use * head_sum(q.astype(F32) * held_total, ones)
    for head in range(a // HEAD_DIM):
        own = (head_of == head).astype(BF)
        scores = dot_nt(q * own, k)
        scores_low = jnp.where(mask, scores, 0.0).astype(BF)
        num = num + dot_nn(scores_low, v * own)
        den = den + dot_nn(scores_low, jnp.broadcast_to(own, (CHUNK, a)))
    ratio = keep / (den + 1.0 - keep)
    att = num * ratio
    ratio_ref[...] = ratio
    att_ref[...] = att
    low_ref[...] = att.astype(BF)
    end = begin[CHUNK - 1 : CHUNK, :]
    place = (row_of((CHUNK, 1)) + step * CHUNK).astype(F32)
    masked = jnp.where(place >= end, k.astype(F32), 0.0)
    passing = jnp.where(end < base, 1.0, 0.0)
    state[...] = passing * held + jnp.where(
        block_diagonal(a), dot_tn(masked.astype(BF), v), 0.0
    )
    total[...] = jnp.broadcast_to(
        passing * held_total + jnp.sum(masked, axis=0, keepdims=True), total.shape
    )


def lower_feed(grad, dw_ref, slope_ref, bias_ref, start):
    @pl.when(start)
    def _():
        bias_ref[...] = jnp.zeros_like(bias_ref)

    d_raised = (dot_nn(grad, dw_ref[...]) * slope_ref[...].astype(F32)).astype(BF)
    bias_ref[...] += jnp.sum(d_raised.astype(F32), axis=0, keepdims=True)
    return d_raised


def lower_attention(grad, ow_ref, ratio, att, qf, begin, ones, out, summed, packed, start):
    num_ref, den_ref = out

    @pl.when(start)
    def _():
        summed[...] = jnp.zeros_like(summed)
        packed[...] = jnp.zeros_like(packed)

    d_num = (dot_nn(grad, ow_ref[...]) * ratio).astype(BF)
    d_den = -head_sum(d_num.astype(F32) * att, ones)
    num_ref[...] = d_num
    den_ref[...] = d_den
    entering = jnp.where(begin < 0.0, qf.astype(F32), 0.0)
    summed[...] += dot_tn(entering.astype(BF), d_num)
    packed[FEATURES : FEATURES + 1, :] += jnp.sum(entering * d_den, axis=0, keepdims=True)


def tile_at(i):
    return pl.ds(pl.multiple_of(i * CHUNK, CHUNK), CHUNK)


def weight_tile(i, x_ref, y, out_ref):
    out_ref[tile_at(i), :] = dot_tn(x_ref[:, tile_at(i)], y).astype(BF)


def attention_back(turn, step, refs, state, total):
    (
        qf_ref,
        kf_ref,
        v_ref,
        num_ref,
        den_ref,
        begin_ref,
        states_ref,
        totals_ref,
        exit_ref,
    ) = refs

    @pl.when(turn == 0)
    def _():
        state[...] = unpack_state(exit_ref[0:FEATURES, :])
        total[...] = jnp.broadcast_to(exit_ref[FEATURES : FEATURES + 1, :], total.shape)

    q = qf_ref[...]
    k = kf_ref[...]
    v = v_ref[...]
    d_num = num_ref[...]
    d_den = den_ref[...]
    begin = begin_ref[...]
    a = q.shape[1]
    mask = pair_mask(begin, step)
    head_of = lane_of((1, a)) // HEAD_DIM
    base = (step * CHUNK).astype(F32)
    use = jnp.where(begin < base, 1.0, 0.0)
    end = begin[CHUNK - 1 : CHUNK, :]
    place = (row_of((CHUNK, 1)) + step * CHUNK).astype(F32)
    inside = jnp.where(place >= end, 1.0, 0.0)
    passing = jnp.where(end < base, 1.0, 0.0)
    held_high, held_low = halves(states_ref[0])
    held_total = totals_ref[0][0:1, :]
    after = state[...]
    after_total = total[0:1, :]
    after_high, after_low = halves(after)
    masked = (k.astype(F32) * inside).astype(BF)
    d_q = use * (dot_nt(d_num, held_high) + dot_nt(d_num, held_low) + d_den * held_total)
    d_k = inside * (dot_nt(v, after_high) + dot_nt(v, after_low) + after_total)
    d_v = dot_nn(masked, after_high) + dot_nn(masked, after_low)
    for head in range(a // HEAD_DIM):
        own = (head_of == head).astype(BF)
        q_own = q * own
        num_own = d_num * own
        scores_low = jnp.where(mask, dot_nt(q_own, k), 0.0).astype(BF)
        column = d_den[:, head * HEAD_DIM : head * HEAD_DIM + 1]
        d_scores = jnp.where(mask, dot_nt(num_own, v) + column, 0.0).astype(BF)
        d_q = d_q + dot_nn(d_scores, k * own)
        d_k = d_k + dot_tn(d_scores, q_own)
        d_v = d_v + dot_tn(scores_low, num_own)
    q_used = q.astype(F32) * use
    state[...] = passing * after + jnp.where(
        block_diagonal(a), dot_tn(q_used.astype(BF), d_num), 0.0
    )
    total[...] = jnp.broadcast_to(
        passing * after_total + jnp.sum(q_used * d_den, axis=0, keepdims=True), total.shape
    )
    return d_q, d_k, d_v


def features_back(grads, refs, feat_ref, bias_ref, start):
    d_q, d_k, d_v = grads
    qf_ref, kf_ref, k_ref, cos_ref, sin_ref, map_ref, ones_ref = refs

    @pl.when(start)
    def _():
        feat_ref[...] = jnp.zeros_like(feat_ref)
        bias_ref[...] = jnp.zeros_like(bias_ref)

    cos = twice(cos_ref[...])
    sin = twice(sin_ref[...])
    d_query = dot_nn(d_q * qf_ref[...].astype(F32), map_ref[...], HIGHEST)
    d_query = d_query * cos - swap_pairs(d_query) * sin
    d_key_log = d_k * kf_ref[...].astype(F32)
    feat_ref[...] += jnp.sum(d_key_log, axis=0, keepdims=True)
    d_key = dot_nn(d_key_log, map_ref[...], HIGHEST)
    d_key = d_key * cos - swap_pairs(d_key) * sin
    d_key = d_key - head_sum(d_key_log, ones_ref[...]) * k_ref[...].astype(F32) * (1.0 / HEAD_DIM)
    d_proj = join_heads(d_query, d_key, d_v).astype(BF)
    bias_ref[...] += jnp.sum(d_proj.astype(F32), axis=0, keepdims=True)
    return d_proj


def inputs_back(l, d_proj, raised_ref, w_ref, up_ref, normed_ref, gain, sums_ref, start):
    @pl.when(start)
    def _():
        sums_ref[...] = jnp.zeros_like(sums_ref)

    normed = normed_ref[...].astype(F32)
    d_attention = dot_nt(d_proj, w_ref[...])
    d_feed = dot_nt(raised_ref[...], up_ref[...])
    sums_ref[0:1, :] += jnp.sum(d_attention * normed, axis=0, keepdims=True)
    sums_ref[1:2, :] += jnp.sum(d_feed * normed, axis=0, keepdims=True)
    sums_ref[2:3, :] += jnp.sum(d_attention, axis=0, keepdims=True)
    sums_ref[3:4, :] += jnp.sum(d_feed, axis=0, keepdims=True)
    d_normed = (d_attention * gain[l, 0:1] + d_feed * gain[l, 1:2]).astype(BF)
    high, low = halves(d_normed.astype(F32) * normed)
    row = jnp.ones((8, D), BF)
    first = dot_nt(row, d_normed)
    second = dot_nt(row, high) + dot_nt(row, low)
    return d_normed, jnp.where(row_of(first.shape) == 0, first, second)


class RowSum:
    def __init__(self, h, buffers, sems):
        self.own, self.got, self.middle, self.across = buffers
        self.send, self.recv = sems
        self.beside = {"head": lax.bitwise_xor(h, 1)}
        self.beyond = {"head": lax.bitwise_xor(h, 2)}

    @staticmethod
    def scratch(rows):
        count = rows // CHUNK
        return [pltpu.VMEM((count, 8, CHUNK), F32)] * 4 + [pltpu.SemaphoreType.DMA((2, count))] * 2

    def copy(self, kind, c):
        source, target, where = (
            (self.own, self.got, self.beside),
            (self.middle, self.across, self.beyond),
        )[kind]
        return push(
            source.at[c], target.at[c], self.send.at[kind, c], self.recv.at[kind, c], where
        )

    def put(self, c, value):
        self.own[c] = value
        self.copy(0, c).start()

    def relay(self, c):
        self.copy(0, c).wait_recv()
        self.middle[c] = self.own[c] + self.got[c]
        self.copy(1, c).start()

    def total(self, c):
        self.copy(1, c).wait_recv()
        value = self.middle[c] + self.across[c]
        shape = (8, 128)
        eye = (row_of(shape) == lane_of(shape)).astype(F32)
        columns = dot_tn(value, eye, HIGHEST)
        return columns[:, 0:1], columns[:, 1:2]

    def finish(self, c):
        self.copy(0, c).wait_send()
        self.copy(1, c).wait_send()


def norm_back(before, inverse, unit, d_normed, sums):
    first, second = sums
    return before + inverse * (d_normed - first * (1.0 / D) - unit * (second * (1.0 / D)))


def ring_place(index, n):
    return jnp.where(index % 2 == 0, index // 2, n - 1 - index // 2)


def ring_index(place, n):
    return jnp.where(place < n // 2, 2 * place, 2 * (n - 1 - place) + 1)


BATCHES = 6


class Ring:
    def __init__(self, n, parts, source, held, sems, since=0, until=BATCHES, incoming=None):
        self.n, self.parts, self.source, self.held = n, parts, source, held
        self.send_sem, self.recv_sem = sems
        self.since, self.until, self.incoming = since, until, incoming
        self.share = D // n
        self.place = ring_place(lax.axis_index("seq"), n)
        self.right = ring_index(lax.rem(self.place + 1, n), n)
        self.left = ring_index(lax.rem(self.place + n - 1, n), n)
        self.base = self.slots(n, since, until)[0]
        self.first = 0 if incoming is None else self.bound(n, since)
        self.last = self.bound(n, until) - 1

    @staticmethod
    def bound(n, batch):
        return 1 + (n - 2) * batch // BATCHES

    @staticmethod
    def slots(n, since, until):
        base = Ring.bound(n, since) - 1
        return base, Ring.bound(n, until) - base

    @staticmethod
    def buffers(n, parts, since=0, until=BATCHES):
        count = Ring.slots(n, since, until)[1]
        return [pltpu.VMEM((count, D // n, part[2]), BF) for part in parts]

    @staticmethod
    def sems(n, parts):
        return [pltpu.SemaphoreType.DMA((len(parts), n - 1))] * 2

    def own(self, part, step):
        array, start, width, way = part
        n = self.n
        ahead = lax.rem(self.place - way * (1 + step) + 2 * n, n)
        rows = pl.ds(pl.multiple_of(ring_index(ahead, n) * self.share, self.share), self.share)
        return self.source[array].at[rows, pl.ds(start, width)]

    def slot(self, r, step):
        return self.held[r].at[step - self.base]

    def copy(self, r, step, block):
        return push(
            block,
            self.slot(r, step),
            self.send_sem.at[r, step],
            self.recv_sem.at[r, step],
            {"seq": self.right if self.parts[r][3] > 0 else self.left},
        )

    def add(self, r, step, arrived):
        own = self.own(self.parts[r], step)[...].astype(F32)
        block = self.slot(r, step - 1)
        block[...] = (arrived[...].astype(F32) + own).astype(BF)
        self.copy(r, step, block).start()

    def start(self):
        for r, part in enumerate(self.parts):
            if self.incoming is not None:
                self.add(r, self.first, self.incoming[r])
            else:
                self.copy(r, 0, self.own(part, 0)).start()

    def tick(self, step):
        for r in range(len(self.parts)):
            block = self.slot(r, step - 1)
            self.copy(r, step - 1, block).wait_recv()
            self.add(r, step, block)

    def batch(self, k):
        low, high = self.bound(self.n, k - 1), self.bound(self.n, k)
        if self.incoming is not None and k - 1 == self.since:
            low += 1
        if high - low == 1:
            self.tick(low)
        elif high > low:

            def one(step, carry):
                self.tick(step)
                return carry

            lax.fori_loop(low, high, one, 0)

    def sent(self):
        def one(step, carry):
            for r in range(len(self.parts)):
                self.copy(r, step, self.slot(r, step)).wait_send()
            return carry

        lax.fori_loop(self.first, self.last + 1, one, 0)

    def pause(self, out):
        for r in range(len(self.parts)):
            block = self.slot(r, self.last)
            self.copy(r, self.last, block).wait_recv()
            out[r][...] = block[...]
        self.sent()

    def finish(self, out):
        n = self.n
        for r, part in enumerate(self.parts):
            block = self.slot(r, n - 2)
            self.copy(r, n - 2, block).wait_recv()
            array, start, width, way = part
            out[array][:, pl.ds(start, width)] = block[...].astype(F32) + self.own(part, n - 1)[
                ...
            ].astype(F32)
        self.sent()


def halved(array, width, start=0):
    return (
        (array, start, width // 2, 1),
        (array, start + width // 2, width // 2, -1),
    )


def ring_out(n, parts):
    return [jax.ShapeDtypeStruct((D // n, part[2]), BF) for part in parts]


CREST_DOWN, CREST_UP, TURN_REST, TURN_DOWN, TURN_UP = 2, 2, 3, 1, 0


def loop(count, body):
    def one(c, carry):
        body(c)
        return carry

    lax.fori_loop(0, count, one, 0)


def unrolled(count, body):
    for c in range(count):
        body(jnp.int32(c))


def crest_kernel(n, hops, l, z):
    step = pl.program_id(0)
    h = lax.axis_index("head")
    rows, hidden = z.act.shape
    width = D // 4
    count = rows // CHUNK
    hand = HandOver(n, hops, rows, 1, z.state_own, z.hand[0], z.hand[1:])
    hand_back = HandOver(n, hops, rows, -1, z.packed, z.hand_back[0], z.hand_back[1:])
    begin, keep = begin_keep(z.columns)
    parts = halved(0, hidden)
    corner = push(
        z.grad_across,
        z.grad_corner,
        z.corner_sems.at[0],
        z.corner_sems.at[1],
        {"head": lax.bitwise_xor(h, 1)},
    )
    down = Ring(n, parts, (z.d_down,), z.down_held, z.down_sems, 0, CREST_DOWN)
    up = Ring(n, parts, (z.d_up,), z.up_held, z.up_sems, 0, CREST_UP)
    columns = pl.ds(pl.multiple_of(h * width, width), width)

    @pl.when(step == 0)
    def _():
        for copy in every(z.late):
            copy.start()
        hand.clear()
        hand_back.clear()
        greet(h, n, hops)
        hand.start()
        z.late.grad_across.wait()
        corner.start()
        z.d_res[...] = jnp.zeros_like(z.d_res)
        z.late.grad_own.wait()
        z.late.grad_beside.wait()
        for r, part in enumerate((z.grad_own, z.grad_beside, z.grad_across)):
            z.grad[:, block_columns(h, r, width)] = part[...]
        corner.wait_recv()
        z.grad[:, block_columns(h, 3, width)] = z.grad_corner[...]
        corner.wait_send()
        z.late.down_w.wait()
        z.late.slope.wait()

        def feed(c):
            here = rows_at(c)
            z.d_raised[here, :] = lower_feed(
                z.grad[here, :], z.down_w, z.slope.at[here, :], z.d_up_b, c == 0
            )
            z.d_res[...] += jnp.sum(z.grad[here, columns].astype(F32), axis=0, keepdims=True)

        unrolled(count, feed)
        z.sent.d_raised.start()
        z.late.act.wait()
        unrolled(D // CHUNK, lambda i: weight_tile(i, z.grad, z.act[...], z.d_down))
        down.start()
        z.sent.d_down.start()
        z.late.fi.wait()
        unrolled(D // CHUNK, lambda i: weight_tile(i, z.fi, z.d_raised[...], z.d_up))
        up.start()
        z.sent.d_up.start()
        z.late.out_w.wait()
        z.state_in[...] = hand.total(z.lengths)

    @pl.when((step >= 1) & (step <= count))
    def _():
        c = step - 1
        here = rows_at(c)
        attention_chunk(
            c,
            (z.qf, z.kf, z.v, begin, keep, z.state_in, z.ones),
            (z.att, z.low_now, z.ratio, z.states, z.totals),
            z.state,
            z.total,
        )
        low = z.low_now[...]
        z.low[here, :] = low
        z.whole[...] = (dot_nt(low, z.out_w[...]) + dot_nt(z.act[here, :], z.down_w[...])).astype(
            BF
        )
        z.near[0] = z.whole[:, block_columns(h, 0, width)]
        z.near[1] = z.whole[:, block_columns(h, 2, width)]
        z.far[0] = z.whole[:, block_columns(h, 1, width)]
        z.far[1] = z.whole[:, block_columns(h, 3, width)]
        lower_attention(
            z.grad[here, :],
            z.out_w,
            z.ratio[...],
            z.att[...],
            z.qf[...],
            begin[...],
            z.ones[...],
            (z.d_num, z.d_den),
            z.summed,
            z.packed,
            c == 0,
        )
        at_steps(
            c,
            (
                (0, lambda: down.batch(1)),
                (1, lambda: up.batch(1)),
                (2, lambda: down.batch(2)),
                (3, lambda: up.batch(2)),
            ),
        )

    @pl.when(step == count + 1)
    def _():
        z.packed[0:FEATURES, :] = pack_state(z.summed[...])
        hand_back.start()
        unrolled(D // CHUNK, lambda i: weight_tile(i, z.grad, z.low[...], z.d_out))
        z.exit_state[...] = hand_back.total(z.lengths)
        down.pause((z.down_fore, z.down_aft))
        up.pause((z.up_fore, z.up_aft))
        for copy in every(z.sent):
            copy.wait()


def crest(n, hops, l, lengths, mid, pieces, tables, params, consts):
    gain, bias, qkv_w, qkv_b, feats, up_w, up_b, out_w, down_w, res_b = params
    cos, sin, columns = tables
    rows, a = mid["qf"].shape
    hidden = up_w.shape[2]
    count = rows // CHUNK
    width = D // 4
    parts = halved(0, hidden)

    def block(w):
        return up_rows(w, 1, count)

    def cube(shape):
        return pl.BlockSpec((1,) + shape, lambda i: (clipped(i, 1, count),) + (0,) * len(shape))

    quarter = pl.BlockSpec((2, CHUNK, width), lambda i: (0, clipped(i, 1, count), 0))
    ins = dict(
        lengths=(lengths, pl.BlockSpec(memory_space=pltpu.SMEM)),
        qf=(mid["qf"], block(a)),
        kf=(mid["kf"], block(a)),
        v=(mid["v"], block(a)),
        columns=(columns, block(128)),
        state_own=(mid["packed"], fixed((STATE_ROWS, a))),
        ones=(consts["ones"], fixed((a, a))),
    )
    late = dict(
        grad_across=pieces[2],
        grad_own=pieces[0],
        grad_beside=pieces[1],
        down_w=(down_w, l),
        slope=mid["slope_next"],
        act=mid["act_next"],
        fi=mid["fi"],
        out_w=(out_w, l),
    )
    fore, aft = ring_out(n, parts)
    outs = dict(
        d_up_b=(struct((1, hidden), F32), full((1, hidden))),
        d_res=(struct((1, width), F32), full((1, width))),
        ratio=(struct((rows, a), F32), block(a)),
        att=(struct((rows, a), F32), block(a)),
        states=(struct((count, a, a), F32), cube((a, a))),
        totals=(struct((count, 8, a), F32), cube((8, a))),
        d_num=(struct((rows, a), BF), block(a)),
        d_den=(struct((rows, a), F32), block(a)),
        near=(struct((2, rows, width), BF), quarter),
        far=(struct((2, rows, width), BF), quarter),
        d_out=(struct((D, a), BF), full((D, a))),
        exit_state=(struct((STATE_ROWS, a), F32), full((STATE_ROWS, a))),
        up_fore=(fore, full(fore.shape)),
        up_aft=(aft, full(aft.shape)),
        down_fore=(fore, full(fore.shape)),
        down_aft=(aft, full(aft.shape)),
    )
    scratch = dict(
        grad=[pltpu.VMEM((rows, D), BF)],
        grad_corner=[pltpu.VMEM((rows, width), BF)],
        corner_sems=[pltpu.SemaphoreType.DMA((2,))],
        hand=HandOver.scratch(hops, a),
        hand_back=HandOver.scratch(hops, a),
        down_held=Ring.buffers(n, parts, 0, CREST_DOWN),
        up_held=Ring.buffers(n, parts, 0, CREST_UP),
        down_sems=Ring.sems(n, parts),
        up_sems=Ring.sems(n, parts),
        state_in=[pltpu.VMEM((STATE_ROWS, a), F32)],
        packed=[pltpu.VMEM((STATE_ROWS, a), F32)],
        summed=[pltpu.VMEM((a, a), F32)],
        state=[pltpu.VMEM((a, a), F32)],
        total=[pltpu.VMEM((8, a), F32)],
        whole=[pltpu.VMEM((CHUNK, D), BF)],
        low_now=[pltpu.VMEM((CHUNK, a), BF)],
        low=[pltpu.VMEM((rows, a), BF)],
    )
    return named_call(
        functools.partial(crest_kernel, n, hops, l),
        "crest",
        4,
        (count + 2,),
        ins,
        outs,
        scratch,
        2 * rows * D * (hidden * 4 + 4 * a) * 2,
        late,
        dict(
            d_raised=struct((rows, hidden), BF),
            d_down=struct((D, hidden), BF),
            d_up=struct((D, hidden), BF),
        ),
    )


def back_step(z, l, h, step, count, scatter, row_sum, middle_work, end_work):
    c = count - 1 - step
    grads = attention_back(
        step,
        c,
        (
            z.qf, z.kf, z.v, z.d_num, z.d_den, begin_keep(z.columns)[0], z.states, z.totals,
            z.exit_state,
        ),
        z.state,
        z.total,
    )

    @pl.when(step >= 1)
    def _():
        scatter.relay(c + 1)
        row_sum.relay(c + 1)

    middle_work()
    start = step == 0
    d_proj = features_back(
        grads,
        (z.qf, z.kf, z.k, z.cos, z.sin, z.map, z.ones),
        z.d_feat,
        z.d_qkv_b,
        start,
    )
    z.proj_all[rows_at(c), :] = d_proj

    @pl.when(start)
    def _():
        z.late.qkv_w.wait()
        z.late.up_w.wait()

    d_normed, sums = inputs_back(
        l, d_proj, z.d_raised_in, z.qkv_w, z.up_w, z.normed, z.gain, z.sums, start
    )
    z.whole[...] = d_normed
    scatter.put(h, c, z.whole)
    row_sum.put(c, sums)
    end_work()


def back_arrays(l, local, lowered, tables, params, consts, exit_state, count):
    gain, bias, qkv_w, qkv_b, feats, up_w, up_b, out_w, down_w, res_b = params
    cos, sin, columns = tables
    qf, kf, v, k, normed, unit, inverse, states, totals = local
    d_raised, d_num, d_den = lowered
    a = qf.shape[1]

    def early(w):
        return down_rows(w, 0, count)

    return dict(
        qf=(qf, early(a)),
        kf=(kf, early(a)),
        v=(v, early(a)),
        k=(k, early(a)),
        d_num=(d_num, early(a)),
        d_den=(d_den, early(a)),
        columns=(columns, early(128)),
        cos=(cos, early(cos.shape[1])),
        sin=(sin, early(sin.shape[1])),
        states=(states, down_cube((a, a), 0, count)),
        totals=(totals, down_cube((8, a), 0, count)),
        exit_state=(exit_state, fixed(exit_state.shape)),
        map=(consts["map"], fixed((a, a))),
        ones=(consts["ones"], fixed((a, a))),
        d_raised_in=(d_raised, early(d_raised.shape[1])),
        normed=(normed, early(D)),
        gain=(gain, fixed(gain.shape)),
    )


def back_scratch(rows, a, width):
    return dict(
        scatter=Scatter.scratch(rows, width),
        row_sum=RowSum.scratch(rows),
        state=[pltpu.VMEM((a, a), F32)],
        total=[pltpu.VMEM((8, a), F32)],
        whole=[pltpu.VMEM((CHUNK, D), BF)],
        proj_all=[pltpu.VMEM((rows, 3 * a), BF)],
    )


def at_steps(step, table):
    for at, work in table:

        @pl.when(step == at)
        def _(work=work):
            work()


def turn_kernel(n, hops, l, z):
    step = pl.program_id(0)
    h = lax.axis_index("head")
    rows, width = z.mine.shape
    hidden = z.act.shape[1]
    count = rows // CHUNK
    scatter = Scatter(h, z.scatter[:5], z.scatter[5:])
    row_sum = RowSum(h, z.row_sum[:4], z.row_sum[4:])
    gather = Gather(h, z.mine, z.gather[:3], z.gather[3:])
    hand = HandOver(n, hops, rows, -1, z.packed, z.hand[0], z.hand[1:])
    parts = halved(0, hidden)
    rest_parts = rest_of(z.d_qkv.shape[1], z.d_out_next.shape[1])
    down = Ring(
        n, parts, (z.d_down_next,), z.down_held, z.down_sems, CREST_DOWN,
        incoming=(z.down_fore, z.down_aft),
    )
    up = Ring(
        n, parts, (z.d_up_next,), z.up_held, z.up_sems, CREST_UP,
        incoming=(z.up_fore_in, z.up_aft_in),
    )
    rest = Ring(n, rest_parts, (z.d_qkv, z.d_out_next), z.rest_held, z.rest_sems, 0, TURN_REST)
    new_down = Ring(n, parts, (z.d_down,), z.new_down_held, z.new_down_sems, 0, TURN_DOWN)
    new_up = Ring(n, parts, (z.d_up,), z.new_up_held, z.new_up_sems, 0, TURN_UP)

    def sum_up(o):
        c = count - 1 - o
        here = rows_at(c)
        new = norm_back(
            z.before[here, :].astype(F32),
            z.inverse[here, 0:1],
            z.unit[here, :],
            scatter.total(c),
            row_sum.total(c),
        )
        z.after[here, :] = new
        z.mine[here, :] = new.astype(BF)
        z.d_res[...] += jnp.sum(new, axis=0, keepdims=True)
        gather.start(c)

    @pl.when(step == 0)
    def _():
        for copy in every(z.late):
            copy.start()
        hand.clear()
        greet(h, n, hops)
        z.late.d_down_next.wait()
        down.start()
        z.late.d_up_next.wait()
        up.start()
        z.d_res[...] = jnp.zeros_like(z.d_res)

    @pl.when(step < count)
    def _():
        def middle_work():
            at_steps(
                step,
                (
                    (1, lambda: up.batch(CREST_UP + 1)),
                    (1, lambda: up.batch(CREST_UP + 2)),
                    (2, lambda: up.batch(CREST_UP + 3)),
                    (2, z.late.before.wait),
                    (2, z.late.inverse.wait),
                    (2, z.late.unit.wait),
                    (3, lambda: up.batch(CREST_UP + 4)),
                ),
            )

        def end_work():
            at_steps(
                step,
                (
                    (0, lambda: down.batch(CREST_DOWN + 1)),
                    (0, lambda: down.batch(CREST_DOWN + 2)),
                    (1, lambda: down.batch(CREST_DOWN + 3)),
                    (2, lambda: down.batch(CREST_DOWN + 4)),
                ),
            )

            @pl.when(step >= 2)
            def _():
                sum_up(step - 2)

        back_step(z, l + 1, h, step, count, scatter, row_sum, middle_work, end_work)

    def feed(c):
        gather.ready(c)
        here = rows_at(c)
        for r, part in enumerate(gather.pieces(c)):
            z.grad[here, block_columns(h, r, width)] = part
        z.d_raised_out[here, :] = lower_feed(
            z.grad[here, :], z.down_w, z.slope.at[here, :], z.d_up_b, c == count - 1
        )

    def attention(c):
        here = rows_at(c)
        lower_attention(
            z.grad[here, :],
            z.out_w,
            z.ratio[here, :],
            z.att[here, :],
            z.qf_late[here, :],
            begin_keep(z.columns_late)[0][here, :],
            z.ones[...],
            (z.d_num_out.at[here, :], z.d_den_out.at[here, :]),
            z.summed,
            z.packed,
            c == count - 1,
        )

    def qkv_tiles(low, high):
        for i in range(low, high):
            weight_tile(i, z.ai, z.proj_all[...], z.d_qkv)

    @pl.when(step == count)
    def _():
        z.late.ai.wait()
        qkv_tiles(0, 1)
        scatter.relay(0)
        row_sum.relay(0)
        gather.relay(count - 1)
        sum_up(count - 2)
        qkv_tiles(1, 4)
        z.late.d_out_next.wait()
        rest.start()
        z.sent.d_qkv.start()
        down.finish((z.sum_down,))
        z.late.down_w.wait()
        z.late.slope.wait()
        sum_up(count - 1)
        feed(jnp.int32(count - 1))
        gather.relay(count - 2)
        up.finish((z.sum_up,))
        feed(jnp.int32(count - 2))
        gather.relay(count - 3)
        for copy in (z.late.out_w, z.late.ratio, z.late.att, z.late.qf_late, z.late.columns_late):
            copy.wait()
        loop(2, lambda i: attention(count - 1 - i))
        gather.relay(0)
        feed(jnp.int32(count - 3))
        attention(jnp.int32(count - 3))
        rest.batch(1)
        feed(jnp.int32(0))
        attention(jnp.int32(0))
        z.packed[0:FEATURES, :] = pack_state(z.summed[...])
        hand.start()
        z.sent.d_raised_out.start()
        z.sent.d_num_out.start()
        z.sent.d_den_out.start()
        z.late.act.wait()
        loop(D // CHUNK, lambda i: weight_tile(i, z.grad, z.act[...], z.d_down))
        new_down.start()
        z.sent.d_down.start()
        rest.batch(2)
        z.late.fi.wait()
        loop(D // CHUNK, lambda i: weight_tile(i, z.fi, z.d_raised_out[...], z.d_up))
        new_up.start()
        z.sent.d_up.start()
        z.late.att_low.wait()
        rest.batch(3)
        new_down.batch(1)
        loop(D // CHUNK, lambda i: weight_tile(i, z.grad, z.att_low[...], z.d_out))
        for i in range(count):
            gather.finish(i)
            scatter.finish(i)
            row_sum.finish(i)
        z.exit_out[...] = hand.total(z.lengths)
        new_up.pause((z.up_fore, z.up_aft))
        rest.pause((z.rest_a, z.rest_b, z.rest_c, z.rest_d))
        new_down.pause((z.new_fore, z.new_aft))
        for copy in every(z.sent):
            copy.wait()


def rest_of(qkv, out):
    return halved(0, qkv) + halved(1, out)


def turn(
    n, hops, l, lengths, local, top, before, ai, lower_in, tables, params, consts
):
    gain, bias, qkv_w, qkv_b, feats, up_w, up_b, out_w, down_w, res_b = params
    cos, sin, columns = tables
    act, slope, ratio, att, att_low, fi, qf = lower_in
    rows, a = qf.shape
    hidden = up_w.shape[2]
    count = rows // CHUNK
    width = D // 4
    share = D // n
    lowered = (top["d_raised"], top["d_num"], top["d_den"])
    parts = halved(0, hidden)
    rest_parts = rest_of(3 * a, a)

    def whole(array):
        return (array, fixed(array.shape))

    ins = dict(
        lengths=(lengths, pl.BlockSpec(memory_space=pltpu.SMEM)),
        **back_arrays(l + 1, local, lowered, tables, params, consts, top["exit_state"], count),
        down_fore=whole(top["down_fore"]),
        down_aft=whole(top["down_aft"]),
        up_fore_in=whole(top["up_fore"]),
        up_aft_in=whole(top["up_aft"]),
    )
    late = dict(
        d_down_next=top["d_down"],
        d_up_next=top["d_up"],
        qkv_w=(qkv_w, l + 1),
        up_w=(up_w, l + 1),
        before=before,
        inverse=local[6],
        unit=local[5],
        ai=ai,
        d_out_next=top["d_out"],
        down_w=(down_w, l),
        slope=slope,
        out_w=(out_w, l),
        ratio=ratio,
        att=att,
        qf_late=qf,
        columns_late=columns,
        act=act,
        fi=fi,
        att_low=att_low,
    )
    rests = ring_out(n, rest_parts)
    fore, aft = ring_out(n, parts)
    outs = dict(
        d_feat=(struct((1, a), F32), full((1, a))),
        d_qkv_b=(struct((1, 3 * a), F32), full((1, 3 * a))),
        sums=(struct((8, D), F32), full((8, D))),
        after=(struct((rows, width), F32), full((rows, width))),
        d_res=(struct((1, width), F32), full((1, width))),
        d_up_b=(struct((1, hidden), F32), full((1, hidden))),
        d_out=(struct((D, a), BF), full((D, a))),
        exit_out=(struct((STATE_ROWS, a), F32), full((STATE_ROWS, a))),
        sum_down=(struct((share, hidden), F32), full((share, hidden))),
        sum_up=(struct((share, hidden), F32), full((share, hidden))),
        rest_a=(rests[0], full(rests[0].shape)),
        rest_b=(rests[1], full(rests[1].shape)),
        rest_c=(rests[2], full(rests[2].shape)),
        rest_d=(rests[3], full(rests[3].shape)),
        new_fore=(fore, full(fore.shape)),
        new_aft=(aft, full(aft.shape)),
        up_fore=(fore, full(fore.shape)),
        up_aft=(aft, full(aft.shape)),
    )
    scratch = dict(
        **back_scratch(rows, a, width),
        gather=Gather.scratch(rows, width),
        hand=HandOver.scratch(hops, a),
        down_held=Ring.buffers(n, parts, CREST_DOWN),
        up_held=Ring.buffers(n, parts, CREST_UP),
        rest_held=Ring.buffers(n, rest_parts, 0, TURN_REST),
        new_down_held=Ring.buffers(n, parts, 0, TURN_DOWN),
        new_up_held=Ring.buffers(n, parts, 0, TURN_UP),
        down_sems=Ring.sems(n, parts),
        up_sems=Ring.sems(n, parts),
        rest_sems=Ring.sems(n, rest_parts),
        new_down_sems=Ring.sems(n, parts),
        new_up_sems=Ring.sems(n, parts),
        mine=[pltpu.VMEM((rows, width), BF)],
        packed=[pltpu.VMEM((STATE_ROWS, a), F32)],
        summed=[pltpu.VMEM((a, a), F32)],
        grad=[pltpu.VMEM((rows, D), BF)],
    )
    return named_call(
        functools.partial(turn_kernel, n, hops, l),
        "turn",
        5,
        (count + 1,),
        ins,
        outs,
        scratch,
        2 * rows * D * (hidden * 4 + 8 * a) * 2,
        late,
        dict(
            d_qkv=struct((D, 3 * a), BF),
            d_num_out=struct((rows, a), BF),
            d_den_out=struct((rows, a), F32),
            d_raised_out=(struct((rows, hidden), BF), "slope"),
            d_down=struct((D, hidden), BF),
            d_up=struct((D, hidden), BF),
        ),
    )


class Small:
    def __init__(self, h, n, refs, sems):
        self.near, self.far, self.got, self.middle, self.across, self.bundle, self.other = refs
        self.head_send, self.head_recv, self.seq_send, self.seq_recv = sems
        self.h, self.n = h, n
        self.here = lax.axis_index("seq")

    @staticmethod
    def rounds(n):
        return max(1, (n - 1).bit_length())

    @staticmethod
    def scratch(n, width):
        r = Small.rounds(n)
        dma = pltpu.SemaphoreType.DMA
        return (
            [pltpu.VMEM((2, 16, width), F32)] * 3
            + [pltpu.VMEM((16, width), F32)] * 2
            + [pltpu.VMEM((r + 1, 32, width), F32), pltpu.VMEM((r, 32, width), F32)]
            + [dma((2,)), dma((2,)), dma((r,)), dma((r,))]
        )

    def head_copy(self, kind):
        source, target, mask = (
            (self.far, self.got, 1),
            (self.middle, self.across, 2),
        )[kind]
        return push(
            source,
            target,
            self.head_send.at[kind],
            self.head_recv.at[kind],
            {"head": lax.bitwise_xor(self.h, mask)},
        )

    def seq_copy(self, k):
        return push(
            self.bundle.at[k],
            self.other.at[k],
            self.seq_send.at[k],
            self.seq_recv.at[k],
            {"seq": lax.bitwise_xor(self.here, 1 << k)},
        )

    def put(self, sums):
        width = self.near.shape[2]
        for l, ref in enumerate(sums):
            at = slice(8 * l, 8 * l + 8)
            self.near[0, at, :] = ref[:, block_columns(self.h, 0, width)]
            self.near[1, at, :] = ref[:, block_columns(self.h, 2, width)]
            self.far[0, at, :] = ref[:, block_columns(self.h, 1, width)]
            self.far[1, at, :] = ref[:, block_columns(self.h, 3, width)]
        self.head_copy(0).start()

    def relay(self):
        self.head_copy(0).wait_recv()
        self.middle[...] = self.near[1] + self.got[1]
        self.head_copy(1).start()

    def pack(self, rows):
        self.head_copy(1).wait_recv()
        norms = self.near[0] + self.got[0] + self.across[...]
        width = self.near.shape[2]
        self.bundle[0] = jnp.zeros_like(self.bundle[0])
        for l, refs in enumerate(rows):
            self.bundle[0, 16 * l : 16 * l + 4, :] = norms[8 * l : 8 * l + 4]
            at = 16 * l + 4
            for ref in refs:
                for i in range(ref.shape[1] // width):
                    self.bundle[0, at : at + 1, :] = ref[:, i * width : (i + 1) * width]
                    at += 1
        self.seq_copy(0).start()

    def round(self, k):
        self.seq_copy(k).wait_recv()
        self.bundle[k + 1] = self.bundle[k] + self.other[k]
        if k + 1 < self.rounds(self.n):
            self.seq_copy(k + 1).start()

    def finish(self):
        for kind in range(2):
            self.head_copy(kind).wait_send()
        for k in range(self.rounds(self.n)):
            self.seq_copy(k).wait_send()


def greet_all(h, n):
    barrier = pltpu.get_barrier_semaphore()

    def signal(where):
        pl.semaphore_signal(barrier, inc=1, device_id=where, device_id_type=pl.DeviceIdType.MESH)

    signal({"head": lax.bitwise_xor(h, 1)})
    signal({"head": lax.bitwise_xor(h, 2)})
    here = lax.axis_index("seq")
    place = ring_place(here, n)
    signal({"seq": ring_index(lax.rem(place + 1, n), n)})
    signal({"seq": ring_index(lax.rem(place + n - 1, n), n)})
    rounds = Small.rounds(n)
    for k in range(rounds):
        signal({"seq": lax.bitwise_xor(here, 1 << k)})
    pl.semaphore_wait(barrier, 4 + rounds)


def leave_kernel(n, z):
    step = pl.program_id(0)
    h = lax.axis_index("head")
    rows = z.proj_all.shape[0]
    count = rows // CHUNK
    hidden, a = z.d_down.shape[1], z.d_out.shape[1]
    scatter = Scatter(h, z.scatter[:5], z.scatter[5:])
    row_sum = RowSum(h, z.row_sum[:4], z.row_sum[4:])
    small = Small(h, n, z.small[:7], z.small[7:])
    rest = Ring(
        n, rest_of(3 * a, a), (z.d_qkv_next, z.d_out_next), z.rest_held, z.rest_sems, TURN_REST,
        incoming=(z.rest_a, z.rest_b, z.rest_c, z.rest_d),
    )
    down = Ring(
        n, halved(0, hidden), (z.d_down,), z.down_held, z.down_sems, TURN_DOWN,
        incoming=(z.new_fore, z.new_aft),
    )
    up = Ring(
        n, halved(0, hidden), (z.d_up,), z.up_held, z.up_sems, TURN_UP,
        incoming=(z.up_fore, z.up_aft),
    )
    out = Ring(n, halved(0, a), (z.d_out,), z.out_held, z.out_sems)
    first_parts, second_parts = split_last(3 * a)
    last = Ring(n, first_parts, (z.d_qkv,), z.last_held, z.last_sems)
    more = Ring(n, second_parts, (z.d_qkv,), z.more_held, z.more_sems)
    width = z.res_b.shape[1] // 4
    columns = pl.ds(pl.multiple_of(h * width, width), width)
    result = Scatter(h, (z.near, z.far) + tuple(z.result[:3]), z.result[3:])

    def sum_up(o):
        here = rows_at(count - 1 - o)
        z.after[here, :] = norm_back(
            z.before[here, :],
            z.inverse[here, 0:1],
            z.unit[here, :],
            scatter.total(count - 1 - o),
            row_sum.total(count - 1 - o),
        )

    @pl.when(step == 0)
    def _():
        for copy in every(z.late):
            copy.start()
        greet_all(h, n)
        z.late.d_qkv_next.wait()
        rest.start()
        z.late.d_down.wait()
        down.start()
        z.late.d_up.wait()
        up.start()
        out.start()
        z.late.near.wait()
        z.late.far.wait()
        for i in range(count):
            result.copy(0, i).start()

    @pl.when(step < count)
    def _():
        def middle_work():
            at_steps(
                step,
                (
                    (1, lambda: down.batch(TURN_DOWN + 1)),
                    (1, lambda: down.batch(TURN_DOWN + 2)),
                    (2, lambda: rest.batch(TURN_REST + 3)),
                    (2, z.late.before.wait),
                    (2, z.late.inverse.wait),
                    (2, z.late.unit.wait),
                    (3, lambda: up.batch(TURN_UP + 3)),
                ),
            )

        def end_work():
            at_steps(
                step,
                (
                    (0, lambda: rest.batch(TURN_REST + 1)),
                    (0, lambda: rest.batch(TURN_REST + 2)),
                    (0, lambda: result.relay(0)),
                    (0, lambda: result.relay(1)),
                    (1, lambda: up.batch(TURN_UP + 1)),
                    (1, lambda: up.batch(TURN_UP + 2)),
                    (1, lambda: out.batch(1)),
                    (1, lambda: result.relay(2)),
                    (1, lambda: result.relay(3)),
                    (2, lambda: down.batch(TURN_DOWN + 3)),
                    (3, lambda: out.batch(2)),
                ),
            )

            @pl.when(step >= 2)
            def _():
                sum_up(step - 2)

        back_step(z, 0, h, step, count, scatter, row_sum, middle_work, end_work)

    @pl.when(step == count)
    def _():
        scatter.relay(0)
        row_sum.relay(0)
        small.put((z.sums, z.sums_next))
        z.late.ai.wait()
        loop(D // CHUNK, lambda i: weight_tile(i, z.ai, z.proj_all[...], z.d_qkv))
        last.start()
        more.start()
        rest.finish((z.sum_qkv_next, z.sum_out_next))
        down.batch(TURN_DOWN + 4)
        small.relay()
        sum_up(2)
        up.batch(TURN_UP + 4)
        out.batch(3)
        sum_up(3)
        small.pack(
            (
                (z.d_qkv_b, z.d_up_b, z.d_feat[...] / feature_row(z.feats, 0), z.d_res),
                (
                    z.d_qkv_b_next,
                    z.d_up_b_next,
                    z.d_feat_next[...] / feature_row(z.feats, 1),
                    z.d_res_next,
                ),
            )
        )
        last.batch(1)
        more.batch(1)
        down.batch(6)
        small.round(0)
        last.batch(2)
        more.batch(2)
        z.late.own.wait()
        for i in range(count):
            here = rows_at(i)
            z.out[here, :] = z.own[here, :] + result.total(i) + z.res_b[1:2, columns]
        up.batch(5)
        out.batch(4)
        last.batch(3)
        more.batch(3)
        for k in range(1, Small.rounds(n)):
            small.round(k)
        down.finish((z.sum_down,))
        last.batch(4)
        more.batch(4)
        up.batch(6)
        out.batch(5)
        last.batch(5)
        more.batch(5)
        out.batch(6)
        last.batch(6)
        more.batch(6)
        up.finish((z.sum_up,))
        out.finish((z.sum_out,))
        z.bundle[...] = small.bundle[Small.rounds(n)]
        small.finish()
        for i in range(count):
            scatter.finish(i)
            row_sum.finish(i)
            result.finish(i)
        last.finish((z.sum_qkv,))
        more.finish((z.sum_qkv,))


def split_last(width):
    third = width // 3
    half = third // 2
    return (
        ((0, 0, third, 1), (0, third, half, -1)),
        ((0, third + half, half, 1), (0, 2 * third, third, -1)),
    )


def leave(n, local, turned, top, before, ai, own, tables, params, consts):
    qf = local[0]
    rows, a = qf.shape
    lowered = (turned["d_raised_out"], turned["d_num_out"], turned["d_den_out"])
    hidden = lowered[0].shape[1]
    count = rows // CHUNK
    width = D // 4
    share = D // n
    rest_parts, wide_parts = rest_of(3 * a, a), halved(0, hidden)
    out_parts = halved(0, a)
    first_parts, second_parts = split_last(3 * a)

    def whole(array):
        return (array, fixed(array.shape))

    ins = dict(
        **back_arrays(0, local, lowered, tables, params, consts, turned["exit_out"], count),
        d_out_next=whole(top["d_out"]),
        d_out=whole(turned["d_out"]),
        new_fore=whole(turned["new_fore"]),
        new_aft=whole(turned["new_aft"]),
        up_fore=whole(turned["up_fore"]),
        up_aft=whole(turned["up_aft"]),
        res_b=whole(params[9]),
        feats=whole(params[4]),
        rest_a=whole(turned["rest_a"]),
        rest_b=whole(turned["rest_b"]),
        rest_c=whole(turned["rest_c"]),
        rest_d=whole(turned["rest_d"]),
        d_up_b=whole(turned["d_up_b"]),
        d_res=whole(turned["d_res"]),
        sums_next=whole(turned["sums"]),
        d_qkv_b_next=whole(turned["d_qkv_b"]),
        d_up_b_next=whole(top["d_up_b"]),
        d_feat_next=whole(turned["d_feat"]),
        d_res_next=whole(top["d_res"]),
    )
    gain, bias, qkv_w, qkv_b, feats, up_w, up_b, out_w, down_w, res_b = params
    late = dict(
        d_qkv_next=turned["d_qkv"],
        d_down=turned["d_down"],
        d_up=turned["d_up"],
        qkv_w=(qkv_w, 0),
        up_w=(up_w, 0),
        before=before,
        inverse=local[6],
        unit=local[5],
        ai=ai,
        near=top["near"],
        far=top["far"],
        own=own,
    )

    def result(shape):
        return (struct(shape, F32), full(shape))

    outs = dict(
        after=result((rows, width)),
        out=result((rows, width)),
        bundle=result((32, width)),
        sum_qkv_next=result((share, 3 * a)),
        sum_out_next=result((share, a)),
        sum_qkv=result((share, 3 * a)),
        sum_out=result((share, a)),
        sum_down=result((share, hidden)),
        sum_up=result((share, hidden)),
    )
    scratch = dict(
        **back_scratch(rows, a, width),
        small=Small.scratch(n, width),
        rest_held=Ring.buffers(n, rest_parts, TURN_REST),
        down_held=Ring.buffers(n, wide_parts, TURN_DOWN),
        up_held=Ring.buffers(n, wide_parts, TURN_UP),
        out_held=Ring.buffers(n, out_parts),
        last_held=Ring.buffers(n, first_parts),
        more_held=Ring.buffers(n, second_parts),
        result=Scatter.scratch(rows, width)[2:],
        rest_sems=Ring.sems(n, rest_parts),
        down_sems=Ring.sems(n, wide_parts),
        up_sems=Ring.sems(n, wide_parts),
        out_sems=Ring.sems(n, out_parts),
        last_sems=Ring.sems(n, first_parts),
        more_sems=Ring.sems(n, second_parts),
        d_qkv=[pltpu.VMEM((D, 3 * a), BF)],
        d_feat=[pltpu.VMEM((1, a), F32)],
        d_qkv_b=[pltpu.VMEM((1, 3 * a), F32)],
        sums=[pltpu.VMEM((8, D), F32)],
    )
    return named_call(
        functools.partial(leave_kernel, n),
        "leave",
        6,
        (count + 1,),
        ins,
        outs,
        scratch,
        2 * rows * D * (hidden + 8 * a) * 3,
        late,
    )


def finish_kernel(pairs, *refs):
    for i, (which, layer) in enumerate(pairs):
        target = refs[len(pairs) + which]
        if layer is None:
            target[...] = refs[i][...]
        else:
            target[layer] = refs[i][...]


def finish(results):
    arrays, pairs, shapes = [], [], []
    for which, result in enumerate(results):
        if isinstance(result, tuple):
            for layer, array in enumerate(result):
                arrays.append(array)
                pairs.append((which, layer))
            shapes.append(struct((len(result),) + result[0].shape, F32))
        else:
            arrays.append(result)
            pairs.append((which, None))
            shapes.append(struct(result.shape, F32))
    space = pl.BlockSpec(memory_space=pltpu.VMEM)
    return pl.pallas_call(
        functools.partial(finish_kernel, tuple(pairs)),
        name="finish",
        in_specs=[space] * len(arrays),
        out_specs=[space] * len(shapes),
        out_shape=shapes,
        compiler_params=pltpu.CompilerParams(vmem_limit_bytes=VMEM_BYTES),
    )(*arrays)


def on_device(
    acts,
    cotangent,
    lengths,
    keep_mask,
    ln_gain,
    ln_bias,
    qkv_w,
    qkv_b,
    feat_w,
    out_w,
    up_w,
    up_b,
    down_w,
    res_b,
):
    rows, width = acts.shape
    heads = feat_w.shape[1]
    a = heads * HEAD_DIM
    n = lax.axis_size("seq")
    tokens = rows * n
    longest = 2048 if tokens <= 8192 else 4096
    hops = -(-longest // rows)
    h = lax.axis_index("head").astype(jnp.int32)
    first = lax.axis_index("seq") * rows

    keep_rows = keep_mask.reshape(rows // 128, 128)
    half = ROT // 2
    rates = np.zeros((2, HEAD_DIM))
    rates[0, :half] = ROTARY_BASE ** (-2.0 * np.arange(half) / ROT)
    rates[0, half:ROT] = rates[0, :half]
    rates[1, :half] = -1.0
    rates[1, half:ROT] = 1.0
    rates = jnp.asarray(np.tile(rates, (1, 2)), F32)

    fold = sample_points(FEATURES, HEAD_DIM) @ cosine_table(HEAD_DIM) / math.sqrt(HEAD_DIM)
    eye = np.eye(heads)
    consts = {
        "map": jnp.asarray(np.kron(eye, fold), F32),
        "map_t": jnp.asarray(np.kron(eye, fold.T), F32),
        "ones": jnp.asarray(np.kron(eye, np.ones((HEAD_DIM, HEAD_DIM))), BF),
    }

    entered = enter(
        n, lengths, acts, keep_rows, ln_gain, ln_bias, qkv_w, qkv_b, feat_w, rates, consts
    )
    tables = (entered["cos"], entered["sin"], entered["columns"])
    params = (ln_gain, ln_bias, qkv_w, qkv_b, feat_w, up_w, up_b, out_w, down_w, res_b)

    def back_local(made, states, totals):
        ai, fi, normed, unit, inverse, qf, kf, v, k = made
        return (qf, kf, v, k, normed, unit, inverse, states, totals)

    first_made = tuple(entered[name] for name, width_of, kind in PROJECT_KINDS)
    own_rows, packed = lax.optimization_barrier((cotangent, entered["packed"]))
    pieces = [own_rows] + [
        lax.ppermute(own_rows, "head", [(i, i ^ mask) for i in range(4)]) for mask in (1, 2)
    ]
    entered["packed"] = packed
    mid = between(n, hops, 0, lengths, entered, params, consts)
    local = back_local(first_made, mid["states"], mid["totals"])
    made = tuple(mid[name] for name, width_of, kind in PROJECT_KINDS)
    lower_in = (
        mid["act"], mid["slope"], mid["ratio"], mid["att"], mid["att_low"], entered["fi"],
        entered["qf"],
    )
    top = crest(n, hops, 1, lengths, mid, pieces, tables, params, consts)
    turned = turn(
        n,
        hops,
        0,
        lengths,
        back_local(made, top["states"], top["totals"]),
        top,
        cotangent,
        made[0],
        lower_in,
        tables,
        params,
        consts,
    )
    left = leave(n, local, turned, top, turned["after"], first_made[0], mid["own"], tables, params, consts)
    out_acts, d_acts, d_qkv, d_out, d_up, d_down = finish(
        (
            left["out"],
            left["after"],
            (left["sum_qkv"], left["sum_qkv_next"]),
            (left["sum_out"], left["sum_out_next"]),
            (left["sum_up"], turned["sum_up"]),
            (left["sum_down"], turned["sum_down"]),
        )
    )
    hidden = up_w.shape[2]
    bundle = left["bundle"].reshape(LAYERS, 16, width)
    kinds = 3 * a // width
    ups = hidden // width
    at = 4 + kinds + ups
    return (
        out_acts,
        d_acts,
        d_qkv,
        d_out,
        d_up,
        d_down,
        bundle[:, 4 : 4 + kinds].reshape(LAYERS, 3 * a),
        bundle[:, 4 + kinds : at].reshape(LAYERS, hidden),
        bundle[:, at].reshape(LAYERS, heads, FEATURES),
        bundle[:, 0:2],
        bundle[:, 2:4],
        bundle[:, at + 1],
    )


def solution(mesh):
    return jax.shard_map(
        on_device,
        mesh=mesh,
        in_specs=(
            P("seq", "head"),
            P("seq", "head"),
            P(),
            P("seq"),
            P(),
            P(),
            P(None, None, "head"),
            P(None, "head"),
            P(None, "head", None),
            P(None, None, "head"),
            P(None, None, "head"),
            P(None, "head"),
            P(None, None, "head"),
            P(),
        ),
        out_specs=(
            P("seq", "head"),
            P("seq", "head"),
            P(None, "seq", "head"),
            P(None, "seq", "head"),
            P(None, "seq", "head"),
            P(None, "seq", "head"),
            P(None, "head"),
            P(None, "head"),
            P(None, "head", None),
            P(None, None, "head"),
            P(None, None, "head"),
            P(None, "head"),
        ),
        check_vma=False,
    )
```

```python
import functools
import math

import jax
import jax.numpy as jnp
import numpy as np
from jax import lax
from jax.experimental import pallas as pl
from jax.experimental.pallas import tpu as pltpu
from jax.sharding import PartitionSpec as P

D = 1024
HEAD_DIM = 64
ROT = 16
FEATURES = 64
LAYERS = 2
CHUNK = 256

EPSILON = 1e-05
ROTARY_BASE = 10000.0
HIGHEST = lax.Precision.HIGHEST
BF = jnp.bfloat16
F32 = jnp.float32
STATE_ROWS = 72
VMEM_BYTES = 60 * 1024 * 1024


def prime_numbers(count):
    found = []
    candidate = 2
    while len(found) < count:
        if all((candidate % prime != 0 for prime in found)):
            found.append(candidate)
        candidate = candidate + 1
    return found


def sample_points(rows, columns):
    roots = np.sqrt(np.array(prime_numbers(2 * columns)) * 1.0)
    fractions = roots - np.floor(roots)
    grid = np.outer(np.arange(1, rows + 1) * 1.0, fractions) % 1.0
    radius = np.sqrt(-2.0 * np.log(1.0 - grid[:, :columns]))
    return radius * np.cos(2.0 * math.pi * grid[:, columns:])


def cosine_table(size):
    wave = np.arange(size)[:, None] * 1.0
    place = np.arange(size)[None, :] * 1.0
    table = np.cos(math.pi * (place + 0.5) * wave / size) * math.sqrt(2.0 / size)
    return table * np.where(wave == 0, math.sqrt(0.5), 1.0)


def dot_nn(a, b, precision=None):
    return lax.dot_general(
        a, b, (((1,), (0,)), ((), ())), precision=precision, preferred_element_type=F32
    )


def dot_nt(a, b, precision=None):
    return lax.dot_general(
        a, b, (((1,), (1,)), ((), ())), precision=precision, preferred_element_type=F32
    )


def dot_tn(a, b, precision=None):
    return lax.dot_general(
        a, b, (((0,), (0,)), ((), ())), precision=precision, preferred_element_type=F32
    )


def halves(wide):
    high = wide.astype(BF)
    return high, (wide - high.astype(F32)).astype(BF)


def lane_of(shape):
    return lax.broadcasted_iota(jnp.int32, shape, 1)


def row_of(shape):
    return lax.broadcasted_iota(jnp.int32, shape, 0)


def swap_pairs(x):
    width = x.shape[1]
    later = pltpu.roll(x, width - ROT // 2, 1)
    earlier = pltpu.roll(x, ROT // 2, 1)
    return jnp.where(lane_of(x.shape) % ROT < ROT // 2, later, earlier)


def twice(table):
    return jnp.concatenate([table, table], axis=1)


def block_columns(h, r, width):
    return pl.ds(pl.multiple_of(lax.bitwise_xor(h, r) * width, width), width)


def split_heads(projected):
    heads = projected.shape[1] // (3 * HEAD_DIM)
    return [
        jnp.concatenate(
            [
                projected[:, (3 * j + kind) * HEAD_DIM : (3 * j + kind + 1) * HEAD_DIM]
                for j in range(heads)
            ],
            axis=1,
        )
        for kind in range(3)
    ]


def join_heads(q, k, v):
    heads = q.shape[1] // HEAD_DIM
    return jnp.concatenate(
        [
            part[:, j * HEAD_DIM : (j + 1) * HEAD_DIM]
            for j in range(heads)
            for part in (q, k, v)
        ],
        axis=1,
    )


def block_diagonal(width):
    shape = (width, width)
    return (row_of(shape) // HEAD_DIM) == (lane_of(shape) // HEAD_DIM)


def pack_state(full):
    width = full.shape[0]
    kept = jnp.where(block_diagonal(width), full, 0.0)
    packed = kept[0:FEATURES]
    for head in range(1, width // FEATURES):
        packed = packed + kept[head * FEATURES : (head + 1) * FEATURES]
    return packed


def unpack_state(packed):
    width = packed.shape[1]
    tall = jnp.concatenate([packed] * (width // FEATURES), axis=0)
    return jnp.where(block_diagonal(width), tall, 0.0)


def head_sum(values, ones):
    high, low = halves(values)
    return dot_nn(high, ones) + dot_nn(low, ones)


def full(shape):
    return pl.BlockSpec(shape, lambda *i: (0,) * len(shape))


def rowed(width):
    return pl.BlockSpec((CHUNK, width), lambda i: (i, 0))


def layered(array, l):
    return pl.BlockSpec((None,) + array.shape[1:], lambda *i: (l, 0, 0))


def rows_at(c):
    return pl.ds(pl.multiple_of(c * CHUNK, CHUNK), CHUNK)


def push(source, target, send, recv, where):
    return pltpu.make_async_remote_copy(
        src_ref=source,
        dst_ref=target,
        send_sem=send,
        recv_sem=recv,
        device_id=where,
        device_id_type=pl.DeviceIdType.MESH,
    )


class Gather:
    def __init__(self, h, own, buffers, sems):
        self.own = own
        self.beside, self.across, self.corner = buffers
        self.send, self.recv = sems
        self.near = {"head": lax.bitwise_xor(h, 1)}
        self.far = {"head": lax.bitwise_xor(h, 2)}

    @staticmethod
    def scratch(rows, width):
        count = rows // CHUNK
        return [pltpu.VMEM((rows, width), BF)] * 3 + [pltpu.SemaphoreType.DMA((3, count))] * 2

    def copy(self, kind, c):
        source, target, where = (
            (self.own, self.across, self.far),
            (self.own, self.beside, self.near),
            (self.across, self.corner, self.near),
        )[kind]
        rows = rows_at(c)
        return push(
            source.at[rows, :],
            target.at[rows, :],
            self.send.at[kind, c],
            self.recv.at[kind, c],
            where,
        )

    def start(self, c):
        self.copy(0, c).start()
        self.copy(1, c).start()

    def relay(self, c):
        self.copy(0, c).wait_recv()
        self.copy(2, c).start()

    def ready(self, c):
        self.copy(1, c).wait_recv()
        self.copy(2, c).wait_recv()

    def pieces(self, c):
        rows = rows_at(c)
        return [ref[rows, :] for ref in (self.own, self.beside, self.across, self.corner)]

    def finish(self, c):
        for kind in range(3):
            self.copy(kind, c).wait_send()


class Scatter:
    def __init__(self, h, buffers, sems):
        self.near, self.far, self.got, self.middle, self.across = buffers
        self.send, self.recv = sems
        self.beside = {"head": lax.bitwise_xor(h, 1)}
        self.beyond = {"head": lax.bitwise_xor(h, 2)}

    @staticmethod
    def scratch(rows, width):
        count = rows // CHUNK
        return (
            [pltpu.VMEM((2, rows, width), BF)] * 3
            + [pltpu.VMEM((rows, width), BF)] * 2
            + [pltpu.SemaphoreType.DMA((2, count))] * 2
        )

    def copy(self, kind, c):
        rows = rows_at(c)
        if kind == 0:
            source, target, where = (
                self.far.at[:, rows, :],
                self.got.at[:, rows, :],
                self.beside,
            )
        else:
            source, target, where = self.middle.at[rows, :], self.across.at[rows, :], self.beyond
        return push(source, target, self.send.at[kind, c], self.recv.at[kind, c], where)

    def put(self, h, c, whole):
        rows = rows_at(c)
        w = self.near.shape[2]
        self.near[0, rows, :] = whole[:, block_columns(h, 0, w)]
        self.near[1, rows, :] = whole[:, block_columns(h, 2, w)]
        self.far[0, rows, :] = whole[:, block_columns(h, 1, w)]
        self.far[1, rows, :] = whole[:, block_columns(h, 3, w)]
        self.copy(0, c).start()

    def relay(self, c):
        self.copy(0, c).wait_recv()
        rows = rows_at(c)
        self.middle[rows, :] = (
            self.near[1, rows, :].astype(F32) + self.got[1, rows, :].astype(F32)
        ).astype(BF)
        self.copy(1, c).start()

    def total(self, c):
        self.copy(1, c).wait_recv()
        rows = rows_at(c)
        return (
            self.near[0, rows, :].astype(F32)
            + self.got[0, rows, :].astype(F32)
            + self.across[rows, :].astype(F32)
        )

    def finish(self, c):
        self.copy(0, c).wait_send()
        self.copy(1, c).wait_send()


def begin_scalar(lengths, slot):
    def one(j, carry):
        at, best = carry
        at = at + lengths[j - 1]
        return at, jnp.where(at <= slot, at, best)

    return lax.fori_loop(1, lengths.shape[0], one, (jnp.int32(0), jnp.int32(0)))[1]


def begin_column(lengths, slots):
    def one(j, carry):
        at, best = carry
        at = at + lengths[j - 1]
        return at, jnp.where(slots >= at, at, best)

    return lax.fori_loop(1, lengths.shape[0], one, (jnp.int32(0), jnp.zeros_like(slots)))[1]


class HandOver:
    def __init__(self, n, hops, rows, sign, packed, buffer, sems):
        self.n, self.hops, self.rows, self.sign = n, hops, rows, sign
        self.packed, self.buffer = packed, buffer
        self.send, self.recv = sems
        self.here = lax.axis_index("seq")

    @staticmethod
    def scratch(hops, width):
        return [pltpu.VMEM((hops, STATE_ROWS, width), F32)] + [
            pltpu.SemaphoreType.DMA((hops,))
        ] * 2

    def inside(self, index):
        return (index >= 0) & (index < self.n)

    def copy(self, j):
        return push(
            self.packed,
            self.buffer.at[j - 1],
            self.send.at[j - 1],
            self.recv.at[j - 1],
            {"seq": lax.rem(self.here + self.sign * j + self.n, self.n)},
        )

    def clear(self):
        self.buffer[...] = jnp.zeros_like(self.buffer)

    def start(self):
        for j in range(1, self.hops + 1):

            @pl.when(self.inside(self.here + self.sign * j))
            def _(j=j):
                self.copy(j).start()

    def total(self, lengths):
        first = self.here * self.rows
        result = None
        for j in range(1, self.hops + 1):

            @pl.when(self.inside(self.here - self.sign * j))
            def _(j=j):
                self.copy(j).wait_recv()

            @pl.when(self.inside(self.here + self.sign * j))
            def _(j=j):
                self.copy(j).wait_send()

            if self.sign > 0:
                edge, held = first - 1, first - 1 - (j - 1) * self.rows
            else:
                edge, held = first + j * self.rows - 1, first + self.rows - 1
            linked = (begin_scalar(lengths, edge) <= held).astype(F32)
            part = self.buffer[j - 1] * linked
            result = part if result is None else result + part
        return result


def greet(h, n, hops):
    barrier = pltpu.get_barrier_semaphore()

    def signal(where):
        pl.semaphore_signal(barrier, inc=1, device_id=where, device_id_type=pl.DeviceIdType.MESH)

    signal({"head": lax.bitwise_xor(h, 1)})
    signal({"head": lax.bitwise_xor(h, 2)})
    here = lax.axis_index("seq")
    expected = jnp.int32(2)
    for j in range(1, hops + 1):
        for sign in (1, -1):
            there = here + sign * j
            inside = (there >= 0) & (there < n)

            @pl.when(inside)
            def _(there=there):
                signal({"seq": lax.rem(there + n, n)})

            expected = expected + inside.astype(jnp.int32)
    pl.semaphore_wait(barrier, expected)


PROJECT_KINDS = (
    ("ai", D, BF),
    ("fi", D, BF),
    ("normed", D, BF),
    ("unit", D // 4, F32),
    ("inverse", 128, F32),
    ("qf", None, BF),
    ("kf", None, BF),
    ("v", None, BF),
    ("k", None, BF),
)


def feature_row(feat_ref, l):
    return jnp.concatenate([feat_ref[l, j : j + 1, :] for j in range(feat_ref.shape[1])], axis=1)


def project_chunk(l, h, c, last, x, params, tables, whole, out, packed, summed):
    gain, bias, w_ref, b_ref, feat_ref, map_ref, ones_ref = params
    cos, sin, keep = tables
    ai_ref, fi_ref, normed_ref, unit_ref, inv_ref, qf_ref, kf_ref, v_ref, k_ref = out
    mean = jnp.sum(x, axis=1, keepdims=True) * (1.0 / D)
    center = x - mean
    inverse = lax.rsqrt(jnp.sum(center * center, axis=1, keepdims=True) * (1.0 / D) + EPSILON)
    normed = center * inverse
    inv_ref[...] = jnp.broadcast_to(inverse, inv_ref.shape)
    normed_ref[...] = normed.astype(BF)
    whole[...] = normed
    unit_ref[...] = whole[:, block_columns(h, 0, unit_ref.shape[1])]
    attention_input = (normed * gain[l, 0:1] + bias[l, 0:1]).astype(BF)
    ai_ref[...] = attention_input
    fi_ref[...] = (normed * gain[l, 1:2] + bias[l, 1:2]).astype(BF)
    projected = dot_nn(attention_input, w_ref[...]) + b_ref[l : l + 1, :]
    q, k, v = split_heads(projected)
    v = v.astype(BF)
    q_turn = q * cos + swap_pairs(q) * sin
    k_turn = k * cos + swap_pairs(k) * sin
    query_feat = jnp.exp(dot_nn(q_turn, map_ref[...], HIGHEST))
    key_norm = head_sum(k * k, ones_ref[...]) * (0.5 / HEAD_DIM)
    key_feat = (
        keep
        * feature_row(feat_ref, l)
        * jnp.exp(dot_nn(k_turn, map_ref[...], HIGHEST) - key_norm)
    ).astype(BF)
    qf_ref[...] = query_feat.astype(BF)
    kf_ref[...] = key_feat
    v_ref[...] = v
    k_ref[...] = k.astype(BF)
    place = (row_of((CHUNK, 1)) + c * CHUNK).astype(F32)
    masked = jnp.where(place >= last, key_feat.astype(F32), 0.0)

    @pl.when(c == 0)
    def _():
        summed[...] = jnp.zeros_like(summed)
        packed[...] = jnp.zeros_like(packed)

    summed[...] += dot_tn(masked.astype(BF), v)
    packed[FEATURES : FEATURES + 1, :] += jnp.sum(masked, axis=0, keepdims=True)


def raise_chunk(l, fi, w_ref, b_ref, act_ref, slope_ref):
    raised = dot_nn(fi, w_ref[...]) + b_ref[l : l + 1, :]
    cumulative = 0.5 + 0.5 * lax.erf(raised * math.sqrt(0.5))
    density = jnp.exp(raised * raised * -0.5) * (1.0 / math.sqrt(2.0 * math.pi))
    act_ref[...] = (raised * cumulative).astype(BF)
    slope_ref[...] = (cumulative + raised * density).astype(BF)


def remote_call(kernel, name, ident, grid, in_specs, out_specs, out_shape, scratch, flops, args):
    moved = sum(int(np.prod(a.shape)) * a.dtype.itemsize for a in list(args) + list(out_shape))
    return pl.pallas_call(
        kernel,
        name=name,
        grid=grid,
        in_specs=in_specs,
        out_specs=out_specs,
        scratch_shapes=scratch,
        out_shape=out_shape,
        compiler_params=pltpu.CompilerParams(
            collective_id=ident, has_side_effects=True, vmem_limit_bytes=VMEM_BYTES
        ),
        cost_estimate=pl.CostEstimate(flops=int(flops), bytes_accessed=moved, transcendentals=0),
    )(*args)


class Names:
    pass


def named_call(kernel, name, ident, grid, ins, outs, scratch, flops, late=None, sent=None):
    late, sent = late or {}, sent or {}
    shared = {k: v[1] for k, v in sent.items() if isinstance(v, tuple)}
    sent = {k: v[0] if isinstance(v, tuple) else v for k, v in sent.items()}
    labels, groups = list(ins) + list(late) + list(outs) + list(sent), list(scratch)
    layers = {k: v if isinstance(v, tuple) else (v, None) for k, v in late.items()}
    anywhere = pl.BlockSpec(memory_space=pl.ANY)

    def body(*refs):
        names = Names()
        names.late, names.sent = Names(), Names()
        far = {}
        for label, ref in zip(labels, refs):
            if label in late or label in sent:
                far[label] = ref
            else:
                setattr(names, label, ref)
        at = len(labels)
        for label in list(late) + list(sent):
            if label in shared:
                held, sem = getattr(names, shared[label]), refs[at]
                at -= 1
            else:
                held, sem = refs[at], refs[at + 1]
            setattr(names, label, held)
            if label in late:
                layer = layers[label][1]
                source = far[label] if layer is None else far[label].at[layer]
                setattr(names.late, label, pltpu.make_async_copy(source, held, sem))
            else:
                setattr(names.sent, label, pltpu.make_async_copy(held, far[label], sem))
            at += 2
        for label in groups:
            size = len(scratch[label])
            held = refs[at : at + size]
            setattr(names, label, held if size > 1 else held[0])
            at += size
        kernel(names)

    moved = []
    for array, layer in layers.values():
        shape = array.shape if layer is None else array.shape[1:]
        moved += [pltpu.VMEM(shape, array.dtype), pltpu.SemaphoreType.DMA]
    for label, shape in sent.items():
        if label not in shared:
            moved.append(pltpu.VMEM(shape.shape, shape.dtype))
        moved.append(pltpu.SemaphoreType.DMA)
    result = remote_call(
        body,
        name,
        ident,
        grid,
        [spec for array, spec in ins.values()] + [anywhere] * len(late),
        [spec for shape, spec in outs.values()] + [anywhere] * len(sent),
        [shape for shape, spec in outs.values()] + list(sent.values()),
        moved + [item for label in groups for item in scratch[label]],
        flops,
        [array for array, spec in ins.values()] + [array for array, layer in layers.values()],
    )
    return dict(zip(list(outs) + list(sent), result))


def every(names):
    return [getattr(names, label) for label in vars(names)]


def fixed(shape):
    return pl.BlockSpec(shape, lambda *i: (0,) * len(shape), pipeline_mode=pl.Buffered(1))


def layer_of(array, l):
    return pl.BlockSpec(
        (None,) + array.shape[1:], lambda *i: (l, 0, 0), pipeline_mode=pl.Buffered(1)
    )


def clipped(step, low, count):
    return jnp.minimum(jnp.maximum(step - low, 0), count - 1)


def up_rows(width, low, count):
    return pl.BlockSpec((CHUNK, width), lambda i: (clipped(i, low, count), 0))


def down_rows(width, low, count):
    return pl.BlockSpec((CHUNK, width), lambda i: (count - 1 - clipped(i, low, count), 0))


def down_cube(shape, low, count):
    return pl.BlockSpec(
        (1,) + shape, lambda i: (count - 1 - clipped(i, low, count),) + (0,) * len(shape)
    )


def struct(shape, kind):
    return jax.ShapeDtypeStruct(shape, kind)


def project_params(z):
    return (z.gain, z.bias, z.qkv_w, z.qkv_b, z.feats, z.map_t, z.ones)


def project_refs(z):
    return (z.ai, z.fi, z.normed, z.unit, z.inverse, z.qf, z.kf, z.v, z.k)


def project_made(rows, a, spec):
    return dict(
        (name, (struct((rows, width or a), kind), spec(width or a)))
        for name, width, kind in PROJECT_KINDS
    )


class Column:
    def __init__(self, ref, lane):
        self.ref, self.lane = ref, lane

    def __getitem__(self, key):
        rows = slice(None) if key is Ellipsis else key[0]
        return self.ref[rows, self.lane : self.lane + 1]


def begin_keep(ref):
    return Column(ref, 0), Column(ref, 64)


def lanes_to_column(row):
    shape = (row.shape[1], row.shape[1])
    eye = row_of(shape) == lane_of(shape)
    return jnp.sum(jnp.where(eye, row, 0.0), axis=1, keepdims=True)


def enter_kernel(n, z):
    c = pl.program_id(0)
    count = pl.num_programs(0)
    h = lax.axis_index("head")
    rows, width = z.acts.shape
    first = lax.axis_index("seq") * rows
    gather = Gather(h, z.acts, z.gather[:3], z.gather[3:])

    @pl.when(c == 0)
    def _():
        for copy in every(z.late):
            copy.start()
        greet(h, n, 0)
        for i in range(rows // CHUNK):
            gather.start(i)
        for i in range(rows // CHUNK):
            part = slice(i * CHUNK, (i + 1) * CHUNK)
            slots = row_of((CHUNK, 1)) + i * CHUNK + first
            begins = begin_column(z.lengths, slots)
            starts = (begins - first).astype(F32)
            keep = jnp.concatenate(
                [
                    lanes_to_column(z.keep_mask[j : j + 1, :].astype(F32))
                    for j in range(i * CHUNK // 128, (i + 1) * CHUNK // 128)
                ],
                axis=0,
            )
            z.columns[part, :] = jnp.where(lane_of((CHUNK, 128)) < 64, starts, keep)
            phase = (slots - begins).astype(F32) * z.rates[0:1, :]
            z.cos[part, :] = jnp.cos(phase)
            z.sin[part, :] = jnp.sin(phase) * z.rates[1:2, :]
        gather.relay(0)
        for copy in every(z.late):
            copy.wait()

    gather.ready(c)
    for r, part in enumerate(gather.pieces(c)):
        z.full[:, block_columns(h, r, width)] = part
    last = (begin_scalar(z.lengths, first + rows - 1) - first).astype(F32)
    here = rows_at(c)
    keep = begin_keep(z.columns)[1]
    tables = (twice(z.cos[here, :]), twice(z.sin[here, :]), keep[here, :])
    project_chunk(
        0,
        h,
        c,
        last,
        z.full[...].astype(F32),
        project_params(z),
        tables,
        z.whole,
        project_refs(z),
        z.packed,
        z.summed,
    )

    @pl.when(c + 1 < count)
    def _():
        gather.relay(c + 1)

    @pl.when(c + 1 == count)
    def _():
        z.packed[0:FEATURES, :] = pack_state(z.summed[...])
        for i in range(rows // CHUNK):
            gather.finish(i)


def enter(n, lengths, acts, keep_mask, gain, bias, qkv_w, qkv_b, feats, rates, consts):
    rows, width = acts.shape
    a = consts["ones"].shape[0]
    table = rates.shape[1]
    ins = dict(
        lengths=(lengths, pl.BlockSpec(memory_space=pltpu.SMEM)),
        acts=(acts, fixed(acts.shape)),
        keep_mask=(keep_mask, fixed(keep_mask.shape)),
        gain=(gain, fixed(gain.shape)),
        bias=(bias, fixed(bias.shape)),
        qkv_b=(qkv_b, fixed(qkv_b.shape)),
        feats=(feats, fixed(feats.shape)),
        rates=(rates, fixed(rates.shape)),
    )
    late = dict(qkv_w=(qkv_w, 0), map_t=consts["map_t"], ones=consts["ones"])
    outs = dict(
        full=(struct((rows, D), BF), rowed(D)),
        cos=(struct((rows, table), F32), full((rows, table))),
        sin=(struct((rows, table), F32), full((rows, table))),
        columns=(struct((rows, 128), F32), full((rows, 128))),
        **project_made(rows, a, rowed),
        packed=(struct((STATE_ROWS, a), F32), full((STATE_ROWS, a))),
    )
    scratch = dict(
        gather=Gather.scratch(rows, width),
        summed=[pltpu.VMEM((a, a), F32)],
        whole=[pltpu.VMEM((CHUNK, D), F32)],
    )
    return named_call(
        functools.partial(enter_kernel, n),
        "enter",
        2,
        (rows // CHUNK,),
        ins,
        outs,
        scratch,
        2 * rows * D * 3 * a * 2,
        late,
    )


def between_kernel(n, hops, l, z):
    step = pl.program_id(0)
    count = pl.num_programs(0) // 2
    h = lax.axis_index("head")
    rows, width = z.mine.shape
    first = lax.axis_index("seq") * rows
    chunks = rows // CHUNK
    gather = Gather(h, z.mine, z.gather[:3], z.gather[3:])
    begin, keep = begin_keep(z.columns)
    scatter = Scatter(h, z.scatter[:5], z.scatter[5:])
    hand = HandOver(n, hops, rows, 1, z.state_own, z.hand[0], z.hand[1:])

    def send_sum(c):
        z.mine[rows_at(c), :] = scatter.total(c).astype(BF)
        gather.start(c)

    @pl.when(step == 0)
    def _():
        z.late.up_w.start()
        hand.clear()
        greet(h, n, hops)
        hand.start()
        z.late.up_w.wait()
        z.late.out_w.start()
        z.late.down_w.start()

    @pl.when(step < count)
    def _():
        raise_chunk(l, z.fi_in[...], z.up_w, z.up_b, z.act, z.slope)

        @pl.when(step == 0)
        def _():
            z.state_in[...] = hand.total(z.lengths)

        @pl.when(step >= 3)
        def _():
            gather.relay(step - 3)

        attention_chunk(
            step,
            (z.qf_in, z.kf_in, z.v_in, begin, keep, z.state_in, z.ones),
            (z.att, z.att_low, z.ratio, z.states, z.totals),
            z.state,
            z.total,
        )

        @pl.when(step == 0)
        def _():
            z.late.out_w.wait()
            z.late.down_w.wait()

        @pl.when(step == 1)
        def _():
            z.late.qkv_w.start()
            z.late.up_w_next.start()

        @pl.when(step >= 1)
        def _():
            scatter.relay(step - 1)

        z.whole_low[...] = (
            dot_nt(z.att_low[...], z.out_w[...]) + dot_nt(z.act[...], z.down_w[...])
        ).astype(BF)
        scatter.put(h, step, z.whole_low)

        @pl.when(step >= 2)
        def _():
            send_sum(step - 2)

    @pl.when(step >= count)
    def _():
        c = step - count

        @pl.when(c == 0)
        def _():
            scatter.relay(chunks - 1)
            z.late.qkv_w.wait()
            z.late.up_w_next.wait()
            gather.relay(1)

        gather.ready(c)
        for r, part in enumerate(gather.pieces(c)):
            z.whole[:, block_columns(h, r, width)] = part.astype(F32)
        x = z.full[...].astype(F32) + z.whole[...] + z.res_b[l : l + 1, :]
        z.whole[...] = x
        z.own[...] = z.whole[:, block_columns(h, 0, width)]
        last = (begin_scalar(z.lengths, first + rows - 1) - first).astype(F32)
        tables = (twice(z.cos[...]), twice(z.sin[...]), begin_keep(z.columns_next)[1][...])
        project_chunk(
            l + 1,
            h,
            c,
            last,
            x,
            project_params(z),
            tables,
            z.whole,
            project_refs(z),
            z.packed,
            z.summed,
        )

        @pl.when(c == 0)
        def _():
            send_sum(chunks - 2)

        @pl.when(c + 1 == chunks)
        def _():
            z.packed[0:FEATURES, :] = pack_state(z.summed[...])

        raise_chunk(l + 1, z.fi[...], z.up_w_next, z.up_b, z.act_next, z.slope_next)

        @pl.when(c == 0)
        def _():
            send_sum(chunks - 1)

        @pl.when((c >= 1) & (c + 1 < chunks))
        def _():
            gather.relay(c + 1)

        @pl.when(c + 1 == chunks)
        def _():
            for i in range(chunks):
                gather.finish(i)
                scatter.finish(i)


def between(n, hops, l, lengths, entered, params, consts):
    gain, bias, qkv_w, qkv_b, feats, up_w, up_b, out_w, down_w, res_b = params
    rows, a = entered["qf"].shape
    hidden = up_w.shape[2]
    chunks = rows // CHUNK
    width = D // 4

    def early(w):
        return up_rows(w, 0, chunks)

    def after(w):
        return up_rows(w, chunks, chunks)

    def cube(shape):
        return pl.BlockSpec((1,) + shape, lambda i: (clipped(i, 0, chunks),) + (0,) * len(shape))

    table = entered["cos"].shape[1]
    ins = dict(
        lengths=(lengths, pl.BlockSpec(memory_space=pltpu.SMEM)),
        qf_in=(entered["qf"], early(a)),
        kf_in=(entered["kf"], early(a)),
        v_in=(entered["v"], early(a)),
        fi_in=(entered["fi"], early(D)),
        columns=(entered["columns"], early(128)),
        state_own=(entered["packed"], fixed((STATE_ROWS, a))),
        up_b=(up_b, fixed(up_b.shape)),
        ones=(consts["ones"], fixed((a, a))),
        full=(entered["full"], after(D)),
        res_b=(res_b, fixed(res_b.shape)),
        gain=(gain, fixed(gain.shape)),
        bias=(bias, fixed(bias.shape)),
        qkv_b=(qkv_b, fixed(qkv_b.shape)),
        feats=(feats, fixed(feats.shape)),
        map_t=(consts["map_t"], fixed((a, a))),
        cos=(entered["cos"], after(table)),
        sin=(entered["sin"], after(table)),
        columns_next=(entered["columns"], after(128)),
    )
    late = dict(
        up_w=(up_w, l),
        out_w=(out_w, l),
        down_w=(down_w, l),
        qkv_w=(qkv_w, l + 1),
        up_w_next=(up_w, l + 1),
    )
    outs = dict(
        att=(struct((rows, a), F32), early(a)),
        att_low=(struct((rows, a), BF), early(a)),
        ratio=(struct((rows, a), F32), early(a)),
        states=(struct((chunks, a, a), F32), cube((a, a))),
        totals=(struct((chunks, 8, a), F32), cube((8, a))),
        act=(struct((rows, hidden), BF), early(hidden)),
        slope=(struct((rows, hidden), BF), early(hidden)),
        own=(struct((rows, width), F32), after(width)),
        **project_made(rows, a, after),
        act_next=(struct((rows, hidden), BF), after(hidden)),
        slope_next=(struct((rows, hidden), BF), after(hidden)),
        packed=(struct((STATE_ROWS, a), F32), full((STATE_ROWS, a))),
    )
    scratch = dict(
        gather=Gather.scratch(rows, width),
        scatter=Scatter.scratch(rows, width),
        hand=HandOver.scratch(hops, a),
        mine=[pltpu.VMEM((rows, width), BF)],
        state_in=[pltpu.VMEM((STATE_ROWS, a), F32)],
        summed=[pltpu.VMEM((a, a), F32)],
        whole=[pltpu.VMEM((CHUNK, D), F32)],
        whole_low=[pltpu.VMEM((CHUNK, D), BF)],
        state=[pltpu.VMEM((a, a), F32)],
        total=[pltpu.VMEM((8, a), F32)],
    )
    return named_call(
        functools.partial(between_kernel, n, hops, l),
        "between",
        3,
        (2 * chunks,),
        ins,
        outs,
        scratch,
        2 * rows * D * (hidden * 3 + 4 * a) * 2,
        late,
    )


def pair_mask(begin, step):
    shape = (CHUNK, CHUNK)
    t = row_of(shape)
    s = lane_of(shape)
    return (s <= t) & ((s + step * CHUNK).astype(F32) >= begin)


def attention_chunk(step, refs, out, state, total):
    qf_ref, kf_ref, v_ref, begin_ref, keep_ref, in_ref, ones_ref = refs
    att_ref, low_ref, ratio_ref, states_ref, totals_ref = out

    @pl.when(step == 0)
    def _():
        state[...] = unpack_state(in_ref[0:FEATURES, :])
        total[...] = jnp.broadcast_to(in_ref[FEATURES : FEATURES + 1, :], total.shape)

    q = qf_ref[...]
    k = kf_ref[...]
    v = v_ref[...]
    begin = begin_ref[...]
    keep = keep_ref[...]
    ones = ones_ref[...]
    a = q.shape[1]
    mask = pair_mask(begin, step)
    head_of = lane_of((1, a)) // HEAD_DIM
    held = state[...]
    held_total = total[0:1, :]
    states_ref[0] = held
    totals_ref[0] = total[...]
    base = (step * CHUNK).astype(F32)
    use = jnp.where(begin < base, 1.0, 0.0)
    high, low = halves(held)
    num = use * (dot_nn(q, high) + dot_nn(q, low))
    den = use * head_sum(q.astype(F32) * held_total, ones)
    for head in range(a // HEAD_DIM):
        own = (head_of == head).astype(BF)
        scores = dot_nt(q * own, k)
        scores_low = jnp.where(mask, scores, 0.0).astype(BF)
        num = num + dot_nn(scores_low, v * own)
        den = den + dot_nn(scores_low, jnp.broadcast_to(own, (CHUNK, a)))
    ratio = keep / (den + 1.0 - keep)
    att = num * ratio
    ratio_ref[...] = ratio
    att_ref[...] = att
    low_ref[...] = att.astype(BF)
    end = begin[CHUNK - 1 : CHUNK, :]
    place = (row_of((CHUNK, 1)) + step * CHUNK).astype(F32)
    masked = jnp.where(place >= end, k.astype(F32), 0.0)
    passing = jnp.where(end < base, 1.0, 0.0)
    state[...] = passing * held + jnp.where(
        block_diagonal(a), dot_tn(masked.astype(BF), v), 0.0
    )
    total[...] = jnp.broadcast_to(
        passing * held_total + jnp.sum(masked, axis=0, keepdims=True), total.shape
    )


def lower_feed(grad, dw_ref, slope_ref, bias_ref, start):
    @pl.when(start)
    def _():
        bias_ref[...] = jnp.zeros_like(bias_ref)

    d_raised = (dot_nn(grad, dw_ref[...]) * slope_ref[...].astype(F32)).astype(BF)
    bias_ref[...] += jnp.sum(d_raised.astype(F32), axis=0, keepdims=True)
    return d_raised


def lower_attention(grad, ow_ref, ratio, att, qf, begin, ones, out, summed, packed, start):
    num_ref, den_ref = out

    @pl.when(start)
    def _():
        summed[...] = jnp.zeros_like(summed)
        packed[...] = jnp.zeros_like(packed)

    d_num = (dot_nn(grad, ow_ref[...]) * ratio).astype(BF)
    d_den = -head_sum(d_num.astype(F32) * att, ones)
    num_ref[...] = d_num
    den_ref[...] = d_den
    entering = jnp.where(begin < 0.0, qf.astype(F32), 0.0)
    summed[...] += dot_tn(entering.astype(BF), d_num)
    packed[FEATURES : FEATURES + 1, :] += jnp.sum(entering * d_den, axis=0, keepdims=True)


def tile_at(i):
    return pl.ds(pl.multiple_of(i * CHUNK, CHUNK), CHUNK)


def weight_tile(i, x_ref, y, out_ref):
    out_ref[tile_at(i), :] = dot_tn(x_ref[:, tile_at(i)], y).astype(BF)


def attention_back(turn, step, refs, state, total):
    (
        qf_ref,
        kf_ref,
        v_ref,
        num_ref,
        den_ref,
        begin_ref,
        states_ref,
        totals_ref,
        exit_ref,
    ) = refs

    @pl.when(turn == 0)
    def _():
        state[...] = unpack_state(exit_ref[0:FEATURES, :])
        total[...] = jnp.broadcast_to(exit_ref[FEATURES : FEATURES + 1, :], total.shape)

    q = qf_ref[...]
    k = kf_ref[...]
    v = v_ref[...]
    d_num = num_ref[...]
    d_den = den_ref[...]
    begin = begin_ref[...]
    a = q.shape[1]
    mask = pair_mask(begin, step)
    head_of = lane_of((1, a)) // HEAD_DIM
    base = (step * CHUNK).astype(F32)
    use = jnp.where(begin < base, 1.0, 0.0)
    end = begin[CHUNK - 1 : CHUNK, :]
    place = (row_of((CHUNK, 1)) + step * CHUNK).astype(F32)
    inside = jnp.where(place >= end, 1.0, 0.0)
    passing = jnp.where(end < base, 1.0, 0.0)
    held_high, held_low = halves(states_ref[0])
    held_total = totals_ref[0][0:1, :]
    after = state[...]
    after_total = total[0:1, :]
    after_high, after_low = halves(after)
    masked = (k.astype(F32) * inside).astype(BF)
    d_q = use * (dot_nt(d_num, held_high) + dot_nt(d_num, held_low) + d_den * held_total)
    d_k = inside * (dot_nt(v, after_high) + dot_nt(v, after_low) + after_total)
    d_v = dot_nn(masked, after_high) + dot_nn(masked, after_low)
    for head in range(a // HEAD_DIM):
        own = (head_of == head).astype(BF)
        q_own = q * own
        num_own = d_num * own
        scores_low = jnp.where(mask, dot_nt(q_own, k), 0.0).astype(BF)
        column = d_den[:, head * HEAD_DIM : head * HEAD_DIM + 1]
        d_scores = jnp.where(mask, dot_nt(num_own, v) + column, 0.0).astype(BF)
        d_q = d_q + dot_nn(d_scores, k * own)
        d_k = d_k + dot_tn(d_scores, q_own)
        d_v = d_v + dot_tn(scores_low, num_own)
    q_used = q.astype(F32) * use
    state[...] = passing * after + jnp.where(
        block_diagonal(a), dot_tn(q_used.astype(BF), d_num), 0.0
    )
    total[...] = jnp.broadcast_to(
        passing * after_total + jnp.sum(q_used * d_den, axis=0, keepdims=True), total.shape
    )
    return d_q, d_k, d_v


def features_back(grads, refs, feat_ref, bias_ref, start):
    d_q, d_k, d_v = grads
    qf_ref, kf_ref, k_ref, cos_ref, sin_ref, map_ref, ones_ref = refs

    @pl.when(start)
    def _():
        feat_ref[...] = jnp.zeros_like(feat_ref)
        bias_ref[...] = jnp.zeros_like(bias_ref)

    cos = twice(cos_ref[...])
    sin = twice(sin_ref[...])
    d_query = dot_nn(d_q * qf_ref[...].astype(F32), map_ref[...], HIGHEST)
    d_query = d_query * cos - swap_pairs(d_query) * sin
    d_key_log = d_k * kf_ref[...].astype(F32)
    feat_ref[...] += jnp.sum(d_key_log, axis=0, keepdims=True)
    d_key = dot_nn(d_key_log, map_ref[...], HIGHEST)
    d_key = d_key * cos - swap_pairs(d_key) * sin
    d_key = d_key - head_sum(d_key_log, ones_ref[...]) * k_ref[...].astype(F32) * (1.0 / HEAD_DIM)
    d_proj = join_heads(d_query, d_key, d_v).astype(BF)
    bias_ref[...] += jnp.sum(d_proj.astype(F32), axis=0, keepdims=True)
    return d_proj


def inputs_back(l, d_proj, raised_ref, w_ref, up_ref, normed_ref, gain, sums_ref, start):
    @pl.when(start)
    def _():
        sums_ref[...] = jnp.zeros_like(sums_ref)

    normed = normed_ref[...].astype(F32)
    d_attention = dot_nt(d_proj, w_ref[...])
    d_feed = dot_nt(raised_ref[...], up_ref[...])
    sums_ref[0:1, :] += jnp.sum(d_attention * normed, axis=0, keepdims=True)
    sums_ref[1:2, :] += jnp.sum(d_feed * normed, axis=0, keepdims=True)
    sums_ref[2:3, :] += jnp.sum(d_attention, axis=0, keepdims=True)
    sums_ref[3:4, :] += jnp.sum(d_feed, axis=0, keepdims=True)
    d_normed = (d_attention * gain[l, 0:1] + d_feed * gain[l, 1:2]).astype(BF)
    high, low = halves(d_normed.astype(F32) * normed)
    row = jnp.ones((8, D), BF)
    first = dot_nt(row, d_normed)
    second = dot_nt(row, high) + dot_nt(row, low)
    return d_normed, jnp.where(row_of(first.shape) == 0, first, second)


class RowSum:
    def __init__(self, h, buffers, sems):
        self.own, self.got, self.middle, self.across = buffers
        self.send, self.recv = sems
        self.beside = {"head": lax.bitwise_xor(h, 1)}
        self.beyond = {"head": lax.bitwise_xor(h, 2)}

    @staticmethod
    def scratch(rows):
        count = rows // CHUNK
        return [pltpu.VMEM((count, 8, CHUNK), F32)] * 4 + [pltpu.SemaphoreType.DMA((2, count))] * 2

    def copy(self, kind, c):
        source, target, where = (
            (self.own, self.got, self.beside),
            (self.middle, self.across, self.beyond),
        )[kind]
        return push(
            source.at[c], target.at[c], self.send.at[kind, c], self.recv.at[kind, c], where
        )

    def put(self, c, value):
        self.own[c] = value
        self.copy(0, c).start()

    def relay(self, c):
        self.copy(0, c).wait_recv()
        self.middle[c] = self.own[c] + self.got[c]
        self.copy(1, c).start()

    def total(self, c):
        self.copy(1, c).wait_recv()
        value = self.middle[c] + self.across[c]
        shape = (8, 128)
        eye = (row_of(shape) == lane_of(shape)).astype(F32)
        columns = dot_tn(value, eye, HIGHEST)
        return columns[:, 0:1], columns[:, 1:2]

    def finish(self, c):
        self.copy(0, c).wait_send()
        self.copy(1, c).wait_send()


def norm_back(before, inverse, unit, d_normed, sums):
    first, second = sums
    return before + inverse * (d_normed - first * (1.0 / D) - unit * (second * (1.0 / D)))


def ring_place(index, n):
    return jnp.where(index % 2 == 0, index // 2, n - 1 - index // 2)


def ring_index(place, n):
    return jnp.where(place < n // 2, 2 * place, 2 * (n - 1 - place) + 1)


BATCHES = 6


class Ring:
    def __init__(self, n, parts, source, held, sems, since=0, until=BATCHES, incoming=None):
        self.n, self.parts, self.source, self.held = n, parts, source, held
        self.send_sem, self.recv_sem = sems
        self.since, self.until, self.incoming = since, until, incoming
        self.share = D // n
        self.place = ring_place(lax.axis_index("seq"), n)
        self.right = ring_index(lax.rem(self.place + 1, n), n)
        self.left = ring_index(lax.rem(self.place + n - 1, n), n)
        self.base = self.slots(n, since, until)[0]
        self.first = 0 if incoming is None else self.bound(n, since)
        self.last = self.bound(n, until) - 1

    @staticmethod
    def bound(n, batch):
        return 1 + (n - 2) * batch // BATCHES

    @staticmethod
    def slots(n, since, until):
        base = Ring.bound(n, since) - 1
        return base, Ring.bound(n, until) - base

    @staticmethod
    def buffers(n, parts, since=0, until=BATCHES):
        count = Ring.slots(n, since, until)[1]
        return [pltpu.VMEM((count, D // n, part[2]), BF) for part in parts]

    @staticmethod
    def sems(n, parts):
        return [pltpu.SemaphoreType.DMA((len(parts), n - 1))] * 2

    def own(self, part, step):
        array, start, width, way = part
        n = self.n
        ahead = lax.rem(self.place - way * (1 + step) + 2 * n, n)
        rows = pl.ds(pl.multiple_of(ring_index(ahead, n) * self.share, self.share), self.share)
        return self.source[array].at[rows, pl.ds(start, width)]

    def slot(self, r, step):
        return self.held[r].at[step - self.base]

    def copy(self, r, step, block):
        return push(
            block,
            self.slot(r, step),
            self.send_sem.at[r, step],
            self.recv_sem.at[r, step],
            {"seq": self.right if self.parts[r][3] > 0 else self.left},
        )

    def add(self, r, step, arrived):
        own = self.own(self.parts[r], step)[...].astype(F32)
        block = self.slot(r, step - 1)
        block[...] = (arrived[...].astype(F32) + own).astype(BF)
        self.copy(r, step, block).start()

    def start(self):
        for r, part in enumerate(self.parts):
            if self.incoming is not None:
                self.add(r, self.first, self.incoming[r])
            else:
                self.copy(r, 0, self.own(part, 0)).start()

    def tick(self, step):
        for r in range(len(self.parts)):
            block = self.slot(r, step - 1)
            self.copy(r, step - 1, block).wait_recv()
            self.add(r, step, block)

    def batch(self, k):
        low, high = self.bound(self.n, k - 1), self.bound(self.n, k)
        if self.incoming is not None and k - 1 == self.since:
            low += 1
        if high - low == 1:
            self.tick(low)
        elif high > low:

            def one(step, carry):
                self.tick(step)
                return carry

            lax.fori_loop(low, high, one, 0)

    def sent(self):
        def one(step, carry):
            for r in range(len(self.parts)):
                self.copy(r, step, self.slot(r, step)).wait_send()
            return carry

        lax.fori_loop(self.first, self.last + 1, one, 0)

    def pause(self, out):
        for r in range(len(self.parts)):
            block = self.slot(r, self.last)
            self.copy(r, self.last, block).wait_recv()
            out[r][...] = block[...]
        self.sent()

    def finish(self, out):
        n = self.n
        for r, part in enumerate(self.parts):
            block = self.slot(r, n - 2)
            self.copy(r, n - 2, block).wait_recv()
            array, start, width, way = part
            out[array][:, pl.ds(start, width)] = block[...].astype(F32) + self.own(part, n - 1)[
                ...
            ].astype(F32)
        self.sent()


def halved(array, width, start=0):
    return (
        (array, start, width // 2, 1),
        (array, start + width // 2, width // 2, -1),
    )


def ring_out(n, parts):
    return [jax.ShapeDtypeStruct((D // n, part[2]), BF) for part in parts]


CREST_DOWN, CREST_UP, TURN_REST, TURN_DOWN, TURN_UP = 2, 2, 4, 1, 0


def loop(count, body):
    def one(c, carry):
        body(c)
        return carry

    lax.fori_loop(0, count, one, 0)


def unrolled(count, body):
    for c in range(count):
        body(jnp.int32(c))


def crest_kernel(n, hops, l, z):
    step = pl.program_id(0)
    h = lax.axis_index("head")
    rows, hidden = z.act.shape
    width = D // 4
    count = rows // CHUNK
    hand = HandOver(n, hops, rows, 1, z.state_own, z.hand[0], z.hand[1:])
    hand_back = HandOver(n, hops, rows, -1, z.packed, z.hand_back[0], z.hand_back[1:])
    begin, keep = begin_keep(z.columns)
    parts = halved(0, hidden)
    corner = push(
        z.grad_across,
        z.grad_corner,
        z.corner_sems.at[0],
        z.corner_sems.at[1],
        {"head": lax.bitwise_xor(h, 1)},
    )
    down = Ring(n, parts, (z.d_down,), z.down_held, z.down_sems, 0, CREST_DOWN)
    up = Ring(n, parts, (z.d_up,), z.up_held, z.up_sems, 0, CREST_UP)
    columns = pl.ds(pl.multiple_of(h * width, width), width)

    @pl.when(step == 0)
    def _():
        for copy in (
            z.late.grad_across,
            z.late.grad_own,
            z.late.grad_beside,
            z.late.down_w,
            z.late.slope,
        ):
            copy.start()
        hand.clear()
        hand_back.clear()
        greet(h, n, hops)
        hand.start()
        z.late.grad_across.wait()
        corner.start()
        z.d_res[...] = jnp.zeros_like(z.d_res)
        z.late.grad_own.wait()
        z.late.grad_beside.wait()
        for r, part in enumerate((z.grad_own, z.grad_beside, z.grad_across)):
            z.grad[:, block_columns(h, r, width)] = part[...]
        corner.wait_recv()
        z.grad[:, block_columns(h, 3, width)] = z.grad_corner[...]
        corner.wait_send()
        z.late.down_w.wait()
        z.late.slope.wait()
        z.late.act.start()

        def feed(c):
            here = rows_at(c)
            z.d_raised[here, :] = lower_feed(
                z.grad[here, :], z.down_w, z.slope.at[here, :], z.d_up_b, c == 0
            )
            z.d_res[...] += jnp.sum(z.grad[here, columns].astype(F32), axis=0, keepdims=True)

        unrolled(count, feed)
        z.sent.d_raised.start()
        z.late.act.wait()
        z.late.fi.start()
        unrolled(D // CHUNK, lambda i: weight_tile(i, z.grad, z.act[...], z.d_down))
        down.start()
        z.sent.d_down.start()
        z.late.fi.wait()
        z.late.out_w.start()
        unrolled(D // CHUNK, lambda i: weight_tile(i, z.fi, z.d_raised[...], z.d_up))
        up.start()
        z.sent.d_up.start()
        z.late.out_w.wait()
        z.state_in[...] = hand.total(z.lengths)

    @pl.when((step >= 1) & (step <= count))
    def _():
        c = step - 1
        here = rows_at(c)
        attention_chunk(
            c,
            (z.qf, z.kf, z.v, begin, keep, z.state_in, z.ones),
            (z.att, z.low_now, z.ratio, z.states, z.totals),
            z.state,
            z.total,
        )
        low = z.low_now[...]
        z.low[here, :] = low
        z.whole[...] = (dot_nt(low, z.out_w[...]) + dot_nt(z.act[here, :], z.down_w[...])).astype(
            BF
        )
        z.near[0] = z.whole[:, block_columns(h, 0, width)]
        z.near[1] = z.whole[:, block_columns(h, 2, width)]
        z.far[0] = z.whole[:, block_columns(h, 1, width)]
        z.far[1] = z.whole[:, block_columns(h, 3, width)]
        lower_attention(
            z.grad[here, :],
            z.out_w,
            z.ratio[...],
            z.att[...],
            z.qf[...],
            begin[...],
            z.ones[...],
            (z.d_num, z.d_den),
            z.summed,
            z.packed,
            c == 0,
        )
        at_steps(
            c,
            (
                (0, lambda: down.batch(1)),
                (1, lambda: up.batch(1)),
                (2, lambda: down.batch(2)),
                (3, lambda: up.batch(2)),
            ),
        )

    @pl.when(step == count + 1)
    def _():
        z.packed[0:FEATURES, :] = pack_state(z.summed[...])
        hand_back.start()
        unrolled(D // CHUNK, lambda i: weight_tile(i, z.grad, z.low[...], z.d_out))
        z.exit_state[...] = hand_back.total(z.lengths)
        down.pause((z.down_fore, z.down_aft))
        up.pause((z.up_fore, z.up_aft))
        for copy in every(z.sent):
            copy.wait()


def crest(n, hops, l, lengths, mid, pieces, tables, params, consts):
    gain, bias, qkv_w, qkv_b, feats, up_w, up_b, out_w, down_w, res_b = params
    cos, sin, columns = tables
    rows, a = mid["qf"].shape
    hidden = up_w.shape[2]
    count = rows // CHUNK
    width = D // 4
    parts = halved(0, hidden)

    def block(w):
        return up_rows(w, 1, count)

    def cube(shape):
        return pl.BlockSpec((1,) + shape, lambda i: (clipped(i, 1, count),) + (0,) * len(shape))

    quarter = pl.BlockSpec((2, CHUNK, width), lambda i: (0, clipped(i, 1, count), 0))
    ins = dict(
        lengths=(lengths, pl.BlockSpec(memory_space=pltpu.SMEM)),
        qf=(mid["qf"], block(a)),
        kf=(mid["kf"], block(a)),
        v=(mid["v"], block(a)),
        columns=(columns, block(128)),
        state_own=(mid["packed"], fixed((STATE_ROWS, a))),
        ones=(consts["ones"], fixed((a, a))),
    )
    late = dict(
        grad_across=pieces[2],
        grad_own=pieces[0],
        grad_beside=pieces[1],
        down_w=(down_w, l),
        slope=mid["slope_next"],
        act=mid["act_next"],
        fi=mid["fi"],
        out_w=(out_w, l),
    )
    fore, aft = ring_out(n, parts)
    outs = dict(
        d_up_b=(struct((1, hidden), F32), full((1, hidden))),
        d_res=(struct((1, width), F32), full((1, width))),
        ratio=(struct((rows, a), F32), block(a)),
        att=(struct((rows, a), F32), block(a)),
        states=(struct((count, a, a), F32), cube((a, a))),
        totals=(struct((count, 8, a), F32), cube((8, a))),
        d_num=(struct((rows, a), BF), block(a)),
        d_den=(struct((rows, a), F32), block(a)),
        near=(struct((2, rows, width), BF), quarter),
        far=(struct((2, rows, width), BF), quarter),
        d_out=(struct((D, a), BF), full((D, a))),
        exit_state=(struct((STATE_ROWS, a), F32), full((STATE_ROWS, a))),
        up_fore=(fore, full(fore.shape)),
        up_aft=(aft, full(aft.shape)),
        down_fore=(fore, full(fore.shape)),
        down_aft=(aft, full(aft.shape)),
    )
    scratch = dict(
        grad=[pltpu.VMEM((rows, D), BF)],
        grad_corner=[pltpu.VMEM((rows, width), BF)],
        corner_sems=[pltpu.SemaphoreType.DMA((2,))],
        hand=HandOver.scratch(hops, a),
        hand_back=HandOver.scratch(hops, a),
        down_held=Ring.buffers(n, parts, 0, CREST_DOWN),
        up_held=Ring.buffers(n, parts, 0, CREST_UP),
        down_sems=Ring.sems(n, parts),
        up_sems=Ring.sems(n, parts),
        state_in=[pltpu.VMEM((STATE_ROWS, a), F32)],
        packed=[pltpu.VMEM((STATE_ROWS, a), F32)],
        summed=[pltpu.VMEM((a, a), F32)],
        state=[pltpu.VMEM((a, a), F32)],
        total=[pltpu.VMEM((8, a), F32)],
        whole=[pltpu.VMEM((CHUNK, D), BF)],
        low_now=[pltpu.VMEM((CHUNK, a), BF)],
        low=[pltpu.VMEM((rows, a), BF)],
    )
    return named_call(
        functools.partial(crest_kernel, n, hops, l),
        "crest",
        4,
        (count + 2,),
        ins,
        outs,
        scratch,
        2 * rows * D * (hidden * 4 + 4 * a) * 2,
        late,
        dict(
            d_raised=struct((rows, hidden), BF),
            d_down=struct((D, hidden), BF),
            d_up=struct((D, hidden), BF),
        ),
    )


def back_step(z, l, h, step, count, scatter, row_sum, middle_work, end_work):
    c = count - 1 - step
    grads = attention_back(
        step,
        c,
        (
            z.qf, z.kf, z.v, z.d_num, z.d_den, begin_keep(z.columns)[0], z.states, z.totals,
            z.exit_state,
        ),
        z.state,
        z.total,
    )

    @pl.when(step >= 1)
    def _():
        scatter.relay(c + 1)
        row_sum.relay(c + 1)

    middle_work()
    start = step == 0
    d_proj = features_back(
        grads,
        (z.qf, z.kf, z.k, z.cos, z.sin, z.map, z.ones),
        z.d_feat,
        z.d_qkv_b,
        start,
    )
    z.proj_all[rows_at(c), :] = d_proj

    @pl.when(start)
    def _():
        z.late.qkv_w.wait()
        z.late.up_w.wait()

    d_normed, sums = inputs_back(
        l, d_proj, z.d_raised_in, z.qkv_w, z.up_w, z.normed, z.gain, z.sums, start
    )
    z.whole[...] = d_normed
    scatter.put(h, c, z.whole)
    row_sum.put(c, sums)
    end_work()


def back_arrays(l, local, lowered, tables, params, consts, exit_state, count):
    gain, bias, qkv_w, qkv_b, feats, up_w, up_b, out_w, down_w, res_b = params
    cos, sin, columns = tables
    qf, kf, v, k, normed, unit, inverse, states, totals = local
    d_raised, d_num, d_den = lowered
    a = qf.shape[1]

    def early(w):
        return down_rows(w, 0, count)

    return dict(
        qf=(qf, early(a)),
        kf=(kf, early(a)),
        v=(v, early(a)),
        k=(k, early(a)),
        d_num=(d_num, early(a)),
        d_den=(d_den, early(a)),
        columns=(columns, early(128)),
        cos=(cos, early(cos.shape[1])),
        sin=(sin, early(sin.shape[1])),
        states=(states, down_cube((a, a), 0, count)),
        totals=(totals, down_cube((8, a), 0, count)),
        exit_state=(exit_state, fixed(exit_state.shape)),
        map=(consts["map"], fixed((a, a))),
        ones=(consts["ones"], fixed((a, a))),
        d_raised_in=(d_raised, early(d_raised.shape[1])),
        normed=(normed, early(D)),
        gain=(gain, fixed(gain.shape)),
    )


def back_scratch(rows, a, width):
    return dict(
        scatter=Scatter.scratch(rows, width),
        row_sum=RowSum.scratch(rows),
        state=[pltpu.VMEM((a, a), F32)],
        total=[pltpu.VMEM((8, a), F32)],
        whole=[pltpu.VMEM((CHUNK, D), BF)],
        proj_all=[pltpu.VMEM((rows, 3 * a), BF)],
    )


def at_steps(step, table):
    for at, work in table:

        @pl.when(step == at)
        def _(work=work):
            work()


def turn_kernel(n, hops, l, z):
    step = pl.program_id(0)
    h = lax.axis_index("head")
    rows, width = z.mine.shape
    hidden = z.act.shape[1]
    count = rows // CHUNK
    scatter = Scatter(h, z.scatter[:5], z.scatter[5:])
    row_sum = RowSum(h, z.row_sum[:4], z.row_sum[4:])
    gather = Gather(h, z.mine, z.gather[:3], z.gather[3:])
    hand = HandOver(n, hops, rows, -1, z.packed, z.hand[0], z.hand[1:])
    parts = halved(0, hidden)
    rest_parts = rest_of(z.d_qkv.shape[1], z.d_out_next.shape[1])
    down = Ring(
        n, parts, (z.d_down_next,), z.down_held, z.down_sems, CREST_DOWN,
        incoming=(z.down_fore, z.down_aft),
    )
    up = Ring(
        n, parts, (z.d_up_next,), z.up_held, z.up_sems, CREST_UP,
        incoming=(z.up_fore_in, z.up_aft_in),
    )
    rest = Ring(n, rest_parts, (z.d_qkv, z.d_out_next), z.rest_held, z.rest_sems, 0, TURN_REST)
    new_down = Ring(n, parts, (z.d_down,), z.new_down_held, z.new_down_sems, 0, TURN_DOWN)
    new_up = Ring(n, parts, (z.d_up,), z.new_up_held, z.new_up_sems, 0, TURN_UP)

    def sum_up(o):
        c = count - 1 - o
        here = rows_at(c)
        new = norm_back(
            z.before[here, :].astype(F32),
            z.inverse[here, 0:1],
            z.unit[here, :],
            scatter.total(c),
            row_sum.total(c),
        )
        z.after[here, :] = new
        z.mine[here, :] = new.astype(BF)
        z.d_res[...] += jnp.sum(new, axis=0, keepdims=True)
        gather.start(c)

    @pl.when(step == 0)
    def _():
        z.late.d_down_next.start()
        z.late.d_up_next.start()
        hand.clear()
        greet(h, n, hops)
        z.late.d_down_next.wait()
        down.start()
        z.late.d_up_next.wait()
        up.start()
        z.late.qkv_w.start()
        z.late.up_w.start()
        z.d_res[...] = jnp.zeros_like(z.d_res)

    @pl.when(step < count)
    def _():
        def middle_work():
            at_steps(
                step,
                (
                    (1, z.late.before.start),
                    (1, z.late.inverse.start),
                    (1, z.late.unit.start),
                    (2, z.late.ai.start),
                    (2, z.late.d_out_next.start),
                    (3, z.late.down_w.start),
                    (3, z.late.slope.start),
                    (1, lambda: up.batch(CREST_UP + 1)),
                    (1, lambda: up.batch(CREST_UP + 2)),
                    (2, lambda: up.batch(CREST_UP + 3)),
                    (2, z.late.before.wait),
                    (2, z.late.inverse.wait),
                    (2, z.late.unit.wait),
                    (3, lambda: up.batch(CREST_UP + 4)),
                ),
            )

        def end_work():
            at_steps(
                step,
                (
                    (0, lambda: down.batch(CREST_DOWN + 1)),
                    (0, lambda: down.batch(CREST_DOWN + 2)),
                    (1, lambda: down.batch(CREST_DOWN + 3)),
                    (2, lambda: down.batch(CREST_DOWN + 4)),
                ),
            )

            @pl.when(step >= 2)
            def _():
                sum_up(step - 2)

        back_step(z, l + 1, h, step, count, scatter, row_sum, middle_work, end_work)

    def feed(c):
        gather.ready(c)
        here = rows_at(c)
        for r, part in enumerate(gather.pieces(c)):
            z.grad[here, block_columns(h, r, width)] = part
        z.d_raised_out[here, :] = lower_feed(
            z.grad[here, :], z.down_w, z.slope.at[here, :], z.d_up_b, c == count - 1
        )

    def attention(c):
        here = rows_at(c)
        lower_attention(
            z.grad[here, :],
            z.out_w,
            z.ratio[here, :],
            z.att[here, :],
            z.qf_late[here, :],
            begin_keep(z.columns_late)[0][here, :],
            z.ones[...],
            (z.d_num_out.at[here, :], z.d_den_out.at[here, :]),
            z.summed,
            z.packed,
            c == count - 1,
        )

    def qkv_tiles(low, high):
        for i in range(low, high):
            weight_tile(i, z.ai, z.proj_all[...], z.d_qkv)

    @pl.when(step == count)
    def _():
        z.late.ai.wait()
        late_attention = (
            z.late.out_w,
            z.late.ratio,
            z.late.att,
            z.late.qf_late,
            z.late.columns_late,
        )
        for copy in late_attention:
            copy.start()
        z.late.act.start()
        qkv_tiles(0, 1)
        scatter.relay(0)
        row_sum.relay(0)
        gather.relay(count - 1)
        sum_up(count - 2)
        qkv_tiles(1, 4)
        z.late.d_out_next.wait()
        rest.start()
        z.sent.d_qkv.start()
        down.finish((z.sum_down,))
        z.late.down_w.wait()
        z.late.slope.wait()
        sum_up(count - 1)
        feed(jnp.int32(count - 1))
        gather.relay(count - 2)
        up.finish((z.sum_up,))
        feed(jnp.int32(count - 2))
        gather.relay(count - 3)
        for copy in late_attention:
            copy.wait()
        z.late.fi.start()
        z.late.att_low.start()
        loop(2, lambda i: attention(count - 1 - i))
        gather.relay(0)
        feed(jnp.int32(count - 3))
        attention(jnp.int32(count - 3))
        rest.batch(1)
        feed(jnp.int32(0))
        attention(jnp.int32(0))
        z.packed[0:FEATURES, :] = pack_state(z.summed[...])
        hand.start()
        rest.batch(2)
        z.sent.d_raised_out.start()
        z.sent.d_num_out.start()
        z.sent.d_den_out.start()
        z.late.act.wait()
        loop(D // CHUNK, lambda i: weight_tile(i, z.grad, z.act[...], z.d_down))
        new_down.start()
        z.sent.d_down.start()
        rest.batch(3)
        z.late.fi.wait()
        loop(D // CHUNK, lambda i: weight_tile(i, z.fi, z.d_raised_out[...], z.d_up))
        new_up.start()
        z.sent.d_up.start()
        z.late.att_low.wait()
        rest.batch(4)
        new_down.batch(1)
        loop(D // CHUNK, lambda i: weight_tile(i, z.grad, z.att_low[...], z.d_out))
        for i in range(count):
            gather.finish(i)
            scatter.finish(i)
            row_sum.finish(i)
        z.exit_out[...] = hand.total(z.lengths)
        new_up.pause((z.up_fore, z.up_aft))
        rest.pause((z.rest_a, z.rest_b, z.rest_c, z.rest_d))
        new_down.pause((z.new_fore, z.new_aft))
        for copy in every(z.sent):
            copy.wait()


def rest_of(qkv, out):
    return halved(0, qkv) + halved(1, out)


def turn(
    n, hops, l, lengths, local, top, before, ai, lower_in, tables, params, consts
):
    gain, bias, qkv_w, qkv_b, feats, up_w, up_b, out_w, down_w, res_b = params
    cos, sin, columns = tables
    act, slope, ratio, att, att_low, fi, qf = lower_in
    rows, a = qf.shape
    hidden = up_w.shape[2]
    count = rows // CHUNK
    width = D // 4
    share = D // n
    lowered = (top["d_raised"], top["d_num"], top["d_den"])
    parts = halved(0, hidden)
    rest_parts = rest_of(3 * a, a)

    def whole(array):
        return (array, fixed(array.shape))

    ins = dict(
        lengths=(lengths, pl.BlockSpec(memory_space=pltpu.SMEM)),
        **back_arrays(l + 1, local, lowered, tables, params, consts, top["exit_state"], count),
        down_fore=whole(top["down_fore"]),
        down_aft=whole(top["down_aft"]),
        up_fore_in=whole(top["up_fore"]),
        up_aft_in=whole(top["up_aft"]),
    )
    late = dict(
        d_down_next=top["d_down"],
        d_up_next=top["d_up"],
        qkv_w=(qkv_w, l + 1),
        up_w=(up_w, l + 1),
        before=before,
        inverse=local[6],
        unit=local[5],
        ai=ai,
        d_out_next=top["d_out"],
        down_w=(down_w, l),
        slope=slope,
        out_w=(out_w, l),
        ratio=ratio,
        att=att,
        qf_late=qf,
        columns_late=columns,
        act=act,
        fi=fi,
        att_low=att_low,
    )
    rests = ring_out(n, rest_parts)
    fore, aft = ring_out(n, parts)
    outs = dict(
        d_feat=(struct((1, a), F32), full((1, a))),
        d_qkv_b=(struct((1, 3 * a), F32), full((1, 3 * a))),
        sums=(struct((8, D), F32), full((8, D))),
        after=(struct((rows, width), F32), full((rows, width))),
        d_res=(struct((1, width), F32), full((1, width))),
        d_up_b=(struct((1, hidden), F32), full((1, hidden))),
        d_out=(struct((D, a), BF), full((D, a))),
        exit_out=(struct((STATE_ROWS, a), F32), full((STATE_ROWS, a))),
        sum_down=(struct((share, hidden), F32), full((share, hidden))),
        sum_up=(struct((share, hidden), F32), full((share, hidden))),
        rest_a=(rests[0], full(rests[0].shape)),
        rest_b=(rests[1], full(rests[1].shape)),
        rest_c=(rests[2], full(rests[2].shape)),
        rest_d=(rests[3], full(rests[3].shape)),
        new_fore=(fore, full(fore.shape)),
        new_aft=(aft, full(aft.shape)),
        up_fore=(fore, full(fore.shape)),
        up_aft=(aft, full(aft.shape)),
    )
    scratch = dict(
        **back_scratch(rows, a, width),
        gather=Gather.scratch(rows, width),
        hand=HandOver.scratch(hops, a),
        down_held=Ring.buffers(n, parts, CREST_DOWN),
        up_held=Ring.buffers(n, parts, CREST_UP),
        rest_held=Ring.buffers(n, rest_parts, 0, TURN_REST),
        new_down_held=Ring.buffers(n, parts, 0, TURN_DOWN),
        new_up_held=Ring.buffers(n, parts, 0, TURN_UP),
        down_sems=Ring.sems(n, parts),
        up_sems=Ring.sems(n, parts),
        rest_sems=Ring.sems(n, rest_parts),
        new_down_sems=Ring.sems(n, parts),
        new_up_sems=Ring.sems(n, parts),
        mine=[pltpu.VMEM((rows, width), BF)],
        packed=[pltpu.VMEM((STATE_ROWS, a), F32)],
        summed=[pltpu.VMEM((a, a), F32)],
        grad=[pltpu.VMEM((rows, D), BF)],
    )
    return named_call(
        functools.partial(turn_kernel, n, hops, l),
        "turn",
        5,
        (count + 1,),
        ins,
        outs,
        scratch,
        2 * rows * D * (hidden * 4 + 8 * a) * 2,
        late,
        dict(
            d_qkv=struct((D, 3 * a), BF),
            d_num_out=struct((rows, a), BF),
            d_den_out=struct((rows, a), F32),
            d_raised_out=(struct((rows, hidden), BF), "slope"),
            d_down=struct((D, hidden), BF),
            d_up=struct((D, hidden), BF),
        ),
    )


class Small:
    def __init__(self, h, n, refs, sems):
        self.near, self.far, self.got, self.middle, self.across, self.bundle, self.other = refs
        self.head_send, self.head_recv, self.seq_send, self.seq_recv = sems
        self.h, self.n = h, n
        self.here = lax.axis_index("seq")

    @staticmethod
    def rounds(n):
        return max(1, (n - 1).bit_length())

    @staticmethod
    def scratch(n, width):
        r = Small.rounds(n)
        dma = pltpu.SemaphoreType.DMA
        return (
            [pltpu.VMEM((2, 16, width), F32)] * 3
            + [pltpu.VMEM((16, width), F32)] * 2
            + [pltpu.VMEM((r + 1, 32, width), F32), pltpu.VMEM((r, 32, width), F32)]
            + [dma((2,)), dma((2,)), dma((r,)), dma((r,))]
        )

    def head_copy(self, kind):
        source, target, mask = (
            (self.far, self.got, 1),
            (self.middle, self.across, 2),
        )[kind]
        return push(
            source,
            target,
            self.head_send.at[kind],
            self.head_recv.at[kind],
            {"head": lax.bitwise_xor(self.h, mask)},
        )

    def seq_copy(self, k):
        return push(
            self.bundle.at[k],
            self.other.at[k],
            self.seq_send.at[k],
            self.seq_recv.at[k],
            {"seq": lax.bitwise_xor(self.here, 1 << k)},
        )

    def put(self, sums):
        width = self.near.shape[2]
        for l, ref in enumerate(sums):
            at = slice(8 * l, 8 * l + 8)
            self.near[0, at, :] = ref[:, block_columns(self.h, 0, width)]
            self.near[1, at, :] = ref[:, block_columns(self.h, 2, width)]
            self.far[0, at, :] = ref[:, block_columns(self.h, 1, width)]
            self.far[1, at, :] = ref[:, block_columns(self.h, 3, width)]
        self.head_copy(0).start()

    def relay(self):
        self.head_copy(0).wait_recv()
        self.middle[...] = self.near[1] + self.got[1]
        self.head_copy(1).start()

    def pack(self, rows):
        self.head_copy(1).wait_recv()
        norms = self.near[0] + self.got[0] + self.across[...]
        width = self.near.shape[2]
        self.bundle[0] = jnp.zeros_like(self.bundle[0])
        for l, refs in enumerate(rows):
            self.bundle[0, 16 * l : 16 * l + 4, :] = norms[8 * l : 8 * l + 4]
            at = 16 * l + 4
            for ref in refs:
                for i in range(ref.shape[1] // width):
                    self.bundle[0, at : at + 1, :] = ref[:, i * width : (i + 1) * width]
                    at += 1
        self.seq_copy(0).start()

    def round(self, k):
        self.seq_copy(k).wait_recv()
        self.bundle[k + 1] = self.bundle[k] + self.other[k]
        if k + 1 < self.rounds(self.n):
            self.seq_copy(k + 1).start()

    def finish(self):
        for kind in range(2):
            self.head_copy(kind).wait_send()
        for k in range(self.rounds(self.n)):
            self.seq_copy(k).wait_send()


def greet_all(h, n):
    barrier = pltpu.get_barrier_semaphore()

    def signal(where):
        pl.semaphore_signal(barrier, inc=1, device_id=where, device_id_type=pl.DeviceIdType.MESH)

    signal({"head": lax.bitwise_xor(h, 1)})
    signal({"head": lax.bitwise_xor(h, 2)})
    here = lax.axis_index("seq")
    place = ring_place(here, n)
    signal({"seq": ring_index(lax.rem(place + 1, n), n)})
    signal({"seq": ring_index(lax.rem(place + n - 1, n), n)})
    rounds = Small.rounds(n)
    for k in range(rounds):
        signal({"seq": lax.bitwise_xor(here, 1 << k)})
    pl.semaphore_wait(barrier, 4 + rounds)


def leave_kernel(n, z):
    step = pl.program_id(0)
    h = lax.axis_index("head")
    rows = z.proj_all.shape[0]
    count = rows // CHUNK
    hidden, a = z.d_down.shape[1], z.d_out.shape[1]
    scatter = Scatter(h, z.scatter[:5], z.scatter[5:])
    row_sum = RowSum(h, z.row_sum[:4], z.row_sum[4:])
    small = Small(h, n, z.small[:7], z.small[7:])
    rest = Ring(
        n, rest_of(3 * a, a), (z.d_qkv_next, z.d_out_next), z.rest_held, z.rest_sems, TURN_REST,
        incoming=(z.rest_a, z.rest_b, z.rest_c, z.rest_d),
    )
    down = Ring(
        n, halved(0, hidden), (z.d_down,), z.down_held, z.down_sems, TURN_DOWN,
        incoming=(z.new_fore, z.new_aft),
    )
    up = Ring(
        n, halved(0, hidden), (z.d_up,), z.up_held, z.up_sems, TURN_UP,
        incoming=(z.up_fore, z.up_aft),
    )
    out = Ring(n, halved(0, a), (z.d_out,), z.out_held, z.out_sems)
    first_parts, second_parts = split_last(3 * a)
    last = Ring(n, first_parts, (z.d_qkv,), z.last_held, z.last_sems)
    more = Ring(n, second_parts, (z.d_qkv,), z.more_held, z.more_sems)
    width = z.res_b.shape[1] // 4
    columns = pl.ds(pl.multiple_of(h * width, width), width)
    result = Scatter(h, (z.near, z.far) + tuple(z.result[:3]), z.result[3:])

    def sum_up(o):
        here = rows_at(count - 1 - o)
        z.after[here, :] = norm_back(
            z.before[here, :],
            z.inverse[here, 0:1],
            z.unit[here, :],
            scatter.total(count - 1 - o),
            row_sum.total(count - 1 - o),
        )

    @pl.when(step == 0)
    def _():
        z.late.d_qkv_next.start()
        z.late.d_down.start()
        z.late.d_up.start()
        greet_all(h, n)
        z.late.d_qkv_next.wait()
        rest.start()
        z.late.d_down.wait()
        down.start()
        z.late.d_up.wait()
        up.start()
        out.start()
        z.late.qkv_w.start()
        z.late.up_w.start()

    @pl.when(step < count)
    def _():
        def middle_work():
            at_steps(
                step,
                (
                    (1, z.late.before.start),
                    (1, z.late.inverse.start),
                    (1, z.late.unit.start),
                    (1, z.late.near.start),
                    (1, z.late.far.start),
                    (2, z.late.ai.start),
                    (3, z.late.own.start),
                    (1, lambda: down.batch(TURN_DOWN + 1)),
                    (1, lambda: down.batch(TURN_DOWN + 2)),
                    (2, lambda: rest.batch(TURN_REST + 2)),
                    (2, z.late.before.wait),
                    (2, z.late.inverse.wait),
                    (2, z.late.unit.wait),
                    (3, lambda: up.batch(TURN_UP + 3)),
                ),
            )

        def end_work():
            at_steps(
                step,
                (
                    (0, lambda: rest.batch(TURN_REST + 1)),
                    (1, lambda: up.batch(TURN_UP + 1)),
                    (1, lambda: up.batch(TURN_UP + 2)),
                    (1, lambda: out.batch(1)),
                    (2, z.late.near.wait),
                    (2, z.late.far.wait),
                    (2, lambda: loop(count, lambda i: result.copy(0, i).start())),
                    (3, lambda: loop(count, result.relay)),
                    (2, lambda: down.batch(TURN_DOWN + 3)),
                    (3, lambda: out.batch(2)),
                ),
            )

            @pl.when(step >= 2)
            def _():
                sum_up(step - 2)

        back_step(z, 0, h, step, count, scatter, row_sum, middle_work, end_work)

    @pl.when(step == count)
    def _():
        scatter.relay(0)
        row_sum.relay(0)
        small.put((z.sums, z.sums_next))
        z.late.ai.wait()
        loop(D // CHUNK, lambda i: weight_tile(i, z.ai, z.proj_all[...], z.d_qkv))
        last.start()
        more.start()
        rest.finish((z.sum_qkv_next, z.sum_out_next))
        down.batch(TURN_DOWN + 4)
        sum_up(2)
        small.relay()
        last.batch(1)
        more.batch(1)
        up.batch(TURN_UP + 4)
        out.batch(3)
        sum_up(3)
        small.pack(
            (
                (z.d_qkv_b, z.d_up_b, z.d_feat[...] / feature_row(z.feats, 0), z.d_res),
                (
                    z.d_qkv_b_next,
                    z.d_up_b_next,
                    z.d_feat_next[...] / feature_row(z.feats, 1),
                    z.d_res_next,
                ),
            )
        )
        last.batch(2)
        more.batch(2)
        down.batch(6)
        out.batch(4)
        small.round(0)
        last.batch(3)
        more.batch(3)
        up.batch(5)
        last.batch(4)
        more.batch(4)
        small.round(1)
        down.finish((z.sum_down,))
        out.batch(5)
        last.batch(5)
        more.batch(5)
        up.batch(6)
        for k in range(2, Small.rounds(n)):
            small.round(k)
        z.late.own.wait()

        def place(i):
            here = rows_at(i)
            z.out[here, :] = z.own[here, :] + result.total(i) + z.res_b[1:2, columns]

        loop(count, place)
        last.batch(6)
        more.batch(6)
        out.batch(6)
        z.bundle[...] = small.bundle[Small.rounds(n)]
        small.finish()
        for i in range(count):
            scatter.finish(i)
            row_sum.finish(i)
            result.finish(i)
        up.finish((z.sum_up,))
        last.finish((z.sum_qkv,))
        more.finish((z.sum_qkv,))
        out.finish((z.sum_out,))


def split_last(width):
    third = width // 3
    half = third // 2
    return (
        ((0, 0, third, 1), (0, third, half, -1)),
        ((0, third + half, half, 1), (0, 2 * third, third, -1)),
    )


def leave(n, local, turned, top, before, ai, own, tables, params, consts):
    qf = local[0]
    rows, a = qf.shape
    lowered = (turned["d_raised_out"], turned["d_num_out"], turned["d_den_out"])
    hidden = lowered[0].shape[1]
    count = rows // CHUNK
    width = D // 4
    share = D // n
    rest_parts, wide_parts = rest_of(3 * a, a), halved(0, hidden)
    out_parts = halved(0, a)
    first_parts, second_parts = split_last(3 * a)

    def whole(array):
        return (array, fixed(array.shape))

    ins = dict(
        **back_arrays(0, local, lowered, tables, params, consts, turned["exit_out"], count),
        d_out_next=whole(top["d_out"]),
        d_out=whole(turned["d_out"]),
        new_fore=whole(turned["new_fore"]),
        new_aft=whole(turned["new_aft"]),
        up_fore=whole(turned["up_fore"]),
        up_aft=whole(turned["up_aft"]),
        res_b=whole(params[9]),
        feats=whole(params[4]),
        rest_a=whole(turned["rest_a"]),
        rest_b=whole(turned["rest_b"]),
        rest_c=whole(turned["rest_c"]),
        rest_d=whole(turned["rest_d"]),
        d_up_b=whole(turned["d_up_b"]),
        d_res=whole(turned["d_res"]),
        sums_next=whole(turned["sums"]),
        d_qkv_b_next=whole(turned["d_qkv_b"]),
        d_up_b_next=whole(top["d_up_b"]),
        d_feat_next=whole(turned["d_feat"]),
        d_res_next=whole(top["d_res"]),
    )
    gain, bias, qkv_w, qkv_b, feats, up_w, up_b, out_w, down_w, res_b = params
    late = dict(
        d_qkv_next=turned["d_qkv"],
        d_down=turned["d_down"],
        d_up=turned["d_up"],
        qkv_w=(qkv_w, 0),
        up_w=(up_w, 0),
        before=before,
        inverse=local[6],
        unit=local[5],
        ai=ai,
        near=top["near"],
        far=top["far"],
        own=own,
    )

    def result(shape):
        return (struct(shape, F32), full(shape))

    outs = dict(
        after=result((rows, width)),
        out=result((rows, width)),
        bundle=result((32, width)),
        sum_qkv_next=result((share, 3 * a)),
        sum_out_next=result((share, a)),
        sum_qkv=result((share, 3 * a)),
        sum_out=result((share, a)),
        sum_down=result((share, hidden)),
        sum_up=result((share, hidden)),
    )
    scratch = dict(
        **back_scratch(rows, a, width),
        small=Small.scratch(n, width),
        rest_held=Ring.buffers(n, rest_parts, TURN_REST),
        down_held=Ring.buffers(n, wide_parts, TURN_DOWN),
        up_held=Ring.buffers(n, wide_parts, TURN_UP),
        out_held=Ring.buffers(n, out_parts),
        last_held=Ring.buffers(n, first_parts),
        more_held=Ring.buffers(n, second_parts),
        result=Scatter.scratch(rows, width)[2:],
        rest_sems=Ring.sems(n, rest_parts),
        down_sems=Ring.sems(n, wide_parts),
        up_sems=Ring.sems(n, wide_parts),
        out_sems=Ring.sems(n, out_parts),
        last_sems=Ring.sems(n, first_parts),
        more_sems=Ring.sems(n, second_parts),
        d_qkv=[pltpu.VMEM((D, 3 * a), BF)],
        d_feat=[pltpu.VMEM((1, a), F32)],
        d_qkv_b=[pltpu.VMEM((1, 3 * a), F32)],
        sums=[pltpu.VMEM((8, D), F32)],
    )
    return named_call(
        functools.partial(leave_kernel, n),
        "leave",
        6,
        (count + 1,),
        ins,
        outs,
        scratch,
        2 * rows * D * (hidden + 8 * a) * 3,
        late,
    )


def on_device(
    acts,
    cotangent,
    lengths,
    keep_mask,
    ln_gain,
    ln_bias,
    qkv_w,
    qkv_b,
    feat_w,
    out_w,
    up_w,
    up_b,
    down_w,
    res_b,
):
    rows, width = acts.shape
    heads = feat_w.shape[1]
    a = heads * HEAD_DIM
    n = lax.axis_size("seq")
    tokens = rows * n
    longest = 2048 if tokens <= 8192 else 4096
    hops = -(-longest // rows)
    h = lax.axis_index("head").astype(jnp.int32)
    first = lax.axis_index("seq") * rows

    keep_rows = keep_mask.reshape(rows // 128, 128)
    half = ROT // 2
    rates = np.zeros((2, HEAD_DIM))
    rates[0, :half] = ROTARY_BASE ** (-2.0 * np.arange(half) / ROT)
    rates[0, half:ROT] = rates[0, :half]
    rates[1, :half] = -1.0
    rates[1, half:ROT] = 1.0
    rates = jnp.asarray(np.tile(rates, (1, 2)), F32)

    fold = sample_points(FEATURES, HEAD_DIM) @ cosine_table(HEAD_DIM) / math.sqrt(HEAD_DIM)
    eye = np.eye(heads)
    consts = {
        "map": jnp.asarray(np.kron(eye, fold), F32),
        "map_t": jnp.asarray(np.kron(eye, fold.T), F32),
        "ones": jnp.asarray(np.kron(eye, np.ones((HEAD_DIM, HEAD_DIM))), BF),
    }

    entered = enter(
        n, lengths, acts, keep_rows, ln_gain, ln_bias, qkv_w, qkv_b, feat_w, rates, consts
    )
    tables = (entered["cos"], entered["sin"], entered["columns"])
    params = (ln_gain, ln_bias, qkv_w, qkv_b, feat_w, up_w, up_b, out_w, down_w, res_b)

    def back_local(made, states, totals):
        ai, fi, normed, unit, inverse, qf, kf, v, k = made
        return (qf, kf, v, k, normed, unit, inverse, states, totals)

    first_made = tuple(entered[name] for name, width_of, kind in PROJECT_KINDS)
    own_rows, packed = lax.optimization_barrier((cotangent, entered["packed"]))
    pieces = [own_rows] + [
        lax.ppermute(own_rows, "head", [(i, i ^ mask) for i in range(4)]) for mask in (1, 2)
    ]
    entered["packed"] = packed
    mid = between(n, hops, 0, lengths, entered, params, consts)
    local = back_local(first_made, mid["states"], mid["totals"])
    made = tuple(mid[name] for name, width_of, kind in PROJECT_KINDS)
    lower_in = (
        mid["act"], mid["slope"], mid["ratio"], mid["att"], mid["att_low"], entered["fi"],
        entered["qf"],
    )
    top = crest(n, hops, 1, lengths, mid, pieces, tables, params, consts)
    turned = turn(
        n,
        hops,
        0,
        lengths,
        back_local(made, top["states"], top["totals"]),
        top,
        cotangent,
        made[0],
        lower_in,
        tables,
        params,
        consts,
    )
    left = leave(n, local, turned, top, turned["after"], first_made[0], mid["own"], tables, params, consts)
    hidden = up_w.shape[2]
    bundle = left["bundle"].reshape(LAYERS, 16, width)
    kinds = 3 * a // width
    ups = hidden // width
    at = 4 + kinds + ups
    return (
        left["out"],
        left["after"],
        jnp.stack([left["sum_qkv"], left["sum_qkv_next"]]),
        jnp.stack([left["sum_out"], left["sum_out_next"]]),
        jnp.stack([left["sum_up"], turned["sum_up"]]),
        jnp.stack([left["sum_down"], turned["sum_down"]]),
        bundle[:, 4 : 4 + kinds].reshape(LAYERS, 3 * a),
        bundle[:, 4 + kinds : at].reshape(LAYERS, hidden),
        bundle[:, at].reshape(LAYERS, heads, FEATURES),
        bundle[:, 0:2],
        bundle[:, 2:4],
        bundle[:, at + 1],
    )


def solution(mesh):
    return jax.shard_map(
        on_device,
        mesh=mesh,
        in_specs=(
            P("seq", "head"),
            P("seq", "head"),
            P(),
            P("seq"),
            P(),
            P(),
            P(None, None, "head"),
            P(None, "head"),
            P(None, "head", None),
            P(None, None, "head"),
            P(None, None, "head"),
            P(None, "head"),
            P(None, None, "head"),
            P(),
        ),
        out_specs=(
            P("seq", "head"),
            P("seq", "head"),
            P(None, "seq", "head"),
            P(None, "seq", "head"),
            P(None, "seq", "head"),
            P(None, "seq", "head"),
            P(None, "head"),
            P(None, "head"),
            P(None, "head", None),
            P(None, None, "head"),
            P(None, None, "head"),
            P(None, "head"),
        ),
        check_vma=False,
    )
```

```python
import functools
import math

import jax
import jax.numpy as jnp
import numpy as np
from jax import lax
from jax.experimental import pallas as pl
from jax.experimental.pallas import tpu as pltpu
from jax.sharding import PartitionSpec as P

D = 1024
HEAD_DIM = 64
ROT = 16
FEATURES = 64
LAYERS = 2
CHUNK = 256

EPSILON = 1e-05
ROTARY_BASE = 10000.0
HIGHEST = lax.Precision.HIGHEST
BF = jnp.bfloat16
F32 = jnp.float32
STATE_ROWS = 72
VMEM_BYTES = 60 * 1024 * 1024


def prime_numbers(count):
    found = []
    candidate = 2
    while len(found) < count:
        if all((candidate % prime != 0 for prime in found)):
            found.append(candidate)
        candidate = candidate + 1
    return found


def sample_points(rows, columns):
    roots = np.sqrt(np.array(prime_numbers(2 * columns)) * 1.0)
    fractions = roots - np.floor(roots)
    grid = np.outer(np.arange(1, rows + 1) * 1.0, fractions) % 1.0
    radius = np.sqrt(-2.0 * np.log(1.0 - grid[:, :columns]))
    return radius * np.cos(2.0 * math.pi * grid[:, columns:])


def cosine_table(size):
    wave = np.arange(size)[:, None] * 1.0
    place = np.arange(size)[None, :] * 1.0
    table = np.cos(math.pi * (place + 0.5) * wave / size) * math.sqrt(2.0 / size)
    return table * np.where(wave == 0, math.sqrt(0.5), 1.0)


def dot_nn(a, b, precision=None):
    return lax.dot_general(
        a, b, (((1,), (0,)), ((), ())), precision=precision, preferred_element_type=F32
    )


def dot_nt(a, b, precision=None):
    return lax.dot_general(
        a, b, (((1,), (1,)), ((), ())), precision=precision, preferred_element_type=F32
    )


def dot_tn(a, b, precision=None):
    return lax.dot_general(
        a, b, (((0,), (0,)), ((), ())), precision=precision, preferred_element_type=F32
    )


def halves(wide):
    high = wide.astype(BF)
    return high, (wide - high.astype(F32)).astype(BF)


def lane_of(shape):
    return lax.broadcasted_iota(jnp.int32, shape, 1)


def row_of(shape):
    return lax.broadcasted_iota(jnp.int32, shape, 0)


def swap_pairs(x):
    width = x.shape[1]
    later = pltpu.roll(x, width - ROT // 2, 1)
    earlier = pltpu.roll(x, ROT // 2, 1)
    return jnp.where(lane_of(x.shape) % ROT < ROT // 2, later, earlier)


def twice(table):
    return jnp.concatenate([table, table], axis=1)


def block_columns(h, r, width):
    return pl.ds(pl.multiple_of(lax.bitwise_xor(h, r) * width, width), width)


def split_heads(projected):
    heads = projected.shape[1] // (3 * HEAD_DIM)
    return [
        jnp.concatenate(
            [
                projected[:, (3 * j + kind) * HEAD_DIM : (3 * j + kind + 1) * HEAD_DIM]
                for j in range(heads)
            ],
            axis=1,
        )
        for kind in range(3)
    ]


def join_heads(q, k, v):
    heads = q.shape[1] // HEAD_DIM
    return jnp.concatenate(
        [
            part[:, j * HEAD_DIM : (j + 1) * HEAD_DIM]
            for j in range(heads)
            for part in (q, k, v)
        ],
        axis=1,
    )


def block_diagonal(width):
    shape = (width, width)
    return (row_of(shape) // HEAD_DIM) == (lane_of(shape) // HEAD_DIM)


def pack_state(full):
    width = full.shape[0]
    kept = jnp.where(block_diagonal(width), full, 0.0)
    packed = kept[0:FEATURES]
    for head in range(1, width // FEATURES):
        packed = packed + kept[head * FEATURES : (head + 1) * FEATURES]
    return packed


def unpack_state(packed):
    width = packed.shape[1]
    tall = jnp.concatenate([packed] * (width // FEATURES), axis=0)
    return jnp.where(block_diagonal(width), tall, 0.0)


def head_sum(values, ones):
    high, low = halves(values)
    return dot_nn(high, ones) + dot_nn(low, ones)


def full(shape):
    return pl.BlockSpec(shape, lambda *i: (0,) * len(shape))


def rowed(width):
    return pl.BlockSpec((CHUNK, width), lambda i: (i, 0))


def layered(array, l):
    return pl.BlockSpec((None,) + array.shape[1:], lambda *i: (l, 0, 0))


def rows_at(c):
    return pl.ds(pl.multiple_of(c * CHUNK, CHUNK), CHUNK)


def push(source, target, send, recv, where):
    return pltpu.make_async_remote_copy(
        src_ref=source,
        dst_ref=target,
        send_sem=send,
        recv_sem=recv,
        device_id=where,
        device_id_type=pl.DeviceIdType.MESH,
    )


class Gather:
    def __init__(self, h, own, buffers, sems):
        self.own = own
        self.beside, self.across, self.corner = buffers
        self.send, self.recv = sems
        self.near = {"head": lax.bitwise_xor(h, 1)}
        self.far = {"head": lax.bitwise_xor(h, 2)}

    @staticmethod
    def scratch(rows, width):
        count = rows // CHUNK
        return [pltpu.VMEM((rows, width), BF)] * 3 + [pltpu.SemaphoreType.DMA((3, count))] * 2

    def copy(self, kind, c):
        source, target, where = (
            (self.own, self.across, self.far),
            (self.own, self.beside, self.near),
            (self.across, self.corner, self.near),
        )[kind]
        rows = rows_at(c)
        return push(
            source.at[rows, :],
            target.at[rows, :],
            self.send.at[kind, c],
            self.recv.at[kind, c],
            where,
        )

    def start(self, c):
        self.copy(0, c).start()
        self.copy(1, c).start()

    def relay(self, c):
        self.copy(0, c).wait_recv()
        self.copy(2, c).start()

    def ready(self, c):
        self.copy(1, c).wait_recv()
        self.copy(2, c).wait_recv()

    def pieces(self, c):
        rows = rows_at(c)
        return [ref[rows, :] for ref in (self.own, self.beside, self.across, self.corner)]

    def finish(self, c):
        for kind in range(3):
            self.copy(kind, c).wait_send()


class Scatter:
    def __init__(self, h, buffers, sems):
        self.near, self.far, self.got, self.middle, self.across = buffers
        self.send, self.recv = sems
        self.beside = {"head": lax.bitwise_xor(h, 1)}
        self.beyond = {"head": lax.bitwise_xor(h, 2)}

    @staticmethod
    def scratch(rows, width):
        count = rows // CHUNK
        return (
            [pltpu.VMEM((2, rows, width), BF)] * 3
            + [pltpu.VMEM((rows, width), BF)] * 2
            + [pltpu.SemaphoreType.DMA((2, count))] * 2
        )

    def copy(self, kind, c):
        rows = rows_at(c)
        if kind == 0:
            source, target, where = (
                self.far.at[:, rows, :],
                self.got.at[:, rows, :],
                self.beside,
            )
        else:
            source, target, where = self.middle.at[rows, :], self.across.at[rows, :], self.beyond
        return push(source, target, self.send.at[kind, c], self.recv.at[kind, c], where)

    def put(self, h, c, whole):
        rows = rows_at(c)
        w = self.near.shape[2]
        self.near[0, rows, :] = whole[:, block_columns(h, 0, w)]
        self.near[1, rows, :] = whole[:, block_columns(h, 2, w)]
        self.far[0, rows, :] = whole[:, block_columns(h, 1, w)]
        self.far[1, rows, :] = whole[:, block_columns(h, 3, w)]
        self.copy(0, c).start()

    def relay(self, c):
        self.copy(0, c).wait_recv()
        rows = rows_at(c)
        self.middle[rows, :] = (
            self.near[1, rows, :].astype(F32) + self.got[1, rows, :].astype(F32)
        ).astype(BF)
        self.copy(1, c).start()

    def total(self, c):
        self.copy(1, c).wait_recv()
        rows = rows_at(c)
        return (
            self.near[0, rows, :].astype(F32)
            + self.got[0, rows, :].astype(F32)
            + self.across[rows, :].astype(F32)
        )

    def finish(self, c):
        self.copy(0, c).wait_send()
        self.copy(1, c).wait_send()


def begin_scalar(lengths, slot):
    def one(j, carry):
        at, best = carry
        at = at + lengths[j - 1]
        return at, jnp.where(at <= slot, at, best)

    return lax.fori_loop(1, lengths.shape[0], one, (jnp.int32(0), jnp.int32(0)))[1]


def begin_column(lengths, slots):
    def one(j, carry):
        at, best = carry
        at = at + lengths[j - 1]
        return at, jnp.where(slots >= at, at, best)

    return lax.fori_loop(1, lengths.shape[0], one, (jnp.int32(0), jnp.zeros_like(slots)))[1]


class HandOver:
    def __init__(self, n, hops, rows, sign, packed, buffer, sems):
        self.n, self.hops, self.rows, self.sign = n, hops, rows, sign
        self.packed, self.buffer = packed, buffer
        self.send, self.recv = sems
        self.here = lax.axis_index("seq")

    @staticmethod
    def scratch(hops, width):
        return [pltpu.VMEM((hops, STATE_ROWS, width), F32)] + [
            pltpu.SemaphoreType.DMA((hops,))
        ] * 2

    def inside(self, index):
        return (index >= 0) & (index < self.n)

    def copy(self, j):
        return push(
            self.packed,
            self.buffer.at[j - 1],
            self.send.at[j - 1],
            self.recv.at[j - 1],
            {"seq": lax.rem(self.here + self.sign * j + self.n, self.n)},
        )

    def clear(self):
        self.buffer[...] = jnp.zeros_like(self.buffer)

    def start(self):
        for j in range(1, self.hops + 1):

            @pl.when(self.inside(self.here + self.sign * j))
            def _(j=j):
                self.copy(j).start()

    def total(self, lengths):
        first = self.here * self.rows
        result = None
        for j in range(1, self.hops + 1):

            @pl.when(self.inside(self.here - self.sign * j))
            def _(j=j):
                self.copy(j).wait_recv()

            @pl.when(self.inside(self.here + self.sign * j))
            def _(j=j):
                self.copy(j).wait_send()

            if self.sign > 0:
                edge, held = first - 1, first - 1 - (j - 1) * self.rows
            else:
                edge, held = first + j * self.rows - 1, first + self.rows - 1
            linked = (begin_scalar(lengths, edge) <= held).astype(F32)
            part = self.buffer[j - 1] * linked
            result = part if result is None else result + part
        return result


def greet(h, n, hops):
    barrier = pltpu.get_barrier_semaphore()

    def signal(where):
        pl.semaphore_signal(barrier, inc=1, device_id=where, device_id_type=pl.DeviceIdType.MESH)

    signal({"head": lax.bitwise_xor(h, 1)})
    signal({"head": lax.bitwise_xor(h, 2)})
    here = lax.axis_index("seq")
    expected = jnp.int32(2)
    for j in range(1, hops + 1):
        for sign in (1, -1):
            there = here + sign * j
            inside = (there >= 0) & (there < n)

            @pl.when(inside)
            def _(there=there):
                signal({"seq": lax.rem(there + n, n)})

            expected = expected + inside.astype(jnp.int32)
    pl.semaphore_wait(barrier, expected)


PROJECT_KINDS = (
    ("ai", D, BF),
    ("fi", D, BF),
    ("normed", D, BF),
    ("unit", D // 4, F32),
    ("inverse", 128, F32),
    ("qf", None, BF),
    ("kf", None, BF),
    ("v", None, BF),
    ("k", None, BF),
)


def feature_row(feat_ref, l):
    return jnp.concatenate([feat_ref[l, j : j + 1, :] for j in range(feat_ref.shape[1])], axis=1)


def project_chunk(l, h, c, last, x, params, tables, whole, out, packed, summed):
    gain, bias, w_ref, b_ref, feat_ref, map_ref, ones_ref = params
    cos, sin, keep = tables
    ai_ref, fi_ref, normed_ref, unit_ref, inv_ref, qf_ref, kf_ref, v_ref, k_ref = out
    mean = jnp.sum(x, axis=1, keepdims=True) * (1.0 / D)
    center = x - mean
    inverse = lax.rsqrt(jnp.sum(center * center, axis=1, keepdims=True) * (1.0 / D) + EPSILON)
    normed = center * inverse
    inv_ref[...] = jnp.broadcast_to(inverse, inv_ref.shape)
    normed_ref[...] = normed.astype(BF)
    whole[...] = normed
    unit_ref[...] = whole[:, block_columns(h, 0, unit_ref.shape[1])]
    attention_input = (normed * gain[l, 0:1] + bias[l, 0:1]).astype(BF)
    ai_ref[...] = attention_input
    fi_ref[...] = (normed * gain[l, 1:2] + bias[l, 1:2]).astype(BF)
    projected = dot_nn(attention_input, w_ref[...]) + b_ref[l : l + 1, :]
    q, k, v = split_heads(projected)
    v = v.astype(BF)
    q_turn = q * cos + swap_pairs(q) * sin
    k_turn = k * cos + swap_pairs(k) * sin
    query_feat = jnp.exp(dot_nn(q_turn, map_ref[...], HIGHEST))
    key_norm = head_sum(k * k, ones_ref[...]) * (0.5 / HEAD_DIM)
    key_feat = (
        keep
        * feature_row(feat_ref, l)
        * jnp.exp(dot_nn(k_turn, map_ref[...], HIGHEST) - key_norm)
    ).astype(BF)
    qf_ref[...] = query_feat.astype(BF)
    kf_ref[...] = key_feat
    v_ref[...] = v
    k_ref[...] = k.astype(BF)
    place = (row_of((CHUNK, 1)) + c * CHUNK).astype(F32)
    masked = jnp.where(place >= last, key_feat.astype(F32), 0.0)

    @pl.when(c == 0)
    def _():
        summed[...] = jnp.zeros_like(summed)
        packed[...] = jnp.zeros_like(packed)

    summed[...] += dot_tn(masked.astype(BF), v)
    packed[FEATURES : FEATURES + 1, :] += jnp.sum(masked, axis=0, keepdims=True)


def raise_chunk(l, fi, w_ref, b_ref, act_ref, slope_ref):
    raised = dot_nn(fi, w_ref[...]) + b_ref[l : l + 1, :]
    cumulative = 0.5 + 0.5 * lax.erf(raised * math.sqrt(0.5))
    density = jnp.exp(raised * raised * -0.5) * (1.0 / math.sqrt(2.0 * math.pi))
    act_ref[...] = (raised * cumulative).astype(BF)
    slope_ref[...] = (cumulative + raised * density).astype(BF)


def remote_call(kernel, name, ident, grid, in_specs, out_specs, out_shape, scratch, flops, args):
    moved = sum(int(np.prod(a.shape)) * a.dtype.itemsize for a in list(args) + list(out_shape))
    return pl.pallas_call(
        kernel,
        name=name,
        grid=grid,
        in_specs=in_specs,
        out_specs=out_specs,
        scratch_shapes=scratch,
        out_shape=out_shape,
        compiler_params=pltpu.CompilerParams(
            collective_id=ident, has_side_effects=True, vmem_limit_bytes=VMEM_BYTES
        ),
        cost_estimate=pl.CostEstimate(flops=int(flops), bytes_accessed=moved, transcendentals=0),
    )(*args)


class Names:
    pass


def named_call(kernel, name, ident, grid, ins, outs, scratch, flops, late=None, sent=None):
    late, sent = late or {}, sent or {}
    shared = {k: v[1] for k, v in sent.items() if isinstance(v, tuple)}
    sent = {k: v[0] if isinstance(v, tuple) else v for k, v in sent.items()}
    labels, groups = list(ins) + list(late) + list(outs) + list(sent), list(scratch)
    layers = {k: v if isinstance(v, tuple) else (v, None) for k, v in late.items()}
    anywhere = pl.BlockSpec(memory_space=pl.ANY)

    def body(*refs):
        names = Names()
        names.late, names.sent = Names(), Names()
        far = {}
        for label, ref in zip(labels, refs):
            if label in late or label in sent:
                far[label] = ref
            else:
                setattr(names, label, ref)
        at = len(labels)
        for label in list(late) + list(sent):
            if label in shared:
                held, sem = getattr(names, shared[label]), refs[at]
                at -= 1
            else:
                held, sem = refs[at], refs[at + 1]
            setattr(names, label, held)
            if label in late:
                layer = layers[label][1]
                source = far[label] if layer is None else far[label].at[layer]
                setattr(names.late, label, pltpu.make_async_copy(source, held, sem))
            else:
                setattr(names.sent, label, pltpu.make_async_copy(held, far[label], sem))
            at += 2
        for label in groups:
            size = len(scratch[label])
            held = refs[at : at + size]
            setattr(names, label, held if size > 1 else held[0])
            at += size
        kernel(names)

    moved = []
    for array, layer in layers.values():
        shape = array.shape if layer is None else array.shape[1:]
        moved += [pltpu.VMEM(shape, array.dtype), pltpu.SemaphoreType.DMA]
    for label, shape in sent.items():
        if label not in shared:
            moved.append(pltpu.VMEM(shape.shape, shape.dtype))
        moved.append(pltpu.SemaphoreType.DMA)
    result = remote_call(
        body,
        name,
        ident,
        grid,
        [spec for array, spec in ins.values()] + [anywhere] * len(late),
        [spec for shape, spec in outs.values()] + [anywhere] * len(sent),
        [shape for shape, spec in outs.values()] + list(sent.values()),
        moved + [item for label in groups for item in scratch[label]],
        flops,
        [array for array, spec in ins.values()] + [array for array, layer in layers.values()],
    )
    return dict(zip(list(outs) + list(sent), result))


def every(names):
    return [getattr(names, label) for label in vars(names)]


def fixed(shape):
    return pl.BlockSpec(shape, lambda *i: (0,) * len(shape), pipeline_mode=pl.Buffered(1))


def layer_of(array, l):
    return pl.BlockSpec(
        (None,) + array.shape[1:], lambda *i: (l, 0, 0), pipeline_mode=pl.Buffered(1)
    )


def clipped(step, low, count):
    return jnp.minimum(jnp.maximum(step - low, 0), count - 1)


def up_rows(width, low, count):
    return pl.BlockSpec((CHUNK, width), lambda i: (clipped(i, low, count), 0))


def down_rows(width, low, count):
    return pl.BlockSpec((CHUNK, width), lambda i: (count - 1 - clipped(i, low, count), 0))


def down_cube(shape, low, count):
    return pl.BlockSpec(
        (1,) + shape, lambda i: (count - 1 - clipped(i, low, count),) + (0,) * len(shape)
    )


def struct(shape, kind):
    return jax.ShapeDtypeStruct(shape, kind)


def project_params(z):
    return (z.gain, z.bias, z.qkv_w, z.qkv_b, z.feats, z.map_t, z.ones)


def project_refs(z):
    return (z.ai, z.fi, z.normed, z.unit, z.inverse, z.qf, z.kf, z.v, z.k)


def project_made(rows, a, spec):
    return dict(
        (name, (struct((rows, width or a), kind), spec(width or a)))
        for name, width, kind in PROJECT_KINDS
    )


class Column:
    def __init__(self, ref, lane):
        self.ref, self.lane = ref, lane

    def __getitem__(self, key):
        rows = slice(None) if key is Ellipsis else key[0]
        return self.ref[rows, self.lane : self.lane + 1]


def begin_keep(ref):
    return Column(ref, 0), Column(ref, 64)


def lanes_to_column(row):
    shape = (row.shape[1], row.shape[1])
    eye = row_of(shape) == lane_of(shape)
    return jnp.sum(jnp.where(eye, row, 0.0), axis=1, keepdims=True)


def enter_kernel(n, z):
    c = pl.program_id(0)
    count = pl.num_programs(0)
    h = lax.axis_index("head")
    rows, width = z.acts.shape
    first = lax.axis_index("seq") * rows
    gather = Gather(h, z.acts, z.gather[:3], z.gather[3:])

    @pl.when(c == 0)
    def _():
        for copy in every(z.late):
            copy.start()
        greet(h, n, 0)
        for i in range(rows // CHUNK):
            gather.start(i)
        for i in range(rows // CHUNK):
            part = slice(i * CHUNK, (i + 1) * CHUNK)
            slots = row_of((CHUNK, 1)) + i * CHUNK + first
            begins = begin_column(z.lengths, slots)
            starts = (begins - first).astype(F32)
            keep = jnp.concatenate(
                [
                    lanes_to_column(z.keep_mask[j : j + 1, :].astype(F32))
                    for j in range(i * CHUNK // 128, (i + 1) * CHUNK // 128)
                ],
                axis=0,
            )
            z.columns[part, :] = jnp.where(lane_of((CHUNK, 128)) < 64, starts, keep)
            phase = (slots - begins).astype(F32) * z.rates[0:1, :]
            z.cos[part, :] = jnp.cos(phase)
            z.sin[part, :] = jnp.sin(phase) * z.rates[1:2, :]
        gather.relay(0)
        for copy in every(z.late):
            copy.wait()

    gather.ready(c)
    for r, part in enumerate(gather.pieces(c)):
        z.full[:, block_columns(h, r, width)] = part
    last = (begin_scalar(z.lengths, first + rows - 1) - first).astype(F32)
    here = rows_at(c)
    keep = begin_keep(z.columns)[1]
    tables = (twice(z.cos[here, :]), twice(z.sin[here, :]), keep[here, :])
    project_chunk(
        0,
        h,
        c,
        last,
        z.full[...].astype(F32),
        project_params(z),
        tables,
        z.whole,
        project_refs(z),
        z.packed,
        z.summed,
    )

    @pl.when(c + 1 < count)
    def _():
        gather.relay(c + 1)

    @pl.when(c + 1 == count)
    def _():
        z.packed[0:FEATURES, :] = pack_state(z.summed[...])
        for i in range(rows // CHUNK):
            gather.finish(i)


def enter(n, lengths, acts, keep_mask, gain, bias, qkv_w, qkv_b, feats, rates, consts):
    rows, width = acts.shape
    a = consts["ones"].shape[0]
    table = rates.shape[1]
    ins = dict(
        lengths=(lengths, pl.BlockSpec(memory_space=pltpu.SMEM)),
        acts=(acts, fixed(acts.shape)),
        keep_mask=(keep_mask, fixed(keep_mask.shape)),
        gain=(gain, fixed(gain.shape)),
        bias=(bias, fixed(bias.shape)),
        qkv_b=(qkv_b, fixed(qkv_b.shape)),
        feats=(feats, fixed(feats.shape)),
        rates=(rates, fixed(rates.shape)),
    )
    late = dict(qkv_w=(qkv_w, 0), map_t=consts["map_t"], ones=consts["ones"])
    outs = dict(
        full=(struct((rows, D), BF), rowed(D)),
        cos=(struct((rows, table), F32), full((rows, table))),
        sin=(struct((rows, table), F32), full((rows, table))),
        columns=(struct((rows, 128), F32), full((rows, 128))),
        **project_made(rows, a, rowed),
        packed=(struct((STATE_ROWS, a), F32), full((STATE_ROWS, a))),
    )
    scratch = dict(
        gather=Gather.scratch(rows, width),
        summed=[pltpu.VMEM((a, a), F32)],
        whole=[pltpu.VMEM((CHUNK, D), F32)],
    )
    return named_call(
        functools.partial(enter_kernel, n),
        "enter",
        2,
        (rows // CHUNK,),
        ins,
        outs,
        scratch,
        2 * rows * D * 3 * a * 2,
        late,
    )


def between_kernel(n, hops, l, z):
    step = pl.program_id(0)
    count = pl.num_programs(0) // 2
    h = lax.axis_index("head")
    rows, width = z.mine.shape
    first = lax.axis_index("seq") * rows
    chunks = rows // CHUNK
    gather = Gather(h, z.mine, z.gather[:3], z.gather[3:])
    begin, keep = begin_keep(z.columns)
    extra = [
        push(
            z.cotangent,
            target,
            z.extra_sems.at[0, i],
            z.extra_sems.at[1, i],
            {"head": lax.bitwise_xor(h, i + 1)},
        )
        for i, target in enumerate((z.from_beside, z.from_across))
    ]
    scatter = Scatter(h, z.scatter[:5], z.scatter[5:])
    hand = HandOver(n, hops, rows, 1, z.state_own, z.hand[0], z.hand[1:])

    def send_sum(c):
        z.mine[rows_at(c), :] = scatter.total(c).astype(BF)
        gather.start(c)

    @pl.when(step == 0)
    def _():
        z.late.up_w.start()
        hand.clear()
        greet(h, n, hops)
        hand.start()
        z.late.up_w.wait()
        z.late.out_w.start()
        z.late.down_w.start()

    @pl.when(step < count)
    def _():
        raise_chunk(l, z.fi_in[...], z.up_w, z.up_b, z.act, z.slope)

        @pl.when(step == 0)
        def _():
            z.state_in[...] = hand.total(z.lengths)

        @pl.when(step >= 3)
        def _():
            gather.relay(step - 3)

        attention_chunk(
            step,
            (z.qf_in, z.kf_in, z.v_in, begin, keep, z.state_in, z.ones),
            (z.att, z.att_low, z.ratio, z.states, z.totals),
            z.state,
            z.total,
        )

        @pl.when(step == 0)
        def _():
            z.late.out_w.wait()
            z.late.down_w.wait()

        @pl.when(step == 1)
        def _():
            z.late.qkv_w.start()
            z.late.up_w_next.start()

        @pl.when(step >= 1)
        def _():
            scatter.relay(step - 1)

        z.whole_low[...] = (
            dot_nt(z.att_low[...], z.out_w[...]) + dot_nt(z.act[...], z.down_w[...])
        ).astype(BF)
        scatter.put(h, step, z.whole_low)

        @pl.when(step >= 2)
        def _():
            send_sum(step - 2)

    @pl.when(step >= count)
    def _():
        c = step - count

        @pl.when(c == 0)
        def _():
            scatter.relay(chunks - 1)
            z.late.qkv_w.wait()
            z.late.up_w_next.wait()
            gather.relay(1)

        gather.ready(c)
        for r, part in enumerate(gather.pieces(c)):
            z.whole[:, block_columns(h, r, width)] = part.astype(F32)
        x = z.full[...].astype(F32) + z.whole[...] + z.res_b[l : l + 1, :]
        z.whole[...] = x
        z.own[...] = z.whole[:, block_columns(h, 0, width)]
        last = (begin_scalar(z.lengths, first + rows - 1) - first).astype(F32)
        tables = (twice(z.cos[...]), twice(z.sin[...]), begin_keep(z.columns_next)[1][...])
        project_chunk(
            l + 1,
            h,
            c,
            last,
            x,
            project_params(z),
            tables,
            z.whole,
            project_refs(z),
            z.packed,
            z.summed,
        )

        @pl.when(c == 0)
        def _():
            send_sum(chunks - 2)

        @pl.when(c + 1 == chunks)
        def _():
            z.packed[0:FEATURES, :] = pack_state(z.summed[...])

        raise_chunk(l + 1, z.fi[...], z.up_w_next, z.up_b, z.act_next, z.slope_next)

        @pl.when(c == 0)
        def _():
            send_sum(chunks - 1)
            for copy in extra:
                copy.start()

        @pl.when((c >= 1) & (c + 1 < chunks))
        def _():
            gather.relay(c + 1)

        @pl.when(c + 1 == chunks)
        def _():
            for i in range(chunks):
                gather.finish(i)
                scatter.finish(i)
            for copy in extra:
                copy.wait_recv()
            z.grad_beside[...] = z.from_beside[...]
            z.grad_across[...] = z.from_across[...]
            for copy in extra:
                copy.wait_send()


def between(n, hops, l, lengths, entered, cotangent, params, consts):
    gain, bias, qkv_w, qkv_b, feats, up_w, up_b, out_w, down_w, res_b = params
    rows, a = entered["qf"].shape
    hidden = up_w.shape[2]
    chunks = rows // CHUNK
    width = D // 4

    def early(w):
        return up_rows(w, 0, chunks)

    def after(w):
        return up_rows(w, chunks, chunks)

    def cube(shape):
        return pl.BlockSpec((1,) + shape, lambda i: (clipped(i, 0, chunks),) + (0,) * len(shape))

    table = entered["cos"].shape[1]
    ins = dict(
        lengths=(lengths, pl.BlockSpec(memory_space=pltpu.SMEM)),
        qf_in=(entered["qf"], early(a)),
        kf_in=(entered["kf"], early(a)),
        v_in=(entered["v"], early(a)),
        fi_in=(entered["fi"], early(D)),
        columns=(entered["columns"], early(128)),
        state_own=(entered["packed"], fixed((STATE_ROWS, a))),
        cotangent=(cotangent, fixed(cotangent.shape)),
        up_b=(up_b, fixed(up_b.shape)),
        ones=(consts["ones"], fixed((a, a))),
        full=(entered["full"], after(D)),
        res_b=(res_b, fixed(res_b.shape)),
        gain=(gain, fixed(gain.shape)),
        bias=(bias, fixed(bias.shape)),
        qkv_b=(qkv_b, fixed(qkv_b.shape)),
        feats=(feats, fixed(feats.shape)),
        map_t=(consts["map_t"], fixed((a, a))),
        cos=(entered["cos"], after(table)),
        sin=(entered["sin"], after(table)),
        columns_next=(entered["columns"], after(128)),
    )
    late = dict(
        up_w=(up_w, l),
        out_w=(out_w, l),
        down_w=(down_w, l),
        qkv_w=(qkv_w, l + 1),
        up_w_next=(up_w, l + 1),
    )
    outs = dict(
        att=(struct((rows, a), F32), early(a)),
        att_low=(struct((rows, a), BF), early(a)),
        ratio=(struct((rows, a), F32), early(a)),
        states=(struct((chunks, a, a), F32), cube((a, a))),
        totals=(struct((chunks, 8, a), F32), cube((8, a))),
        act=(struct((rows, hidden), BF), early(hidden)),
        slope=(struct((rows, hidden), BF), early(hidden)),
        own=(struct((rows, width), F32), after(width)),
        **project_made(rows, a, after),
        act_next=(struct((rows, hidden), BF), after(hidden)),
        slope_next=(struct((rows, hidden), BF), after(hidden)),
        packed=(struct((STATE_ROWS, a), F32), full((STATE_ROWS, a))),
        grad_beside=(struct((rows, width), BF), full((rows, width))),
        grad_across=(struct((rows, width), BF), full((rows, width))),
    )
    scratch = dict(
        gather=Gather.scratch(rows, width),
        scatter=Scatter.scratch(rows, width),
        from_beside=[pltpu.VMEM((rows, width), BF)],
        from_across=[pltpu.VMEM((rows, width), BF)],
        extra_sems=[pltpu.SemaphoreType.DMA((2, 2))],
        hand=HandOver.scratch(hops, a),
        mine=[pltpu.VMEM((rows, width), BF)],
        state_in=[pltpu.VMEM((STATE_ROWS, a), F32)],
        summed=[pltpu.VMEM((a, a), F32)],
        whole=[pltpu.VMEM((CHUNK, D), F32)],
        whole_low=[pltpu.VMEM((CHUNK, D), BF)],
        state=[pltpu.VMEM((a, a), F32)],
        total=[pltpu.VMEM((8, a), F32)],
    )
    return named_call(
        functools.partial(between_kernel, n, hops, l),
        "between",
        3,
        (2 * chunks,),
        ins,
        outs,
        scratch,
        2 * rows * D * (hidden * 3 + 4 * a) * 2,
        late,
    )


def pair_mask(begin, step):
    shape = (CHUNK, CHUNK)
    t = row_of(shape)
    s = lane_of(shape)
    return (s <= t) & ((s + step * CHUNK).astype(F32) >= begin)


def attention_chunk(step, refs, out, state, total):
    qf_ref, kf_ref, v_ref, begin_ref, keep_ref, in_ref, ones_ref = refs
    att_ref, low_ref, ratio_ref, states_ref, totals_ref = out

    @pl.when(step == 0)
    def _():
        state[...] = unpack_state(in_ref[0:FEATURES, :])
        total[...] = jnp.broadcast_to(in_ref[FEATURES : FEATURES + 1, :], total.shape)

    q = qf_ref[...]
    k = kf_ref[...]
    v = v_ref[...]
    begin = begin_ref[...]
    keep = keep_ref[...]
    ones = ones_ref[...]
    a = q.shape[1]
    mask = pair_mask(begin, step)
    head_of = lane_of((1, a)) // HEAD_DIM
    held = state[...]
    held_total = total[0:1, :]
    states_ref[0] = held
    totals_ref[0] = total[...]
    base = (step * CHUNK).astype(F32)
    use = jnp.where(begin < base, 1.0, 0.0)
    high, low = halves(held)
    num = use * (dot_nn(q, high) + dot_nn(q, low))
    den = use * head_sum(q.astype(F32) * held_total, ones)
    for head in range(a // HEAD_DIM):
        own = (head_of == head).astype(BF)
        scores = dot_nt(q * own, k)
        scores_low = jnp.where(mask, scores, 0.0).astype(BF)
        num = num + dot_nn(scores_low, v * own)
        den = den + dot_nn(scores_low, jnp.broadcast_to(own, (CHUNK, a)))
    ratio = keep / (den + 1.0 - keep)
    att = num * ratio
    ratio_ref[...] = ratio
    att_ref[...] = att
    low_ref[...] = att.astype(BF)
    end = begin[CHUNK - 1 : CHUNK, :]
    place = (row_of((CHUNK, 1)) + step * CHUNK).astype(F32)
    masked = jnp.where(place >= end, k.astype(F32), 0.0)
    passing = jnp.where(end < base, 1.0, 0.0)
    state[...] = passing * held + jnp.where(
        block_diagonal(a), dot_tn(masked.astype(BF), v), 0.0
    )
    total[...] = jnp.broadcast_to(
        passing * held_total + jnp.sum(masked, axis=0, keepdims=True), total.shape
    )


def lower_feed(grad, dw_ref, slope_ref, bias_ref, start):
    @pl.when(start)
    def _():
        bias_ref[...] = jnp.zeros_like(bias_ref)

    d_raised = (dot_nn(grad, dw_ref[...]) * slope_ref[...].astype(F32)).astype(BF)
    bias_ref[...] += jnp.sum(d_raised.astype(F32), axis=0, keepdims=True)
    return d_raised


def lower_attention(grad, ow_ref, ratio, att, qf, begin, ones, out, summed, packed, start):
    num_ref, den_ref = out

    @pl.when(start)
    def _():
        summed[...] = jnp.zeros_like(summed)
        packed[...] = jnp.zeros_like(packed)

    d_num = (dot_nn(grad, ow_ref[...]) * ratio).astype(BF)
    d_den = -head_sum(d_num.astype(F32) * att, ones)
    num_ref[...] = d_num
    den_ref[...] = d_den
    entering = jnp.where(begin < 0.0, qf.astype(F32), 0.0)
    summed[...] += dot_tn(entering.astype(BF), d_num)
    packed[FEATURES : FEATURES + 1, :] += jnp.sum(entering * d_den, axis=0, keepdims=True)


def tile_at(i):
    return pl.ds(pl.multiple_of(i * CHUNK, CHUNK), CHUNK)


def weight_tile(i, x_ref, y, out_ref):
    out_ref[tile_at(i), :] = dot_tn(x_ref[:, tile_at(i)], y).astype(BF)


def attention_back(turn, step, refs, state, total):
    (
        qf_ref,
        kf_ref,
        v_ref,
        num_ref,
        den_ref,
        begin_ref,
        states_ref,
        totals_ref,
        exit_ref,
    ) = refs

    @pl.when(turn == 0)
    def _():
        state[...] = unpack_state(exit_ref[0:FEATURES, :])
        total[...] = jnp.broadcast_to(exit_ref[FEATURES : FEATURES + 1, :], total.shape)

    q = qf_ref[...]
    k = kf_ref[...]
    v = v_ref[...]
    d_num = num_ref[...]
    d_den = den_ref[...]
    begin = begin_ref[...]
    a = q.shape[1]
    mask = pair_mask(begin, step)
    head_of = lane_of((1, a)) // HEAD_DIM
    base = (step * CHUNK).astype(F32)
    use = jnp.where(begin < base, 1.0, 0.0)
    end = begin[CHUNK - 1 : CHUNK, :]
    place = (row_of((CHUNK, 1)) + step * CHUNK).astype(F32)
    inside = jnp.where(place >= end, 1.0, 0.0)
    passing = jnp.where(end < base, 1.0, 0.0)
    held_high, held_low = halves(states_ref[0])
    held_total = totals_ref[0][0:1, :]
    after = state[...]
    after_total = total[0:1, :]
    after_high, after_low = halves(after)
    masked = (k.astype(F32) * inside).astype(BF)
    d_q = use * (dot_nt(d_num, held_high) + dot_nt(d_num, held_low) + d_den * held_total)
    d_k = inside * (dot_nt(v, after_high) + dot_nt(v, after_low) + after_total)
    d_v = dot_nn(masked, after_high) + dot_nn(masked, after_low)
    for head in range(a // HEAD_DIM):
        own = (head_of == head).astype(BF)
        q_own = q * own
        num_own = d_num * own
        scores_low = jnp.where(mask, dot_nt(q_own, k), 0.0).astype(BF)
        column = d_den[:, head * HEAD_DIM : head * HEAD_DIM + 1]
        d_scores = jnp.where(mask, dot_nt(num_own, v) + column, 0.0).astype(BF)
        d_q = d_q + dot_nn(d_scores, k * own)
        d_k = d_k + dot_tn(d_scores, q_own)
        d_v = d_v + dot_tn(scores_low, num_own)
    q_used = q.astype(F32) * use
    state[...] = passing * after + jnp.where(
        block_diagonal(a), dot_tn(q_used.astype(BF), d_num), 0.0
    )
    total[...] = jnp.broadcast_to(
        passing * after_total + jnp.sum(q_used * d_den, axis=0, keepdims=True), total.shape
    )
    return d_q, d_k, d_v


def features_back(grads, refs, feat_ref, bias_ref, start):
    d_q, d_k, d_v = grads
    qf_ref, kf_ref, k_ref, cos_ref, sin_ref, map_ref, ones_ref = refs

    @pl.when(start)
    def _():
        feat_ref[...] = jnp.zeros_like(feat_ref)
        bias_ref[...] = jnp.zeros_like(bias_ref)

    cos = twice(cos_ref[...])
    sin = twice(sin_ref[...])
    d_query = dot_nn(d_q * qf_ref[...].astype(F32), map_ref[...], HIGHEST)
    d_query = d_query * cos - swap_pairs(d_query) * sin
    d_key_log = d_k * kf_ref[...].astype(F32)
    feat_ref[...] += jnp.sum(d_key_log, axis=0, keepdims=True)
    d_key = dot_nn(d_key_log, map_ref[...], HIGHEST)
    d_key = d_key * cos - swap_pairs(d_key) * sin
    d_key = d_key - head_sum(d_key_log, ones_ref[...]) * k_ref[...].astype(F32) * (1.0 / HEAD_DIM)
    d_proj = join_heads(d_query, d_key, d_v).astype(BF)
    bias_ref[...] += jnp.sum(d_proj.astype(F32), axis=0, keepdims=True)
    return d_proj


def inputs_back(l, d_proj, raised_ref, w_ref, up_ref, normed_ref, gain, sums_ref, start):
    @pl.when(start)
    def _():
        sums_ref[...] = jnp.zeros_like(sums_ref)

    normed = normed_ref[...].astype(F32)
    d_attention = dot_nt(d_proj, w_ref[...])
    d_feed = dot_nt(raised_ref[...], up_ref[...])
    sums_ref[0:1, :] += jnp.sum(d_attention * normed, axis=0, keepdims=True)
    sums_ref[1:2, :] += jnp.sum(d_feed * normed, axis=0, keepdims=True)
    sums_ref[2:3, :] += jnp.sum(d_attention, axis=0, keepdims=True)
    sums_ref[3:4, :] += jnp.sum(d_feed, axis=0, keepdims=True)
    d_normed = (d_attention * gain[l, 0:1] + d_feed * gain[l, 1:2]).astype(BF)
    high, low = halves(d_normed.astype(F32) * normed)
    row = jnp.ones((8, D), BF)
    first = dot_nt(row, d_normed)
    second = dot_nt(row, high) + dot_nt(row, low)
    return d_normed, jnp.where(row_of(first.shape) == 0, first, second)


class RowSum:
    def __init__(self, h, buffers, sems):
        self.own, self.got, self.middle, self.across = buffers
        self.send, self.recv = sems
        self.beside = {"head": lax.bitwise_xor(h, 1)}
        self.beyond = {"head": lax.bitwise_xor(h, 2)}

    @staticmethod
    def scratch(rows):
        count = rows // CHUNK
        return [pltpu.VMEM((count, 8, CHUNK), F32)] * 4 + [pltpu.SemaphoreType.DMA((2, count))] * 2

    def copy(self, kind, c):
        source, target, where = (
            (self.own, self.got, self.beside),
            (self.middle, self.across, self.beyond),
        )[kind]
        return push(
            source.at[c], target.at[c], self.send.at[kind, c], self.recv.at[kind, c], where
        )

    def put(self, c, value):
        self.own[c] = value
        self.copy(0, c).start()

    def relay(self, c):
        self.copy(0, c).wait_recv()
        self.middle[c] = self.own[c] + self.got[c]
        self.copy(1, c).start()

    def total(self, c):
        self.copy(1, c).wait_recv()
        value = self.middle[c] + self.across[c]
        shape = (8, 128)
        eye = (row_of(shape) == lane_of(shape)).astype(F32)
        columns = dot_tn(value, eye, HIGHEST)
        return columns[:, 0:1], columns[:, 1:2]

    def finish(self, c):
        self.copy(0, c).wait_send()
        self.copy(1, c).wait_send()


def norm_back(before, inverse, unit, d_normed, sums):
    first, second = sums
    return before + inverse * (d_normed - first * (1.0 / D) - unit * (second * (1.0 / D)))


def ring_place(index, n):
    return jnp.where(index % 2 == 0, index // 2, n - 1 - index // 2)


def ring_index(place, n):
    return jnp.where(place < n // 2, 2 * place, 2 * (n - 1 - place) + 1)


BATCHES = 6


class Ring:
    def __init__(self, n, parts, source, held, sems, since=0, until=BATCHES, incoming=None):
        self.n, self.parts, self.source, self.held = n, parts, source, held
        self.send_sem, self.recv_sem = sems
        self.since, self.until, self.incoming = since, until, incoming
        self.share = D // n
        self.place = ring_place(lax.axis_index("seq"), n)
        self.right = ring_index(lax.rem(self.place + 1, n), n)
        self.left = ring_index(lax.rem(self.place + n - 1, n), n)
        self.base = self.slots(n, since, until)[0]
        self.first = 0 if incoming is None else self.bound(n, since)
        self.last = self.bound(n, until) - 1

    @staticmethod
    def bound(n, batch):
        return 1 + (n - 2) * batch // BATCHES

    @staticmethod
    def slots(n, since, until):
        base = Ring.bound(n, since) - 1
        return base, Ring.bound(n, until) - base

    @staticmethod
    def buffers(n, parts, since=0, until=BATCHES):
        count = Ring.slots(n, since, until)[1]
        return [pltpu.VMEM((count, D // n, part[2]), BF) for part in parts]

    @staticmethod
    def sems(n, parts):
        return [pltpu.SemaphoreType.DMA((len(parts), n - 1))] * 2

    def own(self, part, step):
        array, start, width, way = part
        n = self.n
        ahead = lax.rem(self.place - way * (1 + step) + 2 * n, n)
        rows = pl.ds(pl.multiple_of(ring_index(ahead, n) * self.share, self.share), self.share)
        return self.source[array].at[rows, pl.ds(start, width)]

    def slot(self, r, step):
        return self.held[r].at[step - self.base]

    def copy(self, r, step, block):
        return push(
            block,
            self.slot(r, step),
            self.send_sem.at[r, step],
            self.recv_sem.at[r, step],
            {"seq": self.right if self.parts[r][3] > 0 else self.left},
        )

    def add(self, r, step, arrived):
        own = self.own(self.parts[r], step)[...].astype(F32)
        block = self.slot(r, step - 1)
        block[...] = (arrived[...].astype(F32) + own).astype(BF)
        self.copy(r, step, block).start()

    def start(self):
        for r, part in enumerate(self.parts):
            if self.incoming is not None:
                self.add(r, self.first, self.incoming[r])
            else:
                self.copy(r, 0, self.own(part, 0)).start()

    def tick(self, step):
        for r in range(len(self.parts)):
            block = self.slot(r, step - 1)
            self.copy(r, step - 1, block).wait_recv()
            self.add(r, step, block)

    def batch(self, k):
        low, high = self.bound(self.n, k - 1), self.bound(self.n, k)
        if self.incoming is not None and k - 1 == self.since:
            low += 1
        if high - low == 1:
            self.tick(low)
        elif high > low:

            def one(step, carry):
                self.tick(step)
                return carry

            lax.fori_loop(low, high, one, 0)

    def sent(self):
        def one(step, carry):
            for r in range(len(self.parts)):
                self.copy(r, step, self.slot(r, step)).wait_send()
            return carry

        lax.fori_loop(self.first, self.last + 1, one, 0)

    def pause(self, out):
        for r in range(len(self.parts)):
            block = self.slot(r, self.last)
            self.copy(r, self.last, block).wait_recv()
            out[r][...] = block[...]
        self.sent()

    def finish(self, out):
        n = self.n
        for r, part in enumerate(self.parts):
            block = self.slot(r, n - 2)
            self.copy(r, n - 2, block).wait_recv()
            array, start, width, way = part
            out[array][:, pl.ds(start, width)] = block[...].astype(F32) + self.own(part, n - 1)[
                ...
            ].astype(F32)
        self.sent()


def halved(array, width, start=0):
    return (
        (array, start, width // 2, 1),
        (array, start + width // 2, width // 2, -1),
    )


def ring_out(n, parts):
    return [jax.ShapeDtypeStruct((D // n, part[2]), BF) for part in parts]


CREST_DOWN, CREST_UP, TURN_REST, TURN_DOWN, TURN_UP = 2, 2, 4, 1, 0


def loop(count, body):
    def one(c, carry):
        body(c)
        return carry

    lax.fori_loop(0, count, one, 0)


def unrolled(count, body):
    for c in range(count):
        body(jnp.int32(c))


def crest_kernel(n, hops, l, z):
    step = pl.program_id(0)
    h = lax.axis_index("head")
    rows, hidden = z.act.shape
    width = D // 4
    count = rows // CHUNK
    hand = HandOver(n, hops, rows, 1, z.state_own, z.hand[0], z.hand[1:])
    hand_back = HandOver(n, hops, rows, -1, z.packed, z.hand_back[0], z.hand_back[1:])
    begin, keep = begin_keep(z.columns)
    parts = halved(0, hidden)
    corner = push(
        z.grad_across,
        z.grad_corner,
        z.corner_sems.at[0],
        z.corner_sems.at[1],
        {"head": lax.bitwise_xor(h, 1)},
    )
    down = Ring(n, parts, (z.d_down,), z.down_held, z.down_sems, 0, CREST_DOWN)
    up = Ring(n, parts, (z.d_up,), z.up_held, z.up_sems, 0, CREST_UP)
    columns = pl.ds(pl.multiple_of(h * width, width), width)

    @pl.when(step == 0)
    def _():
        for copy in (
            z.late.grad_across,
            z.late.grad_own,
            z.late.grad_beside,
            z.late.down_w,
            z.late.slope,
        ):
            copy.start()
        hand.clear()
        hand_back.clear()
        greet(h, n, hops)
        hand.start()
        z.late.grad_across.wait()
        corner.start()
        z.d_res[...] = jnp.zeros_like(z.d_res)
        z.late.grad_own.wait()
        z.late.grad_beside.wait()
        for r, part in enumerate((z.grad_own, z.grad_beside, z.grad_across)):
            z.grad[:, block_columns(h, r, width)] = part[...]
        corner.wait_recv()
        z.grad[:, block_columns(h, 3, width)] = z.grad_corner[...]
        corner.wait_send()
        z.late.down_w.wait()
        z.late.slope.wait()
        z.late.act.start()

        def feed(c):
            here = rows_at(c)
            z.d_raised[here, :] = lower_feed(
                z.grad[here, :], z.down_w, z.slope.at[here, :], z.d_up_b, c == 0
            )
            z.d_res[...] += jnp.sum(z.grad[here, columns].astype(F32), axis=0, keepdims=True)

        unrolled(count, feed)
        z.sent.d_raised.start()
        z.late.act.wait()
        z.late.fi.start()
        unrolled(D // CHUNK, lambda i: weight_tile(i, z.grad, z.act[...], z.d_down))
        down.start()
        z.sent.d_down.start()
        z.late.fi.wait()
        z.late.out_w.start()
        unrolled(D // CHUNK, lambda i: weight_tile(i, z.fi, z.d_raised[...], z.d_up))
        up.start()
        z.sent.d_up.start()
        z.late.out_w.wait()
        z.state_in[...] = hand.total(z.lengths)

    @pl.when((step >= 1) & (step <= count))
    def _():
        c = step - 1
        here = rows_at(c)
        attention_chunk(
            c,
            (z.qf, z.kf, z.v, begin, keep, z.state_in, z.ones),
            (z.att, z.low_now, z.ratio, z.states, z.totals),
            z.state,
            z.total,
        )
        low = z.low_now[...]
        z.low[here, :] = low
        z.whole[...] = (dot_nt(low, z.out_w[...]) + dot_nt(z.act[here, :], z.down_w[...])).astype(
            BF
        )
        z.near[0] = z.whole[:, block_columns(h, 0, width)]
        z.near[1] = z.whole[:, block_columns(h, 2, width)]
        z.far[0] = z.whole[:, block_columns(h, 1, width)]
        z.far[1] = z.whole[:, block_columns(h, 3, width)]
        lower_attention(
            z.grad[here, :],
            z.out_w,
            z.ratio[...],
            z.att[...],
            z.qf[...],
            begin[...],
            z.ones[...],
            (z.d_num, z.d_den),
            z.summed,
            z.packed,
            c == 0,
        )
        at_steps(
            c,
            (
                (0, lambda: down.batch(1)),
                (1, lambda: up.batch(1)),
                (2, lambda: down.batch(2)),
                (3, lambda: up.batch(2)),
            ),
        )

    @pl.when(step == count + 1)
    def _():
        z.packed[0:FEATURES, :] = pack_state(z.summed[...])
        hand_back.start()
        unrolled(D // CHUNK, lambda i: weight_tile(i, z.grad, z.low[...], z.d_out))
        z.exit_state[...] = hand_back.total(z.lengths)
        down.pause((z.down_fore, z.down_aft))
        up.pause((z.up_fore, z.up_aft))
        for copy in every(z.sent):
            copy.wait()


def crest(n, hops, l, lengths, mid, pieces, tables, params, consts):
    gain, bias, qkv_w, qkv_b, feats, up_w, up_b, out_w, down_w, res_b = params
    cos, sin, columns = tables
    rows, a = mid["qf"].shape
    hidden = up_w.shape[2]
    count = rows // CHUNK
    width = D // 4
    parts = halved(0, hidden)

    def block(w):
        return up_rows(w, 1, count)

    def cube(shape):
        return pl.BlockSpec((1,) + shape, lambda i: (clipped(i, 1, count),) + (0,) * len(shape))

    quarter = pl.BlockSpec((2, CHUNK, width), lambda i: (0, clipped(i, 1, count), 0))
    ins = dict(
        lengths=(lengths, pl.BlockSpec(memory_space=pltpu.SMEM)),
        qf=(mid["qf"], block(a)),
        kf=(mid["kf"], block(a)),
        v=(mid["v"], block(a)),
        columns=(columns, block(128)),
        state_own=(mid["packed"], fixed((STATE_ROWS, a))),
        ones=(consts["ones"], fixed((a, a))),
    )
    late = dict(
        grad_across=pieces[2],
        grad_own=pieces[0],
        grad_beside=pieces[1],
        down_w=(down_w, l),
        slope=mid["slope_next"],
        act=mid["act_next"],
        fi=mid["fi"],
        out_w=(out_w, l),
    )
    fore, aft = ring_out(n, parts)
    outs = dict(
        d_up_b=(struct((1, hidden), F32), full((1, hidden))),
        d_res=(struct((1, width), F32), full((1, width))),
        ratio=(struct((rows, a), F32), block(a)),
        att=(struct((rows, a), F32), block(a)),
        states=(struct((count, a, a), F32), cube((a, a))),
        totals=(struct((count, 8, a), F32), cube((8, a))),
        d_num=(struct((rows, a), BF), block(a)),
        d_den=(struct((rows, a), F32), block(a)),
        near=(struct((2, rows, width), BF), quarter),
        far=(struct((2, rows, width), BF), quarter),
        d_out=(struct((D, a), BF), full((D, a))),
        exit_state=(struct((STATE_ROWS, a), F32), full((STATE_ROWS, a))),
        up_fore=(fore, full(fore.shape)),
        up_aft=(aft, full(aft.shape)),
        down_fore=(fore, full(fore.shape)),
        down_aft=(aft, full(aft.shape)),
    )
    scratch = dict(
        grad=[pltpu.VMEM((rows, D), BF)],
        grad_corner=[pltpu.VMEM((rows, width), BF)],
        corner_sems=[pltpu.SemaphoreType.DMA((2,))],
        hand=HandOver.scratch(hops, a),
        hand_back=HandOver.scratch(hops, a),
        down_held=Ring.buffers(n, parts, 0, CREST_DOWN),
        up_held=Ring.buffers(n, parts, 0, CREST_UP),
        down_sems=Ring.sems(n, parts),
        up_sems=Ring.sems(n, parts),
        state_in=[pltpu.VMEM((STATE_ROWS, a), F32)],
        packed=[pltpu.VMEM((STATE_ROWS, a), F32)],
        summed=[pltpu.VMEM((a, a), F32)],
        state=[pltpu.VMEM((a, a), F32)],
        total=[pltpu.VMEM((8, a), F32)],
        whole=[pltpu.VMEM((CHUNK, D), BF)],
        low_now=[pltpu.VMEM((CHUNK, a), BF)],
        low=[pltpu.VMEM((rows, a), BF)],
    )
    return named_call(
        functools.partial(crest_kernel, n, hops, l),
        "crest",
        4,
        (count + 2,),
        ins,
        outs,
        scratch,
        2 * rows * D * (hidden * 4 + 4 * a) * 2,
        late,
        dict(
            d_raised=struct((rows, hidden), BF),
            d_down=struct((D, hidden), BF),
            d_up=struct((D, hidden), BF),
        ),
    )


def back_step(z, l, h, step, count, scatter, row_sum, middle_work, end_work):
    c = count - 1 - step
    grads = attention_back(
        step,
        c,
        (
            z.qf, z.kf, z.v, z.d_num, z.d_den, begin_keep(z.columns)[0], z.states, z.totals,
            z.exit_state,
        ),
        z.state,
        z.total,
    )

    @pl.when(step >= 1)
    def _():
        scatter.relay(c + 1)
        row_sum.relay(c + 1)

    middle_work()
    start = step == 0
    d_proj = features_back(
        grads,
        (z.qf, z.kf, z.k, z.cos, z.sin, z.map, z.ones),
        z.d_feat,
        z.d_qkv_b,
        start,
    )
    z.proj_all[rows_at(c), :] = d_proj

    @pl.when(start)
    def _():
        z.late.qkv_w.wait()
        z.late.up_w.wait()

    d_normed, sums = inputs_back(
        l, d_proj, z.d_raised_in, z.qkv_w, z.up_w, z.normed, z.gain, z.sums, start
    )
    z.whole[...] = d_normed
    scatter.put(h, c, z.whole)
    row_sum.put(c, sums)
    end_work()


def back_arrays(l, local, lowered, tables, params, consts, exit_state, count):
    gain, bias, qkv_w, qkv_b, feats, up_w, up_b, out_w, down_w, res_b = params
    cos, sin, columns = tables
    qf, kf, v, k, normed, unit, inverse, states, totals = local
    d_raised, d_num, d_den = lowered
    a = qf.shape[1]

    def early(w):
        return down_rows(w, 0, count)

    return dict(
        qf=(qf, early(a)),
        kf=(kf, early(a)),
        v=(v, early(a)),
        k=(k, early(a)),
        d_num=(d_num, early(a)),
        d_den=(d_den, early(a)),
        columns=(columns, early(128)),
        cos=(cos, early(cos.shape[1])),
        sin=(sin, early(sin.shape[1])),
        states=(states, down_cube((a, a), 0, count)),
        totals=(totals, down_cube((8, a), 0, count)),
        exit_state=(exit_state, fixed(exit_state.shape)),
        map=(consts["map"], fixed((a, a))),
        ones=(consts["ones"], fixed((a, a))),
        d_raised_in=(d_raised, early(d_raised.shape[1])),
        normed=(normed, early(D)),
        gain=(gain, fixed(gain.shape)),
    )


def back_scratch(rows, a, width):
    return dict(
        scatter=Scatter.scratch(rows, width),
        row_sum=RowSum.scratch(rows),
        state=[pltpu.VMEM((a, a), F32)],
        total=[pltpu.VMEM((8, a), F32)],
        whole=[pltpu.VMEM((CHUNK, D), BF)],
        proj_all=[pltpu.VMEM((rows, 3 * a), BF)],
    )


def at_steps(step, table):
    for at, work in table:

        @pl.when(step == at)
        def _(work=work):
            work()


def turn_kernel(n, hops, l, z):
    step = pl.program_id(0)
    h = lax.axis_index("head")
    rows, width = z.mine.shape
    hidden = z.act.shape[1]
    count = rows // CHUNK
    scatter = Scatter(h, z.scatter[:5], z.scatter[5:])
    row_sum = RowSum(h, z.row_sum[:4], z.row_sum[4:])
    gather = Gather(h, z.mine, z.gather[:3], z.gather[3:])
    hand = HandOver(n, hops, rows, -1, z.packed, z.hand[0], z.hand[1:])
    parts = halved(0, hidden)
    rest_parts = rest_of(z.d_qkv.shape[1], z.d_out_next.shape[1])
    down = Ring(
        n, parts, (z.d_down_next,), z.down_held, z.down_sems, CREST_DOWN,
        incoming=(z.down_fore, z.down_aft),
    )
    up = Ring(
        n, parts, (z.d_up_next,), z.up_held, z.up_sems, CREST_UP,
        incoming=(z.up_fore_in, z.up_aft_in),
    )
    rest = Ring(n, rest_parts, (z.d_qkv, z.d_out_next), z.rest_held, z.rest_sems, 0, TURN_REST)
    new_down = Ring(n, parts, (z.d_down,), z.new_down_held, z.new_down_sems, 0, TURN_DOWN)
    new_up = Ring(n, parts, (z.d_up,), z.new_up_held, z.new_up_sems, 0, TURN_UP)

    def sum_up(o):
        c = count - 1 - o
        here = rows_at(c)
        new = norm_back(
            z.before[here, :].astype(F32),
            z.inverse[here, 0:1],
            z.unit[here, :],
            scatter.total(c),
            row_sum.total(c),
        )
        z.after[here, :] = new
        z.mine[here, :] = new.astype(BF)
        z.d_res[...] += jnp.sum(new, axis=0, keepdims=True)
        gather.start(c)

    @pl.when(step == 0)
    def _():
        z.late.d_down_next.start()
        z.late.d_up_next.start()
        hand.clear()
        greet(h, n, hops)
        z.late.d_down_next.wait()
        down.start()
        z.late.d_up_next.wait()
        up.start()
        z.late.qkv_w.start()
        z.late.up_w.start()
        z.d_res[...] = jnp.zeros_like(z.d_res)

    @pl.when(step < count)
    def _():
        def middle_work():
            at_steps(
                step,
                (
                    (1, z.late.before.start),
                    (1, z.late.inverse.start),
                    (1, z.late.unit.start),
                    (2, z.late.ai.start),
                    (2, z.late.d_out_next.start),
                    (3, z.late.down_w.start),
                    (3, z.late.slope.start),
                    (1, lambda: up.batch(CREST_UP + 1)),
                    (1, lambda: up.batch(CREST_UP + 2)),
                    (2, lambda: up.batch(CREST_UP + 3)),
                    (2, z.late.before.wait),
                    (2, z.late.inverse.wait),
                    (2, z.late.unit.wait),
                    (3, lambda: up.batch(CREST_UP + 4)),
                ),
            )

        def end_work():
            at_steps(
                step,
                (
                    (0, lambda: down.batch(CREST_DOWN + 1)),
                    (0, lambda: down.batch(CREST_DOWN + 2)),
                    (1, lambda: down.batch(CREST_DOWN + 3)),
                    (2, lambda: down.batch(CREST_DOWN + 4)),
                ),
            )

            @pl.when(step >= 2)
            def _():
                sum_up(step - 2)

        back_step(z, l + 1, h, step, count, scatter, row_sum, middle_work, end_work)

    def feed(c):
        gather.ready(c)
        here = rows_at(c)
        for r, part in enumerate(gather.pieces(c)):
            z.grad[here, block_columns(h, r, width)] = part
        z.d_raised_out[here, :] = lower_feed(
            z.grad[here, :], z.down_w, z.slope.at[here, :], z.d_up_b, c == count - 1
        )

    def attention(c):
        here = rows_at(c)
        lower_attention(
            z.grad[here, :],
            z.out_w,
            z.ratio[here, :],
            z.att[here, :],
            z.qf_late[here, :],
            begin_keep(z.columns_late)[0][here, :],
            z.ones[...],
            (z.d_num_out.at[here, :], z.d_den_out.at[here, :]),
            z.summed,
            z.packed,
            c == count - 1,
        )

    def qkv_tiles(low, high):
        for i in range(low, high):
            weight_tile(i, z.ai, z.proj_all[...], z.d_qkv)

    @pl.when(step == count)
    def _():
        z.late.ai.wait()
        late_attention = (
            z.late.out_w,
            z.late.ratio,
            z.late.att,
            z.late.qf_late,
            z.late.columns_late,
        )
        for copy in late_attention:
            copy.start()
        z.late.act.start()
        qkv_tiles(0, 1)
        scatter.relay(0)
        row_sum.relay(0)
        gather.relay(count - 1)
        sum_up(count - 2)
        qkv_tiles(1, 4)
        z.late.d_out_next.wait()
        rest.start()
        z.sent.d_qkv.start()
        down.finish((z.sum_down,))
        z.late.down_w.wait()
        z.late.slope.wait()
        sum_up(count - 1)
        feed(jnp.int32(count - 1))
        gather.relay(count - 2)
        up.finish((z.sum_up,))
        feed(jnp.int32(count - 2))
        gather.relay(count - 3)
        for copy in late_attention:
            copy.wait()
        z.late.fi.start()
        z.late.att_low.start()
        loop(2, lambda i: attention(count - 1 - i))
        gather.relay(0)
        feed(jnp.int32(count - 3))
        attention(jnp.int32(count - 3))
        rest.batch(1)
        feed(jnp.int32(0))
        attention(jnp.int32(0))
        z.packed[0:FEATURES, :] = pack_state(z.summed[...])
        hand.start()
        rest.batch(2)
        z.sent.d_raised_out.start()
        z.sent.d_num_out.start()
        z.sent.d_den_out.start()
        z.late.act.wait()
        loop(D // CHUNK, lambda i: weight_tile(i, z.grad, z.act[...], z.d_down))
        new_down.start()
        z.sent.d_down.start()
        rest.batch(3)
        z.late.fi.wait()
        loop(D // CHUNK, lambda i: weight_tile(i, z.fi, z.d_raised_out[...], z.d_up))
        new_up.start()
        z.sent.d_up.start()
        z.late.att_low.wait()
        rest.batch(4)
        new_down.batch(1)
        loop(D // CHUNK, lambda i: weight_tile(i, z.grad, z.att_low[...], z.d_out))
        for i in range(count):
            gather.finish(i)
            scatter.finish(i)
            row_sum.finish(i)
        z.exit_out[...] = hand.total(z.lengths)
        new_up.pause((z.up_fore, z.up_aft))
        rest.pause((z.rest_a, z.rest_b, z.rest_c, z.rest_d))
        new_down.pause((z.new_fore, z.new_aft))
        for copy in every(z.sent):
            copy.wait()


def rest_of(qkv, out):
    return halved(0, qkv) + halved(1, out)


def turn(
    n, hops, l, lengths, local, top, before, ai, lower_in, tables, params, consts
):
    gain, bias, qkv_w, qkv_b, feats, up_w, up_b, out_w, down_w, res_b = params
    cos, sin, columns = tables
    act, slope, ratio, att, att_low, fi, qf = lower_in
    rows, a = qf.shape
    hidden = up_w.shape[2]
    count = rows // CHUNK
    width = D // 4
    share = D // n
    lowered = (top["d_raised"], top["d_num"], top["d_den"])
    parts = halved(0, hidden)
    rest_parts = rest_of(3 * a, a)

    def whole(array):
        return (array, fixed(array.shape))

    ins = dict(
        lengths=(lengths, pl.BlockSpec(memory_space=pltpu.SMEM)),
        **back_arrays(l + 1, local, lowered, tables, params, consts, top["exit_state"], count),
        down_fore=whole(top["down_fore"]),
        down_aft=whole(top["down_aft"]),
        up_fore_in=whole(top["up_fore"]),
        up_aft_in=whole(top["up_aft"]),
    )
    late = dict(
        d_down_next=top["d_down"],
        d_up_next=top["d_up"],
        qkv_w=(qkv_w, l + 1),
        up_w=(up_w, l + 1),
        before=before,
        inverse=local[6],
        unit=local[5],
        ai=ai,
        d_out_next=top["d_out"],
        down_w=(down_w, l),
        slope=slope,
        out_w=(out_w, l),
        ratio=ratio,
        att=att,
        qf_late=qf,
        columns_late=columns,
        act=act,
        fi=fi,
        att_low=att_low,
    )
    rests = ring_out(n, rest_parts)
    fore, aft = ring_out(n, parts)
    outs = dict(
        d_feat=(struct((1, a), F32), full((1, a))),
        d_qkv_b=(struct((1, 3 * a), F32), full((1, 3 * a))),
        sums=(struct((8, D), F32), full((8, D))),
        after=(struct((rows, width), F32), full((rows, width))),
        d_res=(struct((1, width), F32), full((1, width))),
        d_up_b=(struct((1, hidden), F32), full((1, hidden))),
        d_out=(struct((D, a), BF), full((D, a))),
        exit_out=(struct((STATE_ROWS, a), F32), full((STATE_ROWS, a))),
        sum_down=(struct((share, hidden), F32), full((share, hidden))),
        sum_up=(struct((share, hidden), F32), full((share, hidden))),
        rest_a=(rests[0], full(rests[0].shape)),
        rest_b=(rests[1], full(rests[1].shape)),
        rest_c=(rests[2], full(rests[2].shape)),
        rest_d=(rests[3], full(rests[3].shape)),
        new_fore=(fore, full(fore.shape)),
        new_aft=(aft, full(aft.shape)),
        up_fore=(fore, full(fore.shape)),
        up_aft=(aft, full(aft.shape)),
    )
    scratch = dict(
        **back_scratch(rows, a, width),
        gather=Gather.scratch(rows, width),
        hand=HandOver.scratch(hops, a),
        down_held=Ring.buffers(n, parts, CREST_DOWN),
        up_held=Ring.buffers(n, parts, CREST_UP),
        rest_held=Ring.buffers(n, rest_parts, 0, TURN_REST),
        new_down_held=Ring.buffers(n, parts, 0, TURN_DOWN),
        new_up_held=Ring.buffers(n, parts, 0, TURN_UP),
        down_sems=Ring.sems(n, parts),
        up_sems=Ring.sems(n, parts),
        rest_sems=Ring.sems(n, rest_parts),
        new_down_sems=Ring.sems(n, parts),
        new_up_sems=Ring.sems(n, parts),
        mine=[pltpu.VMEM((rows, width), BF)],
        packed=[pltpu.VMEM((STATE_ROWS, a), F32)],
        summed=[pltpu.VMEM((a, a), F32)],
        grad=[pltpu.VMEM((rows, D), BF)],
    )
    return named_call(
        functools.partial(turn_kernel, n, hops, l),
        "turn",
        5,
        (count + 1,),
        ins,
        outs,
        scratch,
        2 * rows * D * (hidden * 4 + 8 * a) * 2,
        late,
        dict(
            d_qkv=struct((D, 3 * a), BF),
            d_num_out=struct((rows, a), BF),
            d_den_out=struct((rows, a), F32),
            d_raised_out=(struct((rows, hidden), BF), "slope"),
            d_down=struct((D, hidden), BF),
            d_up=struct((D, hidden), BF),
        ),
    )


class Small:
    def __init__(self, h, n, refs, sems):
        self.near, self.far, self.got, self.middle, self.across, self.bundle, self.other = refs
        self.head_send, self.head_recv, self.seq_send, self.seq_recv = sems
        self.h, self.n = h, n
        self.here = lax.axis_index("seq")

    @staticmethod
    def rounds(n):
        return max(1, (n - 1).bit_length())

    @staticmethod
    def scratch(n, width):
        r = Small.rounds(n)
        dma = pltpu.SemaphoreType.DMA
        return (
            [pltpu.VMEM((2, 16, width), F32)] * 3
            + [pltpu.VMEM((16, width), F32)] * 2
            + [pltpu.VMEM((r + 1, 32, width), F32), pltpu.VMEM((r, 32, width), F32)]
            + [dma((2,)), dma((2,)), dma((r,)), dma((r,))]
        )

    def head_copy(self, kind):
        source, target, mask = (
            (self.far, self.got, 1),
            (self.middle, self.across, 2),
        )[kind]
        return push(
            source,
            target,
            self.head_send.at[kind],
            self.head_recv.at[kind],
            {"head": lax.bitwise_xor(self.h, mask)},
        )

    def seq_copy(self, k):
        return push(
            self.bundle.at[k],
            self.other.at[k],
            self.seq_send.at[k],
            self.seq_recv.at[k],
            {"seq": lax.bitwise_xor(self.here, 1 << k)},
        )

    def put(self, sums):
        width = self.near.shape[2]
        for l, ref in enumerate(sums):
            at = slice(8 * l, 8 * l + 8)
            self.near[0, at, :] = ref[:, block_columns(self.h, 0, width)]
            self.near[1, at, :] = ref[:, block_columns(self.h, 2, width)]
            self.far[0, at, :] = ref[:, block_columns(self.h, 1, width)]
            self.far[1, at, :] = ref[:, block_columns(self.h, 3, width)]
        self.head_copy(0).start()

    def relay(self):
        self.head_copy(0).wait_recv()
        self.middle[...] = self.near[1] + self.got[1]
        self.head_copy(1).start()

    def pack(self, rows):
        self.head_copy(1).wait_recv()
        norms = self.near[0] + self.got[0] + self.across[...]
        width = self.near.shape[2]
        self.bundle[0] = jnp.zeros_like(self.bundle[0])
        for l, refs in enumerate(rows):
            self.bundle[0, 16 * l : 16 * l + 4, :] = norms[8 * l : 8 * l + 4]
            at = 16 * l + 4
            for ref in refs:
                for i in range(ref.shape[1] // width):
                    self.bundle[0, at : at + 1, :] = ref[:, i * width : (i + 1) * width]
                    at += 1
        self.seq_copy(0).start()

    def round(self, k):
        self.seq_copy(k).wait_recv()
        self.bundle[k + 1] = self.bundle[k] + self.other[k]
        if k + 1 < self.rounds(self.n):
            self.seq_copy(k + 1).start()

    def finish(self):
        for kind in range(2):
            self.head_copy(kind).wait_send()
        for k in range(self.rounds(self.n)):
            self.seq_copy(k).wait_send()


def greet_all(h, n):
    barrier = pltpu.get_barrier_semaphore()

    def signal(where):
        pl.semaphore_signal(barrier, inc=1, device_id=where, device_id_type=pl.DeviceIdType.MESH)

    signal({"head": lax.bitwise_xor(h, 1)})
    signal({"head": lax.bitwise_xor(h, 2)})
    here = lax.axis_index("seq")
    place = ring_place(here, n)
    signal({"seq": ring_index(lax.rem(place + 1, n), n)})
    signal({"seq": ring_index(lax.rem(place + n - 1, n), n)})
    rounds = Small.rounds(n)
    for k in range(rounds):
        signal({"seq": lax.bitwise_xor(here, 1 << k)})
    pl.semaphore_wait(barrier, 4 + rounds)


def leave_kernel(n, z):
    step = pl.program_id(0)
    h = lax.axis_index("head")
    rows = z.proj_all.shape[0]
    count = rows // CHUNK
    hidden, a = z.d_down.shape[1], z.d_out.shape[1]
    scatter = Scatter(h, z.scatter[:5], z.scatter[5:])
    row_sum = RowSum(h, z.row_sum[:4], z.row_sum[4:])
    small = Small(h, n, z.small[:7], z.small[7:])
    rest = Ring(
        n, rest_of(3 * a, a), (z.d_qkv_next, z.d_out_next), z.rest_held, z.rest_sems, TURN_REST,
        incoming=(z.rest_a, z.rest_b, z.rest_c, z.rest_d),
    )
    down = Ring(
        n, halved(0, hidden), (z.d_down,), z.down_held, z.down_sems, TURN_DOWN,
        incoming=(z.new_fore, z.new_aft),
    )
    up = Ring(
        n, halved(0, hidden), (z.d_up,), z.up_held, z.up_sems, TURN_UP,
        incoming=(z.up_fore, z.up_aft),
    )
    out = Ring(n, halved(0, a), (z.d_out,), z.out_held, z.out_sems)
    first_parts, second_parts = split_last(3 * a)
    last = Ring(n, first_parts, (z.d_qkv,), z.last_held, z.last_sems)
    more = Ring(n, second_parts, (z.d_qkv,), z.more_held, z.more_sems)
    width = z.res_b.shape[1] // 4
    columns = pl.ds(pl.multiple_of(h * width, width), width)
    result = Scatter(h, (z.near, z.far) + tuple(z.result[:3]), z.result[3:])

    def sum_up(o):
        here = rows_at(count - 1 - o)
        z.after[here, :] = norm_back(
            z.before[here, :],
            z.inverse[here, 0:1],
            z.unit[here, :],
            scatter.total(count - 1 - o),
            row_sum.total(count - 1 - o),
        )

    @pl.when(step == 0)
    def _():
        z.late.d_qkv_next.start()
        z.late.d_down.start()
        z.late.d_up.start()
        greet_all(h, n)
        z.late.d_qkv_next.wait()
        rest.start()
        z.late.d_down.wait()
        down.start()
        z.late.d_up.wait()
        up.start()
        out.start()
        z.late.qkv_w.start()
        z.late.up_w.start()

    @pl.when(step < count)
    def _():
        def middle_work():
            at_steps(
                step,
                (
                    (1, z.late.before.start),
                    (1, z.late.inverse.start),
                    (1, z.late.unit.start),
                    (1, z.late.near.start),
                    (1, z.late.far.start),
                    (2, z.late.ai.start),
                    (3, z.late.own.start),
                    (1, lambda: down.batch(TURN_DOWN + 1)),
                    (1, lambda: down.batch(TURN_DOWN + 2)),
                    (2, lambda: rest.batch(TURN_REST + 2)),
                    (2, z.late.before.wait),
                    (2, z.late.inverse.wait),
                    (2, z.late.unit.wait),
                    (3, lambda: up.batch(TURN_UP + 3)),
                ),
            )

        def end_work():
            at_steps(
                step,
                (
                    (0, lambda: rest.batch(TURN_REST + 1)),
                    (1, lambda: up.batch(TURN_UP + 1)),
                    (1, lambda: up.batch(TURN_UP + 2)),
                    (1, lambda: out.batch(1)),
                    (2, z.late.near.wait),
                    (2, z.late.far.wait),
                    (2, lambda: loop(count, lambda i: result.copy(0, i).start())),
                    (3, lambda: loop(count, result.relay)),
                    (2, lambda: down.batch(TURN_DOWN + 3)),
                    (3, lambda: out.batch(2)),
                ),
            )

            @pl.when(step >= 2)
            def _():
                sum_up(step - 2)

        back_step(z, 0, h, step, count, scatter, row_sum, middle_work, end_work)

    @pl.when(step == count)
    def _():
        scatter.relay(0)
        row_sum.relay(0)
        small.put((z.sums, z.sums_next))
        z.late.ai.wait()
        loop(D // CHUNK, lambda i: weight_tile(i, z.ai, z.proj_all[...], z.d_qkv))
        last.start()
        more.start()
        rest.finish((z.sum_qkv_next, z.sum_out_next))
        down.batch(TURN_DOWN + 4)
        sum_up(2)
        small.relay()
        last.batch(1)
        more.batch(1)
        up.batch(TURN_UP + 4)
        out.batch(3)
        sum_up(3)
        small.pack(
            (
                (z.d_qkv_b, z.d_up_b, z.d_feat[...] / feature_row(z.feats, 0), z.d_res),
                (
                    z.d_qkv_b_next,
                    z.d_up_b_next,
                    z.d_feat_next[...] / feature_row(z.feats, 1),
                    z.d_res_next,
                ),
            )
        )
        last.batch(2)
        more.batch(2)
        down.batch(6)
        out.batch(4)
        small.round(0)
        last.batch(3)
        more.batch(3)
        up.batch(5)
        last.batch(4)
        more.batch(4)
        small.round(1)
        down.finish((z.sum_down,))
        out.batch(5)
        last.batch(5)
        more.batch(5)
        up.batch(6)
        for k in range(2, Small.rounds(n)):
            small.round(k)
        z.late.own.wait()

        def place(i):
            here = rows_at(i)
            z.out[here, :] = z.own[here, :] + result.total(i) + z.res_b[1:2, columns]

        loop(count, place)
        last.batch(6)
        more.batch(6)
        out.batch(6)
        z.bundle[...] = small.bundle[Small.rounds(n)]
        small.finish()
        for i in range(count):
            scatter.finish(i)
            row_sum.finish(i)
            result.finish(i)
        up.finish((z.sum_up,))
        last.finish((z.sum_qkv,))
        more.finish((z.sum_qkv,))
        out.finish((z.sum_out,))


def split_last(width):
    third = width // 3
    half = third // 2
    return (
        ((0, 0, third, 1), (0, third, half, -1)),
        ((0, third + half, half, 1), (0, 2 * third, third, -1)),
    )


def leave(n, local, turned, top, before, ai, own, tables, params, consts):
    qf = local[0]
    rows, a = qf.shape
    lowered = (turned["d_raised_out"], turned["d_num_out"], turned["d_den_out"])
    hidden = lowered[0].shape[1]
    count = rows // CHUNK
    width = D // 4
    share = D // n
    rest_parts, wide_parts = rest_of(3 * a, a), halved(0, hidden)
    out_parts = halved(0, a)
    first_parts, second_parts = split_last(3 * a)

    def whole(array):
        return (array, fixed(array.shape))

    ins = dict(
        **back_arrays(0, local, lowered, tables, params, consts, turned["exit_out"], count),
        d_out_next=whole(top["d_out"]),
        d_out=whole(turned["d_out"]),
        new_fore=whole(turned["new_fore"]),
        new_aft=whole(turned["new_aft"]),
        up_fore=whole(turned["up_fore"]),
        up_aft=whole(turned["up_aft"]),
        res_b=whole(params[9]),
        feats=whole(params[4]),
        rest_a=whole(turned["rest_a"]),
        rest_b=whole(turned["rest_b"]),
        rest_c=whole(turned["rest_c"]),
        rest_d=whole(turned["rest_d"]),
        d_up_b=whole(turned["d_up_b"]),
        d_res=whole(turned["d_res"]),
        sums_next=whole(turned["sums"]),
        d_qkv_b_next=whole(turned["d_qkv_b"]),
        d_up_b_next=whole(top["d_up_b"]),
        d_feat_next=whole(turned["d_feat"]),
        d_res_next=whole(top["d_res"]),
    )
    gain, bias, qkv_w, qkv_b, feats, up_w, up_b, out_w, down_w, res_b = params
    late = dict(
        d_qkv_next=turned["d_qkv"],
        d_down=turned["d_down"],
        d_up=turned["d_up"],
        qkv_w=(qkv_w, 0),
        up_w=(up_w, 0),
        before=before,
        inverse=local[6],
        unit=local[5],
        ai=ai,
        near=top["near"],
        far=top["far"],
        own=own,
    )

    def result(shape):
        return (struct(shape, F32), full(shape))

    outs = dict(
        after=result((rows, width)),
        out=result((rows, width)),
        bundle=result((32, width)),
        sum_qkv_next=result((share, 3 * a)),
        sum_out_next=result((share, a)),
        sum_qkv=result((share, 3 * a)),
        sum_out=result((share, a)),
        sum_down=result((share, hidden)),
        sum_up=result((share, hidden)),
    )
    scratch = dict(
        **back_scratch(rows, a, width),
        small=Small.scratch(n, width),
        rest_held=Ring.buffers(n, rest_parts, TURN_REST),
        down_held=Ring.buffers(n, wide_parts, TURN_DOWN),
        up_held=Ring.buffers(n, wide_parts, TURN_UP),
        out_held=Ring.buffers(n, out_parts),
        last_held=Ring.buffers(n, first_parts),
        more_held=Ring.buffers(n, second_parts),
        result=Scatter.scratch(rows, width)[2:],
        rest_sems=Ring.sems(n, rest_parts),
        down_sems=Ring.sems(n, wide_parts),
        up_sems=Ring.sems(n, wide_parts),
        out_sems=Ring.sems(n, out_parts),
        last_sems=Ring.sems(n, first_parts),
        more_sems=Ring.sems(n, second_parts),
        d_qkv=[pltpu.VMEM((D, 3 * a), BF)],
        d_feat=[pltpu.VMEM((1, a), F32)],
        d_qkv_b=[pltpu.VMEM((1, 3 * a), F32)],
        sums=[pltpu.VMEM((8, D), F32)],
    )
    return named_call(
        functools.partial(leave_kernel, n),
        "leave",
        6,
        (count + 1,),
        ins,
        outs,
        scratch,
        2 * rows * D * (hidden + 8 * a) * 3,
        late,
    )


def on_device(
    acts,
    cotangent,
    lengths,
    keep_mask,
    ln_gain,
    ln_bias,
    qkv_w,
    qkv_b,
    feat_w,
    out_w,
    up_w,
    up_b,
    down_w,
    res_b,
):
    rows, width = acts.shape
    heads = feat_w.shape[1]
    a = heads * HEAD_DIM
    n = lax.axis_size("seq")
    tokens = rows * n
    longest = 2048 if tokens <= 8192 else 4096
    hops = -(-longest // rows)
    h = lax.axis_index("head").astype(jnp.int32)
    first = lax.axis_index("seq") * rows

    keep_rows = keep_mask.reshape(rows // 128, 128)
    half = ROT // 2
    rates = np.zeros((2, HEAD_DIM))
    rates[0, :half] = ROTARY_BASE ** (-2.0 * np.arange(half) / ROT)
    rates[0, half:ROT] = rates[0, :half]
    rates[1, :half] = -1.0
    rates[1, half:ROT] = 1.0
    rates = jnp.asarray(np.tile(rates, (1, 2)), F32)

    fold = sample_points(FEATURES, HEAD_DIM) @ cosine_table(HEAD_DIM) / math.sqrt(HEAD_DIM)
    eye = np.eye(heads)
    consts = {
        "map": jnp.asarray(np.kron(eye, fold), F32),
        "map_t": jnp.asarray(np.kron(eye, fold.T), F32),
        "ones": jnp.asarray(np.kron(eye, np.ones((HEAD_DIM, HEAD_DIM))), BF),
    }

    entered = enter(
        n, lengths, acts, keep_rows, ln_gain, ln_bias, qkv_w, qkv_b, feat_w, rates, consts
    )
    tables = (entered["cos"], entered["sin"], entered["columns"])
    params = (ln_gain, ln_bias, qkv_w, qkv_b, feat_w, up_w, up_b, out_w, down_w, res_b)

    def back_local(made, states, totals):
        ai, fi, normed, unit, inverse, qf, kf, v, k = made
        return (qf, kf, v, k, normed, unit, inverse, states, totals)

    first_made = tuple(entered[name] for name, width_of, kind in PROJECT_KINDS)
    mid = between(n, hops, 0, lengths, entered, cotangent, params, consts)
    pieces = (cotangent, mid["grad_beside"], mid["grad_across"])
    local = back_local(first_made, mid["states"], mid["totals"])
    made = tuple(mid[name] for name, width_of, kind in PROJECT_KINDS)
    lower_in = (
        mid["act"], mid["slope"], mid["ratio"], mid["att"], mid["att_low"], entered["fi"],
        entered["qf"],
    )
    top = crest(n, hops, 1, lengths, mid, pieces, tables, params, consts)
    turned = turn(
        n,
        hops,
        0,
        lengths,
        back_local(made, top["states"], top["totals"]),
        top,
        cotangent,
        made[0],
        lower_in,
        tables,
        params,
        consts,
    )
    left = leave(n, local, turned, top, turned["after"], first_made[0], mid["own"], tables, params, consts)
    hidden = up_w.shape[2]
    bundle = left["bundle"].reshape(LAYERS, 16, width)
    kinds = 3 * a // width
    ups = hidden // width
    at = 4 + kinds + ups
    return (
        left["out"],
        left["after"],
        jnp.stack([left["sum_qkv"], left["sum_qkv_next"]]),
        jnp.stack([left["sum_out"], left["sum_out_next"]]),
        jnp.stack([left["sum_up"], turned["sum_up"]]),
        jnp.stack([left["sum_down"], turned["sum_down"]]),
        bundle[:, 4 : 4 + kinds].reshape(LAYERS, 3 * a),
        bundle[:, 4 + kinds : at].reshape(LAYERS, hidden),
        bundle[:, at].reshape(LAYERS, heads, FEATURES),
        bundle[:, 0:2],
        bundle[:, 2:4],
        bundle[:, at + 1],
    )


def solution(mesh):
    return jax.shard_map(
        on_device,
        mesh=mesh,
        in_specs=(
            P("seq", "head"),
            P("seq", "head"),
            P(),
            P("seq"),
            P(),
            P(),
            P(None, None, "head"),
            P(None, "head"),
            P(None, "head", None),
            P(None, None, "head"),
            P(None, None, "head"),
            P(None, "head"),
            P(None, None, "head"),
            P(),
        ),
        out_specs=(
            P("seq", "head"),
            P("seq", "head"),
            P(None, "seq", "head"),
            P(None, "seq", "head"),
            P(None, "seq", "head"),
            P(None, "seq", "head"),
            P(None, "head"),
            P(None, "head"),
            P(None, "head", None),
            P(None, None, "head"),
            P(None, None, "head"),
            P(None, "head"),
        ),
        check_vma=False,
    )
```

```python
import functools
import math

import jax
import jax.numpy as jnp
import numpy as np
from jax import lax
from jax.experimental import pallas as pl
from jax.experimental.pallas import tpu as pltpu
from jax.sharding import PartitionSpec as P

D = 1024
HEAD_DIM = 64
ROT = 16
FEATURES = 64
LAYERS = 2
CHUNK = 256

EPSILON = 1e-05
ROTARY_BASE = 10000.0
HIGHEST = lax.Precision.HIGHEST
BF = jnp.bfloat16
F32 = jnp.float32
STATE_ROWS = 72
VMEM_BYTES = 60 * 1024 * 1024


def prime_numbers(count):
    found = []
    candidate = 2
    while len(found) < count:
        if all((candidate % prime != 0 for prime in found)):
            found.append(candidate)
        candidate = candidate + 1
    return found


def sample_points(rows, columns):
    roots = np.sqrt(np.array(prime_numbers(2 * columns)) * 1.0)
    fractions = roots - np.floor(roots)
    grid = np.outer(np.arange(1, rows + 1) * 1.0, fractions) % 1.0
    radius = np.sqrt(-2.0 * np.log(1.0 - grid[:, :columns]))
    return radius * np.cos(2.0 * math.pi * grid[:, columns:])


def cosine_table(size):
    wave = np.arange(size)[:, None] * 1.0
    place = np.arange(size)[None, :] * 1.0
    table = np.cos(math.pi * (place + 0.5) * wave / size) * math.sqrt(2.0 / size)
    return table * np.where(wave == 0, math.sqrt(0.5), 1.0)


def dot_nn(a, b, precision=None):
    return lax.dot_general(
        a, b, (((1,), (0,)), ((), ())), precision=precision, preferred_element_type=F32
    )


def dot_nt(a, b, precision=None):
    return lax.dot_general(
        a, b, (((1,), (1,)), ((), ())), precision=precision, preferred_element_type=F32
    )


def dot_tn(a, b, precision=None):
    return lax.dot_general(
        a, b, (((0,), (0,)), ((), ())), precision=precision, preferred_element_type=F32
    )


def halves(wide):
    high = wide.astype(BF)
    return high, (wide - high.astype(F32)).astype(BF)


def lane_of(shape):
    return lax.broadcasted_iota(jnp.int32, shape, 1)


def row_of(shape):
    return lax.broadcasted_iota(jnp.int32, shape, 0)


def swap_pairs(x):
    width = x.shape[1]
    later = pltpu.roll(x, width - ROT // 2, 1)
    earlier = pltpu.roll(x, ROT // 2, 1)
    return jnp.where(lane_of(x.shape) % ROT < ROT // 2, later, earlier)


def twice(table):
    return jnp.concatenate([table, table], axis=1)


def block_columns(h, r, width):
    return pl.ds(pl.multiple_of(lax.bitwise_xor(h, r) * width, width), width)


def split_heads(projected):
    heads = projected.shape[1] // (3 * HEAD_DIM)
    return [
        jnp.concatenate(
            [
                projected[:, (3 * j + kind) * HEAD_DIM : (3 * j + kind + 1) * HEAD_DIM]
                for j in range(heads)
            ],
            axis=1,
        )
        for kind in range(3)
    ]


def join_heads(q, k, v):
    heads = q.shape[1] // HEAD_DIM
    return jnp.concatenate(
        [
            part[:, j * HEAD_DIM : (j + 1) * HEAD_DIM]
            for j in range(heads)
            for part in (q, k, v)
        ],
        axis=1,
    )


def block_diagonal(width):
    shape = (width, width)
    return (row_of(shape) // HEAD_DIM) == (lane_of(shape) // HEAD_DIM)


def pack_state(full):
    width = full.shape[0]
    kept = jnp.where(block_diagonal(width), full, 0.0)
    packed = kept[0:FEATURES]
    for head in range(1, width // FEATURES):
        packed = packed + kept[head * FEATURES : (head + 1) * FEATURES]
    return packed


def unpack_state(packed):
    width = packed.shape[1]
    tall = jnp.concatenate([packed] * (width // FEATURES), axis=0)
    return jnp.where(block_diagonal(width), tall, 0.0)


def head_sum(values, ones):
    high, low = halves(values)
    return dot_nn(high, ones) + dot_nn(low, ones)


def full(shape):
    return pl.BlockSpec(shape, lambda *i: (0,) * len(shape))


def rowed(width):
    return pl.BlockSpec((CHUNK, width), lambda i: (i, 0))


def layered(array, l):
    return pl.BlockSpec((None,) + array.shape[1:], lambda *i: (l, 0, 0))


def rows_at(c):
    return pl.ds(pl.multiple_of(c * CHUNK, CHUNK), CHUNK)


def push(source, target, send, recv, where):
    return pltpu.make_async_remote_copy(
        src_ref=source,
        dst_ref=target,
        send_sem=send,
        recv_sem=recv,
        device_id=where,
        device_id_type=pl.DeviceIdType.MESH,
    )


class Gather:
    def __init__(self, h, own, buffers, sems):
        self.own = own
        self.beside, self.across, self.corner = buffers
        self.send, self.recv = sems
        self.near = {"head": lax.bitwise_xor(h, 1)}
        self.far = {"head": lax.bitwise_xor(h, 2)}

    @staticmethod
    def scratch(rows, width):
        count = rows // CHUNK
        return [pltpu.VMEM((rows, width), BF)] * 3 + [pltpu.SemaphoreType.DMA((3, count))] * 2

    def copy(self, kind, c):
        source, target, where = (
            (self.own, self.across, self.far),
            (self.own, self.beside, self.near),
            (self.across, self.corner, self.near),
        )[kind]
        rows = rows_at(c)
        return push(
            source.at[rows, :],
            target.at[rows, :],
            self.send.at[kind, c],
            self.recv.at[kind, c],
            where,
        )

    def start(self, c):
        self.copy(0, c).start()
        self.copy(1, c).start()

    def relay(self, c):
        self.copy(0, c).wait_recv()
        self.copy(2, c).start()

    def ready(self, c):
        self.copy(1, c).wait_recv()
        self.copy(2, c).wait_recv()

    def pieces(self, c):
        rows = rows_at(c)
        return [ref[rows, :] for ref in (self.own, self.beside, self.across, self.corner)]

    def finish(self, c):
        for kind in range(3):
            self.copy(kind, c).wait_send()


class Scatter:
    def __init__(self, h, buffers, sems):
        self.near, self.far, self.got, self.middle, self.across = buffers
        self.send, self.recv = sems
        self.beside = {"head": lax.bitwise_xor(h, 1)}
        self.beyond = {"head": lax.bitwise_xor(h, 2)}

    @staticmethod
    def scratch(rows, width):
        count = rows // CHUNK
        return (
            [pltpu.VMEM((2, rows, width), BF)] * 3
            + [pltpu.VMEM((rows, width), BF)] * 2
            + [pltpu.SemaphoreType.DMA((2, count))] * 2
        )

    def copy(self, kind, c):
        rows = rows_at(c)
        if kind == 0:
            source, target, where = (
                self.far.at[:, rows, :],
                self.got.at[:, rows, :],
                self.beside,
            )
        else:
            source, target, where = self.middle.at[rows, :], self.across.at[rows, :], self.beyond
        return push(source, target, self.send.at[kind, c], self.recv.at[kind, c], where)

    def put(self, h, c, whole):
        rows = rows_at(c)
        w = self.near.shape[2]
        self.near[0, rows, :] = whole[:, block_columns(h, 0, w)]
        self.near[1, rows, :] = whole[:, block_columns(h, 2, w)]
        self.far[0, rows, :] = whole[:, block_columns(h, 1, w)]
        self.far[1, rows, :] = whole[:, block_columns(h, 3, w)]
        self.copy(0, c).start()

    def relay(self, c):
        self.copy(0, c).wait_recv()
        rows = rows_at(c)
        self.middle[rows, :] = (
            self.near[1, rows, :].astype(F32) + self.got[1, rows, :].astype(F32)
        ).astype(BF)
        self.copy(1, c).start()

    def total(self, c):
        self.copy(1, c).wait_recv()
        rows = rows_at(c)
        return (
            self.near[0, rows, :].astype(F32)
            + self.got[0, rows, :].astype(F32)
            + self.across[rows, :].astype(F32)
        )

    def finish(self, c):
        self.copy(0, c).wait_send()
        self.copy(1, c).wait_send()


def begin_scalar(lengths, slot):
    def one(j, carry):
        at, best = carry
        at = at + lengths[j - 1]
        return at, jnp.where(at <= slot, at, best)

    return lax.fori_loop(1, lengths.shape[0], one, (jnp.int32(0), jnp.int32(0)))[1]


def begin_column(lengths, slots):
    def one(j, carry):
        at, best = carry
        at = at + lengths[j - 1]
        return at, jnp.where(slots >= at, at, best)

    return lax.fori_loop(1, lengths.shape[0], one, (jnp.int32(0), jnp.zeros_like(slots)))[1]


class HandOver:
    def __init__(self, n, hops, rows, sign, packed, buffer, sems):
        self.n, self.hops, self.rows, self.sign = n, hops, rows, sign
        self.packed, self.buffer = packed, buffer
        self.send, self.recv = sems
        self.here = lax.axis_index("seq")

    @staticmethod
    def scratch(hops, width):
        return [pltpu.VMEM((hops, STATE_ROWS, width), F32)] + [
            pltpu.SemaphoreType.DMA((hops,))
        ] * 2

    def inside(self, index):
        return (index >= 0) & (index < self.n)

    def copy(self, j):
        return push(
            self.packed,
            self.buffer.at[j - 1],
            self.send.at[j - 1],
            self.recv.at[j - 1],
            {"seq": lax.rem(self.here + self.sign * j + self.n, self.n)},
        )

    def clear(self):
        self.buffer[...] = jnp.zeros_like(self.buffer)

    def start(self):
        for j in range(1, self.hops + 1):

            @pl.when(self.inside(self.here + self.sign * j))
            def _(j=j):
                self.copy(j).start()

    def total(self, lengths):
        first = self.here * self.rows
        result = None
        for j in range(1, self.hops + 1):

            @pl.when(self.inside(self.here - self.sign * j))
            def _(j=j):
                self.copy(j).wait_recv()

            @pl.when(self.inside(self.here + self.sign * j))
            def _(j=j):
                self.copy(j).wait_send()

            if self.sign > 0:
                edge, held = first - 1, first - 1 - (j - 1) * self.rows
            else:
                edge, held = first + j * self.rows - 1, first + self.rows - 1
            linked = (begin_scalar(lengths, edge) <= held).astype(F32)
            part = self.buffer[j - 1] * linked
            result = part if result is None else result + part
        return result


def greet(h, n, hops):
    barrier = pltpu.get_barrier_semaphore()

    def signal(where):
        pl.semaphore_signal(barrier, inc=1, device_id=where, device_id_type=pl.DeviceIdType.MESH)

    signal({"head": lax.bitwise_xor(h, 1)})
    signal({"head": lax.bitwise_xor(h, 2)})
    here = lax.axis_index("seq")
    expected = jnp.int32(2)
    for j in range(1, hops + 1):
        for sign in (1, -1):
            there = here + sign * j
            inside = (there >= 0) & (there < n)

            @pl.when(inside)
            def _(there=there):
                signal({"seq": lax.rem(there + n, n)})

            expected = expected + inside.astype(jnp.int32)
    pl.semaphore_wait(barrier, expected)


PROJECT_KINDS = (
    ("ai", D, BF),
    ("fi", D, BF),
    ("normed", D, BF),
    ("unit", D // 4, F32),
    ("inverse", 128, F32),
    ("qf", None, BF),
    ("kf", None, BF),
    ("v", None, BF),
    ("k", None, BF),
)


def feature_row(feat_ref, l):
    return jnp.concatenate([feat_ref[l, j : j + 1, :] for j in range(feat_ref.shape[1])], axis=1)


def project_chunk(l, h, c, last, x, params, tables, whole, out, packed, summed):
    gain, bias, w_ref, b_ref, feat_ref, map_ref, ones_ref = params
    cos, sin, keep = tables
    ai_ref, fi_ref, normed_ref, unit_ref, inv_ref, qf_ref, kf_ref, v_ref, k_ref = out
    mean = jnp.sum(x, axis=1, keepdims=True) * (1.0 / D)
    center = x - mean
    inverse = lax.rsqrt(jnp.sum(center * center, axis=1, keepdims=True) * (1.0 / D) + EPSILON)
    normed = center * inverse
    inv_ref[...] = jnp.broadcast_to(inverse, inv_ref.shape)
    normed_ref[...] = normed.astype(BF)
    whole[...] = normed
    unit_ref[...] = whole[:, block_columns(h, 0, unit_ref.shape[1])]
    attention_input = (normed * gain[l, 0:1] + bias[l, 0:1]).astype(BF)
    ai_ref[...] = attention_input
    fi_ref[...] = (normed * gain[l, 1:2] + bias[l, 1:2]).astype(BF)
    projected = dot_nn(attention_input, w_ref[...]) + b_ref[l : l + 1, :]
    q, k, v = split_heads(projected)
    v = v.astype(BF)
    q_turn = q * cos + swap_pairs(q) * sin
    k_turn = k * cos + swap_pairs(k) * sin
    query_feat = jnp.exp(dot_nn(q_turn, map_ref[...], HIGHEST))
    key_norm = head_sum(k * k, ones_ref[...]) * (0.5 / HEAD_DIM)
    key_feat = (
        keep
        * feature_row(feat_ref, l)
        * jnp.exp(dot_nn(k_turn, map_ref[...], HIGHEST) - key_norm)
    ).astype(BF)
    qf_ref[...] = query_feat.astype(BF)
    kf_ref[...] = key_feat
    v_ref[...] = v
    k_ref[...] = k.astype(BF)
    place = (row_of((CHUNK, 1)) + c * CHUNK).astype(F32)
    masked = jnp.where(place >= last, key_feat.astype(F32), 0.0)

    @pl.when(c == 0)
    def _():
        summed[...] = jnp.zeros_like(summed)
        packed[...] = jnp.zeros_like(packed)

    summed[...] += dot_tn(masked.astype(BF), v)
    packed[FEATURES : FEATURES + 1, :] += jnp.sum(masked, axis=0, keepdims=True)


def raise_chunk(l, fi, w_ref, b_ref, act_ref, slope_ref):
    raised = dot_nn(fi, w_ref[...]) + b_ref[l : l + 1, :]
    cumulative = 0.5 + 0.5 * lax.erf(raised * math.sqrt(0.5))
    density = jnp.exp(raised * raised * -0.5) * (1.0 / math.sqrt(2.0 * math.pi))
    act_ref[...] = (raised * cumulative).astype(BF)
    slope_ref[...] = (cumulative + raised * density).astype(BF)


def remote_call(kernel, name, ident, grid, in_specs, out_specs, out_shape, scratch, flops, args):
    moved = sum(int(np.prod(a.shape)) * a.dtype.itemsize for a in list(args) + list(out_shape))
    return pl.pallas_call(
        kernel,
        name=name,
        grid=grid,
        in_specs=in_specs,
        out_specs=out_specs,
        scratch_shapes=scratch,
        out_shape=out_shape,
        compiler_params=pltpu.CompilerParams(
            collective_id=ident, has_side_effects=True, vmem_limit_bytes=VMEM_BYTES
        ),
        cost_estimate=pl.CostEstimate(flops=int(flops), bytes_accessed=moved, transcendentals=0),
    )(*args)


class Names:
    pass


def named_call(kernel, name, ident, grid, ins, outs, scratch, flops, late=None, sent=None):
    late, sent = late or {}, sent or {}
    shared = {k: v[1] for k, v in sent.items() if isinstance(v, tuple)}
    sent = {k: v[0] if isinstance(v, tuple) else v for k, v in sent.items()}
    labels, groups = list(ins) + list(late) + list(outs) + list(sent), list(scratch)
    layers = {k: v if isinstance(v, tuple) else (v, None) for k, v in late.items()}
    anywhere = pl.BlockSpec(memory_space=pl.ANY)

    def body(*refs):
        names = Names()
        names.late, names.sent = Names(), Names()
        far = {}
        for label, ref in zip(labels, refs):
            if label in late or label in sent:
                far[label] = ref
            else:
                setattr(names, label, ref)
        at = len(labels)
        for label in list(late) + list(sent):
            if label in shared:
                held, sem = getattr(names, shared[label]), refs[at]
                at -= 1
            else:
                held, sem = refs[at], refs[at + 1]
            setattr(names, label, held)
            if label in late:
                layer = layers[label][1]
                source = far[label] if layer is None else far[label].at[layer]
                setattr(names.late, label, pltpu.make_async_copy(source, held, sem))
            else:
                setattr(names.sent, label, pltpu.make_async_copy(held, far[label], sem))
            at += 2
        for label in groups:
            size = len(scratch[label])
            held = refs[at : at + size]
            setattr(names, label, held if size > 1 else held[0])
            at += size
        kernel(names)

    moved = []
    for array, layer in layers.values():
        shape = array.shape if layer is None else array.shape[1:]
        moved += [pltpu.VMEM(shape, array.dtype), pltpu.SemaphoreType.DMA]
    for label, shape in sent.items():
        if label not in shared:
            moved.append(pltpu.VMEM(shape.shape, shape.dtype))
        moved.append(pltpu.SemaphoreType.DMA)
    result = remote_call(
        body,
        name,
        ident,
        grid,
        [spec for array, spec in ins.values()] + [anywhere] * len(late),
        [spec for shape, spec in outs.values()] + [anywhere] * len(sent),
        [shape for shape, spec in outs.values()] + list(sent.values()),
        moved + [item for label in groups for item in scratch[label]],
        flops,
        [array for array, spec in ins.values()] + [array for array, layer in layers.values()],
    )
    return dict(zip(list(outs) + list(sent), result))


def every(names):
    return [getattr(names, label) for label in vars(names)]


def fixed(shape):
    return pl.BlockSpec(shape, lambda *i: (0,) * len(shape), pipeline_mode=pl.Buffered(1))


def layer_of(array, l):
    return pl.BlockSpec(
        (None,) + array.shape[1:], lambda *i: (l, 0, 0), pipeline_mode=pl.Buffered(1)
    )


def clipped(step, low, count):
    return jnp.minimum(jnp.maximum(step - low, 0), count - 1)


def up_rows(width, low, count):
    return pl.BlockSpec((CHUNK, width), lambda i: (clipped(i, low, count), 0))


def down_rows(width, low, count):
    return pl.BlockSpec((CHUNK, width), lambda i: (count - 1 - clipped(i, low, count), 0))


def down_cube(shape, low, count):
    return pl.BlockSpec(
        (1,) + shape, lambda i: (count - 1 - clipped(i, low, count),) + (0,) * len(shape)
    )


def struct(shape, kind):
    return jax.ShapeDtypeStruct(shape, kind)


def project_params(z):
    return (z.gain, z.bias, z.qkv_w, z.qkv_b, z.feats, z.map_t, z.ones)


def project_refs(z):
    return (z.ai, z.fi, z.normed, z.unit, z.inverse, z.qf, z.kf, z.v, z.k)


def project_made(rows, a, spec):
    return dict(
        (name, (struct((rows, width or a), kind), spec(width or a)))
        for name, width, kind in PROJECT_KINDS
    )


class Column:
    def __init__(self, ref, lane):
        self.ref, self.lane = ref, lane

    def __getitem__(self, key):
        rows = slice(None) if key is Ellipsis else key[0]
        return self.ref[rows, self.lane : self.lane + 1]


def begin_keep(ref):
    return Column(ref, 0), Column(ref, 64)


def lanes_to_column(row):
    shape = (row.shape[1], row.shape[1])
    eye = row_of(shape) == lane_of(shape)
    return jnp.sum(jnp.where(eye, row, 0.0), axis=1, keepdims=True)


def enter_kernel(n, z):
    c = pl.program_id(0)
    count = pl.num_programs(0)
    h = lax.axis_index("head")
    rows, width = z.acts.shape
    first = lax.axis_index("seq") * rows
    gather = Gather(h, z.acts, z.gather[:3], z.gather[3:])

    @pl.when(c == 0)
    def _():
        for copy in every(z.late):
            copy.start()
        greet(h, n, 0)
        for i in range(rows // CHUNK):
            gather.start(i)
        for i in range(rows // CHUNK):
            part = slice(i * CHUNK, (i + 1) * CHUNK)
            slots = row_of((CHUNK, 1)) + i * CHUNK + first
            begins = begin_column(z.lengths, slots)
            starts = (begins - first).astype(F32)
            keep = jnp.concatenate(
                [
                    lanes_to_column(z.keep_mask[j : j + 1, :].astype(F32))
                    for j in range(i * CHUNK // 128, (i + 1) * CHUNK // 128)
                ],
                axis=0,
            )
            z.columns[part, :] = jnp.where(lane_of((CHUNK, 128)) < 64, starts, keep)
            phase = (slots - begins).astype(F32) * z.rates[0:1, :]
            z.cos[part, :] = jnp.cos(phase)
            z.sin[part, :] = jnp.sin(phase) * z.rates[1:2, :]
        gather.relay(0)
        for copy in every(z.late):
            copy.wait()

    gather.ready(c)
    for r, part in enumerate(gather.pieces(c)):
        z.full[:, block_columns(h, r, width)] = part
    last = (begin_scalar(z.lengths, first + rows - 1) - first).astype(F32)
    here = rows_at(c)
    keep = begin_keep(z.columns)[1]
    tables = (twice(z.cos[here, :]), twice(z.sin[here, :]), keep[here, :])
    project_chunk(
        0,
        h,
        c,
        last,
        z.full[...].astype(F32),
        project_params(z),
        tables,
        z.whole,
        project_refs(z),
        z.packed,
        z.summed,
    )

    @pl.when(c + 1 < count)
    def _():
        gather.relay(c + 1)

    @pl.when(c + 1 == count)
    def _():
        z.packed[0:FEATURES, :] = pack_state(z.summed[...])
        for i in range(rows // CHUNK):
            gather.finish(i)


def enter(n, lengths, acts, keep_mask, gain, bias, qkv_w, qkv_b, feats, rates, consts):
    rows, width = acts.shape
    a = consts["ones"].shape[0]
    table = rates.shape[1]
    ins = dict(
        lengths=(lengths, pl.BlockSpec(memory_space=pltpu.SMEM)),
        acts=(acts, fixed(acts.shape)),
        keep_mask=(keep_mask, fixed(keep_mask.shape)),
        gain=(gain, fixed(gain.shape)),
        bias=(bias, fixed(bias.shape)),
        qkv_b=(qkv_b, fixed(qkv_b.shape)),
        feats=(feats, fixed(feats.shape)),
        rates=(rates, fixed(rates.shape)),
    )
    late = dict(qkv_w=(qkv_w, 0), map_t=consts["map_t"], ones=consts["ones"])
    outs = dict(
        full=(struct((rows, D), BF), rowed(D)),
        cos=(struct((rows, table), F32), full((rows, table))),
        sin=(struct((rows, table), F32), full((rows, table))),
        columns=(struct((rows, 128), F32), full((rows, 128))),
        **project_made(rows, a, rowed),
        packed=(struct((STATE_ROWS, a), F32), full((STATE_ROWS, a))),
    )
    scratch = dict(
        gather=Gather.scratch(rows, width),
        summed=[pltpu.VMEM((a, a), F32)],
        whole=[pltpu.VMEM((CHUNK, D), F32)],
    )
    return named_call(
        functools.partial(enter_kernel, n),
        "enter",
        2,
        (rows // CHUNK,),
        ins,
        outs,
        scratch,
        2 * rows * D * 3 * a * 2,
        late,
    )


def between_kernel(n, hops, l, z):
    step = pl.program_id(0)
    count = pl.num_programs(0) // 2
    h = lax.axis_index("head")
    rows, width = z.mine.shape
    first = lax.axis_index("seq") * rows
    chunks = rows // CHUNK
    gather = Gather(h, z.mine, z.gather[:3], z.gather[3:])
    begin, keep = begin_keep(z.columns)
    extra = [
        push(
            z.cotangent,
            target,
            z.extra_sems.at[0, i],
            z.extra_sems.at[1, i],
            {"head": lax.bitwise_xor(h, i + 1)},
        )
        for i, target in enumerate((z.from_beside, z.from_across))
    ]
    scatter = Scatter(h, z.scatter[:5], z.scatter[5:])
    hand = HandOver(n, hops, rows, 1, z.state_own, z.hand[0], z.hand[1:])

    def send_sum(c):
        z.mine[rows_at(c), :] = scatter.total(c).astype(BF)
        gather.start(c)

    @pl.when(step == 0)
    def _():
        z.late.up_w.start()
        hand.clear()
        greet(h, n, hops)
        hand.start()
        z.late.up_w.wait()
        z.late.out_w.start()
        z.late.down_w.start()

    @pl.when(step < count)
    def _():
        raise_chunk(l, z.fi_in[...], z.up_w, z.up_b, z.act, z.slope)

        @pl.when(step == 0)
        def _():
            z.state_in[...] = hand.total(z.lengths)

        @pl.when(step >= 3)
        def _():
            gather.relay(step - 3)

        attention_chunk(
            step,
            (z.qf_in, z.kf_in, z.v_in, begin, keep, z.state_in, z.ones),
            (z.att, z.att_low, z.ratio, z.states, z.totals),
            z.state,
            z.total,
        )

        @pl.when(step == 0)
        def _():
            z.late.out_w.wait()
            z.late.down_w.wait()

        @pl.when(step == 1)
        def _():
            z.late.qkv_w.start()
            z.late.up_w_next.start()

        @pl.when(step >= 1)
        def _():
            scatter.relay(step - 1)

        z.whole_low[...] = (
            dot_nt(z.att_low[...], z.out_w[...]) + dot_nt(z.act[...], z.down_w[...])
        ).astype(BF)
        scatter.put(h, step, z.whole_low)

        @pl.when(step >= 2)
        def _():
            send_sum(step - 2)

    @pl.when(step >= count)
    def _():
        c = step - count

        @pl.when(c == 0)
        def _():
            scatter.relay(chunks - 1)
            z.late.qkv_w.wait()
            z.late.up_w_next.wait()
            gather.relay(1)

        gather.ready(c)
        for r, part in enumerate(gather.pieces(c)):
            z.whole[:, block_columns(h, r, width)] = part.astype(F32)
        x = z.full[...].astype(F32) + z.whole[...] + z.res_b[l : l + 1, :]
        z.whole[...] = x
        z.own[...] = z.whole[:, block_columns(h, 0, width)]
        last = (begin_scalar(z.lengths, first + rows - 1) - first).astype(F32)
        tables = (twice(z.cos[...]), twice(z.sin[...]), begin_keep(z.columns_next)[1][...])
        project_chunk(
            l + 1,
            h,
            c,
            last,
            x,
            project_params(z),
            tables,
            z.whole,
            project_refs(z),
            z.packed,
            z.summed,
        )

        @pl.when(c == 0)
        def _():
            send_sum(chunks - 2)

        @pl.when(c + 1 == chunks)
        def _():
            z.packed[0:FEATURES, :] = pack_state(z.summed[...])

        raise_chunk(l + 1, z.fi[...], z.up_w_next, z.up_b, z.act_next, z.slope_next)

        @pl.when(c == 0)
        def _():
            send_sum(chunks - 1)
            for copy in extra:
                copy.start()

        @pl.when((c >= 1) & (c + 1 < chunks))
        def _():
            gather.relay(c + 1)

        @pl.when(c + 1 == chunks)
        def _():
            for i in range(chunks):
                gather.finish(i)
                scatter.finish(i)
            for copy in extra:
                copy.wait_recv()
            z.grad_beside[...] = z.from_beside[...]
            z.grad_across[...] = z.from_across[...]
            for copy in extra:
                copy.wait_send()


def between(n, hops, l, lengths, entered, cotangent, params, consts):
    gain, bias, qkv_w, qkv_b, feats, up_w, up_b, out_w, down_w, res_b = params
    rows, a = entered["qf"].shape
    hidden = up_w.shape[2]
    chunks = rows // CHUNK
    width = D // 4

    def early(w):
        return up_rows(w, 0, chunks)

    def after(w):
        return up_rows(w, chunks, chunks)

    def cube(shape):
        return pl.BlockSpec((1,) + shape, lambda i: (clipped(i, 0, chunks),) + (0,) * len(shape))

    table = entered["cos"].shape[1]
    ins = dict(
        lengths=(lengths, pl.BlockSpec(memory_space=pltpu.SMEM)),
        qf_in=(entered["qf"], early(a)),
        kf_in=(entered["kf"], early(a)),
        v_in=(entered["v"], early(a)),
        fi_in=(entered["fi"], early(D)),
        columns=(entered["columns"], early(128)),
        state_own=(entered["packed"], fixed((STATE_ROWS, a))),
        cotangent=(cotangent, fixed(cotangent.shape)),
        up_b=(up_b, fixed(up_b.shape)),
        ones=(consts["ones"], fixed((a, a))),
        full=(entered["full"], after(D)),
        res_b=(res_b, fixed(res_b.shape)),
        gain=(gain, fixed(gain.shape)),
        bias=(bias, fixed(bias.shape)),
        qkv_b=(qkv_b, fixed(qkv_b.shape)),
        feats=(feats, fixed(feats.shape)),
        map_t=(consts["map_t"], fixed((a, a))),
        cos=(entered["cos"], after(table)),
        sin=(entered["sin"], after(table)),
        columns_next=(entered["columns"], after(128)),
    )
    late = dict(
        up_w=(up_w, l),
        out_w=(out_w, l),
        down_w=(down_w, l),
        qkv_w=(qkv_w, l + 1),
        up_w_next=(up_w, l + 1),
    )
    outs = dict(
        att=(struct((rows, a), F32), early(a)),
        att_low=(struct((rows, a), BF), early(a)),
        ratio=(struct((rows, a), F32), early(a)),
        states=(struct((chunks, a, a), F32), cube((a, a))),
        totals=(struct((chunks, 8, a), F32), cube((8, a))),
        act=(struct((rows, hidden), BF), early(hidden)),
        slope=(struct((rows, hidden), BF), early(hidden)),
        own=(struct((rows, width), F32), after(width)),
        **project_made(rows, a, after),
        act_next=(struct((rows, hidden), BF), after(hidden)),
        slope_next=(struct((rows, hidden), BF), after(hidden)),
        packed=(struct((STATE_ROWS, a), F32), full((STATE_ROWS, a))),
        grad_beside=(struct((rows, width), BF), full((rows, width))),
        grad_across=(struct((rows, width), BF), full((rows, width))),
    )
    scratch = dict(
        gather=Gather.scratch(rows, width),
        scatter=Scatter.scratch(rows, width),
        from_beside=[pltpu.VMEM((rows, width), BF)],
        from_across=[pltpu.VMEM((rows, width), BF)],
        extra_sems=[pltpu.SemaphoreType.DMA((2, 2))],
        hand=HandOver.scratch(hops, a),
        mine=[pltpu.VMEM((rows, width), BF)],
        state_in=[pltpu.VMEM((STATE_ROWS, a), F32)],
        summed=[pltpu.VMEM((a, a), F32)],
        whole=[pltpu.VMEM((CHUNK, D), F32)],
        whole_low=[pltpu.VMEM((CHUNK, D), BF)],
        state=[pltpu.VMEM((a, a), F32)],
        total=[pltpu.VMEM((8, a), F32)],
    )
    return named_call(
        functools.partial(between_kernel, n, hops, l),
        "between",
        3,
        (2 * chunks,),
        ins,
        outs,
        scratch,
        2 * rows * D * (hidden * 3 + 4 * a) * 2,
        late,
    )


def pair_mask(begin, step):
    shape = (CHUNK, CHUNK)
    t = row_of(shape)
    s = lane_of(shape)
    return (s <= t) & ((s + step * CHUNK).astype(F32) >= begin)


def attention_chunk(step, refs, out, state, total):
    qf_ref, kf_ref, v_ref, begin_ref, keep_ref, in_ref, ones_ref = refs
    att_ref, low_ref, ratio_ref, states_ref, totals_ref = out

    @pl.when(step == 0)
    def _():
        state[...] = unpack_state(in_ref[0:FEATURES, :])
        total[...] = jnp.broadcast_to(in_ref[FEATURES : FEATURES + 1, :], total.shape)

    q = qf_ref[...]
    k = kf_ref[...]
    v = v_ref[...]
    begin = begin_ref[...]
    keep = keep_ref[...]
    ones = ones_ref[...]
    a = q.shape[1]
    mask = pair_mask(begin, step)
    head_of = lane_of((1, a)) // HEAD_DIM
    held = state[...]
    held_total = total[0:1, :]
    states_ref[0] = held
    totals_ref[0] = total[...]
    base = (step * CHUNK).astype(F32)
    use = jnp.where(begin < base, 1.0, 0.0)
    high, low = halves(held)
    num = use * (dot_nn(q, high) + dot_nn(q, low))
    den = use * head_sum(q.astype(F32) * held_total, ones)
    for head in range(a // HEAD_DIM):
        own = (head_of == head).astype(BF)
        scores = dot_nt(q * own, k)
        scores_low = jnp.where(mask, scores, 0.0).astype(BF)
        num = num + dot_nn(scores_low, v * own)
        den = den + dot_nn(scores_low, jnp.broadcast_to(own, (CHUNK, a)))
    ratio = keep / (den + 1.0 - keep)
    att = num * ratio
    ratio_ref[...] = ratio
    att_ref[...] = att
    low_ref[...] = att.astype(BF)
    end = begin[CHUNK - 1 : CHUNK, :]
    place = (row_of((CHUNK, 1)) + step * CHUNK).astype(F32)
    masked = jnp.where(place >= end, k.astype(F32), 0.0)
    passing = jnp.where(end < base, 1.0, 0.0)
    state[...] = passing * held + jnp.where(
        block_diagonal(a), dot_tn(masked.astype(BF), v), 0.0
    )
    total[...] = jnp.broadcast_to(
        passing * held_total + jnp.sum(masked, axis=0, keepdims=True), total.shape
    )


def lower_feed(grad, dw_ref, slope_ref, bias_ref, start):
    @pl.when(start)
    def _():
        bias_ref[...] = jnp.zeros_like(bias_ref)

    d_raised = (dot_nn(grad, dw_ref[...]) * slope_ref[...].astype(F32)).astype(BF)
    bias_ref[...] += jnp.sum(d_raised.astype(F32), axis=0, keepdims=True)
    return d_raised


def lower_attention(grad, ow_ref, ratio, att, qf, begin, ones, out, summed, packed, start):
    num_ref, den_ref = out

    @pl.when(start)
    def _():
        summed[...] = jnp.zeros_like(summed)
        packed[...] = jnp.zeros_like(packed)

    d_num = (dot_nn(grad, ow_ref[...]) * ratio).astype(BF)
    d_den = -head_sum(d_num.astype(F32) * att, ones)
    num_ref[...] = d_num
    den_ref[...] = d_den
    entering = jnp.where(begin < 0.0, qf.astype(F32), 0.0)
    summed[...] += dot_tn(entering.astype(BF), d_num)
    packed[FEATURES : FEATURES + 1, :] += jnp.sum(entering * d_den, axis=0, keepdims=True)


def tile_at(i):
    return pl.ds(pl.multiple_of(i * CHUNK, CHUNK), CHUNK)


def weight_tile(i, x_ref, y, out_ref):
    out_ref[tile_at(i), :] = dot_tn(x_ref[:, tile_at(i)], y).astype(BF)


def attention_back(turn, step, refs, state, total):
    (
        qf_ref,
        kf_ref,
        v_ref,
        num_ref,
        den_ref,
        begin_ref,
        states_ref,
        totals_ref,
        exit_ref,
    ) = refs

    @pl.when(turn == 0)
    def _():
        state[...] = unpack_state(exit_ref[0:FEATURES, :])
        total[...] = jnp.broadcast_to(exit_ref[FEATURES : FEATURES + 1, :], total.shape)

    q = qf_ref[...]
    k = kf_ref[...]
    v = v_ref[...]
    d_num = num_ref[...]
    d_den = den_ref[...]
    begin = begin_ref[...]
    a = q.shape[1]
    mask = pair_mask(begin, step)
    head_of = lane_of((1, a)) // HEAD_DIM
    base = (step * CHUNK).astype(F32)
    use = jnp.where(begin < base, 1.0, 0.0)
    end = begin[CHUNK - 1 : CHUNK, :]
    place = (row_of((CHUNK, 1)) + step * CHUNK).astype(F32)
    inside = jnp.where(place >= end, 1.0, 0.0)
    passing = jnp.where(end < base, 1.0, 0.0)
    held_high, held_low = halves(states_ref[0])
    held_total = totals_ref[0][0:1, :]
    after = state[...]
    after_total = total[0:1, :]
    after_high, after_low = halves(after)
    masked = (k.astype(F32) * inside).astype(BF)
    d_q = use * (dot_nt(d_num, held_high) + dot_nt(d_num, held_low) + d_den * held_total)
    d_k = inside * (dot_nt(v, after_high) + dot_nt(v, after_low) + after_total)
    d_v = dot_nn(masked, after_high) + dot_nn(masked, after_low)
    for head in range(a // HEAD_DIM):
        own = (head_of == head).astype(BF)
        q_own = q * own
        num_own = d_num * own
        scores_low = jnp.where(mask, dot_nt(q_own, k), 0.0).astype(BF)
        column = d_den[:, head * HEAD_DIM : head * HEAD_DIM + 1]
        d_scores = jnp.where(mask, dot_nt(num_own, v) + column, 0.0).astype(BF)
        d_q = d_q + dot_nn(d_scores, k * own)
        d_k = d_k + dot_tn(d_scores, q_own)
        d_v = d_v + dot_tn(scores_low, num_own)
    q_used = q.astype(F32) * use
    state[...] = passing * after + jnp.where(
        block_diagonal(a), dot_tn(q_used.astype(BF), d_num), 0.0
    )
    total[...] = jnp.broadcast_to(
        passing * after_total + jnp.sum(q_used * d_den, axis=0, keepdims=True), total.shape
    )
    return d_q, d_k, d_v


def features_back(grads, refs, feat_ref, bias_ref, start):
    d_q, d_k, d_v = grads
    qf_ref, kf_ref, k_ref, cos_ref, sin_ref, map_ref, ones_ref = refs

    @pl.when(start)
    def _():
        feat_ref[...] = jnp.zeros_like(feat_ref)
        bias_ref[...] = jnp.zeros_like(bias_ref)

    cos = twice(cos_ref[...])
    sin = twice(sin_ref[...])
    d_query = dot_nn(d_q * qf_ref[...].astype(F32), map_ref[...], HIGHEST)
    d_query = d_query * cos - swap_pairs(d_query) * sin
    d_key_log = d_k * kf_ref[...].astype(F32)
    feat_ref[...] += jnp.sum(d_key_log, axis=0, keepdims=True)
    d_key = dot_nn(d_key_log, map_ref[...], HIGHEST)
    d_key = d_key * cos - swap_pairs(d_key) * sin
    d_key = d_key - head_sum(d_key_log, ones_ref[...]) * k_ref[...].astype(F32) * (1.0 / HEAD_DIM)
    d_proj = join_heads(d_query, d_key, d_v).astype(BF)
    bias_ref[...] += jnp.sum(d_proj.astype(F32), axis=0, keepdims=True)
    return d_proj


def inputs_back(l, d_proj, raised_ref, w_ref, up_ref, normed_ref, gain, sums_ref, start):
    @pl.when(start)
    def _():
        sums_ref[...] = jnp.zeros_like(sums_ref)

    normed = normed_ref[...].astype(F32)
    d_attention = dot_nt(d_proj, w_ref[...])
    d_feed = dot_nt(raised_ref[...], up_ref[...])
    sums_ref[0:1, :] += jnp.sum(d_attention * normed, axis=0, keepdims=True)
    sums_ref[1:2, :] += jnp.sum(d_feed * normed, axis=0, keepdims=True)
    sums_ref[2:3, :] += jnp.sum(d_attention, axis=0, keepdims=True)
    sums_ref[3:4, :] += jnp.sum(d_feed, axis=0, keepdims=True)
    d_normed = (d_attention * gain[l, 0:1] + d_feed * gain[l, 1:2]).astype(BF)
    high, low = halves(d_normed.astype(F32) * normed)
    row = jnp.ones((8, D), BF)
    first = dot_nt(row, d_normed)
    second = dot_nt(row, high) + dot_nt(row, low)
    return d_normed, jnp.where(row_of(first.shape) == 0, first, second)


class RowSum:
    def __init__(self, h, buffers, sems):
        self.own, self.got, self.middle, self.across = buffers
        self.send, self.recv = sems
        self.beside = {"head": lax.bitwise_xor(h, 1)}
        self.beyond = {"head": lax.bitwise_xor(h, 2)}

    @staticmethod
    def scratch(rows):
        count = rows // CHUNK
        return [pltpu.VMEM((count, 8, CHUNK), F32)] * 4 + [pltpu.SemaphoreType.DMA((2, count))] * 2

    def copy(self, kind, c):
        source, target, where = (
            (self.own, self.got, self.beside),
            (self.middle, self.across, self.beyond),
        )[kind]
        return push(
            source.at[c], target.at[c], self.send.at[kind, c], self.recv.at[kind, c], where
        )

    def put(self, c, value):
        self.own[c] = value
        self.copy(0, c).start()

    def relay(self, c):
        self.copy(0, c).wait_recv()
        self.middle[c] = self.own[c] + self.got[c]
        self.copy(1, c).start()

    def total(self, c):
        self.copy(1, c).wait_recv()
        value = self.middle[c] + self.across[c]
        shape = (8, 128)
        eye = (row_of(shape) == lane_of(shape)).astype(F32)
        columns = dot_tn(value, eye, HIGHEST)
        return columns[:, 0:1], columns[:, 1:2]

    def finish(self, c):
        self.copy(0, c).wait_send()
        self.copy(1, c).wait_send()


def norm_back(before, inverse, unit, d_normed, sums):
    first, second = sums
    return before + inverse * (d_normed - first * (1.0 / D) - unit * (second * (1.0 / D)))


def ring_place(index, n):
    return jnp.where(index % 2 == 0, index // 2, n - 1 - index // 2)


def ring_index(place, n):
    return jnp.where(place < n // 2, 2 * place, 2 * (n - 1 - place) + 1)


BATCHES = 6


class Ring:
    def __init__(self, n, parts, source, held, sems, since=0, until=BATCHES, incoming=None):
        self.n, self.parts, self.source, self.held = n, parts, source, held
        self.send_sem, self.recv_sem = sems
        self.since, self.until, self.incoming = since, until, incoming
        self.share = D // n
        self.place = ring_place(lax.axis_index("seq"), n)
        self.right = ring_index(lax.rem(self.place + 1, n), n)
        self.left = ring_index(lax.rem(self.place + n - 1, n), n)
        self.base = self.slots(n, since, until)[0]
        self.first = 0 if incoming is None else self.bound(n, since)
        self.last = self.bound(n, until) - 1

    @staticmethod
    def bound(n, batch):
        return 1 + (n - 2) * batch // BATCHES

    @staticmethod
    def slots(n, since, until):
        base = Ring.bound(n, since) - 1
        return base, Ring.bound(n, until) - base

    @staticmethod
    def buffers(n, parts, since=0, until=BATCHES):
        count = Ring.slots(n, since, until)[1]
        return [pltpu.VMEM((count, D // n, part[2]), BF) for part in parts]

    @staticmethod
    def sems(n, parts):
        return [pltpu.SemaphoreType.DMA((len(parts), n - 1))] * 2

    def own(self, part, step):
        array, start, width, way = part
        n = self.n
        ahead = lax.rem(self.place - way * (1 + step) + 2 * n, n)
        rows = pl.ds(pl.multiple_of(ring_index(ahead, n) * self.share, self.share), self.share)
        return self.source[array].at[rows, pl.ds(start, width)]

    def slot(self, r, step):
        return self.held[r].at[step - self.base]

    def copy(self, r, step, block):
        return push(
            block,
            self.slot(r, step),
            self.send_sem.at[r, step],
            self.recv_sem.at[r, step],
            {"seq": self.right if self.parts[r][3] > 0 else self.left},
        )

    def add(self, r, step, arrived):
        own = self.own(self.parts[r], step)[...].astype(F32)
        block = self.slot(r, step - 1)
        block[...] = (arrived[...].astype(F32) + own).astype(BF)
        self.copy(r, step, block).start()

    def start(self):
        for r, part in enumerate(self.parts):
            if self.incoming is not None:
                self.add(r, self.first, self.incoming[r])
            else:
                self.copy(r, 0, self.own(part, 0)).start()

    def tick(self, step):
        for r in range(len(self.parts)):
            block = self.slot(r, step - 1)
            self.copy(r, step - 1, block).wait_recv()
            self.add(r, step, block)

    def batch(self, k):
        low, high = self.bound(self.n, k - 1), self.bound(self.n, k)
        if self.incoming is not None and k - 1 == self.since:
            low += 1
        if high - low == 1:
            self.tick(low)
        elif high > low:

            def one(step, carry):
                self.tick(step)
                return carry

            lax.fori_loop(low, high, one, 0)

    def sent(self):
        def one(step, carry):
            for r in range(len(self.parts)):
                self.copy(r, step, self.slot(r, step)).wait_send()
            return carry

        lax.fori_loop(self.first, self.last + 1, one, 0)

    def pause(self, out):
        for r in range(len(self.parts)):
            block = self.slot(r, self.last)
            self.copy(r, self.last, block).wait_recv()
            out[r][...] = block[...]
        self.sent()

    def finish(self, out):
        n = self.n
        for r, part in enumerate(self.parts):
            block = self.slot(r, n - 2)
            self.copy(r, n - 2, block).wait_recv()
            array, start, width, way = part
            out[array][:, pl.ds(start, width)] = block[...].astype(F32) + self.own(part, n - 1)[
                ...
            ].astype(F32)
        self.sent()


def halved(array, width, start=0):
    return (
        (array, start, width // 2, 1),
        (array, start + width // 2, width // 2, -1),
    )


def ring_out(n, parts):
    return [jax.ShapeDtypeStruct((D // n, part[2]), BF) for part in parts]


CREST_DOWN, CREST_UP, TURN_REST, TURN_DOWN, TURN_UP = 2, 2, 4, 1, 0


def loop(count, body):
    def one(c, carry):
        body(c)
        return carry

    lax.fori_loop(0, count, one, 0)


def unrolled(count, body):
    for c in range(count):
        body(jnp.int32(c))


def crest_kernel(n, hops, l, z):
    step = pl.program_id(0)
    h = lax.axis_index("head")
    rows, hidden = z.act.shape
    width = D // 4
    count = rows // CHUNK
    hand = HandOver(n, hops, rows, 1, z.state_own, z.hand[0], z.hand[1:])
    hand_back = HandOver(n, hops, rows, -1, z.packed, z.hand_back[0], z.hand_back[1:])
    begin, keep = begin_keep(z.columns)
    parts = halved(0, hidden)
    corner = push(
        z.grad_across,
        z.grad_corner,
        z.corner_sems.at[0],
        z.corner_sems.at[1],
        {"head": lax.bitwise_xor(h, 1)},
    )
    down = Ring(n, parts, (z.d_down,), z.down_held, z.down_sems, 0, CREST_DOWN)
    up = Ring(n, parts, (z.d_up,), z.up_held, z.up_sems, 0, CREST_UP)
    columns = pl.ds(pl.multiple_of(h * width, width), width)

    @pl.when(step == 0)
    def _():
        for copy in (
            z.late.grad_across,
            z.late.grad_own,
            z.late.grad_beside,
            z.late.down_w,
            z.late.slope,
        ):
            copy.start()
        hand.clear()
        hand_back.clear()
        greet(h, n, hops)
        hand.start()
        z.late.grad_across.wait()
        corner.start()
        z.d_res[...] = jnp.zeros_like(z.d_res)
        z.late.grad_own.wait()
        z.late.grad_beside.wait()
        for r, part in enumerate((z.grad_own, z.grad_beside, z.grad_across)):
            z.grad[:, block_columns(h, r, width)] = part[...]
        corner.wait_recv()
        z.grad[:, block_columns(h, 3, width)] = z.grad_corner[...]
        corner.wait_send()
        z.late.down_w.wait()
        z.late.slope.wait()
        z.late.act.start()

        def feed(c):
            here = rows_at(c)
            z.d_raised[here, :] = lower_feed(
                z.grad[here, :], z.down_w, z.slope.at[here, :], z.d_up_b, c == 0
            )
            z.d_res[...] += jnp.sum(z.grad[here, columns].astype(F32), axis=0, keepdims=True)

        unrolled(count, feed)
        z.sent.d_raised.start()
        z.late.act.wait()
        z.late.fi.start()
        unrolled(D // CHUNK, lambda i: weight_tile(i, z.grad, z.act[...], z.d_down))
        down.start()
        z.sent.d_down.start()
        z.late.fi.wait()
        z.late.out_w.start()
        unrolled(D // CHUNK, lambda i: weight_tile(i, z.fi, z.d_raised[...], z.d_up))
        up.start()
        z.sent.d_up.start()
        z.late.out_w.wait()
        z.state_in[...] = hand.total(z.lengths)

    @pl.when((step >= 1) & (step <= count))
    def _():
        c = step - 1
        here = rows_at(c)
        attention_chunk(
            c,
            (z.qf, z.kf, z.v, begin, keep, z.state_in, z.ones),
            (z.att, z.low_now, z.ratio, z.states, z.totals),
            z.state,
            z.total,
        )
        low = z.low_now[...]
        z.low[here, :] = low
        z.whole[...] = (dot_nt(low, z.out_w[...]) + dot_nt(z.act[here, :], z.down_w[...])).astype(
            BF
        )
        z.near[0] = z.whole[:, block_columns(h, 0, width)]
        z.near[1] = z.whole[:, block_columns(h, 2, width)]
        z.far[0] = z.whole[:, block_columns(h, 1, width)]
        z.far[1] = z.whole[:, block_columns(h, 3, width)]
        lower_attention(
            z.grad[here, :],
            z.out_w,
            z.ratio[...],
            z.att[...],
            z.qf[...],
            begin[...],
            z.ones[...],
            (z.d_num, z.d_den),
            z.summed,
            z.packed,
            c == 0,
        )
        at_steps(
            c,
            (
                (0, lambda: down.batch(1)),
                (1, lambda: up.batch(1)),
                (2, lambda: down.batch(2)),
                (3, lambda: up.batch(2)),
            ),
        )

    @pl.when(step == count + 1)
    def _():
        z.packed[0:FEATURES, :] = pack_state(z.summed[...])
        hand_back.start()
        unrolled(D // CHUNK, lambda i: weight_tile(i, z.grad, z.low[...], z.d_out))
        z.exit_state[...] = hand_back.total(z.lengths)
        down.pause((z.down_fore, z.down_aft))
        up.pause((z.up_fore, z.up_aft))
        for copy in every(z.sent):
            copy.wait()


def crest(n, hops, l, lengths, mid, pieces, tables, params, consts):
    gain, bias, qkv_w, qkv_b, feats, up_w, up_b, out_w, down_w, res_b = params
    cos, sin, columns = tables
    rows, a = mid["qf"].shape
    hidden = up_w.shape[2]
    count = rows // CHUNK
    width = D // 4
    parts = halved(0, hidden)

    def block(w):
        return up_rows(w, 1, count)

    def cube(shape):
        return pl.BlockSpec((1,) + shape, lambda i: (clipped(i, 1, count),) + (0,) * len(shape))

    quarter = pl.BlockSpec((2, CHUNK, width), lambda i: (0, clipped(i, 1, count), 0))
    ins = dict(
        lengths=(lengths, pl.BlockSpec(memory_space=pltpu.SMEM)),
        qf=(mid["qf"], block(a)),
        kf=(mid["kf"], block(a)),
        v=(mid["v"], block(a)),
        columns=(columns, block(128)),
        state_own=(mid["packed"], fixed((STATE_ROWS, a))),
        ones=(consts["ones"], fixed((a, a))),
    )
    late = dict(
        grad_across=pieces[2],
        grad_own=pieces[0],
        grad_beside=pieces[1],
        down_w=(down_w, l),
        slope=mid["slope_next"],
        act=mid["act_next"],
        fi=mid["fi"],
        out_w=(out_w, l),
    )
    fore, aft = ring_out(n, parts)
    outs = dict(
        d_up_b=(struct((1, hidden), F32), full((1, hidden))),
        d_res=(struct((1, width), F32), full((1, width))),
        ratio=(struct((rows, a), F32), block(a)),
        att=(struct((rows, a), F32), block(a)),
        states=(struct((count, a, a), F32), cube((a, a))),
        totals=(struct((count, 8, a), F32), cube((8, a))),
        d_num=(struct((rows, a), BF), block(a)),
        d_den=(struct((rows, a), F32), block(a)),
        near=(struct((2, rows, width), BF), quarter),
        far=(struct((2, rows, width), BF), quarter),
        d_out=(struct((D, a), BF), full((D, a))),
        exit_state=(struct((STATE_ROWS, a), F32), full((STATE_ROWS, a))),
        up_fore=(fore, full(fore.shape)),
        up_aft=(aft, full(aft.shape)),
        down_fore=(fore, full(fore.shape)),
        down_aft=(aft, full(aft.shape)),
    )
    scratch = dict(
        grad=[pltpu.VMEM((rows, D), BF)],
        grad_corner=[pltpu.VMEM((rows, width), BF)],
        corner_sems=[pltpu.SemaphoreType.DMA((2,))],
        hand=HandOver.scratch(hops, a),
        hand_back=HandOver.scratch(hops, a),
        down_held=Ring.buffers(n, parts, 0, CREST_DOWN),
        up_held=Ring.buffers(n, parts, 0, CREST_UP),
        down_sems=Ring.sems(n, parts),
        up_sems=Ring.sems(n, parts),
        state_in=[pltpu.VMEM((STATE_ROWS, a), F32)],
        packed=[pltpu.VMEM((STATE_ROWS, a), F32)],
        summed=[pltpu.VMEM((a, a), F32)],
        state=[pltpu.VMEM((a, a), F32)],
        total=[pltpu.VMEM((8, a), F32)],
        whole=[pltpu.VMEM((CHUNK, D), BF)],
        low_now=[pltpu.VMEM((CHUNK, a), BF)],
        low=[pltpu.VMEM((rows, a), BF)],
    )
    return named_call(
        functools.partial(crest_kernel, n, hops, l),
        "crest",
        4,
        (count + 2,),
        ins,
        outs,
        scratch,
        2 * rows * D * (hidden * 4 + 4 * a) * 2,
        late,
        dict(
            d_raised=struct((rows, hidden), BF),
            d_down=struct((D, hidden), BF),
            d_up=struct((D, hidden), BF),
        ),
    )


def back_step(z, l, h, step, count, scatter, row_sum, middle_work, end_work):
    c = count - 1 - step
    grads = attention_back(
        step,
        c,
        (
            z.qf, z.kf, z.v, z.d_num, z.d_den, begin_keep(z.columns)[0], z.states, z.totals,
            z.exit_state,
        ),
        z.state,
        z.total,
    )

    @pl.when(step >= 1)
    def _():
        scatter.relay(c + 1)
        row_sum.relay(c + 1)

    middle_work()
    start = step == 0
    d_proj = features_back(
        grads,
        (z.qf, z.kf, z.k, z.cos, z.sin, z.map, z.ones),
        z.d_feat,
        z.d_qkv_b,
        start,
    )
    z.proj_all[rows_at(c), :] = d_proj

    @pl.when(start)
    def _():
        z.late.qkv_w.wait()
        z.late.up_w.wait()

    d_normed, sums = inputs_back(
        l, d_proj, z.d_raised_in, z.qkv_w, z.up_w, z.normed, z.gain, z.sums, start
    )
    z.whole[...] = d_normed
    scatter.put(h, c, z.whole)
    row_sum.put(c, sums)
    end_work()


def back_arrays(l, local, lowered, tables, params, consts, exit_state, count):
    gain, bias, qkv_w, qkv_b, feats, up_w, up_b, out_w, down_w, res_b = params
    cos, sin, columns = tables
    qf, kf, v, k, normed, unit, inverse, states, totals = local
    d_raised, d_num, d_den = lowered
    a = qf.shape[1]

    def early(w):
        return down_rows(w, 0, count)

    return dict(
        qf=(qf, early(a)),
        kf=(kf, early(a)),
        v=(v, early(a)),
        k=(k, early(a)),
        d_num=(d_num, early(a)),
        d_den=(d_den, early(a)),
        columns=(columns, early(128)),
        cos=(cos, early(cos.shape[1])),
        sin=(sin, early(sin.shape[1])),
        states=(states, down_cube((a, a), 0, count)),
        totals=(totals, down_cube((8, a), 0, count)),
        exit_state=(exit_state, fixed(exit_state.shape)),
        map=(consts["map"], fixed((a, a))),
        ones=(consts["ones"], fixed((a, a))),
        d_raised_in=(d_raised, early(d_raised.shape[1])),
        normed=(normed, early(D)),
        gain=(gain, fixed(gain.shape)),
    )


def back_scratch(rows, a, width):
    return dict(
        scatter=Scatter.scratch(rows, width),
        row_sum=RowSum.scratch(rows),
        state=[pltpu.VMEM((a, a), F32)],
        total=[pltpu.VMEM((8, a), F32)],
        whole=[pltpu.VMEM((CHUNK, D), BF)],
        proj_all=[pltpu.VMEM((rows, 3 * a), BF)],
    )


def at_steps(step, table):
    for at, work in table:

        @pl.when(step == at)
        def _(work=work):
            work()


def turn_kernel(n, hops, l, z):
    step = pl.program_id(0)
    h = lax.axis_index("head")
    rows, width = z.mine.shape
    hidden = z.act.shape[1]
    count = rows // CHUNK
    scatter = Scatter(h, z.scatter[:5], z.scatter[5:])
    row_sum = RowSum(h, z.row_sum[:4], z.row_sum[4:])
    gather = Gather(h, z.mine, z.gather[:3], z.gather[3:])
    hand = HandOver(n, hops, rows, -1, z.packed, z.hand[0], z.hand[1:])
    parts = halved(0, hidden)
    rest_parts = rest_of(z.d_qkv.shape[1], z.d_out_next.shape[1])
    down = Ring(
        n, parts, (z.d_down_next,), z.down_held, z.down_sems, CREST_DOWN,
        incoming=(z.down_fore, z.down_aft),
    )
    up = Ring(
        n, parts, (z.d_up_next,), z.up_held, z.up_sems, CREST_UP,
        incoming=(z.up_fore_in, z.up_aft_in),
    )
    rest = Ring(n, rest_parts, (z.d_qkv, z.d_out_next), z.rest_held, z.rest_sems, 0, TURN_REST)
    new_down = Ring(n, parts, (z.d_down,), z.new_down_held, z.new_down_sems, 0, TURN_DOWN)
    new_up = Ring(n, parts, (z.d_up,), z.new_up_held, z.new_up_sems, 0, TURN_UP)

    def sum_up(o):
        c = count - 1 - o
        here = rows_at(c)
        new = norm_back(
            z.before[here, :].astype(F32),
            z.inverse[here, 0:1],
            z.unit[here, :],
            scatter.total(c),
            row_sum.total(c),
        )
        z.after[here, :] = new
        z.mine[here, :] = new.astype(BF)
        z.d_res[...] += jnp.sum(new, axis=0, keepdims=True)
        gather.start(c)

    @pl.when(step == 0)
    def _():
        z.late.d_down_next.start()
        z.late.d_up_next.start()
        hand.clear()
        greet(h, n, hops)
        z.late.d_down_next.wait()
        down.start()
        z.late.d_up_next.wait()
        up.start()
        z.late.qkv_w.start()
        z.late.up_w.start()
        z.d_res[...] = jnp.zeros_like(z.d_res)

    @pl.when(step < count)
    def _():
        def middle_work():
            at_steps(
                step,
                (
                    (1, z.late.before.start),
                    (1, z.late.inverse.start),
                    (1, z.late.unit.start),
                    (2, z.late.ai.start),
                    (2, z.late.d_out_next.start),
                    (3, z.late.down_w.start),
                    (3, z.late.slope.start),
                    (1, lambda: up.batch(CREST_UP + 1)),
                    (1, lambda: up.batch(CREST_UP + 2)),
                    (2, lambda: up.batch(CREST_UP + 3)),
                    (2, z.late.before.wait),
                    (2, z.late.inverse.wait),
                    (2, z.late.unit.wait),
                    (3, lambda: up.batch(CREST_UP + 4)),
                ),
            )

        def end_work():
            at_steps(
                step,
                (
                    (0, lambda: down.batch(CREST_DOWN + 1)),
                    (0, lambda: down.batch(CREST_DOWN + 2)),
                    (1, lambda: down.batch(CREST_DOWN + 3)),
                    (2, lambda: down.batch(CREST_DOWN + 4)),
                ),
            )

            @pl.when(step >= 2)
            def _():
                sum_up(step - 2)

        back_step(z, l + 1, h, step, count, scatter, row_sum, middle_work, end_work)

    def feed(c):
        gather.ready(c)
        here = rows_at(c)
        for r, part in enumerate(gather.pieces(c)):
            z.grad[here, block_columns(h, r, width)] = part
        z.d_raised_out[here, :] = lower_feed(
            z.grad[here, :], z.down_w, z.slope.at[here, :], z.d_up_b, c == count - 1
        )

    def attention(c):
        here = rows_at(c)
        lower_attention(
            z.grad[here, :],
            z.out_w,
            z.ratio[here, :],
            z.att[here, :],
            z.qf_late[here, :],
            begin_keep(z.columns_late)[0][here, :],
            z.ones[...],
            (z.d_num_out.at[here, :], z.d_den_out.at[here, :]),
            z.summed,
            z.packed,
            c == count - 1,
        )

    def qkv_tiles(low, high):
        for i in range(low, high):
            weight_tile(i, z.ai, z.proj_all[...], z.d_qkv)

    @pl.when(step == count)
    def _():
        z.late.ai.wait()
        late_attention = (
            z.late.out_w,
            z.late.ratio,
            z.late.att,
            z.late.qf_late,
            z.late.columns_late,
        )
        for copy in late_attention:
            copy.start()
        z.late.act.start()
        qkv_tiles(0, 1)
        scatter.relay(0)
        row_sum.relay(0)
        gather.relay(count - 1)
        sum_up(count - 2)
        qkv_tiles(1, 4)
        z.late.d_out_next.wait()
        rest.start()
        z.sent.d_qkv.start()
        down.finish((z.sum_down,))
        z.late.down_w.wait()
        z.late.slope.wait()
        sum_up(count - 1)
        feed(jnp.int32(count - 1))
        gather.relay(count - 2)
        up.finish((z.sum_up,))
        feed(jnp.int32(count - 2))
        gather.relay(count - 3)
        for copy in late_attention:
            copy.wait()
        z.late.fi.start()
        z.late.att_low.start()
        loop(2, lambda i: attention(count - 1 - i))
        gather.relay(0)
        feed(jnp.int32(count - 3))
        attention(jnp.int32(count - 3))
        rest.batch(1)
        feed(jnp.int32(0))
        attention(jnp.int32(0))
        z.packed[0:FEATURES, :] = pack_state(z.summed[...])
        hand.start()
        rest.batch(2)
        z.sent.d_raised_out.start()
        z.sent.d_num_out.start()
        z.sent.d_den_out.start()
        z.late.act.wait()
        loop(D // CHUNK, lambda i: weight_tile(i, z.grad, z.act[...], z.d_down))
        new_down.start()
        z.sent.d_down.start()
        rest.batch(3)
        z.late.fi.wait()
        loop(D // CHUNK, lambda i: weight_tile(i, z.fi, z.d_raised_out[...], z.d_up))
        new_up.start()
        z.sent.d_up.start()
        z.late.att_low.wait()
        rest.batch(4)
        new_down.batch(1)
        loop(D // CHUNK, lambda i: weight_tile(i, z.grad, z.att_low[...], z.d_out))
        for i in range(count):
            gather.finish(i)
            scatter.finish(i)
            row_sum.finish(i)
        z.exit_out[...] = hand.total(z.lengths)
        new_up.pause((z.up_fore, z.up_aft))
        rest.pause((z.rest_a, z.rest_b, z.rest_c, z.rest_d))
        new_down.pause((z.new_fore, z.new_aft))
        for copy in every(z.sent):
            copy.wait()


def rest_of(qkv, out):
    return halved(0, qkv) + halved(1, out)


def turn(
    n, hops, l, lengths, local, top, before, ai, lower_in, tables, params, consts
):
    gain, bias, qkv_w, qkv_b, feats, up_w, up_b, out_w, down_w, res_b = params
    cos, sin, columns = tables
    act, slope, ratio, att, att_low, fi, qf = lower_in
    rows, a = qf.shape
    hidden = up_w.shape[2]
    count = rows // CHUNK
    width = D // 4
    share = D // n
    lowered = (top["d_raised"], top["d_num"], top["d_den"])
    parts = halved(0, hidden)
    rest_parts = rest_of(3 * a, a)

    def whole(array):
        return (array, fixed(array.shape))

    ins = dict(
        lengths=(lengths, pl.BlockSpec(memory_space=pltpu.SMEM)),
        **back_arrays(l + 1, local, lowered, tables, params, consts, top["exit_state"], count),
        down_fore=whole(top["down_fore"]),
        down_aft=whole(top["down_aft"]),
        up_fore_in=whole(top["up_fore"]),
        up_aft_in=whole(top["up_aft"]),
    )
    late = dict(
        d_down_next=top["d_down"],
        d_up_next=top["d_up"],
        qkv_w=(qkv_w, l + 1),
        up_w=(up_w, l + 1),
        before=before,
        inverse=local[6],
        unit=local[5],
        ai=ai,
        d_out_next=top["d_out"],
        down_w=(down_w, l),
        slope=slope,
        out_w=(out_w, l),
        ratio=ratio,
        att=att,
        qf_late=qf,
        columns_late=columns,
        act=act,
        fi=fi,
        att_low=att_low,
    )
    rests = ring_out(n, rest_parts)
    fore, aft = ring_out(n, parts)
    outs = dict(
        d_feat=(struct((1, a), F32), full((1, a))),
        d_qkv_b=(struct((1, 3 * a), F32), full((1, 3 * a))),
        sums=(struct((8, D), F32), full((8, D))),
        after=(struct((rows, width), F32), full((rows, width))),
        d_res=(struct((1, width), F32), full((1, width))),
        d_up_b=(struct((1, hidden), F32), full((1, hidden))),
        d_out=(struct((D, a), BF), full((D, a))),
        exit_out=(struct((STATE_ROWS, a), F32), full((STATE_ROWS, a))),
        sum_down=(struct((share, hidden), F32), full((share, hidden))),
        sum_up=(struct((share, hidden), F32), full((share, hidden))),
        rest_a=(rests[0], full(rests[0].shape)),
        rest_b=(rests[1], full(rests[1].shape)),
        rest_c=(rests[2], full(rests[2].shape)),
        rest_d=(rests[3], full(rests[3].shape)),
        new_fore=(fore, full(fore.shape)),
        new_aft=(aft, full(aft.shape)),
        up_fore=(fore, full(fore.shape)),
        up_aft=(aft, full(aft.shape)),
    )
    scratch = dict(
        **back_scratch(rows, a, width),
        gather=Gather.scratch(rows, width),
        hand=HandOver.scratch(hops, a),
        down_held=Ring.buffers(n, parts, CREST_DOWN),
        up_held=Ring.buffers(n, parts, CREST_UP),
        rest_held=Ring.buffers(n, rest_parts, 0, TURN_REST),
        new_down_held=Ring.buffers(n, parts, 0, TURN_DOWN),
        new_up_held=Ring.buffers(n, parts, 0, TURN_UP),
        down_sems=Ring.sems(n, parts),
        up_sems=Ring.sems(n, parts),
        rest_sems=Ring.sems(n, rest_parts),
        new_down_sems=Ring.sems(n, parts),
        new_up_sems=Ring.sems(n, parts),
        mine=[pltpu.VMEM((rows, width), BF)],
        packed=[pltpu.VMEM((STATE_ROWS, a), F32)],
        summed=[pltpu.VMEM((a, a), F32)],
        grad=[pltpu.VMEM((rows, D), BF)],
    )
    return named_call(
        functools.partial(turn_kernel, n, hops, l),
        "turn",
        5,
        (count + 1,),
        ins,
        outs,
        scratch,
        2 * rows * D * (hidden * 4 + 8 * a) * 2,
        late,
        dict(
            d_qkv=struct((D, 3 * a), BF),
            d_num_out=struct((rows, a), BF),
            d_den_out=struct((rows, a), F32),
            d_raised_out=(struct((rows, hidden), BF), "slope"),
            d_down=struct((D, hidden), BF),
            d_up=struct((D, hidden), BF),
        ),
    )


class Small:
    def __init__(self, h, n, refs, sems):
        self.near, self.far, self.got, self.middle, self.across, self.bundle, self.other = refs
        self.head_send, self.head_recv, self.seq_send, self.seq_recv = sems
        self.h, self.n = h, n
        self.here = lax.axis_index("seq")

    @staticmethod
    def rounds(n):
        return max(1, (n - 1).bit_length())

    @staticmethod
    def scratch(n, width):
        r = Small.rounds(n)
        dma = pltpu.SemaphoreType.DMA
        return (
            [pltpu.VMEM((2, 16, width), F32)] * 3
            + [pltpu.VMEM((16, width), F32)] * 2
            + [pltpu.VMEM((r + 1, 32, width), F32), pltpu.VMEM((r, 32, width), F32)]
            + [dma((2,)), dma((2,)), dma((r,)), dma((r,))]
        )

    def head_copy(self, kind):
        source, target, mask = (
            (self.far, self.got, 1),
            (self.middle, self.across, 2),
        )[kind]
        return push(
            source,
            target,
            self.head_send.at[kind],
            self.head_recv.at[kind],
            {"head": lax.bitwise_xor(self.h, mask)},
        )

    def seq_copy(self, k):
        return push(
            self.bundle.at[k],
            self.other.at[k],
            self.seq_send.at[k],
            self.seq_recv.at[k],
            {"seq": lax.bitwise_xor(self.here, 1 << k)},
        )

    def put(self, sums):
        width = self.near.shape[2]
        for l, ref in enumerate(sums):
            at = slice(8 * l, 8 * l + 8)
            self.near[0, at, :] = ref[:, block_columns(self.h, 0, width)]
            self.near[1, at, :] = ref[:, block_columns(self.h, 2, width)]
            self.far[0, at, :] = ref[:, block_columns(self.h, 1, width)]
            self.far[1, at, :] = ref[:, block_columns(self.h, 3, width)]
        self.head_copy(0).start()

    def relay(self):
        self.head_copy(0).wait_recv()
        self.middle[...] = self.near[1] + self.got[1]
        self.head_copy(1).start()

    def pack(self, rows):
        self.head_copy(1).wait_recv()
        norms = self.near[0] + self.got[0] + self.across[...]
        width = self.near.shape[2]
        self.bundle[0] = jnp.zeros_like(self.bundle[0])
        for l, refs in enumerate(rows):
            self.bundle[0, 16 * l : 16 * l + 4, :] = norms[8 * l : 8 * l + 4]
            at = 16 * l + 4
            for ref in refs:
                for i in range(ref.shape[1] // width):
                    self.bundle[0, at : at + 1, :] = ref[:, i * width : (i + 1) * width]
                    at += 1
        self.seq_copy(0).start()

    def round(self, k):
        self.seq_copy(k).wait_recv()
        self.bundle[k + 1] = self.bundle[k] + self.other[k]
        if k + 1 < self.rounds(self.n):
            self.seq_copy(k + 1).start()

    def finish(self):
        for kind in range(2):
            self.head_copy(kind).wait_send()
        for k in range(self.rounds(self.n)):
            self.seq_copy(k).wait_send()


def greet_all(h, n):
    barrier = pltpu.get_barrier_semaphore()

    def signal(where):
        pl.semaphore_signal(barrier, inc=1, device_id=where, device_id_type=pl.DeviceIdType.MESH)

    signal({"head": lax.bitwise_xor(h, 1)})
    signal({"head": lax.bitwise_xor(h, 2)})
    here = lax.axis_index("seq")
    place = ring_place(here, n)
    signal({"seq": ring_index(lax.rem(place + 1, n), n)})
    signal({"seq": ring_index(lax.rem(place + n - 1, n), n)})
    rounds = Small.rounds(n)
    for k in range(rounds):
        signal({"seq": lax.bitwise_xor(here, 1 << k)})
    pl.semaphore_wait(barrier, 4 + rounds)


def place_small(z, rows):
    width = rows.shape[1]
    for l in range(LAYERS):
        at = 16 * l
        z.d_gain_sum[l] = rows[at : at + 2, :]
        z.d_bias_sum[l] = rows[at + 2 : at + 4, :]
        at += 4
        for out in (z.d_qkv_b_sum, z.d_up_b_sum, z.d_feat_sum, z.d_res_sum):
            for i in range(out.shape[1] // width):
                out[l : l + 1, i * width : (i + 1) * width] = rows[at : at + 1, :]
                at += 1


def leave_kernel(n, z):
    step = pl.program_id(0)
    h = lax.axis_index("head")
    rows = z.proj_all.shape[0]
    count = rows // CHUNK
    hidden, a = z.d_down.shape[1], z.d_out.shape[1]
    scatter = Scatter(h, z.scatter[:5], z.scatter[5:])
    row_sum = RowSum(h, z.row_sum[:4], z.row_sum[4:])
    small = Small(h, n, z.small[:7], z.small[7:])
    rest = Ring(
        n, rest_of(3 * a, a), (z.d_qkv_next, z.d_out_next), z.rest_held, z.rest_sems, TURN_REST,
        incoming=(z.rest_a, z.rest_b, z.rest_c, z.rest_d),
    )
    down = Ring(
        n, halved(0, hidden), (z.d_down,), z.down_held, z.down_sems, TURN_DOWN,
        incoming=(z.new_fore, z.new_aft),
    )
    up = Ring(
        n, halved(0, hidden), (z.d_up,), z.up_held, z.up_sems, TURN_UP,
        incoming=(z.up_fore, z.up_aft),
    )
    out = Ring(n, halved(0, a), (z.d_out,), z.out_held, z.out_sems)
    first_parts, second_parts = split_last(3 * a)
    last = Ring(n, first_parts, (z.d_qkv,), z.last_held, z.last_sems)
    more = Ring(n, second_parts, (z.d_qkv,), z.more_held, z.more_sems)
    width = z.res_b.shape[1] // 4
    columns = pl.ds(pl.multiple_of(h * width, width), width)
    result = Scatter(h, (z.near, z.far) + tuple(z.result[:3]), z.result[3:])

    def sum_up(o):
        here = rows_at(count - 1 - o)
        z.after[here, :] = norm_back(
            z.before[here, :],
            z.inverse[here, 0:1],
            z.unit[here, :],
            scatter.total(count - 1 - o),
            row_sum.total(count - 1 - o),
        )

    @pl.when(step == 0)
    def _():
        z.late.d_qkv_next.start()
        z.late.d_down.start()
        z.late.d_up.start()
        greet_all(h, n)
        z.late.d_qkv_next.wait()
        rest.start()
        z.late.d_down.wait()
        down.start()
        z.late.d_up.wait()
        up.start()
        out.start()
        z.late.qkv_w.start()
        z.late.up_w.start()

    @pl.when(step < count)
    def _():
        def middle_work():
            at_steps(
                step,
                (
                    (1, z.late.before.start),
                    (1, z.late.inverse.start),
                    (1, z.late.unit.start),
                    (1, z.late.near.start),
                    (1, z.late.far.start),
                    (2, z.late.ai.start),
                    (3, z.late.own.start),
                    (1, lambda: down.batch(TURN_DOWN + 1)),
                    (1, lambda: down.batch(TURN_DOWN + 2)),
                    (2, lambda: rest.batch(TURN_REST + 2)),
                    (2, z.late.before.wait),
                    (2, z.late.inverse.wait),
                    (2, z.late.unit.wait),
                    (3, lambda: up.batch(TURN_UP + 3)),
                ),
            )

        def end_work():
            at_steps(
                step,
                (
                    (0, lambda: rest.batch(TURN_REST + 1)),
                    (1, lambda: up.batch(TURN_UP + 1)),
                    (1, lambda: up.batch(TURN_UP + 2)),
                    (1, lambda: out.batch(1)),
                    (2, z.late.near.wait),
                    (2, z.late.far.wait),
                    (2, lambda: loop(count, lambda i: result.copy(0, i).start())),
                    (3, lambda: loop(count, result.relay)),
                    (2, lambda: down.batch(TURN_DOWN + 3)),
                    (3, lambda: out.batch(2)),
                ),
            )

            @pl.when(step >= 2)
            def _():
                sum_up(step - 2)

        back_step(z, 0, h, step, count, scatter, row_sum, middle_work, end_work)

    @pl.when(step == count)
    def _():
        scatter.relay(0)
        row_sum.relay(0)
        small.put((z.sums, z.sums_next))
        z.late.ai.wait()
        loop(D // CHUNK, lambda i: weight_tile(i, z.ai, z.proj_all[...], z.d_qkv))
        last.start()
        more.start()
        rest.finish((z.sum_qkv_next, z.sum_out_next))
        down.batch(TURN_DOWN + 4)
        sum_up(2)
        small.relay()
        last.batch(1)
        more.batch(1)
        up.batch(TURN_UP + 4)
        out.batch(3)
        sum_up(3)
        small.pack(
            (
                (z.d_qkv_b, z.d_up_b, z.d_feat[...] / feature_row(z.feats, 0), z.d_res),
                (
                    z.d_qkv_b_next,
                    z.d_up_b_next,
                    z.d_feat_next[...] / feature_row(z.feats, 1),
                    z.d_res_next,
                ),
            )
        )
        last.batch(2)
        more.batch(2)
        down.batch(6)
        out.batch(4)
        small.round(0)
        last.batch(3)
        more.batch(3)
        up.batch(5)
        last.batch(4)
        more.batch(4)
        small.round(1)
        down.finish((z.sum_down,))
        out.batch(5)
        last.batch(5)
        more.batch(5)
        up.batch(6)
        for k in range(2, Small.rounds(n)):
            small.round(k)
        z.late.own.wait()

        def place(i):
            here = rows_at(i)
            z.out[here, :] = z.own[here, :] + result.total(i) + z.res_b[1:2, columns]

        loop(count, place)
        last.batch(6)
        more.batch(6)
        out.batch(6)
        place_small(z, small.bundle.at[Small.rounds(n)])
        small.finish()
        for i in range(count):
            scatter.finish(i)
            row_sum.finish(i)
            result.finish(i)
        up.finish((z.sum_up,))
        last.finish((z.sum_qkv,))
        more.finish((z.sum_qkv,))
        out.finish((z.sum_out,))


def split_last(width):
    third = width // 3
    half = third // 2
    return (
        ((0, 0, third, 1), (0, third, half, -1)),
        ((0, third + half, half, 1), (0, 2 * third, third, -1)),
    )


def leave(n, local, turned, top, before, ai, own, tables, params, consts):
    qf = local[0]
    rows, a = qf.shape
    lowered = (turned["d_raised_out"], turned["d_num_out"], turned["d_den_out"])
    hidden = lowered[0].shape[1]
    count = rows // CHUNK
    width = D // 4
    share = D // n
    rest_parts, wide_parts = rest_of(3 * a, a), halved(0, hidden)
    out_parts = halved(0, a)
    first_parts, second_parts = split_last(3 * a)

    def whole(array):
        return (array, fixed(array.shape))

    ins = dict(
        **back_arrays(0, local, lowered, tables, params, consts, turned["exit_out"], count),
        d_out_next=whole(top["d_out"]),
        d_out=whole(turned["d_out"]),
        new_fore=whole(turned["new_fore"]),
        new_aft=whole(turned["new_aft"]),
        up_fore=whole(turned["up_fore"]),
        up_aft=whole(turned["up_aft"]),
        res_b=whole(params[9]),
        feats=whole(params[4]),
        rest_a=whole(turned["rest_a"]),
        rest_b=whole(turned["rest_b"]),
        rest_c=whole(turned["rest_c"]),
        rest_d=whole(turned["rest_d"]),
        d_up_b=whole(turned["d_up_b"]),
        d_res=whole(turned["d_res"]),
        sums_next=whole(turned["sums"]),
        d_qkv_b_next=whole(turned["d_qkv_b"]),
        d_up_b_next=whole(top["d_up_b"]),
        d_feat_next=whole(turned["d_feat"]),
        d_res_next=whole(top["d_res"]),
    )
    gain, bias, qkv_w, qkv_b, feats, up_w, up_b, out_w, down_w, res_b = params
    late = dict(
        d_qkv_next=turned["d_qkv"],
        d_down=turned["d_down"],
        d_up=turned["d_up"],
        qkv_w=(qkv_w, 0),
        up_w=(up_w, 0),
        before=before,
        inverse=local[6],
        unit=local[5],
        ai=ai,
        near=top["near"],
        far=top["far"],
        own=own,
    )

    def result(shape):
        return (struct(shape, F32), full(shape))

    outs = dict(
        after=result((rows, width)),
        out=result((rows, width)),
        d_gain_sum=result((LAYERS, 2, width)),
        d_bias_sum=result((LAYERS, 2, width)),
        d_qkv_b_sum=result((LAYERS, 3 * a)),
        d_up_b_sum=result((LAYERS, hidden)),
        d_feat_sum=result((LAYERS, a)),
        d_res_sum=result((LAYERS, width)),
        sum_qkv_next=result((share, 3 * a)),
        sum_out_next=result((share, a)),
        sum_qkv=result((share, 3 * a)),
        sum_out=result((share, a)),
        sum_down=result((share, hidden)),
        sum_up=result((share, hidden)),
    )
    scratch = dict(
        **back_scratch(rows, a, width),
        small=Small.scratch(n, width),
        rest_held=Ring.buffers(n, rest_parts, TURN_REST),
        down_held=Ring.buffers(n, wide_parts, TURN_DOWN),
        up_held=Ring.buffers(n, wide_parts, TURN_UP),
        out_held=Ring.buffers(n, out_parts),
        last_held=Ring.buffers(n, first_parts),
        more_held=Ring.buffers(n, second_parts),
        result=Scatter.scratch(rows, width)[2:],
        rest_sems=Ring.sems(n, rest_parts),
        down_sems=Ring.sems(n, wide_parts),
        up_sems=Ring.sems(n, wide_parts),
        out_sems=Ring.sems(n, out_parts),
        last_sems=Ring.sems(n, first_parts),
        more_sems=Ring.sems(n, second_parts),
        d_qkv=[pltpu.VMEM((D, 3 * a), BF)],
        d_feat=[pltpu.VMEM((1, a), F32)],
        d_qkv_b=[pltpu.VMEM((1, 3 * a), F32)],
        sums=[pltpu.VMEM((8, D), F32)],
    )
    return named_call(
        functools.partial(leave_kernel, n),
        "leave",
        6,
        (count + 1,),
        ins,
        outs,
        scratch,
        2 * rows * D * (hidden + 8 * a) * 3,
        late,
    )


def on_device(
    acts,
    cotangent,
    lengths,
    keep_mask,
    ln_gain,
    ln_bias,
    qkv_w,
    qkv_b,
    feat_w,
    out_w,
    up_w,
    up_b,
    down_w,
    res_b,
):
    rows, width = acts.shape
    heads = feat_w.shape[1]
    a = heads * HEAD_DIM
    n = lax.axis_size("seq")
    tokens = rows * n
    longest = 2048 if tokens <= 8192 else 4096
    hops = -(-longest // rows)
    h = lax.axis_index("head").astype(jnp.int32)
    first = lax.axis_index("seq") * rows

    keep_rows = keep_mask.reshape(rows // 128, 128)
    half = ROT // 2
    rates = np.zeros((2, HEAD_DIM))
    rates[0, :half] = ROTARY_BASE ** (-2.0 * np.arange(half) / ROT)
    rates[0, half:ROT] = rates[0, :half]
    rates[1, :half] = -1.0
    rates[1, half:ROT] = 1.0
    rates = jnp.asarray(np.tile(rates, (1, 2)), F32)

    fold = sample_points(FEATURES, HEAD_DIM) @ cosine_table(HEAD_DIM) / math.sqrt(HEAD_DIM)
    eye = np.eye(heads)
    consts = {
        "map": jnp.asarray(np.kron(eye, fold), F32),
        "map_t": jnp.asarray(np.kron(eye, fold.T), F32),
        "ones": jnp.asarray(np.kron(eye, np.ones((HEAD_DIM, HEAD_DIM))), BF),
    }

    entered = enter(
        n, lengths, acts, keep_rows, ln_gain, ln_bias, qkv_w, qkv_b, feat_w, rates, consts
    )
    tables = (entered["cos"], entered["sin"], entered["columns"])
    params = (ln_gain, ln_bias, qkv_w, qkv_b, feat_w, up_w, up_b, out_w, down_w, res_b)

    def back_local(made, states, totals):
        ai, fi, normed, unit, inverse, qf, kf, v, k = made
        return (qf, kf, v, k, normed, unit, inverse, states, totals)

    first_made = tuple(entered[name] for name, width_of, kind in PROJECT_KINDS)
    mid = between(n, hops, 0, lengths, entered, cotangent, params, consts)
    pieces = (cotangent, mid["grad_beside"], mid["grad_across"])
    local = back_local(first_made, mid["states"], mid["totals"])
    made = tuple(mid[name] for name, width_of, kind in PROJECT_KINDS)
    lower_in = (
        mid["act"], mid["slope"], mid["ratio"], mid["att"], mid["att_low"], entered["fi"],
        entered["qf"],
    )
    top = crest(n, hops, 1, lengths, mid, pieces, tables, params, consts)
    turned = turn(
        n,
        hops,
        0,
        lengths,
        back_local(made, top["states"], top["totals"]),
        top,
        cotangent,
        made[0],
        lower_in,
        tables,
        params,
        consts,
    )
    left = leave(n, local, turned, top, turned["after"], first_made[0], mid["own"], tables, params, consts)
    return (
        left["out"],
        left["after"],
        jnp.stack([left["sum_qkv"], left["sum_qkv_next"]]),
        jnp.stack([left["sum_out"], left["sum_out_next"]]),
        jnp.stack([left["sum_up"], turned["sum_up"]]),
        jnp.stack([left["sum_down"], turned["sum_down"]]),
        left["d_qkv_b_sum"],
        left["d_up_b_sum"],
        left["d_feat_sum"].reshape(LAYERS, heads, FEATURES),
        left["d_gain_sum"],
        left["d_bias_sum"],
        left["d_res_sum"],
    )


def solution(mesh):
    return jax.shard_map(
        on_device,
        mesh=mesh,
        in_specs=(
            P("seq", "head"),
            P("seq", "head"),
            P(),
            P("seq"),
            P(),
            P(),
            P(None, None, "head"),
            P(None, "head"),
            P(None, "head", None),
            P(None, None, "head"),
            P(None, None, "head"),
            P(None, "head"),
            P(None, None, "head"),
            P(),
        ),
        out_specs=(
            P("seq", "head"),
            P("seq", "head"),
            P(None, "seq", "head"),
            P(None, "seq", "head"),
            P(None, "seq", "head"),
            P(None, "seq", "head"),
            P(None, "head"),
            P(None, "head"),
            P(None, "head", None),
            P(None, None, "head"),
            P(None, None, "head"),
            P(None, "head"),
        ),
        check_vma=False,
    )
```
